32 devices in a mesh: pipe: 2 (over x), dp: 4 (over y, core), tensor: 4 (over z).
Axes of the slice: x: 2, y: 2, z: 4, core: 2. Of those that a mesh axis runs over, the one named last changes fastest.
Arguments:
- tokens_in: bfloat16 [12, 1024, 1536], P('dp', 'tensor'), may hold values from -6 to 6
- cotangent: bfloat16 [12, 1024, 1536], P('dp', 'tensor'), may hold values from -6 to 6
- lengths: int32 [12], P('dp'), may hold values from 512 to 1024, as said below
- in_gate: bfloat16 [2, 1536, 3072], P('pipe', 'dp', 'tensor'), may hold values from -0.15625 to 0.15625
- in_value: bfloat16 [2, 1536, 3072], P('pipe', 'dp', 'tensor'), may hold values from -0.15625 to 0.15625
- in_state: bfloat16 [2, 1536, 256], P('pipe', 'dp'), may hold values from -0.15625 to 0.15625
- in_step: bfloat16 [2, 1536, 48], P('pipe', 'dp', 'tensor'), may hold values from -0.15625 to 0.15625
- out_proj: bfloat16 [2, 1536, 3072], P('pipe', 'dp', 'tensor'), may hold values from -0.109375 to 0.109375
- norm_gain: float32 [2, 1536], P('pipe'), may hold values from 0.5 to 1.5
- conv_value: float32 [2, 4, 3072], P('pipe', None, 'tensor'), may hold values from -3 to 3
- conv_state: float32 [2, 4, 256], P('pipe'), may hold values from -3 to 3
- bias_value: float32 [2, 3072], P('pipe', 'tensor'), may hold values from -1.5 to 1.5
- bias_state: float32 [2, 256], P('pipe'), may hold values from -1.5 to 1.5
- step_bias: float32 [2, 48], P('pipe', 'tensor'), may hold values from -7 to -2.2
- decay_log: float32 [2, 48], P('pipe', 'tensor'), may hold values from 0 to 2.77
- skip_gain: float32 [2, 48], P('pipe', 'tensor'), may hold values from 0.5 to 1.5
- gate_gain: float32 [2, 3072], P('pipe', 'tensor'), may hold values from 0.5 to 1.5
Outputs:
- outputs_both: bfloat16 [2, 12, 1024, 1536], P('pipe', 'dp', 'tensor')
- input_grads: bfloat16 [2, 12, 1024, 1536], P('pipe', 'dp', 'tensor')
- grad_in_gate: float32 [2, 1536, 3072], P('pipe', 'dp', 'tensor')
- grad_in_value: float32 [2, 1536, 3072], P('pipe', 'dp', 'tensor')
- grad_in_state: float32 [2, 1536, 256], P('pipe', None, ('dp', 'tensor'))
- grad_in_step: float32 [2, 1536, 48], P('pipe', 'dp', 'tensor')
- grad_out_proj: float32 [2, 1536, 3072], P('pipe', 'dp', 'tensor')
- grad_norm_gain: float32 [2, 1536], P('pipe', ('dp', 'tensor'))
- grad_conv_value: float32 [2, 4, 3072], P('pipe', None, 'tensor')
- grad_conv_state: float32 [2, 4, 256], P('pipe', None, ('dp', 'tensor'))
- grad_bias_value: float32 [2, 3072], P('pipe', 'tensor')
- grad_bias_state: float32 [2, 256], P('pipe', ('dp', 'tensor'))
- grad_step_bias: float32 [2, 48], P('pipe', 'tensor')
- grad_decay_log: float32 [2, 48], P('pipe', 'tensor')
- grad_skip_gain: float32 [2, 48], P('pipe', 'tensor')
- grad_gate_gain: float32 [2, 3072], P('pipe', 'tensor')
The draws below stay inside these ranges and needn't reach their ends.
Inputs may be any that keep to these rules, and one draw needn't show every extreme that they name: `lengths`: in each group of 3 consecutive sequences one, drawn from the seed, has all 1024 positions valid.
All inputs are finite; a program needn't handle non-finite values.
Results may differ from the reference program's by a relative error of at most 0.03.
Values may be sent and summed in bfloat16 or wider, within the bound.
A program may use at most 320 MiB of HBM per device.

```python
import jax
import jax.numpy as jnp
from jax import lax

D = 1536
H = 48
N = 128
CONV = 4
SPAN = 256
MICRO = 3
DI = 3072
SEQ_LEN = 1024
SEQS = 12


def draw_lengths(key, part):
    key = jax.random.fold_in(key, 11)
    key_len, key_pick = jax.random.split(key)
    drawn = jax.random.randint(key_len, (SEQS,), SEQ_LEN // 2, SEQ_LEN + 1)
    chosen = jax.random.randint(key_pick, (SEQS // MICRO,), 0, MICRO)
    group_pos = jnp.arange(SEQS) % MICRO
    group_ids = jnp.arange(SEQS) // MICRO
    full_rows = group_pos == chosen[group_ids]
    return jnp.where(full_rows, SEQ_LEN, drawn).astype(jnp.int32)


def block_scale(own_key, extent, cuts, smallest, high):
    def one(position, parts):
        heights = jax.random.uniform(jax.random.fold_in(jax.random.fold_in(own_key, 6), position), (parts,), jnp.float32, smallest / len(cuts), high / len(cuts))
        return jnp.repeat(jnp.exp(heights), extent[position] // parts).reshape((-1,) + (1,) * (len(extent) - position - 1))

    level = one(*cuts[0])
    for cut in cuts[1:]:
        level = level * one(*cut)
    return level


def gaussian(own_key, shape, width, limit, cuts=(), kind=jnp.bfloat16):
    values = width * jax.random.normal(own_key, shape, jnp.float32)
    if cuts:
        values = values * block_scale(own_key, shape, cuts, -0.22, 0.18)
    return jnp.clip(values, -limit, limit).astype(kind)


def setup_inputs(seed: int = 0) -> dict:
    key_list = jax.random.split(jax.random.key(seed), 18)
    tokens_in = gaussian(key_list[0], (SEQS, SEQ_LEN, D), 1.0, 6.0, ((0, 4), (1, 4)))
    cotangent = gaussian(key_list[1], (SEQS, SEQ_LEN, D), 1.0, 6.0, ((0, 4), (1, 4)))
    lengths = draw_lengths(jax.random.fold_in(key_list[17], 71), 0)
    in_gate = gaussian(key_list[3], (2, D, DI), D ** -0.5, 0.15625, ((0, 2), (1, 4), (2, 4)))
    in_value = gaussian(key_list[4], (2, D, DI), D ** -0.5, 0.15625, ((0, 2), (1, 4), (2, 4)))
    in_state = gaussian(key_list[5], (2, D, 2 * N), D ** -0.5, 0.15625, ((0, 2), (1, 4)))
    in_step = gaussian(key_list[6], (2, D, H), D ** -0.5, 0.15625, ((0, 2), (1, 4), (2, 4)))
    out_proj = gaussian(key_list[7], (2, D, DI), DI ** -0.5, 0.109375, ((0, 2), (1, 4), (2, 4)))
    norm_gain = jnp.clip(1.0 + 0.1 * jax.random.normal(key_list[8], (2, D), jnp.float32), 0.5, 1.5)
    conv_value = gaussian(key_list[9], (2, CONV, DI), CONV ** -0.5, 3.0, ((0, 2), (2, 4)), jnp.float32)
    conv_state = gaussian(key_list[10], (2, CONV, 2 * N), CONV ** -0.5, 3.0, ((0, 2),), jnp.float32)
    bias_value = gaussian(key_list[11], (2, DI), 0.3, 1.5, ((0, 2), (1, 4)), jnp.float32)
    bias_state = gaussian(key_list[12], (2, 2 * N), 0.3, 1.5, ((0, 2),), jnp.float32)
    step_bias = jnp.clip(-7.0 + 4.8 * jax.random.uniform(key_list[13], (2, H), jnp.float32) ** block_scale(key_list[13], (2, H), ((0, 2), (1, 4)), -0.2, 0.2), -7.0, -2.2)
    decay_log = jnp.clip(2.77 * jax.random.uniform(key_list[14], (2, H), jnp.float32) ** block_scale(key_list[14], (2, H), ((0, 2), (1, 4)), -0.2, 0.2), 0.0, 2.77)
    skip_gain = jnp.clip(1.0 + 0.1 * jax.random.normal(key_list[15], (2, H), jnp.float32), 0.5, 1.5)
    gate_gain = jnp.clip(1.0 + 0.1 * jax.random.normal(key_list[16], (2, DI), jnp.float32), 0.5, 1.5)
    return dict(tokens_in=tokens_in, cotangent=cotangent, lengths=lengths, in_gate=in_gate, in_value=in_value, in_state=in_state, in_step=in_step, out_proj=out_proj, norm_gain=norm_gain, conv_value=conv_value, conv_state=conv_state, bias_value=bias_value, bias_state=bias_state, step_bias=step_bias, decay_log=decay_log, skip_gain=skip_gain, gate_gain=gate_gain)


EPS = 1e-05
HIGHEST = lax.Precision.HIGHEST

@jax.custom_vjp
def low(v):
    return lax.optimization_barrier(v.astype(jnp.bfloat16)).astype(jnp.float32)

@jax.custom_vjp
def low_back(v):
    return v

def low_keep(v):
    return (low(v), None)

def low_pass(kept, grad):
    return (grad,)

def back_keep(v):
    return (v, None)

def back_low(kept, grad):
    return (low(grad),)
low.defvjp(low_keep, low_pass)
low_back.defvjp(back_keep, back_low)

def causal_conv(values, taps, offsets):
    length = values.shape[0]
    tap_count = taps.shape[0]
    padded = jnp.concatenate([jnp.zeros((tap_count - 1, values.shape[1]), values.dtype), values], axis=0)
    summed = offsets[None, :] + jnp.zeros_like(values)
    for shift_idx in range(tap_count):
        summed = summed + taps[shift_idx][None, :] * padded[shift_idx:shift_idx + length]
    return jax.nn.silu(summed)

def ssd_block(carry_state, pieces):
    head_values, step_size, log_decay, in_mat, out_mat = pieces
    cumulated = jnp.cumsum(log_decay, axis=0)
    block_len = log_decay.shape[0]
    lower_mask = (jnp.arange(block_len)[:, None] >= jnp.arange(block_len)[None, :])[:, :, None]
    spread = cumulated[:, None, :] - cumulated[None, :, :]
    decay_mat = jnp.where(lower_mask, jnp.exp(jnp.where(lower_mask, spread, 0.0)), 0.0)
    scores = jnp.dot(out_mat, in_mat.T, precision=HIGHEST)
    mixing = decay_mat * scores[:, :, None] * step_size[None, :, :]
    within = jnp.einsum('ijh,jhp->ihp', mixing, head_values, precision=HIGHEST)
    carried = jnp.einsum('hpn,in->ihp', carry_state, out_mat, precision=HIGHEST) * jnp.exp(cumulated)[:, :, None]
    remain = jnp.exp(cumulated[-1][None, :] - cumulated) * step_size
    new_state = jnp.exp(cumulated[-1])[:, None, None] * carry_state + jnp.einsum('jh,jhp,jn->hpn', remain, head_values, in_mat, precision=HIGHEST)
    return (new_state, within + carried)

def ssd_scan(head_values, step_size, log_decay, in_mat, out_mat):
    length, head_count, head_dim = head_values.shape
    block_count = length // SPAN
    start_state = jnp.zeros((head_count, head_dim, in_mat.shape[1]), head_values.dtype)
    pieces = (head_values.reshape(block_count, SPAN, head_count, head_dim), step_size.reshape(block_count, SPAN, head_count), log_decay.reshape(block_count, SPAN, head_count), in_mat.reshape(block_count, SPAN, -1), out_mat.reshape(block_count, SPAN, -1))
    final_state, result = lax.scan(jax.checkpoint(ssd_block), start_state, pieces)
    return result.reshape(length, head_count, head_dim)

def mixer(gate_pre, value_pre, state_pre, step_pre, conv_value, bias_value, conv_state, bias_state, step_bias, decay_log, skip_gain):
    length = gate_pre.shape[0]
    head_count = step_bias.shape[0]
    value_act = causal_conv(value_pre, conv_value, bias_value)
    state_act = causal_conv(state_pre, conv_state, bias_state)
    state_size = state_act.shape[1] // 2
    step_size = jax.nn.softplus(step_pre + step_bias[None, :])
    log_decay = -step_size * jnp.exp(decay_log)[None, :]
    head_values = value_act.reshape(length, head_count, -1)
    output = ssd_scan(head_values, step_size, log_decay, state_act[:, :state_size], state_act[:, state_size:])
    output = output + skip_gain[None, :, None] * head_values
    return output.reshape(length, -1) * jax.nn.silu(gate_pre)

def rms_scale(values, gain_vec):
    return values * lax.rsqrt(lax.optimization_barrier(jnp.mean(values * values, axis=-1, keepdims=True)) + EPS) * gain_vec

def layer(tokens, row_mask, weights):
    in_gate, in_value, in_state, in_step, out_proj, norm_gain, conv_value, conv_state, bias_value, bias_state, step_bias, decay_log, skip_gain, gate_gain = weights
    normed = low(rms_scale(tokens, norm_gain[None, :]))
    gate_pre = low_back(jnp.dot(normed, in_gate, precision=HIGHEST))
    value_pre = low_back(jnp.dot(normed, in_value, precision=HIGHEST))
    state_pre = low_back(jnp.dot(normed, in_state, precision=HIGHEST))
    step_pre = low_back(jnp.dot(normed, in_step, precision=HIGHEST))
    gated = mixer(gate_pre, value_pre, state_pre, step_pre, conv_value, bias_value, conv_state, bias_state, step_bias, decay_log, skip_gain)
    scaled = low(rms_scale(gated, gate_gain[None, :]))
    mixed = low_back(jnp.dot(scaled, out_proj.T, precision=HIGHEST))
    return row_mask[:, None] * (tokens + mixed)

def reference(tokens_in, cotangent, lengths, in_gate, in_value, in_state, in_step, out_proj, norm_gain, conv_value, conv_state, bias_value, bias_state, step_bias, decay_log, skip_gain, gate_gain):
    params = tuple((weight_arr.astype(jnp.float32) for weight_arr in (in_gate, in_value, in_state, in_step, out_proj, norm_gain, conv_value, conv_state, bias_value, bias_state, step_bias, decay_log, skip_gain, gate_gain)))
    positions = jnp.arange(SEQ_LEN).astype(jnp.int32)
    row_masks = (positions[None, :] < lengths[:, None]).astype(jnp.float32)
    inputs = tokens_in.astype(jnp.float32)
    probes = jnp.zeros_like(inputs)

    def forward(inputs, probes, params):
        first_layer = tuple((weight_arr[0] for weight_arr in params))
        second_layer = tuple((weight_arr[1] for weight_arr in params))

        def one_sequence(pieces):
            tokens, row_mask, probe_row = pieces
            early_out = layer(tokens, row_mask, first_layer)
            middle = low(low_back(early_out)) + probe_row
            return (layer(middle, row_mask, second_layer), early_out)
        late_out, early_out = lax.map(one_sequence, (inputs, row_masks, probes))
        return (late_out, early_out)
    late_out, backward, early_out = jax.vjp(forward, inputs, probes, params, has_aux=True)
    grad_inputs, grad_probes, grad_params = backward(cotangent.astype(jnp.float32))
    outputs_both = jnp.stack([early_out, late_out]).astype(jnp.bfloat16)
    input_grads = jnp.stack([grad_inputs, grad_probes]).astype(jnp.bfloat16)
    return (outputs_both, input_grads, grad_params[0], grad_params[1], grad_params[2], grad_params[3], grad_params[4], grad_params[5], grad_params[6], grad_params[7], grad_params[8], grad_params[9], grad_params[10], grad_params[11], grad_params[12], grad_params[13])
```

```python
import functools
import types

import jax
import jax.numpy as jnp
from jax import lax
from jax.experimental import pallas as pl
from jax.experimental.pallas import tpu as pltpu
from jax.sharding import PartitionSpec as P

EPS = 1e-05
PIPE, DP, TENSOR = "pipe", "dp", "tensor"
SEQUENTIAL = "arbitrary"
Bundle = types.SimpleNamespace
HIGHEST = lax.Precision.HIGHEST
BF = jnp.bfloat16
F32 = jnp.float32
HALO = 16
GC = 256
LANES = 128


def nn(a, b):
    return jnp.dot(a, b, preferred_element_type=F32)


def nt(a, b):
    return lax.dot_general(a, b, (((1,), (1,)), ((), ())), preferred_element_type=F32)


def tn(a, b):
    return lax.dot_general(a, b, (((0,), (0,)), ((), ())), preferred_element_type=F32)


def exact(a, b):
    return jnp.dot(a, b, precision=HIGHEST, preferred_element_type=F32)


def sigmoid(v):
    return 1.0 / (1.0 + jnp.exp(-v))


def iota(shape, dim):
    return lax.broadcasted_iota(jnp.int32, shape, dim)


def spread(per_head, width, head_dim):
    lane = iota(per_head.shape, 1)
    parts = []
    for pair in range(width // LANES):
        parts.append(
            jnp.where(lane < head_dim, per_head[:, 2 * pair : 2 * pair + 1], per_head[:, 2 * pair + 1 : 2 * pair + 2])
        )
    return jnp.concatenate(parts, axis=1)


def conv_rows(pre, taps, rows):
    total = taps[4:5, :] + taps[3:4, :] * pre[HALO : HALO + rows, :]
    for k in range(3):
        total = total + taps[k : k + 1, :] * pre[HALO - 3 + k : HALO - 3 + k + rows, :]
    return total


def conv_sums(grad, pre, rows):
    sums = [jnp.sum(grad * pre[HALO - 3 + k : HALO - 3 + k + rows, :], axis=0, keepdims=True) for k in range(4)]
    sums.append(jnp.sum(grad, axis=0, keepdims=True))
    return sums


def conv_transposed(grad, halo, taps, rows):
    ext = jnp.concatenate([grad, halo], axis=0)
    total = taps[3:4, :] * grad
    for k in range(3):
        total = total + taps[k : k + 1, :] * ext[3 - k : 3 - k + rows, :]
    return total


def silu_slope(v):
    s = sigmoid(v)
    return s * (1.0 + v * (1.0 - s))


def group_lanes(values, dst, groups, per_group):
    for g in range(groups):
        dst[g] = values if g == 0 else pltpu.roll(values, LANES - per_group * g, 1)


def group_rows(values, dst, groups, per_group):
    turned = values.T
    for g in range(groups):
        dst[g, 0:per_group, :] = turned[per_group * g : per_group * (g + 1), :]


def scan_front(
    head_dim, nx, wv, ws, wt, pv, ps, ph, vpre_o, spre_o, x_o, bc_o, dtc_o, yw_o, loc_o, sc_s, dt_s, cum_s, cumt_s
):
    g = pl.program_id(0)
    groups = pl.num_programs(0)
    rows = x_o.shape[0]
    state = bc_o.shape[1] // 2
    per_group = GC // head_dim

    @pl.when(g == 0)
    def _():
        spre = nn(nx[...], ws[...])
        spre_o[...] = spre
        conv = conv_rows(spre, ps, rows)
        bc = (conv * sigmoid(conv)).astype(BF)
        bc_o[...] = bc
        scores = nt(bc[:, state:], bc[:, :state])
        lower = iota((rows, rows), 0) >= iota((rows, rows), 1)
        sc_s[...] = jnp.where(lower, scores, 0.0)
        raw = nn(nx[HALO:, :], wt[...]) + ph[0:1, :]
        step = jnp.maximum(raw, 0.0) + jnp.log(1.0 + jnp.exp(-jnp.abs(raw)))
        decay = -step * jnp.exp(ph[1:2, :])
        cum = exact(lower.astype(F32), decay)
        dtc_o[0] = step
        dtc_o[1] = cum
        dtc_o[2] = sigmoid(raw)
        group_lanes(step, dt_s, dt_s.shape[0], per_group)
        group_lanes(cum, cum_s, cum_s.shape[0], per_group)
        group_rows(cum, cumt_s, cumt_s.shape[0], per_group)

    pre = nn(nx[...], wv[...])
    vpre_o[...] = pre
    conv = conv_rows(pre, pv, rows)
    x = conv * sigmoid(conv)
    x_o[...] = x.astype(BF)
    step, cum, cumt = dt_s[g], cum_s[g], cumt_s[g]
    to_end = jnp.exp(cum[rows - 1 : rows, :] - cum)
    xp = (x * spread(step, GC, head_dim)).astype(BF)
    xr = (x * spread(step * to_end, GC, head_dim)).astype(BF)
    loc_o[...] = tn(xr, bc_o[:, :state])
    scores = sc_s[...]
    lane = iota((rows, LANES), 1)
    for pair in range(GC // LANES):
        cols = slice(LANES * pair, LANES * (pair + 1))
        outs = []
        for i in (2 * pair, 2 * pair + 1):
            diff = cum[:, i : i + 1] - cumt[i : i + 1, :]
            mix = (jnp.exp(jnp.minimum(diff, 0.0)) * scores).astype(BF)
            outs.append(nn(mix, xp[:, cols]))
        yw_o[:, cols] = jnp.where(lane < head_dim, outs[0], outs[1]) + pv[6:7, cols] * x[:, cols]


def scan_finish(
    head_dim, nx, wg, wo, yw, s_in, bc, dtc, pv, gate_o, y_o, gg_o, p_o, sq_o, acc_s, sq_s, cum_s
):
    g = pl.program_id(0)
    rows = yw.shape[0]
    state = bc.shape[1] // 2

    @pl.when(g == 0)
    def _():
        group_lanes(dtc[1], cum_s, cum_s.shape[0], GC // head_dim)
        acc_s[...] = jnp.zeros_like(acc_s)
        sq_s[...] = jnp.zeros_like(sq_s)

    gate = nn(nx[HALO:, :], wg[...])
    gate_o[...] = gate
    carried = nt(bc[:, state:], s_in[...])
    y = yw[...] + spread(jnp.exp(cum_s[g]), GC, head_dim) * carried
    y_o[...] = y
    gated = y * (gate * sigmoid(gate))
    gg = (gated * pv[5:6, :]).astype(BF)
    gg_o[...] = gg
    squares = gated * gated
    for part in range(GC // LANES):
        sq_s[...] += squares[:, LANES * part : LANES * (part + 1)]
    acc_s[...] += nt(gg, wo[...])

    @pl.when(g == pl.num_programs(0) - 1)
    def _():
        p_o[...] = acc_s[...].astype(BF)
        sq_o[...] = jnp.broadcast_to(jnp.sum(sq_s[...], axis=1, keepdims=True), sq_o.shape)


def gate_backward(head_dim, gm, wo, y, gate, rowsc, pv, bc, dtc, dy_o, dgate_o, dsl_o, dgain_o, cum_s):
    g = pl.program_id(0)
    state = bc.shape[1] // 2

    @pl.when(g == 0)
    def _():
        group_lanes(dtc[1], cum_s, cum_s.shape[0], GC // head_dim)

    gs = nn(gm[...], wo[...])
    inverse, shrink = rowsc[:, 0:1], rowsc[:, 1:2]
    gv, yv = gate[...], y[...]
    s = sigmoid(gv)
    silu = gv * s
    gated = yv * silu
    dgain = jnp.sum(gs * gated * inverse, axis=0, keepdims=True)
    dgain_o[...] = jnp.broadcast_to(dgain, dgain_o.shape)
    dgated = inverse * (gs * pv[5:6, :]) - gated * shrink
    dgate_o[...] = (dgated * yv * (s * (1.0 + gv * (1.0 - s)))).astype(BF)
    dy = dgated * silu
    dy_o[...] = dy.astype(BF)
    dye = (dy * spread(jnp.exp(cum_s[g]), GC, head_dim)).astype(BF)
    dsl_o[...] = tn(dye, bc[:, state:])


def scan_backward(
    head_dim,
    dy,
    x,
    vpre,
    spre,
    bc,
    dtc,
    s_in,
    g_in,
    pv,
    ps,
    ph,
    dconv_o,
    dsc_o,
    dstep_o,
    vs_o,
    ss_o,
    hs_o,
    sct_s,
    scts_s,
    wsum_s,
    dbc_s,
    dt_s,
    cum_s,
    cumt_s,
    net_s,
    rv_s,
    ddir_s,
    k_s,
    rt_s,
    rall_s,
):
    g = pl.program_id(0)
    rows = x.shape[0]
    state = bc.shape[1] // 2
    per_group = GC // head_dim
    groups = dt_s.shape[0]

    @pl.when(g == 0)
    def _():
        scores = nt(bc[:, :state], bc[:, state:])
        first, second = iota((rows, rows), 0), iota((rows, rows), 1)
        sct_s[...] = jnp.where(second >= first, scores, 0.0)
        scts_s[...] = jnp.where(second > first, scores, 0.0)
        wsum_s[...] = jnp.zeros_like(wsum_s)
        dbc_s[...] = jnp.zeros_like(dbc_s)
        rall_s[...] = jnp.zeros_like(rall_s)
        group_lanes(dtc[0], dt_s, groups, per_group)
        group_lanes(dtc[1], cum_s, groups, per_group)
        group_rows(dtc[1], cumt_s, groups, per_group)

    step, cum, cumt = dt_s[g], cum_s[g], cumt_s[g]
    last = cum[rows - 1 : rows, :]
    to_end = jnp.exp(last - cum)
    stepx = spread(step, GC, head_dim)
    endx = spread(to_end, GC, head_dim)
    fromx = spread(jnp.exp(cum), GC, head_dim)
    xf = x[...].astype(F32)
    dyb = dy[...]
    dyf = dyb.astype(F32)
    xp = (xf * stepx).astype(BF)
    xr = (xf * stepx * endx).astype(BF)
    dyef = dyf * fromx
    dye = dyef.astype(BF)
    gb = nt(bc[:, :state], g_in[...])
    cs = nt(bc[:, state:], s_in[...])
    dbc_s[:, :state] += nn(xr, g_in[...])
    dbc_s[:, state:] += nn(dye, s_in[...])

    lane = iota((rows, LANES), 1)
    wsum = wsum_s[...]
    colsum = jnp.zeros((rows, LANES), F32)
    within = []
    for pair in range(GC // LANES):
        cols = slice(LANES * pair, LANES * (pair + 1))
        xpp, dyp = xp[:, cols], dyb[:, cols]
        outs = []
        for side in range(2):
            i = 2 * pair + side
            mine = (lane < head_dim) if side == 0 else (lane >= head_dim)
            decay = jnp.exp(jnp.minimum(cumt[i : i + 1, :] - cum[:, i : i + 1], 0.0))
            outs.append(nn((decay * sct_s[...]).astype(BF), dyp))
            weight = decay * nt(jnp.where(mine, xpp, jnp.zeros_like(xpp)), dyp)
            wsum = wsum + weight
            pairs = (weight * scts_s[...]).astype(BF)
            colsum = colsum + nn(pairs, (lane == i).astype(BF))
            rt_s[g, i : i + 1, :] = jnp.sum(pairs.astype(F32), axis=0, keepdims=True)
        within.append(jnp.where(lane < head_dim, outs[0], outs[1]))
    wsum_s[...] = wsum
    u = jnp.concatenate(within, axis=1) + endx * gb

    heads = (iota((GC, LANES), 0) // head_dim == iota((GC, LANES), 1)).astype(BF)
    ddir_s[g] = nn((xf * u).astype(BF), heads)
    net_s[g] = nn((dyef * cs).astype(BF), heads) - colsum
    rv_s[g] = step * to_end * nn((xf * gb).astype(BF), heads)
    inner = g_in[...].astype(F32) * s_in[...].astype(F32)
    per_channel = lax.dot_general(
        jnp.ones((8, inner.shape[1]), F32), inner, (((1,), (1,)), ((), ())), precision=HIGHEST, preferred_element_type=F32
    )
    k_s[g] = jnp.exp(last) * exact(per_channel, heads.astype(F32))

    dx = stepx * u + pv[6:7, :] * dyf
    dconv = dx * silu_slope(conv_rows(vpre, pv, rows))
    dconv_o[...] = dconv
    sums = conv_sums(dconv, vpre, rows)
    sums.append(jnp.sum(dyf * xf, axis=0, keepdims=True))
    sums.append(jnp.zeros((2, GC), F32))
    vs_o[...] = jnp.concatenate(sums, axis=0)

    @pl.when(g == pl.num_programs(0) - 1)
    def _():
        first, second = iota((rows, rows), 0), iota((rows, rows), 1)
        net, rv, ddir, const = net_s[0], rv_s[0], ddir_s[0], k_s[0]
        rall_s[0:per_group, :] = rt_s[0, 0:per_group, :]
        for other in range(1, groups):
            shift = per_group * other
            net = net + pltpu.roll(net_s[other], shift, 1)
            rv = rv + pltpu.roll(rv_s[other], shift, 1)
            ddir = ddir + pltpu.roll(ddir_s[other], shift, 1)
            const = const + pltpu.roll(k_s[other], shift, 1)
            rall_s[shift : shift + per_group, :] = rt_s[other, 0:per_group, :]
        net = net + rall_s[...].T
        da = exact((second >= first).astype(F32), net) + exact((second < first).astype(F32), rv) + const[0:1, :]
        rate = jnp.exp(ph[1:2, :])
        dstep = (ddir - da * rate) * dtc[2]
        dstep_o[...] = dstep.astype(BF)
        hs_o[...] = jnp.concatenate(
            [
                jnp.sum(dstep, axis=0, keepdims=True),
                jnp.sum(-da * dtc[0] * rate, axis=0, keepdims=True),
                jnp.zeros((6, LANES), F32),
            ],
            axis=0,
        )
        weights = jnp.where(second >= first, wsum_s[...], 0.0).astype(BF)
        db = dbc_s[:, :state] + nn(weights, bc[:, state:])
        dc = dbc_s[:, state:] + tn(weights, bc[:, :state])
        dsc = jnp.concatenate([db, dc], axis=1) * silu_slope(conv_rows(spre, ps, rows))
        dsc_o[...] = dsc
        ssums = conv_sums(dsc, spre, rows)
        ssums.append(jnp.zeros((3, 2 * state), F32))
        ss_o[...] = jnp.concatenate(ssums, axis=0)


def conv_backward(dconv, halo_v, dsc, halo_s, dgate, dstep, pv, ps, wv, wg, ws, wt, dval_o, dst_o, p_o, acc_s):
    g = pl.program_id(0)
    rows = dconv.shape[0]

    @pl.when(g == 0)
    def _():
        dst = conv_transposed(dsc[...], halo_s[...], ps, rows).astype(BF)
        dst_o[...] = dst
        acc_s[...] = nt(dst, ws[...]) + nt(dstep[...], wt[...])

    dval = conv_transposed(dconv[...], halo_v[...], pv, rows).astype(BF)
    dval_o[...] = dval
    acc_s[...] += nt(dval, wv[...]) + nt(dgate[...], wg[...])

    @pl.when(g == pl.num_programs(0) - 1)
    def _():
        p_o[...] = acc_s[...].astype(BF)


def whole(shape):
    return pl.BlockSpec(shape, lambda g: (0,) * len(shape))


def by_cols(rows):
    return pl.BlockSpec((rows, GC), lambda g: (0, g))


def by_rows(cols):
    return pl.BlockSpec((GC, cols), lambda g: (g, 0))


def call(kernel, groups, ins, outs, scratch, flops, traffic, exps=0):
    arrays, in_specs = zip(*ins)
    shapes, out_specs = zip(*outs)
    return pl.pallas_call(
        kernel,
        grid=(groups,),
        in_specs=list(in_specs),
        out_specs=list(out_specs),
        out_shape=[jax.ShapeDtypeStruct(s, d) for s, d in shapes],
        scratch_shapes=scratch,
        cost_estimate=pl.CostEstimate(flops=flops, bytes_accessed=traffic, transcendentals=exps),
        compiler_params=pltpu.CompilerParams(vmem_limit_bytes=40 * 2**20, dimension_semantics=(SEQUENTIAL,)),
    )(*arrays)


def front_call(nx, w, par, head_dim, state):
    rows, width = nx.shape[0] - HALO, w.value.shape[1]
    model = nx.shape[1]
    groups = width // GC
    return call(
        functools.partial(scan_front, head_dim),
        groups,
        [
            (nx, whole(nx.shape)),
            (w.value, by_cols(model)),
            (w.state, whole(w.state.shape)),
            (w.step, whole(w.step.shape)),
            (par.value, by_cols(8)),
            (par.state, whole(par.state.shape)),
            (par.head, whole(par.head.shape)),
        ],
        [
            (((rows + HALO, width), F32), by_cols(rows + HALO)),
            (((rows + HALO, 2 * state), F32), whole((rows + HALO, 2 * state))),
            (((rows, width), BF), by_cols(rows)),
            (((rows, 2 * state), BF), whole((rows, 2 * state))),
            (((3, rows, LANES), F32), whole((3, rows, LANES))),
            (((rows, width), F32), by_cols(rows)),
            (((width, state), F32), by_rows(state)),
        ],
        [
            pltpu.VMEM((rows, rows), F32),
            pltpu.VMEM((groups, rows, LANES), F32),
            pltpu.VMEM((groups, rows, LANES), F32),
            pltpu.VMEM((groups, 8, rows), F32),
        ],
        2 * rows * model * (width + 3 * LANES) + 4 * rows * rows * width,
        2 * model * width + 12 * rows * width,
        rows * rows * width // head_dim,
    )


def finish_call(nx, w, par, yw, s_in, bc, dtc, head_dim):
    rows, width = yw.shape
    model = nx.shape[1]
    groups = width // GC
    state = s_in.shape[1]
    return call(
        functools.partial(scan_finish, head_dim),
        groups,
        [
            (nx, whole(nx.shape)),
            (w.gate, by_cols(model)),
            (w.out, by_cols(model)),
            (yw, by_cols(rows)),
            (s_in, by_rows(state)),
            (bc, whole(bc.shape)),
            (dtc, whole(dtc.shape)),
            (par.value, by_cols(8)),
        ],
        [
            (((rows, width), F32), by_cols(rows)),
            (((rows, width), F32), by_cols(rows)),
            (((rows, width), BF), by_cols(rows)),
            (((rows, model), BF), whole((rows, model))),
            (((rows, LANES), F32), whole((rows, LANES))),
        ],
        [
            pltpu.VMEM((rows, model), F32),
            pltpu.VMEM((rows, LANES), F32),
            pltpu.VMEM((groups, rows, LANES), F32),
        ],
        4 * rows * model * width,
        4 * model * width + 14 * rows * width,
    )


def gate_call(gm, w, par, y, gate, rowsc, bc, dtc, head_dim):
    rows, width = y.shape
    model = gm.shape[1]
    groups = width // GC
    state = bc.shape[1] // 2
    return call(
        functools.partial(gate_backward, head_dim),
        groups,
        [
            (gm, whole(gm.shape)),
            (w.out, by_cols(model)),
            (y, by_cols(rows)),
            (gate, by_cols(rows)),
            (rowsc, whole(rowsc.shape)),
            (par.value, by_cols(8)),
            (bc, whole(bc.shape)),
            (dtc, whole(dtc.shape)),
        ],
        [
            (((rows, width), BF), by_cols(rows)),
            (((rows, width), BF), by_cols(rows)),
            (((width, state), F32), by_rows(state)),
            (((8, width), F32), by_cols(8)),
        ],
        [pltpu.VMEM((groups, rows, LANES), F32)],
        2 * rows * model * width,
        2 * model * width + 14 * rows * width,
    )


def backward_call(dy, x, vpre, spre, bc, dtc, s_in, g_in, par, head_dim):
    rows, width = x.shape
    groups = width // GC
    state = bc.shape[1] // 2
    lanes = pltpu.VMEM((groups, rows, LANES), F32)
    square = pltpu.VMEM((rows, rows), F32)
    return call(
        functools.partial(scan_backward, head_dim),
        groups,
        [
            (dy, by_cols(rows)),
            (x, by_cols(rows)),
            (vpre, by_cols(rows + HALO)),
            (spre, whole(spre.shape)),
            (bc, whole(bc.shape)),
            (dtc, whole(dtc.shape)),
            (s_in, by_rows(state)),
            (g_in, by_rows(state)),
            (par.value, by_cols(8)),
            (par.state, whole(par.state.shape)),
            (par.head, whole(par.head.shape)),
        ],
        [
            (((rows, width), F32), by_cols(rows)),
            (((rows, 2 * state), F32), whole((rows, 2 * state))),
            (((rows, LANES), BF), whole((rows, LANES))),
            (((8, width), F32), by_cols(8)),
            (((8, 2 * state), F32), whole((8, 2 * state))),
            (((8, LANES), F32), whole((8, LANES))),
        ],
        [
            square,
            square,
            square,
            pltpu.VMEM((rows, 2 * state), F32),
            lanes,
            lanes,
            pltpu.VMEM((groups, 8, rows), F32),
            lanes,
            lanes,
            lanes,
            pltpu.VMEM((groups, 8, LANES), F32),
            pltpu.VMEM((groups, 8, rows), F32),
            pltpu.VMEM((LANES, rows), F32),
        ],
        12 * rows * rows * width,
        14 * rows * width,
        3 * rows * rows * width // head_dim,
    )


def conv_call(dconv, halo, dsc, dgate, dstep, w, par):
    rows, width = dconv.shape
    model = w.value.shape[0]
    groups = width // GC
    states = dsc.shape[1]
    halo_v, halo_s = halo[:, :width], halo[:, width:]
    return call(
        conv_backward,
        groups,
        [
            (dconv, by_cols(rows)),
            (halo_v, by_cols(8)),
            (dsc, whole(dsc.shape)),
            (halo_s, whole(halo_s.shape)),
            (dgate, by_cols(rows)),
            (dstep, whole(dstep.shape)),
            (par.value, by_cols(8)),
            (par.state, whole(par.state.shape)),
            (w.value, by_cols(model)),
            (w.gate, by_cols(model)),
            (w.state, whole(w.state.shape)),
            (w.step, whole(w.step.shape)),
        ],
        [
            (((rows, width), BF), by_cols(rows)),
            (((rows, states), BF), whole((rows, states))),
            (((rows, model), BF), whole((rows, model))),
        ],
        [pltpu.VMEM((rows, model), F32)],
        4 * rows * model * width,
        4 * model * width + 10 * rows * width,
    )


def swap_pipe(value):
    return lax.ppermute(value, PIPE, [(0, 1), (1, 0)])


def shift_tensor(value, by):
    count = lax.axis_size(TENSOR)
    return lax.ppermute(value, TENSOR, [(i, i + by) for i in range(count) if 0 <= i + by < count])


def flip_dp(value, bit):
    return lax.ppermute(value, DP, [(i, i ^ bit) for i in range(lax.axis_size(DP))])


def dp_bits():
    bits, bit = [], 1
    while bit < lax.axis_size(DP):
        bits.append(bit)
        bit *= 2
    return bits


def gather_tensor(piece):
    count, me = lax.axis_size(TENSOR), lax.axis_index(TENSOR)
    rows, cols = piece.shape
    right, left = [piece], [piece]
    for _ in range(count - 1):
        right.append(shift_tensor(right[-1], 1))
        left.append(shift_tensor(left[-1], -1))
    full = jnp.zeros((rows, count * cols), piece.dtype)
    for k in range(count):
        part = piece if k == 0 else jnp.where(me >= k, right[k], left[count - k])
        full = lax.dynamic_update_slice(full, part, (0, lax.rem(me - k + count, count) * cols))
    return full


def gather_dp(piece):
    count, me = lax.axis_size(DP), lax.axis_index(DP)
    rows, cols = piece.shape
    held = {0: piece}
    for bit in reversed(dp_bits()):
        for offset in list(held):
            held[offset ^ bit] = flip_dp(held[offset], bit)
    full = jnp.zeros((count * rows, cols), piece.dtype)
    for offset, part in held.items():
        full = lax.dynamic_update_slice(full, part, ((me ^ offset) * rows, 0))
    return full


def add_low(a, b):
    return (a.astype(F32) + b.astype(F32)).astype(a.dtype)


def reduce_dp(value):
    me = lax.axis_index(DP)
    count = lax.axis_size(DP)
    rows, cols = value.shape[0] // count, value.shape[1]
    for bit in dp_bits():
        count //= 2
        split = value.reshape(count, 2, rows, cols)
        mine = (me // bit) % 2
        keep = lax.dynamic_index_in_dim(split, mine, 1, keepdims=False)
        send = lax.dynamic_index_in_dim(split, 1 - mine, 1, keepdims=False)
        value = add_low(keep, flip_dp(send, bit)).reshape(count * rows, cols)
    return value


def reduce_tensor(take):
    count, me = lax.axis_size(TENSOR), lax.axis_index(TENSOR)
    moving_right = moving_left = None
    for k in range(count - 1, 0, -1):
        right, left = take(jnp.minimum(me + k, count - 1)), take(jnp.maximum(me - k, 0))
        if moving_right is not None:
            right, left = add_low(right, moving_right), add_low(left, moving_left)
        moving_right, moving_left = shift_tensor(right, 1), shift_tensor(left, -1)
    own = take(me)
    if moving_right is None:
        return own.astype(F32)
    return own.astype(F32) + moving_right.astype(F32) + moving_left.astype(F32)


def take_cols(value):
    width = value.shape[1] // lax.axis_size(TENSOR)
    return lambda j: lax.dynamic_slice_in_dim(value, j * width, width, 1)


def take_first(value):
    return lambda j: lax.dynamic_index_in_dim(value, j, 0, keepdims=False)


def sum_all_dp(value):
    for bit in dp_bits():
        value = value + flip_dp(value, bit)
    return value


def sum_all_tensor(value):
    count, bit = lax.axis_size(TENSOR), 1
    while bit < count:
        value = value + lax.ppermute(value, TENSOR, [(i, i ^ bit) for i in range(count)])
        bit *= 2
    return value


MESH = pl.DeviceIdType.MESH
VMEM_LIMIT = 60 * 2**20


def remote(src, dst, send, recv, axis, index):
    return pltpu.make_async_remote_copy(
        src_ref=src, dst_ref=dst, send_sem=send, recv_sem=recv, device_id={axis: index}, device_id_type=MESH
    )


def greet(partners):
    barrier = pltpu.get_barrier_semaphore()
    for axis, index in partners:
        pl.semaphore_signal(barrier, inc=1, device_id={axis: index}, device_id_type=MESH)
    pl.semaphore_wait(barrier, len(partners))


def ring_neighbours(count):
    t = lax.axis_index(TENSOR)
    return [(TENSOR, lax.rem(t + 1, count)), (TENSOR, lax.rem(t + count - 1, count))]


def aligned(index, size):
    return pl.ds(pl.multiple_of(index * size, size), size)


def gather_weights(count, *refs):
    (value, gate, out, step, state, chan, shared, wv, wg, wo, wt, ws, ch, sh) = refs[:14]
    (own_sem, xs_sem, xr_sem, right_sem, left_sem, zr_sem, ys_sem, yr_sem, cs_sem, cr_sem) = refs[14:24]
    (st_own, st_xs, st_xr, st_ys, st_yr, st_cs, st_cr, ch_s, ch_r) = refs[24:]
    p, d, t = lax.axis_index(PIPE), lax.axis_index(DP), lax.axis_index(TENSOR)
    y, c = d // 2, lax.rem(d, 2)
    y_mate, core_mate, far_mate = 2 * (1 - y) + c, 2 * y + 1 - c, 2 * (1 - y) + 1 - c
    sources, targets = (value, gate, out, step), (wv, wg, wo, wt)
    kinds = len(sources)
    rows = value.shape[0]

    def half(kind):
        return sources[kind].shape[1] // 2

    def region(item, row, col):
        kind = item % kinds
        return targets[kind].at[item // kinds, aligned(row, rows), aligned(col, half(kind))]

    def strip(item, row):
        return targets[item % kinds].at[item // kinds, aligned(row, rows), :]

    def own_copy(w):
        src = sources[w].at[:, aligned(p, half(w))]
        return pltpu.make_async_copy(src, targets[w].at[p, aligned(d, rows), aligned(t, half(w))], own_sem.at[w])

    def swap_copy(w):
        src = sources[w].at[:, aligned(1 - p, half(w))]
        dst = targets[w].at[p, aligned(d, rows), aligned(t, half(w))]
        return remote(src, dst, xs_sem.at[w], xr_sem.at[w], PIPE, 1 - p)

    def z_copy(item, src, by, sem):
        ref = region(item, d, src)
        return remote(ref, ref, sem.at[item, src], zr_sem.at[item, src], TENSOR, t + by)

    def y_copy(item, src):
        ref = region(item, d, src)
        return remote(ref, ref, ys_sem.at[item, src], yr_sem.at[item, src], DP, y_mate)

    def core_copy(item, which):
        ref = strip(item, d if which == 0 else y_mate)
        return remote(ref, ref, cs_sem.at[item, which], cr_sem.at[item, which], DP, core_mate)

    def y_arrival(item, src):
        ref = region(item, y_mate, src)
        return remote(ref, ref, ys_sem.at[item, src], yr_sem.at[item, src], DP, y_mate)

    def core_arrival(item, which):
        ref = strip(item, core_mate if which == 0 else far_mate)
        return remote(ref, ref, cs_sem.at[item, which], cr_sem.at[item, which], DP, core_mate)

    def swap_arrival(w):
        ref = targets[w].at[1 - p, aligned(d, rows), aligned(t, half(w))]
        return remote(sources[w].at[:, aligned(1 - p, half(w))], ref, xs_sem.at[w], xr_sem.at[w], PIPE, 1 - p)

    def state_rows(layer, row):
        return ws.at[layer, aligned(row, rows), :]

    small = ((state, state_rows(p, d), state_rows(1 - p, d)), (chan, ch.at[p, t], ch.at[1 - p, t]), (shared, sh.at[p], sh.at[1 - p]))

    def small_own(k):
        return pltpu.make_async_copy(small[k][0], small[k][1], st_own.at[k])

    def small_swap(k):
        return remote(small[k][0], small[k][1], st_xs.at[k], st_xr.at[k], PIPE, 1 - p)

    def small_arrival(k):
        return remote(small[k][0], small[k][2], st_xs.at[k], st_xr.at[k], PIPE, 1 - p)

    def state_y(layer):
        ref = state_rows(layer, d)
        return remote(ref, ref, st_ys.at[layer], st_yr.at[layer], DP, y_mate)

    def state_y_arrival(layer):
        ref = state_rows(layer, y_mate)
        return remote(ref, ref, st_ys.at[layer], st_yr.at[layer], DP, y_mate)

    def state_core(layer, which):
        ref = state_rows(layer, d if which == 0 else y_mate)
        return remote(ref, ref, st_cs.at[layer, which], st_cr.at[layer, which], DP, core_mate)

    def state_core_arrival(layer, which):
        ref = state_rows(layer, core_mate if which == 0 else far_mate)
        return remote(ref, ref, st_cs.at[layer, which], st_cr.at[layer, which], DP, core_mate)

    def chan_copy(k):
        ref = ch.at[:, t]
        return remote(ref, ref, ch_s.at[k], ch_r.at[k], TENSOR, lax.rem(t + k, count))

    def chan_arrival(k):
        ref = ch.at[:, lax.rem(t - k + count, count)]
        return remote(ref, ref, ch_s.at[k], ch_r.at[k], TENSOR, lax.rem(t + k, count))

    def begin(item):
        if item < kinds:
            own_copy(item).wait()
            swap_arrival(item).wait_recv()

        @pl.when(t < count - 1)
        def _():
            z_copy(item, t, 1, right_sem).start()

        @pl.when(t > 0)
        def _():
            z_copy(item, t, -1, left_sem).start()

        y_copy(item, t).start()

    def relay(item):
        for hop in range(1, count):
            lower, upper = t - hop, t + hop

            @pl.when(lower >= 0)
            def _():
                z_copy(item, lower, 1, right_sem).wait_recv()

                @pl.when(t < count - 1)
                def _():
                    z_copy(item, lower, 1, right_sem).start()

                y_copy(item, lower).start()

            @pl.when(upper < count)
            def _():
                z_copy(item, upper, -1, left_sem).wait_recv()

                @pl.when(t > 0)
                def _():
                    z_copy(item, upper, -1, left_sem).start()

                y_copy(item, upper).start()

        core_copy(item, 0).start()

    def share(item):
        for src in range(count):
            y_arrival(item, src).wait_recv()
        core_copy(item, 1).start()

    others = [(TENSOR, lax.rem(t + k, count)) for k in range(1, count)]
    greet(others + [(PIPE, 1 - p), (DP, y_mate), (DP, core_mate)])
    for k in range(3):
        small_swap(k).start()
        small_own(k).start()
    order = [kinds - 1] + list(range(kinds - 1))
    for w in order:
        swap_copy(w).start()
        own_copy(w).start()
    for k in range(3):
        small_own(k).wait()
        small_arrival(k).wait_recv()
    for layer in range(2):
        state_y(layer).start()
        state_core(layer, 0).start()
    for k in range(1, count):
        chan_copy(k).start()
    order = order + [kinds + w for w in order]
    begin(order[0])
    for n, item in enumerate(order):
        if n + 1 < len(order):
            begin(order[n + 1])
        relay(item)
        if n == 0:
            for layer in range(2):
                state_y_arrival(layer).wait_recv()
                state_core(layer, 1).start()
        else:
            share(order[n - 1])
    share(order[-1])
    for k in range(3):
        small_swap(k).wait_send()
    for k in range(1, count):
        chan_copy(k).wait_send()
        chan_arrival(k).wait_recv()
    for layer in range(2):
        state_y(layer).wait_send()
        for which in range(2):
            state_core_arrival(layer, which).wait_recv()
            state_core(layer, which).wait_send()
    for w in range(kinds):
        swap_copy(w).wait_send()
    for item in order:
        for which in range(2):
            core_arrival(item, which).wait_recv()
            core_copy(item, which).wait_send()
        for src in range(count):
            y_copy(item, src).wait_send()

            @pl.when((src <= t) & (t < count - 1))
            def _():
                z_copy(item, src, 1, right_sem).wait_send()

            @pl.when((src >= t) & (t > 0))
            def _():
                z_copy(item, src, -1, left_sem).wait_send()


def gather_call(value, gate, out, step, state, chan, shared, count, groups):
    rows = value.shape[0]
    model = groups * rows
    dma = pltpu.SemaphoreType.DMA
    big = [jax.ShapeDtypeStruct((2, model, count * v.shape[1] // 2), BF) for v in (value, gate, out, step)]
    shapes = big + [
        jax.ShapeDtypeStruct((2, model, state.shape[1]), BF),
        jax.ShapeDtypeStruct((2, count) + chan.shape, F32),
        jax.ShapeDtypeStruct((2,) + shared.shape, F32),
    ]
    return pl.pallas_call(
        functools.partial(gather_weights, count),
        in_specs=[pl.BlockSpec(memory_space=pl.ANY)] * 7,
        out_specs=[pl.BlockSpec(memory_space=pl.ANY)] * 7,
        out_shape=shapes,
        scratch_shapes=[dma((4,))] * 3
        + [dma((8, count))] * 5
        + [dma((8, 2))] * 2
        + [dma((3,))] * 3
        + [dma((2,))] * 2
        + [dma((2, 2))] * 2
        + [dma((count,))] * 2,
        compiler_params=pltpu.CompilerParams(collective_id=0, has_side_effects=True),
    )(value, gate, out, step, state, chan, shared)


def add_into(dst, src, chunk=64):
    def step(i, carry):
        at = aligned(i, chunk)
        dst[at, :] = (dst[at, :].astype(F32) + src[at, :].astype(F32)).astype(BF)
        return carry

    lax.fori_loop(0, dst.shape[0] // chunk, step, 0)


def reduce_grads(count, *refs):
    grads, pack, results, (chan_o, step_o, rest_o) = refs[:6], refs[6], refs[7:10], refs[10:13]
    (own, crecv, yrecv, rrecv, lrecv, xsend, xrecv) = refs[13:20]
    (own_sem, cs_sem, cr_sem, ys_sem, yr_sem, rs_sem, rr_sem, ls_sem, lr_sem, xs_sem, xr_sem) = refs[20:31]
    (total_s, part_s, far_s, sum_ss, sum_rs) = refs[31:]
    p, d, t = lax.axis_index(PIPE), lax.axis_index(DP), lax.axis_index(TENSOR)
    y, c = d // 2, lax.rem(d, 2)
    y_mate, core_mate = 2 * (1 - y) + c, 2 * y + 1 - c
    items, kinds = 6, 3
    rows, half = xsend.shape[1], xsend.shape[2]

    def core_copy(item, row):
        src = grads[item].at[aligned(2 * row + 1 - c, rows), :]
        return remote(src, crecv.at[item, row], cs_sem.at[item, row], cr_sem.at[item, row], DP, core_mate)

    def own_copy(item, row):
        src = grads[item].at[aligned(2 * row + c, rows), :]
        return pltpu.make_async_copy(src, own.at[item % 2, row], own_sem.at[item % 2, row])

    def y_copy(item):
        return remote(crecv.at[item, 1 - y], yrecv.at[item], ys_sem.at[item], yr_sem.at[item], DP, y_mate)

    def right_copy(item, j):
        ref = rrecv.at[item, j]
        return remote(ref, ref, rs_sem.at[item, j], rr_sem.at[item, j], TENSOR, t + 1)

    def left_copy(item, j):
        ref = lrecv.at[item, j]
        return remote(ref, ref, ls_sem.at[item, j], lr_sem.at[item, j], TENSOR, t - 1)

    def x_copy(item):
        return remote(xsend.at[item], xrecv.at[item % kinds], xs_sem.at[item], xr_sem.at[item % kinds], PIPE, 1 - p)

    def near(item):
        for row in range(2):
            own_copy(item, row).wait()
            core_copy(item, row).wait_recv()
            add_into(crecv.at[item, row], own.at[item % 2, row])
        y_copy(item).start()
        if item + 2 < items:
            for row in range(2):
                own_copy(item + 2, row).start()

    def far(item):
        y_copy(item).wait_recv()
        add_into(yrecv.at[item], crecv.at[item, y])

        def column(j):
            return yrecv.at[item, :, aligned(j, half)]

        for j in range(count - 1, 0, -1):

            @pl.when(t < j)
            def _():
                @pl.when(t == 0)
                def _():
                    rrecv[item, j] = column(j)[...]

                @pl.when(t > 0)
                def _():
                    right_copy(item, j).wait_recv()
                    add_into(rrecv.at[item, j], column(j))

                right_copy(item, j).start()

        for j in range(count - 1):

            @pl.when(t > j)
            def _():
                @pl.when(t == count - 1)
                def _():
                    lrecv[item, j] = column(j)[...]

                @pl.when(t < count - 1)
                def _():
                    left_copy(item, j).wait_recv()
                    add_into(lrecv.at[item, j], column(j))

                left_copy(item, j).start()

    def close(item):
        w = item % kinds
        total = xsend.at[item]
        total[...] = yrecv[item, :, aligned(t, half)]

        @pl.when(t > 0)
        def _():
            right_copy(item, t).wait_recv()
            add_into(total, rrecv.at[item, t])

        @pl.when(t < count - 1)
        def _():
            left_copy(item, t).wait_recv()
            add_into(total, lrecv.at[item, t])

        @pl.when(p != item // kinds)
        def _():
            x_copy(item).start()

        @pl.when(p == item // kinds)
        def _():
            results[w][:, aligned(p, half)] = total[...].astype(F32)

    steps, bit = [(DP, core_mate), (DP, y_mate)], 1
    while bit < count:
        steps.append((TENSOR, t + bit * (1 - 2 * lax.rem(t // bit, 2))))
        bit *= 2

    def sum_copy(k):
        axis, index = steps[k]
        return remote(total_s.at[k], part_s.at[k], sum_ss.at[k], sum_rs.at[k], axis, index)

    def pipe_copy():
        k = len(steps)
        return remote(total_s.at[k, 1 - p], far_s, sum_ss.at[k], sum_rs.at[k], PIPE, 1 - p)

    def sum_step(k):
        sum_copy(k).wait_recv()
        total_s[k + 1] = total_s[k] + part_s[k]
        if k + 1 < len(steps):
            sum_copy(k + 1).start()
        else:
            pipe_copy().start()

    def sum_close():
        k = len(steps)
        pipe_copy().wait_recv()
        mine = total_s.at[k, p]
        for ref, where in ((mine, p), (far_s, 1 - p)):
            chan_o[:, aligned(where, half)] = ref[0:8, aligned(t, half)]
            step_o[aligned(where, 8), :] = ref[pl.ds(pl.multiple_of(8 + 8 * t, 8), 8), aligned(d, rows)]
        last = total_s.shape[2] - 8
        row = iota((8, total_s.shape[3]), 0)
        rest_o[...] = mine[last:, :] + jnp.where(row == 0, 0.0, far_s[last:, :])

    others = [axis_index for axis_index in steps if axis_index[0] == TENSOR]
    greet(ring_neighbours(count) + [(PIPE, 1 - p), (DP, y_mate), (DP, core_mate)] + others)
    total_s[0] = pack[...]
    sum_copy(0).start()
    for item in range(items):
        for row in range(2):
            core_copy(item, row).start()
            if item < 2:
                own_copy(item, row).start()
    for k in range(items + 2):
        if k < items:
            near(k)
        if 1 <= k <= items:
            far(k - 1)
        if k >= 2:
            close(k - 2)
        if 1 <= k <= len(steps):
            sum_step(k - 1)
    sum_close()
    for k in range(len(steps)):
        sum_copy(k).wait_send()
    pipe_copy().wait_send()
    for w in range(kinds):
        x_copy(w).wait_recv()
        results[w][:, aligned(1 - p, half)] = xrecv[w].astype(F32)
    for item in range(items):
        for row in range(2):
            core_copy(item, row).wait_send()
        y_copy(item).wait_send()

        @pl.when(p != item // kinds)
        def _():
            x_copy(item).wait_send()

        for j in range(count):

            @pl.when(t < j)
            def _():
                right_copy(item, j).wait_send()

            @pl.when(t > j)
            def _():
                left_copy(item, j).wait_send()


def reduce_call(grads, pack, count, groups):
    model, width = grads[0].shape
    rows, half = model // groups, width // count
    dma = pltpu.SemaphoreType.DMA
    vmem = pltpu.VMEM
    steps = 2 + (count - 1).bit_length()
    inside = pl.BlockSpec(memory_space=pltpu.VMEM)
    return pl.pallas_call(
        functools.partial(reduce_grads, count),
        in_specs=[pl.BlockSpec(memory_space=pl.ANY)] * 6 + [inside],
        out_specs=[inside] * 6,
        out_shape=[jax.ShapeDtypeStruct((rows, 2 * half), F32)] * 3
        + [
            jax.ShapeDtypeStruct((8, 2 * half), F32),
            jax.ShapeDtypeStruct((16, rows), F32),
            jax.ShapeDtypeStruct((8, width), F32),
        ],
        scratch_shapes=[
            vmem((2, 2, rows, width), BF),
            vmem((6, 2, rows, width), BF),
            vmem((6, rows, width), BF),
            vmem((6, count, rows, half), BF),
            vmem((6, count, rows, half), BF),
            vmem((6, rows, half), BF),
            vmem((3, rows, half), BF),
            dma((2, 2)),
            dma((6, 2)),
            dma((6, 2)),
            dma((6,)),
            dma((6,)),
            dma((6, count)),
            dma((6, count)),
            dma((6, count)),
            dma((6, count)),
            dma((6,)),
            dma((3,)),
            vmem((steps + 1,) + pack.shape, F32),
            vmem((steps,) + pack.shape, F32),
            vmem(pack.shape[1:], F32),
            dma((steps + 1,)),
            dma((steps + 1,)),
        ],
        compiler_params=pltpu.CompilerParams(collective_id=1, has_side_effects=True, vmem_limit_bytes=VMEM_LIMIT),
    )(*grads, pack)


def fused_forward(count, head_dim, micro, *refs):
    (tokens, mask, wv, wg, wo, ws, wt, pv, ps, ph, pn) = refs[:11]
    (out_h, low_h, mix_h, inv_o, nx_o, vpre_o, spre_o, x_o, bc_o, dtc_o, gate_o, y_o, gg_o, sin_o) = refs[11:25]
    (nx_s, sc_s, dt_s, cum_s, cumt_s, acc_s, sq_s, psend, precv, sqsend, sqrecv, csend, crecv, hrecv, trecv) = refs[25:40]
    (ps_sem, pr_sem, ss_sem, sr_sem, cs_sem, cr_sem, hs_sem, hr_sem, ts_sem, tr_sem, low_sem, out_sem, mix_sem) = refs[40:]
    q, s, g = pl.program_id(0), pl.program_id(1), pl.program_id(2)
    groups = dt_s.shape[0]
    p, t = lax.axis_index(PIPE), lax.axis_index(TENSOR)
    idx = q * micro + s
    slot = idx * groups + g
    total_idx = 2 * micro
    rows, model = tokens.shape[1], tokens.shape[2]
    state = bc_o.shape[1] // 2
    per_group = GC // head_dim
    inner_total = 2 * groups * GC

    def part_copy(i):
        return remote(psend.at[i], precv.at[i], ps_sem.at[i], pr_sem.at[i], PIPE, 1 - p)

    def square_copy(i):
        return remote(sqsend.at[i], sqrecv.at[i], ss_sem.at[i], sr_sem.at[i], PIPE, 1 - p)

    def chain_copy(i):
        return remote(csend.at[i], crecv.at[i], cs_sem.at[i], cr_sem.at[i], TENSOR, t + 1)

    def halo_copy(i):
        return remote(psend.at[i, rows - HALO :, :], hrecv.at[i], hs_sem.at[i], hr_sem.at[i], TENSOR, t + 1)

    def tokens_copy():
        return remote(tokens.at[:, rows - HALO :, :], trecv, ts_sem.at[0], tr_sem.at[0], TENSOR, t + 1)

    def low_copy(i):
        return pltpu.make_async_copy(psend.at[i], low_h.at[i], low_sem.at[i])

    def out_copy(i):
        return pltpu.make_async_copy(psend.at[i], out_h.at[lax.rem(i, micro)], out_sem.at[i])

    def mix_copy(i):
        return pltpu.make_async_copy(precv.at[i], mix_h.at[i], mix_sem.at[i])

    @pl.when((idx == 0) & (g == 0))
    def _():
        greet(ring_neighbours(count) + [(PIPE, 1 - p)])

        @pl.when(t < count - 1)
        def _():
            tokens_copy().start()

    def normed(u):
        uf = u.astype(F32)
        return (uf * lax.rsqrt(jnp.mean(uf * uf, axis=1, keepdims=True) + EPS) * pn[0:1, :]).astype(BF)

    @pl.when((g == 0) & (q == 0))
    def _():
        nx_s[HALO:, :] = normed(tokens[s])

        @pl.when(t == 0)
        def _():
            nx_s[:HALO, :] = jnp.zeros((HALO, model), BF)

        @pl.when(t > 0)
        def _():
            @pl.when(s == 0)
            def _():
                tokens_copy().wait_recv()

            nx_s[:HALO, :] = normed(trecv[s])

    @pl.when((g == 0) & (q == 1))
    def _():
        nx_s[HALO:, :] = normed(psend[s])

        @pl.when(t == 0)
        def _():
            nx_s[:HALO, :] = jnp.zeros((HALO, model), BF)

        @pl.when(t > 0)
        def _():
            halo_copy(s).wait_recv()
            nx_s[:HALO, :] = normed(hrecv[s])

    @pl.when(g == 0)
    def _():
        nx_o[...] = nx_s[HALO:, :]
        spre = nn(nx_s[...], ws[...])
        spre_o[...] = spre
        conv = conv_rows(spre, ps, rows)
        bc = (conv * sigmoid(conv)).astype(BF)
        bc_o[...] = bc
        scores = nt(bc[:, state:], bc[:, :state])
        lower = iota((rows, rows), 0) >= iota((rows, rows), 1)
        sc_s[...] = jnp.where(lower, scores, 0.0)
        raw = nn(nx_s[HALO:, :], wt[...]) + ph[0:1, :]
        step = jnp.maximum(raw, 0.0) + jnp.log(1.0 + jnp.exp(-jnp.abs(raw)))
        cum = exact(lower.astype(F32), -step * jnp.exp(ph[1:2, :]))
        dtc_o[0] = step
        dtc_o[1] = cum
        dtc_o[2] = sigmoid(raw)
        group_lanes(step, dt_s, groups, per_group)
        group_lanes(cum, cum_s, groups, per_group)
        group_rows(cum, cumt_s, groups, per_group)
        acc_s[...] = jnp.zeros_like(acc_s)
        sq_s[...] = jnp.zeros_like(sq_s)

    pre = nn(nx_s[...], wv[...])
    vpre_o[...] = pre
    conv = conv_rows(pre, pv, rows)
    x = conv * sigmoid(conv)
    x_o[...] = x.astype(BF)
    step, cum, cumt = dt_s[g], cum_s[g], cumt_s[g]
    to_end = jnp.exp(cum[rows - 1 : rows, :] - cum)
    xp = (x * spread(step, GC, head_dim)).astype(BF)
    xr = (x * spread(step * to_end, GC, head_dim)).astype(BF)
    local = tn(xr, bc_o[:, :state])

    @pl.when(t == 0)
    def _():
        sin_o[...] = jnp.zeros_like(sin_o)

    @pl.when(t > 0)
    def _():
        chain_copy(slot).wait_recv()
        sin_o[...] = crecv[slot]

    @pl.when(t < count - 1)
    def _():
        csend[slot] = (through_rows(cumt, rows, head_dim, state) * sin_o[...].astype(F32) + local).astype(BF)
        chain_copy(slot).start()

    scores = sc_s[...]
    lane = iota((rows, LANES), 1)
    within = []
    for pair in range(GC // LANES):
        cols = slice(LANES * pair, LANES * (pair + 1))
        outs = []
        for i in (2 * pair, 2 * pair + 1):
            diff = cum[:, i : i + 1] - cumt[i : i + 1, :]
            mix = (jnp.exp(jnp.minimum(diff, 0.0)) * scores).astype(BF)
            outs.append(nn(mix, xp[:, cols]))
        within.append(jnp.where(lane < head_dim, outs[0], outs[1]))
    gate = nn(nx_s[HALO:, :], wg[...])
    gate_o[...] = gate
    carried = nt(bc_o[:, state:], sin_o[...])
    y = jnp.concatenate(within, axis=1) + pv[6:7, :] * x + spread(jnp.exp(cum), GC, head_dim) * carried
    y_o[...] = y
    gated = y * (gate * sigmoid(gate))
    gg = (gated * pv[5:6, :]).astype(BF)
    gg_o[...] = gg
    squares = gated * gated
    for part in range(GC // LANES):
        sq_s[...] += squares[:, LANES * part : LANES * (part + 1)]
    acc_s[...] += nt(gg, wo[...])

    @pl.when(g == groups - 1)
    def _():
        psend[idx] = acc_s[...].astype(BF)
        sqsend[idx] = jnp.broadcast_to(jnp.sum(sq_s[...], axis=1, keepdims=True), (rows, LANES))
        part_copy(idx).start()
        square_copy(idx).start()

    def finish(i):
        j = lax.rem(i, micro)
        part_copy(i).wait()
        square_copy(i).wait()
        inverse = lax.rsqrt((sqsend[i] + sqrecv[i]) / inner_total + EPS)
        inv_o[i] = inverse
        mixed = inverse[:, 0:1] * (psend[i].astype(F32) + precv[i].astype(F32))
        precv[i] = mixed.astype(BF)
        row_mask = mask[j][:, 0:1]

        @pl.when(i < micro)
        def _():
            psend[i] = (row_mask * (tokens[j].astype(F32) + mixed)).astype(BF)

            @pl.when(t < count - 1)
            def _():
                halo_copy(j).start()

            low_copy(j).start()

        @pl.when(i >= micro)
        def _():
            psend[i] = (row_mask * (psend[j].astype(F32) + mixed)).astype(BF)

        @pl.when(i // micro == p)
        def _():
            out_copy(i).start()

        mix_copy(i).start()

    @pl.when((g == 1) & (idx > 1))
    def _():
        finish(idx - 2)

    @pl.when((g == groups - 1) & (idx == total_idx - 1))
    def _():
        finish(idx - 1)
        finish(idx)
        for i in range(total_idx):
            mix_copy(i).wait()

            @pl.when(i // micro == p)
            def _():
                out_copy(i).wait()

        for i in range(micro):
            low_copy(i).wait()

        @pl.when(t < count - 1)
        def _():
            tokens_copy().wait_send()
            for i in range(micro):
                halo_copy(i).wait_send()

            def drain(i, carry):
                chain_copy(i).wait_send()
                return carry

            lax.fori_loop(0, total_idx * groups, drain, 0)


def through_rows(cumt, rows, head_dim, state):
    end = jnp.exp(cumt[:, rows - 1 : rows])
    parts = [jnp.broadcast_to(end[i : i + 1, :], (head_dim, state)) for i in range(GC // head_dim)]
    return jnp.concatenate(parts, axis=0)


def fused_backward(count, head_dim, micro, *refs):
    (cot, tokens, out0, mask, inv, mix, vpre, spre, x, bc, dtc, gate, y, s_in) = refs[:14]
    (wv, wg, wo, ws, wt, pv, ps, ph, pn) = refs[14:23]
    (grad_h, dval_o, dgate_o, dst_o, dstep_o, sgm_o, vs_o, ss_o, hs_o, norm_o) = refs[23:33]
    (gm_s, rowsc_s, gin_s, halo_s, halo2_s, acc_s, nacc_s) = refs[33:40]
    (sct_s, scts_s, wsum_s, dbc_s, dt_s, cum_s, cumt_s, net_s, rv_s, ddir_s, k_s, rt_s, rall_s) = refs[40:53]
    (psend, precv, csend, crecv, hsend, hrecv, tsend, trecv) = refs[53:61]
    (ps_sem, pr_sem, cs_sem, cr_sem, hs_sem, hr_sem, ts_sem, tr_sem, out_sem) = refs[61:]
    turn, s, g = pl.program_id(0), pl.program_id(1), pl.program_id(2)
    groups = dt_s.shape[0]
    p, t = lax.axis_index(PIPE), lax.axis_index(TENSOR)
    idx = turn * micro + s
    slot = idx * groups + g
    total_idx = 2 * micro
    rows, model = cot.shape[1], cot.shape[2]
    state = bc.shape[1] // 2
    per_group = GC // head_dim
    inner_total = 2 * groups * GC

    def part_copy(i):
        return remote(psend.at[i], precv.at[i], ps_sem.at[i], pr_sem.at[i], PIPE, 1 - p)

    def chain_copy(i):
        return remote(csend.at[i], crecv.at[i], cs_sem.at[i], cr_sem.at[i], TENSOR, t - 1)

    def halo_copy(i):
        return remote(hsend.at[i], hrecv.at[i], hs_sem.at[i], hr_sem.at[i], TENSOR, t - 1)

    def tail_copy(i):
        return remote(tsend.at[i], trecv.at[i], ts_sem.at[i], tr_sem.at[i], TENSOR, t - 1)

    def out_copy(i):
        return pltpu.make_async_copy(psend.at[i], grad_h.at[lax.rem(i, micro)], out_sem.at[i])

    @pl.when((idx == 0) & (g == 0))
    def _():
        greet(ring_neighbours(count) + [(PIPE, 1 - p)])
        nacc_s[...] = jnp.zeros_like(nacc_s)

    @pl.when((g == 0) & (turn == 0))
    def _():
        gm_s[...] = (mask[s][:, 0:1] * cot[s].astype(F32)).astype(BF)

    @pl.when((g == 0) & (turn == 1))
    def _():
        gm_s[...] = (mask[s][:, 0:1] * psend[s].astype(F32)).astype(BF)

    @pl.when(g == 0)
    def _():
        gmf = gm_s[...].astype(F32)
        inverse = inv[...]
        dot = jnp.sum(gmf * mix[...].astype(F32), axis=1, keepdims=True)
        rowsc_s[...] = inverse * inverse * dot / inner_total
        sgm_o[...] = (gmf * inverse[:, 0:1]).astype(BF)
        scores = nt(bc[:, :state], bc[:, state:])
        first, second = iota((rows, rows), 0), iota((rows, rows), 1)
        sct_s[...] = jnp.where(second >= first, scores, 0.0)
        scts_s[...] = jnp.where(second > first, scores, 0.0)
        wsum_s[...] = jnp.zeros_like(wsum_s)
        dbc_s[...] = jnp.zeros_like(dbc_s)
        rall_s[...] = jnp.zeros_like(rall_s)
        acc_s[...] = jnp.zeros_like(acc_s)
        group_lanes(dtc[0], dt_s, groups, per_group)
        group_lanes(dtc[1], cum_s, groups, per_group)
        group_rows(dtc[1], cumt_s, groups, per_group)

    step, cum, cumt = dt_s[g], cum_s[g], cumt_s[g]
    last = cum[rows - 1 : rows, :]
    fromx = spread(jnp.exp(cum), GC, head_dim)

    gs = nn(gm_s[...], wo[...])
    inverse, shrink = inv[:, 0:1], rowsc_s[:, 0:1]
    gv, yv = gate[...], y[...]
    sig = sigmoid(gv)
    silu = gv * sig
    gated = yv * silu
    dgain = jnp.sum(gs * gated * inverse, axis=0, keepdims=True)
    dgated = inverse * (gs * pv[5:6, :]) - gated * shrink
    dgate = (dgated * yv * (sig * (1.0 + gv * (1.0 - sig)))).astype(BF)
    dgate_o[...] = dgate
    dyb = (dgated * silu).astype(BF)
    dyf = dyb.astype(F32)
    dyef = dyf * fromx
    dye = dyef.astype(BF)
    dsl = tn(dye, bc[:, state:])

    @pl.when(t == count - 1)
    def _():
        gin_s[...] = jnp.zeros_like(gin_s)

    @pl.when(t < count - 1)
    def _():
        chain_copy(slot).wait_recv()
        gin_s[...] = crecv[slot]

    @pl.when(t > 0)
    def _():
        csend[slot] = (through_rows(cumt, rows, head_dim, state) * gin_s[...].astype(F32) + dsl).astype(BF)
        chain_copy(slot).start()

    to_end = jnp.exp(last - cum)
    stepx = spread(step, GC, head_dim)
    endx = spread(to_end, GC, head_dim)
    xf = x[...].astype(F32)
    xp = (xf * stepx).astype(BF)
    xr = (xf * stepx * endx).astype(BF)
    gb = nt(bc[:, :state], gin_s[...])
    cs = nt(bc[:, state:], s_in[...])
    dbc_s[:, :state] += nn(xr, gin_s[...])
    dbc_s[:, state:] += nn(dye, s_in[...])

    lane = iota((rows, LANES), 1)
    wsum = wsum_s[...]
    colsum = jnp.zeros((rows, LANES), F32)
    within = []
    for pair in range(GC // LANES):
        cols = slice(LANES * pair, LANES * (pair + 1))
        xpp, dyp = xp[:, cols], dyb[:, cols]
        outs = []
        for side in range(2):
            i = 2 * pair + side
            mine = (lane < head_dim) if side == 0 else (lane >= head_dim)
            decay = jnp.exp(jnp.minimum(cumt[i : i + 1, :] - cum[:, i : i + 1], 0.0))
            outs.append(nn((decay * sct_s[...]).astype(BF), dyp))
            weight = decay * nt(jnp.where(mine, xpp, jnp.zeros_like(xpp)), dyp)
            wsum = wsum + weight
            pairs = (weight * scts_s[...]).astype(BF)
            colsum = colsum + nn(pairs, (lane == i).astype(BF))
            rt_s[g, i : i + 1, :] = jnp.sum(pairs.astype(F32), axis=0, keepdims=True)
        within.append(jnp.where(lane < head_dim, outs[0], outs[1]))
    wsum_s[...] = wsum
    u = jnp.concatenate(within, axis=1) + endx * gb

    heads = (iota((GC, LANES), 0) // head_dim == iota((GC, LANES), 1)).astype(BF)
    ddir_s[g] = nn((xf * u).astype(BF), heads)
    net_s[g] = nn((dyef * cs).astype(BF), heads) - colsum
    rv_s[g] = step * to_end * nn((xf * gb).astype(BF), heads)
    inner = gin_s[...].astype(F32) * s_in[...].astype(F32)
    per_channel = lax.dot_general(
        jnp.ones((8, inner.shape[1]), F32), inner, (((1,), (1,)), ((), ())), precision=HIGHEST, preferred_element_type=F32
    )
    k_s[g] = jnp.exp(last) * exact(per_channel, heads.astype(F32))

    dx = stepx * u + pv[6:7, :] * dyf
    dconv = dx * silu_slope(conv_rows(vpre, pv, rows))

    @pl.when(t > 0)
    def _():
        hsend[slot] = dconv[:8, :]
        halo_copy(slot).start()

    sums = conv_sums(dconv, vpre, rows)
    sums.append(dgain)
    sums.append(jnp.sum(dyf * xf, axis=0, keepdims=True))
    sums.append(jnp.zeros((1, GC), F32))
    vs_o[...] = jnp.concatenate(sums, axis=0)
    acc_s[...] += nt(dgate, wg[...])

    @pl.when(t == count - 1)
    def _():
        halo_s[...] = jnp.zeros_like(halo_s)

    @pl.when(t < count - 1)
    def _():
        halo_copy(slot).wait_recv()
        halo_s[...] = hrecv[slot]

    dval = conv_transposed(dconv, halo_s[...], pv, rows).astype(BF)
    dval_o[...] = dval
    acc_s[...] += nt(dval, wv[...])

    @pl.when(g == groups - 1)
    def _():
        first, second = iota((rows, rows), 0), iota((rows, rows), 1)
        weights = jnp.where(second >= first, wsum_s[...], 0.0).astype(BF)
        db = dbc_s[:, :state] + nn(weights, bc[:, state:])
        dc = dbc_s[:, state:] + tn(weights, bc[:, :state])
        dsc = jnp.concatenate([db, dc], axis=1) * silu_slope(conv_rows(spre, ps, rows))

        @pl.when(t > 0)
        def _():
            tsend[idx] = dsc[:8, :]
            tail_copy(idx).start()

        ssums = conv_sums(dsc, spre, rows)
        ssums.append(jnp.zeros((3, 2 * state), F32))
        ss_o[...] = jnp.concatenate(ssums, axis=0)
        net, rv, ddir, const = net_s[0], rv_s[0], ddir_s[0], k_s[0]
        rall_s[0:per_group, :] = rt_s[0, 0:per_group, :]
        for other in range(1, groups):
            shift = per_group * other
            net = net + pltpu.roll(net_s[other], shift, 1)
            rv = rv + pltpu.roll(rv_s[other], shift, 1)
            ddir = ddir + pltpu.roll(ddir_s[other], shift, 1)
            const = const + pltpu.roll(k_s[other], shift, 1)
            rall_s[shift : shift + per_group, :] = rt_s[other, 0:per_group, :]
        net = net + rall_s[...].T
        da = exact((second >= first).astype(F32), net) + exact((second < first).astype(F32), rv) + const[0:1, :]
        rate = jnp.exp(ph[1:2, :])
        dstep = (ddir - da * rate) * dtc[2]
        dstep_o[...] = dstep.astype(BF)
        hs_o[...] = jnp.concatenate(
            [
                jnp.sum(dstep, axis=0, keepdims=True),
                jnp.sum(-da * dtc[0] * rate, axis=0, keepdims=True),
                jnp.zeros((6, LANES), F32),
            ],
            axis=0,
        )

        @pl.when(t == count - 1)
        def _():
            halo2_s[...] = jnp.zeros_like(halo2_s)

        @pl.when(t < count - 1)
        def _():
            tail_copy(idx).wait_recv()
            halo2_s[...] = trecv[idx]

        dst = conv_transposed(dsc, halo2_s[...], ps, rows).astype(BF)
        dst_o[...] = dst
        psend[idx] = (acc_s[...] + nt(dst, ws[...]) + nt(dstep_o[...], wt[...])).astype(BF)
        part_copy(idx).start()

    def finish(i):
        j = lax.rem(i, micro)
        part_copy(i).wait()
        which = 1 - i // micro
        row_mask = mask[j][:, 0:1]

        def close(u, incoming):
            uf = u.astype(F32)
            grad_normed = psend[i].astype(F32) + precv[i].astype(F32)
            root_inv = lax.rsqrt(jnp.mean(uf * uf, axis=1, keepdims=True) + EPS)
            nacc_s[which] += jnp.broadcast_to(jnp.sum(grad_normed * uf * root_inv, axis=0, keepdims=True), (8, model))
            weighted = grad_normed * pn[which][0:1, :]
            shared = jnp.mean(weighted * uf, axis=1, keepdims=True) * root_inv * root_inv * root_inv
            kept = (row_mask * incoming.astype(F32)).astype(BF).astype(F32)
            psend[i] = (root_inv * weighted - uf * shared + kept).astype(BF)

        @pl.when(i < micro)
        def _():
            close(out0[j], cot[j])

        @pl.when(i >= micro)
        def _():
            close(tokens[j], psend[j])

        @pl.when(which == p)
        def _():
            out_copy(i).start()

    @pl.when((g == 1) & (idx > 1))
    def _():
        finish(idx - 2)

    @pl.when((g == groups - 1) & (idx == total_idx - 1))
    def _():
        finish(idx - 1)
        finish(idx)
        norm_o[...] = nacc_s[...]
        for i in range(total_idx):

            @pl.when(1 - i // micro == p)
            def _():
                out_copy(i).wait()

        @pl.when(t > 0)
        def _():
            for i in range(total_idx):
                tail_copy(i).wait_send()

            def drain(i, carry):
                chain_copy(i).wait_send()
                halo_copy(i).wait_send()
                return carry

            lax.fori_loop(0, total_idx * groups, drain, 0)


def all_of(shape, buffers=2):
    spec = functools.partial(pl.BlockSpec, shape, lambda q, s, g: (0,) * len(shape))
    return spec(pipeline_mode=pl.Buffered(buffers)) if buffers != 2 else spec()


def fused_specs(turned):
    def layer(q):
        return 1 - q if turned else q

    def item(*shape):
        zeros = (0,) * len(shape)
        return pl.BlockSpec((None, None) + shape, lambda q, s, g: (layer(q), s) + zeros)

    def item_cols(rows):
        return pl.BlockSpec((None, None, rows, GC), lambda q, s, g: (layer(q), s, 0, g))

    def item_rows(cols):
        return pl.BlockSpec((None, None, GC, cols), lambda q, s, g: (layer(q), s, g, 0))

    def layer_cols(rows):
        return pl.BlockSpec((None, rows, GC), lambda q, s, g: (layer(q), 0, g))

    def layer_all(*shape):
        zeros = (0,) * len(shape)
        return pl.BlockSpec((None,) + shape, lambda q, s, g: (layer(q),) + zeros)

    return item, item_cols, item_rows, layer_cols, layer_all


def forward_call(tokens, mask, w, par, count, head_dim):
    micro, rows, model = tokens.shape
    width, states = w.value.shape[2], w.state.shape[2]
    state = states // 2
    groups = width // GC
    item, item_cols, item_rows, layer_cols, layer_all = fused_specs(False)
    slots = 2 * micro
    dma = pltpu.SemaphoreType.DMA
    vmem = pltpu.VMEM
    ins = [
        (tokens, all_of(tokens.shape, 1)),
        (mask, all_of(mask.shape, 1)),
        (w.value, layer_cols(model)),
        (w.gate, layer_cols(model)),
        (w.out, layer_cols(model)),
        (w.state, layer_all(model, states)),
        (w.step, layer_all(model, LANES)),
        (par.value, layer_cols(8)),
        (par.state, layer_all(8, states)),
        (par.head, layer_all(8, LANES)),
        (par.norm, layer_all(8, model)),
    ]
    anywhere = pl.BlockSpec(memory_space=pl.ANY)
    pair = (2, micro)
    outs = [
        (((micro, rows, model), BF), anywhere),
        (((micro, rows, model), BF), anywhere),
        (((slots, rows, model), BF), anywhere),
        (((slots, rows, LANES), F32), all_of((slots, rows, LANES))),
        ((pair + (rows, model), BF), item(rows, model)),
        ((pair + (rows + HALO, width), F32), item_cols(rows + HALO)),
        ((pair + (rows + HALO, states), F32), item(rows + HALO, states)),
        ((pair + (rows, width), BF), item_cols(rows)),
        ((pair + (rows, states), BF), item(rows, states)),
        ((pair + (3, rows, LANES), F32), item(3, rows, LANES)),
        ((pair + (rows, width), F32), item_cols(rows)),
        ((pair + (rows, width), F32), item_cols(rows)),
        ((pair + (rows, width), BF), item_cols(rows)),
        ((pair + (width, state), BF), item_rows(state)),
    ]
    lanes = vmem((groups, rows, LANES), F32)
    scratch = [
        vmem((rows + HALO, model), BF),
        vmem((rows, rows), F32),
        lanes,
        lanes,
        vmem((groups, 8, rows), F32),
        vmem((rows, model), F32),
        vmem((rows, LANES), F32),
        vmem((slots, rows, model), BF),
        vmem((slots, rows, model), BF),
        vmem((slots, rows, LANES), F32),
        vmem((slots, rows, LANES), F32),
        vmem((slots * groups, GC, state), BF),
        vmem((slots * groups, GC, state), BF),
        vmem((micro, HALO, model), BF),
        vmem((micro, HALO, model), BF),
        dma((slots,)),
        dma((slots,)),
        dma((slots,)),
        dma((slots,)),
        dma((slots * groups,)),
        dma((slots * groups,)),
        dma((micro,)),
        dma((micro,)),
        dma((1,)),
        dma((1,)),
        dma((micro,)),
        dma((slots,)),
        dma((slots,)),
    ]
    kernel = functools.partial(fused_forward, count, head_dim, micro)
    flops = slots * (6 * rows * model * width + 6 * rows * rows * width)
    options = fused_options(pair + (groups,), ins, outs, scratch, 2, flops, 60 * slots * rows * width)
    return pl.pallas_call(kernel, **options)(*[array for array, _ in ins])


def fused_options(grid, ins, outs, scratch, collective, flops, traffic):
    return dict(
        grid=grid,
        in_specs=[spec for _, spec in ins],
        out_specs=[spec for _, spec in outs],
        out_shape=[jax.ShapeDtypeStruct(*kind) for kind, _ in outs],
        scratch_shapes=scratch,
        cost_estimate=pl.CostEstimate(flops=flops, bytes_accessed=traffic, transcendentals=0),
        compiler_params=pltpu.CompilerParams(
            collective_id=collective,
            has_side_effects=True,
            vmem_limit_bytes=VMEM_LIMIT,
            dimension_semantics=(SEQUENTIAL,) * len(grid),
        ),
    )


def backward_fused_call(cot, tokens, out0, mask, kept, w, par, count, head_dim):
    micro, rows, model = tokens.shape
    width, states = w.value.shape[2], w.state.shape[2]
    state = states // 2
    groups = width // GC
    item, item_cols, item_rows, layer_cols, layer_all = fused_specs(True)
    slots = 2 * micro
    dma = pltpu.SemaphoreType.DMA
    vmem = pltpu.VMEM
    ins = [
        (cot, all_of(cot.shape, 1)),
        (tokens, all_of(tokens.shape, 1)),
        (out0, all_of(out0.shape, 1)),
        (mask, all_of(mask.shape, 1)),
        (kept.inv, item(rows, LANES)),
        (kept.mix, item(rows, model)),
        (kept.vpre, item_cols(rows + HALO)),
        (kept.spre, item(rows + HALO, states)),
        (kept.x, item_cols(rows)),
        (kept.bc, item(rows, states)),
        (kept.dtc, item(3, rows, LANES)),
        (kept.gate, item_cols(rows)),
        (kept.y, item_cols(rows)),
        (kept.s_in, item_rows(state)),
        (w.value, layer_cols(model)),
        (w.gate, layer_cols(model)),
        (w.out, layer_cols(model)),
        (w.state, layer_all(model, states)),
        (w.step, layer_all(model, LANES)),
        (par.value, layer_cols(8)),
        (par.state, layer_all(8, states)),
        (par.head, layer_all(8, LANES)),
        (par.norm, all_of(par.norm.shape, 1)),
    ]
    pair = (2, micro)
    outs = [
        (((micro, rows, model), BF), pl.BlockSpec(memory_space=pl.ANY)),
        ((pair + (rows, width), BF), item_cols(rows)),
        ((pair + (rows, width), BF), item_cols(rows)),
        ((pair + (rows, states), BF), item(rows, states)),
        ((pair + (rows, LANES), BF), item(rows, LANES)),
        ((pair + (rows, model), BF), item(rows, model)),
        ((pair + (8, width), F32), item_cols(8)),
        ((pair + (8, states), F32), item(8, states)),
        ((pair + (8, LANES), F32), item(8, LANES)),
        (((2, 8, model), F32), all_of((2, 8, model))),
    ]
    lanes = vmem((groups, rows, LANES), F32)
    square = vmem((rows, rows), F32)
    scratch = [
        vmem((rows, model), BF),
        vmem((rows, LANES), F32),
        vmem((GC, state), BF),
        vmem((8, GC), F32),
        vmem((8, states), F32),
        vmem((rows, model), F32),
        vmem((2, 8, model), F32),
        square,
        square,
        square,
        vmem((rows, states), F32),
        lanes,
        lanes,
        vmem((groups, 8, rows), F32),
        lanes,
        lanes,
        lanes,
        vmem((groups, 8, LANES), F32),
        vmem((groups, 8, rows), F32),
        vmem((LANES, rows), F32),
        vmem((slots, rows, model), BF),
        vmem((slots, rows, model), BF),
        vmem((slots * groups, GC, state), BF),
        vmem((slots * groups, GC, state), BF),
        vmem((slots * groups, 8, GC), F32),
        vmem((slots * groups, 8, GC), F32),
        vmem((slots, 8, states), F32),
        vmem((slots, 8, states), F32),
        dma((slots,)),
        dma((slots,)),
        dma((slots * groups,)),
        dma((slots * groups,)),
        dma((slots * groups,)),
        dma((slots * groups,)),
        dma((slots,)),
        dma((slots,)),
        dma((slots,)),
    ]
    kernel = functools.partial(fused_backward, count, head_dim, micro)
    flops = slots * (8 * rows * model * width + 16 * rows * rows * width)
    options = fused_options(pair + (groups,), ins, outs, scratch, 3, flops, 60 * slots * rows * width)
    return pl.pallas_call(kernel, **options)(*[array for array, _ in ins])


def fused_body(
    tokens_in,
    cotangent,
    lengths,
    in_gate,
    in_value,
    in_state,
    in_step,
    out_proj,
    norm_gain,
    conv_value,
    conv_state,
    bias_value,
    bias_state,
    step_bias,
    decay_log,
    skip_gain,
    gate_gain,
):
    layer, group, block = lax.axis_index(PIPE), lax.axis_index(DP), lax.axis_index(TENSOR)
    blocks, groups = lax.axis_size(TENSOR), lax.axis_size(DP)
    first_half = layer == 0
    micro, rows, model = tokens_in.shape
    shard_rows = in_value.shape[1]
    half = in_value.shape[2] // 2
    heads = step_bias.shape[1] // 2
    head_dim = half // heads
    width = half * blocks
    all_heads = heads * blocks
    states = in_state.shape[2]

    place = jnp.arange(2 * LANES)[None, :]
    head = jnp.arange(2 * heads)[:, None]
    step_lanes = (place == head // heads * LANES + lax.rem(head, heads)).astype(BF)
    per_head = jnp.pad(jnp.concatenate([step_bias, decay_log], axis=1), ((0, 0), (0, 2 * half - 4 * heads)))
    skip = jnp.repeat(skip_gain, head_dim, axis=1)
    channel = jnp.concatenate([conv_value[0], bias_value, gate_gain, skip, per_head], axis=0)
    shared = jnp.concatenate([norm_gain[0], conv_state[0].reshape(-1), bias_state[0]], axis=0)
    shared = jnp.pad(shared, (0, -shared.shape[0] % (8 * LANES))).reshape(-1, LANES)
    wv, wg, wo, wt, ws, channel, shared = gather_call(
        in_value[0],
        in_gate[0],
        out_proj[0],
        nn(in_step[0], step_lanes).astype(BF),
        in_state[0],
        channel,
        shared,
        blocks,
        groups,
    )
    place = jnp.arange(blocks * LANES)[:, None]
    packed = lax.rem(place, LANES) + heads * (place // LANES) == jnp.arange(LANES)[None, :]
    packed = (packed & (lax.rem(place, LANES) < heads)).astype(BF)
    step_w = nn(wt.reshape(2 * model, blocks * LANES), packed).astype(BF).reshape(2, model, LANES)
    per_head = channel[:, :, 7, : 4 * heads].reshape(2, blocks, 2, 2, heads)
    per_head = lax.dynamic_index_in_dim(per_head, layer, 3, keepdims=False)
    head_par = per_head.transpose(0, 2, 1, 3).reshape(2, 2, all_heads)
    head_par = jnp.pad(head_par, ((0, 0), (0, 6), (0, LANES - all_heads)))
    channel = lax.dynamic_slice_in_dim(channel, layer * half, half, 3)
    value_par = channel.transpose(0, 2, 1, 3).reshape(2, 8, width)
    shared = shared.reshape(2, -1)
    state_par = jnp.pad(shared[:, model : model + 5 * states].reshape(2, 5, states), ((0, 0), (0, 3), (0, 0)))
    norm_par = jnp.broadcast_to(shared[:, None, :model], (2, 8, model))
    par = Bundle(value=value_par, head=head_par, state=state_par, norm=norm_par)
    w = Bundle(value=wv, gate=wg, out=wo, state=ws, step=step_w)

    valid = block * rows + jnp.arange(rows)[None, :] < lengths[:, None]
    mask = jnp.broadcast_to(valid.astype(F32)[:, :, None], (micro, rows, LANES))

    out, low_out, mix, inv, nx, vpre, spre, x, bc, dtc, gate, y, gg, s_in = forward_call(
        tokens_in, mask, w, par, blocks, head_dim
    )
    kept = Bundle(
        inv=inv.reshape(2, micro, rows, LANES),
        mix=mix.reshape(2, micro, rows, model),
        vpre=vpre,
        spre=spre,
        x=x,
        bc=bc,
        dtc=dtc,
        gate=gate,
        y=y,
        s_in=s_in,
    )
    grads, dval, dgate, dst, dstep, sgm, vsums, ssums, hsums, nsums = backward_fused_call(
        cotangent, tokens_in, low_out, mask, kept, w, par, blocks, head_dim
    )

    def long(value, q):
        return value[q].reshape(micro * rows, value.shape[3])

    lane = jnp.arange(LANES)[:, None]
    by_block = (8 * (lane // heads) + lax.rem(lane, heads) == jnp.arange(LANES)[None, :]) & (lane < all_heads)
    big, pack, turned = [], [], []
    for q in range(2):
        normed = long(nx, q)
        big += [
            tn(normed, long(dval, q)).astype(BF),
            tn(normed, long(dgate, q)).astype(BF),
            tn(long(sgm, q), long(gg, q)).astype(BF),
        ]
        turned.append(tn(long(dst, q), normed))
        step_lanes = nn(long(dstep, q), by_block.astype(BF)).astype(BF)
        step_grad = tn(step_lanes[:, : 8 * blocks], normed)
        ssum, hsum = jnp.sum(ssums[q], axis=0), jnp.sum(hsums[q], axis=0)
        rest = [
            nsums[q, 0][None],
            jnp.pad(ssum[:5].reshape(1, -1), ((0, 0), (0, width - 5 * states))),
            jnp.zeros((6, width), F32),
        ]
        hsum = hsum[:2, :all_heads].reshape(2, blocks, heads).transpose(1, 0, 2).reshape(blocks, 2 * heads)
        hsum = jnp.pad(hsum, ((0, 0), (0, half - 2 * heads))).reshape(1, width)
        pack.append(jnp.concatenate([jnp.sum(vsums[q], axis=0)[:7], hsum, step_grad] + rest, axis=0))
    turned = lax.psum_scatter(
        jnp.concatenate(turned, axis=0), (PIPE, DP, TENSOR), scatter_dimension=0, tiled=True
    )
    grad_value, grad_gate, grad_out, chan, step_grad, rest = reduce_call(big, jnp.stack(pack), blocks, groups)

    step_grad = step_grad.reshape(2, 8, shard_rows)[:, :heads].reshape(2 * heads, shard_rows).T
    grad_state = turned.T
    position = group * blocks + block
    ranks = groups * blocks

    def share(value):
        size = value.shape[-1] // ranks
        return lax.dynamic_slice_in_dim(value, position * size, size, value.ndim - 1)

    head_sums = chan[7].reshape(2, half)[:, : 2 * heads].reshape(2, 2, heads).transpose(1, 0, 2).reshape(2, -1)
    norm_sum = share(rest[0])
    conv_sum = share(rest[1, : 5 * states].reshape(5, states))
    return (
        out[None],
        grads[None],
        grad_gate[None],
        grad_value[None],
        grad_state[None],
        step_grad[None],
        grad_out[None],
        norm_sum[None],
        chan[None, :4],
        conv_sum[None, :4],
        chan[None, 4],
        conv_sum[None, 4],
        head_sums[None, 0],
        head_sums[None, 1],
        jnp.sum(chan[6].reshape(2 * heads, head_dim), axis=1)[None],
        chan[None, 5],
    )


def body(
    tokens_in,
    cotangent,
    lengths,
    in_gate,
    in_value,
    in_state,
    in_step,
    out_proj,
    norm_gain,
    conv_value,
    conv_state,
    bias_value,
    bias_state,
    step_bias,
    decay_log,
    skip_gain,
    gate_gain,
):
    layer = lax.axis_index(PIPE)
    block = lax.axis_index(TENSOR)
    blocks = lax.axis_size(TENSOR)
    group = lax.axis_index(DP)
    groups = lax.axis_size(DP)
    first_half = layer == 0
    micro, rows, model = tokens_in.shape
    shard_rows = in_value.shape[1]
    half = in_value.shape[2] // 2
    heads = step_bias.shape[1] // 2
    head_dim = half // heads
    width = half * blocks
    all_heads = heads * blocks
    states = in_state.shape[2]
    state = states // 2
    inner_total = 2 * width

    def halves(value):
        keep = lax.dynamic_slice_in_dim(value, layer * half_of(value), half_of(value), value.ndim - 1)
        send = lax.dynamic_slice_in_dim(value, (1 - layer) * half_of(value), half_of(value), value.ndim - 1)
        return by_layer(keep, swap_pipe(send))

    def half_of(value):
        return value.shape[-1] // 2

    def by_layer(own, other):
        return jnp.where(first_half, own, other), jnp.where(first_half, other, own)

    channel = jnp.concatenate([conv_value[0], bias_value, gate_gain], axis=0)
    channel_both = halves(channel)
    head_both = halves(jnp.concatenate([step_bias, decay_log, skip_gain], axis=0))
    flat_heads = [jnp.pad(v.reshape(1, 3 * heads), ((0, 0), (0, half - 3 * heads))) for v in head_both]
    packed = gather_tensor(jnp.concatenate(list(channel_both) + flat_heads + [jnp.zeros((2, half), F32)], axis=0))
    shared = jnp.concatenate([norm_gain[0], conv_state[0].reshape(-1), bias_state[0]], axis=0)
    shared_both = by_layer(shared, swap_pipe(shared))
    params = []
    for q in range(2):
        per_head = packed[12 + q].reshape(blocks, half)[:, : 3 * heads].reshape(blocks, 3, heads)
        per_head = per_head.transpose(1, 0, 2).reshape(3, all_heads)
        skip = jnp.repeat(per_head[2:3], head_dim, axis=1)
        value_par = jnp.concatenate([packed[6 * q : 6 * q + 6], skip, jnp.zeros((1, width), F32)], axis=0)
        head_par = jnp.pad(per_head, ((0, 5), (0, LANES - all_heads)))
        state_par = jnp.concatenate(
            [
                shared_both[q][model : model + 4 * states].reshape(4, states),
                shared_both[q][model + 4 * states :].reshape(1, states),
                jnp.zeros((3, states), F32),
            ],
            axis=0,
        )
        params.append(Bundle(value=value_par, head=head_par, state=state_par, norm=shared_both[q][:model]))

    step_both = halves(in_step[0])
    step_all = gather_tensor(jnp.concatenate(step_both, axis=1)).reshape(shard_rows, blocks, 2, heads)
    state_both = by_layer(in_state[0], swap_pipe(in_state[0]))
    value_both, gate_both, out_both = halves(in_value[0]), halves(in_gate[0]), halves(out_proj[0])
    weights = []
    for q in range(2):
        step_q = jnp.pad(step_all[:, :, q].reshape(shard_rows, all_heads), ((0, 0), (0, LANES - all_heads)))
        small = gather_dp(jnp.concatenate([state_both[q], step_q], axis=1))
        weights.append(
            Bundle(
                state=small[:, :states],
                step=small[:, states:],
                value=gather_dp(gather_tensor(value_both[q])),
                gate=gather_dp(gather_tensor(gate_both[q])),
                out=gather_dp(gather_tensor(out_both[q])),
            )
        )

    masks = [
        (block * rows + jnp.arange(rows) < lengths[s]).astype(F32)[:, None] for s in range(micro)
    ]

    def forward(u, s, q):
        w, par = weights[q], params[q]
        ext = jnp.concatenate([shift_tensor(u[-HALO:], 1), u], axis=0).astype(F32)
        root_inv = lax.rsqrt(jnp.mean(ext * ext, axis=1, keepdims=True) + EPS)
        nx = (ext * root_inv * par.norm[None, :]).astype(BF)
        vpre, spre, x, bc, dtc, yw, loc = front_call(nx, w, par, head_dim, state)
        through = jnp.repeat(jnp.exp(dtc[1, rows - 1, :all_heads]), head_dim)[:, None]
        s_in = jnp.zeros((width, state), BF)
        for k in range(1, blocks):
            sent = (through * s_in.astype(F32) + loc).astype(BF)
            got = lax.ppermute(sent, TENSOR, [(k - 1, k)])
            s_in = got if k == 1 else jnp.where(block == k, got, s_in)
        gate, y, gg, part, squares = finish_call(nx, w, par, yw, s_in, bc, dtc, head_dim)
        total = squares[:, 0]
        total = total + swap_pipe(total)
        inverse = lax.rsqrt(total / inner_total + EPS)[:, None]
        mixed = inverse * (part.astype(F32) + swap_pipe(part).astype(F32))
        result = (masks[s] * (u.astype(F32) + mixed)).astype(BF)
        kept = Bundle(
            u=u, nx=nx, root_inv=root_inv[HALO:], vpre=vpre, spre=spre, x=x, bc=bc, dtc=dtc, s_in=s_in, through=through,
            gate=gate, y=y, gg=gg, inverse=inverse, mixed=mixed,
        )
        return result, kept

    def backward(incoming, s, q, kept):
        w, par = weights[q], params[q]
        gm = (masks[s] * incoming.astype(F32)).astype(BF)
        gmf = gm.astype(F32)
        inverse = kept.inverse
        dot = jnp.sum(gmf * kept.mixed, axis=1, keepdims=True)
        shrink = inverse * inverse * dot / inner_total
        rowsc = jnp.concatenate([inverse, shrink, jnp.zeros((rows, LANES - 2), F32)], axis=1)
        dy, dgate, dsl, dgain = gate_call(gm, w, par, kept.y, kept.gate, rowsc, kept.bc, kept.dtc, head_dim)
        g_in = jnp.zeros((width, state), BF)
        for k in range(blocks - 2, -1, -1):
            sent = (kept.through * g_in.astype(F32) + dsl).astype(BF)
            got = lax.ppermute(sent, TENSOR, [(k + 1, k)])
            g_in = got if k == blocks - 2 else jnp.where(block == k, got, g_in)
        dconv, dsc, dstep, vsums, ssums, hsums = backward_call(
            dy, kept.x, kept.vpre, kept.spre, kept.bc, kept.dtc, kept.s_in, g_in, par, head_dim
        )
        halo = shift_tensor(jnp.concatenate([dconv[:8], dsc[:8]], axis=1), -1)
        dval, dst, part = conv_call(dconv, halo, dsc, dgate, dstep, w, par)
        grad_normed = part.astype(F32) + swap_pipe(part).astype(F32)
        uf, root_inv = kept.u.astype(F32), kept.root_inv
        grad_norm = jnp.sum(grad_normed * uf * root_inv, axis=0)
        weighted = grad_normed * par.norm[None, :]
        grad_u = root_inv * weighted - uf * root_inv**3 * jnp.mean(weighted * uf, axis=1, keepdims=True) + gmf
        scaled_gm = (gmf * inverse).astype(BF)
        channel_sums = jnp.concatenate([vsums[:5], dgain[:1], vsums[5:6]], axis=0)
        sums = (channel_sums, ssums[:5], hsums[:2, :all_heads], grad_norm)
        return grad_u.astype(BF), (dval, dgate, dst, dstep, scaled_gm), sums

    outs, kept = [], []
    current = [tokens_in[s] for s in range(micro)]
    for q in range(2):
        pairs = [forward(current[s], s, q) for s in range(micro)]
        current = [pair[0] for pair in pairs]
        outs.append(jnp.stack(current))
        kept.append([pair[1] for pair in pairs])

    grads = [None, None]
    reduced = [None, None]
    incoming = [cotangent[s] for s in range(micro)]
    for q in (1, 0):
        results = [backward(incoming[s], s, q, kept[q][s]) for s in range(micro)]
        incoming = [r[0] for r in results]
        grads[q] = jnp.stack(incoming)
        stacked = [jnp.concatenate([r[1][k] for r in results], axis=0) for k in range(5)]
        dval, dgate, dst, dstep, scaled_gm = stacked
        normed = jnp.concatenate([kept[q][s].nx[HALO:] for s in range(micro)], axis=0)
        gg = jnp.concatenate([kept[q][s].gg for s in range(micro)], axis=0)
        sums = [functools.reduce(jnp.add, [r[2][k] for r in results]) for k in range(4)]

        big = [tn(scaled_gm, gg).astype(BF), tn(normed, dgate).astype(BF), tn(normed, dval).astype(BF)]
        big = [reduce_tensor(take_cols(reduce_dp(v))) for v in big]
        turned = reduce_dp(tn(dst, normed).astype(BF))
        turned = reduce_tensor(take_first(turned.reshape(blocks, -1, model)))
        step_grad = tn(dstep, normed)[:all_heads]
        by_block = jnp.concatenate(
            [
                sums[0].reshape(7, blocks, half).transpose(1, 0, 2).reshape(blocks, -1),
                step_grad.reshape(blocks, -1),
                sums[2].reshape(2, blocks, heads).transpose(1, 0, 2).reshape(blocks, -1),
            ],
            axis=1,
        )
        per_block = reduce_tensor(take_first(sum_all_dp(by_block)))
        common = sum_all_tensor(sum_all_dp(jnp.concatenate([sums[1].reshape(-1), sums[3]], axis=0)))
        reduced[q] = (big, turned, per_block, common)

    def own_and_other(kind):
        return jnp.where(first_half, kind(0), kind(1)), jnp.where(first_half, kind(1), kind(0))

    def join(kind):
        own, other = own_and_other(kind)
        got = swap_pipe(other)
        return jnp.where(first_half, own, got), jnp.where(first_half, got, own)

    def columns(k):
        low, high = join(lambda q: reduced[q][0][k].astype(BF))
        return jnp.concatenate([low, high], axis=1).astype(F32)

    grad_out, grad_gate, grad_value = columns(0), columns(1), columns(2)
    own, other = own_and_other(lambda q: reduced[q][1])
    grad_state = (own + swap_pipe(other.astype(BF)).astype(F32)).T
    low, high = join(lambda q: reduced[q][2])
    cut1, cut2 = 7 * half, 7 * half + heads * model
    chan = jnp.concatenate([low[:cut1].reshape(7, half), high[:cut1].reshape(7, half)], axis=1)
    step_grad = jnp.concatenate([low[cut1:cut2].reshape(heads, model), high[cut1:cut2].reshape(heads, model)], axis=0)
    step_grad = lax.dynamic_slice_in_dim(step_grad, group * shard_rows, shard_rows, 1).T
    head_sums = jnp.concatenate([low[cut2:].reshape(2, heads), high[cut2:].reshape(2, heads)], axis=1)
    own, other = own_and_other(lambda q: reduced[q][3])
    conv_sum = own[: 5 * states] + swap_pipe(other[: 5 * states])
    norm_sum = own[5 * states :]
    position = group * blocks + block
    ranks = groups * blocks

    def share(value):
        size = value.shape[-1] // ranks
        return lax.dynamic_slice_in_dim(value, position * size, size, value.ndim - 1)

    conv_sum = share(conv_sum.reshape(5, states))
    return (
        jnp.where(first_half, outs[0], outs[1])[None],
        jnp.where(first_half, grads[0], grads[1])[None],
        grad_gate[None],
        grad_value[None],
        grad_state[None],
        step_grad[None],
        grad_out[None],
        share(norm_sum)[None],
        chan[None, :4],
        conv_sum[None, :4],
        chan[None, 4],
        conv_sum[None, 4],
        head_sums[None, 0],
        head_sums[None, 1],
        jnp.sum(chan[6].reshape(2 * heads, head_dim), axis=1)[None],
        chan[None, 5],
    )


def solution(mesh):
    in_specs = (
        P(DP, TENSOR, None),
        P(DP, TENSOR, None),
        P(DP),
        P(PIPE, DP, TENSOR),
        P(PIPE, DP, TENSOR),
        P(PIPE, DP, None),
        P(PIPE, DP, TENSOR),
        P(PIPE, DP, TENSOR),
        P(PIPE, None),
        P(PIPE, None, TENSOR),
        P(PIPE, None, None),
        P(PIPE, TENSOR),
        P(PIPE, None),
        P(PIPE, TENSOR),
        P(PIPE, TENSOR),
        P(PIPE, TENSOR),
        P(PIPE, TENSOR),
    )
    out_specs = (
        P(PIPE, DP, TENSOR, None),
        P(PIPE, DP, TENSOR, None),
        P(PIPE, DP, TENSOR),
        P(PIPE, DP, TENSOR),
        P(PIPE, None, (DP, TENSOR)),
        P(PIPE, DP, TENSOR),
        P(PIPE, DP, TENSOR),
        P(PIPE, (DP, TENSOR)),
        P(PIPE, None, TENSOR),
        P(PIPE, None, (DP, TENSOR)),
        P(PIPE, TENSOR),
        P(PIPE, (DP, TENSOR)),
        P(PIPE, TENSOR),
        P(PIPE, TENSOR),
        P(PIPE, TENSOR),
        P(PIPE, TENSOR),
    )

    def program(*args):
        columns = args[4].shape[2] // mesh.shape[TENSOR]
        fused = mesh.shape[DP] == 4 and mesh.shape[TENSOR] > 2 and columns // 2 % LANES == 0
        return mapped(fused_body if fused else body)(*args)

    def mapped(function):
        return jax.shard_map(function, mesh=mesh, in_specs=in_specs, out_specs=out_specs, check_vma=False)

    return program
```

```python
import functools
import types

import jax
import jax.numpy as jnp
from jax import lax
from jax.experimental import pallas as pl
from jax.experimental.pallas import tpu as pltpu
from jax.sharding import PartitionSpec as P

EPS = 1e-05
PIPE, DP, TENSOR = "pipe", "dp", "tensor"
SEQUENTIAL = "arbitrary"
Bundle = types.SimpleNamespace
HIGHEST = lax.Precision.HIGHEST
BF = jnp.bfloat16
F32 = jnp.float32
HALO = 16
GC = 256
LANES = 128


def nn(a, b):
    return jnp.dot(a, b, preferred_element_type=F32)


def nt(a, b):
    return lax.dot_general(a, b, (((1,), (1,)), ((), ())), preferred_element_type=F32)


def tn(a, b):
    return lax.dot_general(a, b, (((0,), (0,)), ((), ())), preferred_element_type=F32)


def exact(a, b):
    return jnp.dot(a, b, precision=HIGHEST, preferred_element_type=F32)


def sigmoid(v):
    return 1.0 / (1.0 + jnp.exp(-v))


def iota(shape, dim):
    return lax.broadcasted_iota(jnp.int32, shape, dim)


def spread(per_head, width, head_dim):
    lane = iota(per_head.shape, 1)
    parts = []
    for pair in range(width // LANES):
        parts.append(
            jnp.where(lane < head_dim, per_head[:, 2 * pair : 2 * pair + 1], per_head[:, 2 * pair + 1 : 2 * pair + 2])
        )
    return jnp.concatenate(parts, axis=1)


def conv_rows(pre, taps, rows):
    total = taps[4:5, :] + taps[3:4, :] * pre[HALO : HALO + rows, :]
    for k in range(3):
        total = total + taps[k : k + 1, :] * pre[HALO - 3 + k : HALO - 3 + k + rows, :]
    return total


def conv_sums(grad, pre, rows):
    sums = [jnp.sum(grad * pre[HALO - 3 + k : HALO - 3 + k + rows, :], axis=0, keepdims=True) for k in range(4)]
    sums.append(jnp.sum(grad, axis=0, keepdims=True))
    return sums


def conv_transposed(grad, halo, taps, rows):
    ext = jnp.concatenate([grad, halo], axis=0)
    total = taps[3:4, :] * grad
    for k in range(3):
        total = total + taps[k : k + 1, :] * ext[3 - k : 3 - k + rows, :]
    return total


def silu_slope(v):
    s = sigmoid(v)
    return s * (1.0 + v * (1.0 - s))


def group_lanes(values, dst, groups, per_group):
    for g in range(groups):
        dst[g] = values if g == 0 else pltpu.roll(values, LANES - per_group * g, 1)


def group_rows(values, dst, groups, per_group):
    turned = values.T
    for g in range(groups):
        dst[g, 0:per_group, :] = turned[per_group * g : per_group * (g + 1), :]


def scan_front(
    head_dim, nx, wv, ws, wt, pv, ps, ph, vpre_o, spre_o, x_o, bc_o, dtc_o, yw_o, loc_o, sc_s, dt_s, cum_s, cumt_s
):
    g = pl.program_id(0)
    groups = pl.num_programs(0)
    rows = x_o.shape[0]
    state = bc_o.shape[1] // 2
    per_group = GC // head_dim

    @pl.when(g == 0)
    def _():
        spre = nn(nx[...], ws[...])
        spre_o[...] = spre
        conv = conv_rows(spre, ps, rows)
        bc = (conv * sigmoid(conv)).astype(BF)
        bc_o[...] = bc
        scores = nt(bc[:, state:], bc[:, :state])
        lower = iota((rows, rows), 0) >= iota((rows, rows), 1)
        sc_s[...] = jnp.where(lower, scores, 0.0)
        raw = nn(nx[HALO:, :], wt[...]) + ph[0:1, :]
        step = jnp.maximum(raw, 0.0) + jnp.log(1.0 + jnp.exp(-jnp.abs(raw)))
        decay = -step * jnp.exp(ph[1:2, :])
        cum = exact(lower.astype(F32), decay)
        dtc_o[0] = step
        dtc_o[1] = cum
        dtc_o[2] = sigmoid(raw)
        group_lanes(step, dt_s, dt_s.shape[0], per_group)
        group_lanes(cum, cum_s, cum_s.shape[0], per_group)
        group_rows(cum, cumt_s, cumt_s.shape[0], per_group)

    pre = nn(nx[...], wv[...])
    vpre_o[...] = pre
    conv = conv_rows(pre, pv, rows)
    x = conv * sigmoid(conv)
    x_o[...] = x.astype(BF)
    step, cum, cumt = dt_s[g], cum_s[g], cumt_s[g]
    to_end = jnp.exp(cum[rows - 1 : rows, :] - cum)
    xp = (x * spread(step, GC, head_dim)).astype(BF)
    xr = (x * spread(step * to_end, GC, head_dim)).astype(BF)
    loc_o[...] = tn(xr, bc_o[:, :state])
    scores = sc_s[...]
    lane = iota((rows, LANES), 1)
    for pair in range(GC // LANES):
        cols = slice(LANES * pair, LANES * (pair + 1))
        outs = []
        for i in (2 * pair, 2 * pair + 1):
            diff = cum[:, i : i + 1] - cumt[i : i + 1, :]
            mix = (jnp.exp(jnp.minimum(diff, 0.0)) * scores).astype(BF)
            outs.append(nn(mix, xp[:, cols]))
        yw_o[:, cols] = jnp.where(lane < head_dim, outs[0], outs[1]) + pv[6:7, cols] * x[:, cols]


def scan_finish(
    head_dim, nx, wg, wo, yw, s_in, bc, dtc, pv, gate_o, y_o, gg_o, p_o, sq_o, acc_s, sq_s, cum_s
):
    g = pl.program_id(0)
    rows = yw.shape[0]
    state = bc.shape[1] // 2

    @pl.when(g == 0)
    def _():
        group_lanes(dtc[1], cum_s, cum_s.shape[0], GC // head_dim)
        acc_s[...] = jnp.zeros_like(acc_s)
        sq_s[...] = jnp.zeros_like(sq_s)

    gate = nn(nx[HALO:, :], wg[...])
    gate_o[...] = gate
    carried = nt(bc[:, state:], s_in[...])
    y = yw[...] + spread(jnp.exp(cum_s[g]), GC, head_dim) * carried
    y_o[...] = y
    gated = y * (gate * sigmoid(gate))
    gg = (gated * pv[5:6, :]).astype(BF)
    gg_o[...] = gg
    squares = gated * gated
    for part in range(GC // LANES):
        sq_s[...] += squares[:, LANES * part : LANES * (part + 1)]
    acc_s[...] += nt(gg, wo[...])

    @pl.when(g == pl.num_programs(0) - 1)
    def _():
        p_o[...] = acc_s[...].astype(BF)
        sq_o[...] = jnp.broadcast_to(jnp.sum(sq_s[...], axis=1, keepdims=True), sq_o.shape)


def gate_backward(head_dim, gm, wo, y, gate, rowsc, pv, bc, dtc, dy_o, dgate_o, dsl_o, dgain_o, cum_s):
    g = pl.program_id(0)
    state = bc.shape[1] // 2

    @pl.when(g == 0)
    def _():
        group_lanes(dtc[1], cum_s, cum_s.shape[0], GC // head_dim)

    gs = nn(gm[...], wo[...])
    inverse, shrink = rowsc[:, 0:1], rowsc[:, 1:2]
    gv, yv = gate[...], y[...]
    s = sigmoid(gv)
    silu = gv * s
    gated = yv * silu
    dgain = jnp.sum(gs * gated * inverse, axis=0, keepdims=True)
    dgain_o[...] = jnp.broadcast_to(dgain, dgain_o.shape)
    dgated = inverse * (gs * pv[5:6, :]) - gated * shrink
    dgate_o[...] = (dgated * yv * (s * (1.0 + gv * (1.0 - s)))).astype(BF)
    dy = dgated * silu
    dy_o[...] = dy.astype(BF)
    dye = (dy * spread(jnp.exp(cum_s[g]), GC, head_dim)).astype(BF)
    dsl_o[...] = tn(dye, bc[:, state:])


def scan_backward(
    head_dim,
    dy,
    x,
    vpre,
    spre,
    bc,
    dtc,
    s_in,
    g_in,
    pv,
    ps,
    ph,
    dconv_o,
    dsc_o,
    dstep_o,
    vs_o,
    ss_o,
    hs_o,
    sct_s,
    scts_s,
    wsum_s,
    dbc_s,
    dt_s,
    cum_s,
    cumt_s,
    net_s,
    rv_s,
    ddir_s,
    k_s,
    rt_s,
    rall_s,
):
    g = pl.program_id(0)
    rows = x.shape[0]
    state = bc.shape[1] // 2
    per_group = GC // head_dim
    groups = dt_s.shape[0]

    @pl.when(g == 0)
    def _():
        scores = nt(bc[:, :state], bc[:, state:])
        first, second = iota((rows, rows), 0), iota((rows, rows), 1)
        sct_s[...] = jnp.where(second >= first, scores, 0.0)
        scts_s[...] = jnp.where(second > first, scores, 0.0)
        wsum_s[...] = jnp.zeros_like(wsum_s)
        dbc_s[...] = jnp.zeros_like(dbc_s)
        rall_s[...] = jnp.zeros_like(rall_s)
        group_lanes(dtc[0], dt_s, groups, per_group)
        group_lanes(dtc[1], cum_s, groups, per_group)
        group_rows(dtc[1], cumt_s, groups, per_group)

    step, cum, cumt = dt_s[g], cum_s[g], cumt_s[g]
    last = cum[rows - 1 : rows, :]
    to_end = jnp.exp(last - cum)
    stepx = spread(step, GC, head_dim)
    endx = spread(to_end, GC, head_dim)
    fromx = spread(jnp.exp(cum), GC, head_dim)
    xf = x[...].astype(F32)
    dyb = dy[...]
    dyf = dyb.astype(F32)
    xp = (xf * stepx).astype(BF)
    xr = (xf * stepx * endx).astype(BF)
    dyef = dyf * fromx
    dye = dyef.astype(BF)
    gb = nt(bc[:, :state], g_in[...])
    cs = nt(bc[:, state:], s_in[...])
    dbc_s[:, :state] += nn(xr, g_in[...])
    dbc_s[:, state:] += nn(dye, s_in[...])

    lane = iota((rows, LANES), 1)
    wsum = wsum_s[...]
    colsum = jnp.zeros((rows, LANES), F32)
    within = []
    for pair in range(GC // LANES):
        cols = slice(LANES * pair, LANES * (pair + 1))
        xpp, dyp = xp[:, cols], dyb[:, cols]
        outs = []
        for side in range(2):
            i = 2 * pair + side
            mine = (lane < head_dim) if side == 0 else (lane >= head_dim)
            decay = jnp.exp(jnp.minimum(cumt[i : i + 1, :] - cum[:, i : i + 1], 0.0))
            outs.append(nn((decay * sct_s[...]).astype(BF), dyp))
            weight = decay * nt(jnp.where(mine, xpp, jnp.zeros_like(xpp)), dyp)
            wsum = wsum + weight
            pairs = (weight * scts_s[...]).astype(BF)
            colsum = colsum + nn(pairs, (lane == i).astype(BF))
            rt_s[g, i : i + 1, :] = jnp.sum(pairs.astype(F32), axis=0, keepdims=True)
        within.append(jnp.where(lane < head_dim, outs[0], outs[1]))
    wsum_s[...] = wsum
    u = jnp.concatenate(within, axis=1) + endx * gb

    heads = (iota((GC, LANES), 0) // head_dim == iota((GC, LANES), 1)).astype(BF)
    ddir_s[g] = nn((xf * u).astype(BF), heads)
    net_s[g] = nn((dyef * cs).astype(BF), heads) - colsum
    rv_s[g] = step * to_end * nn((xf * gb).astype(BF), heads)
    inner = g_in[...].astype(F32) * s_in[...].astype(F32)
    per_channel = lax.dot_general(
        jnp.ones((8, inner.shape[1]), F32), inner, (((1,), (1,)), ((), ())), precision=HIGHEST, preferred_element_type=F32
    )
    k_s[g] = jnp.exp(last) * exact(per_channel, heads.astype(F32))

    dx = stepx * u + pv[6:7, :] * dyf
    dconv = dx * silu_slope(conv_rows(vpre, pv, rows))
    dconv_o[...] = dconv
    sums = conv_sums(dconv, vpre, rows)
    sums.append(jnp.sum(dyf * xf, axis=0, keepdims=True))
    sums.append(jnp.zeros((2, GC), F32))
    vs_o[...] = jnp.concatenate(sums, axis=0)

    @pl.when(g == pl.num_programs(0) - 1)
    def _():
        first, second = iota((rows, rows), 0), iota((rows, rows), 1)
        net, rv, ddir, const = net_s[0], rv_s[0], ddir_s[0], k_s[0]
        rall_s[0:per_group, :] = rt_s[0, 0:per_group, :]
        for other in range(1, groups):
            shift = per_group * other
            net = net + pltpu.roll(net_s[other], shift, 1)
            rv = rv + pltpu.roll(rv_s[other], shift, 1)
            ddir = ddir + pltpu.roll(ddir_s[other], shift, 1)
            const = const + pltpu.roll(k_s[other], shift, 1)
            rall_s[shift : shift + per_group, :] = rt_s[other, 0:per_group, :]
        net = net + rall_s[...].T
        da = exact((second >= first).astype(F32), net) + exact((second < first).astype(F32), rv) + const[0:1, :]
        rate = jnp.exp(ph[1:2, :])
        dstep = (ddir - da * rate) * dtc[2]
        dstep_o[...] = dstep.astype(BF)
        hs_o[...] = jnp.concatenate(
            [
                jnp.sum(dstep, axis=0, keepdims=True),
                jnp.sum(-da * dtc[0] * rate, axis=0, keepdims=True),
                jnp.zeros((6, LANES), F32),
            ],
            axis=0,
        )
        weights = jnp.where(second >= first, wsum_s[...], 0.0).astype(BF)
        db = dbc_s[:, :state] + nn(weights, bc[:, state:])
        dc = dbc_s[:, state:] + tn(weights, bc[:, :state])
        dsc = jnp.concatenate([db, dc], axis=1) * silu_slope(conv_rows(spre, ps, rows))
        dsc_o[...] = dsc
        ssums = conv_sums(dsc, spre, rows)
        ssums.append(jnp.zeros((3, 2 * state), F32))
        ss_o[...] = jnp.concatenate(ssums, axis=0)


def conv_backward(dconv, halo_v, dsc, halo_s, dgate, dstep, pv, ps, wv, wg, ws, wt, dval_o, dst_o, p_o, acc_s):
    g = pl.program_id(0)
    rows = dconv.shape[0]

    @pl.when(g == 0)
    def _():
        dst = conv_transposed(dsc[...], halo_s[...], ps, rows).astype(BF)
        dst_o[...] = dst
        acc_s[...] = nt(dst, ws[...]) + nt(dstep[...], wt[...])

    dval = conv_transposed(dconv[...], halo_v[...], pv, rows).astype(BF)
    dval_o[...] = dval
    acc_s[...] += nt(dval, wv[...]) + nt(dgate[...], wg[...])

    @pl.when(g == pl.num_programs(0) - 1)
    def _():
        p_o[...] = acc_s[...].astype(BF)


def whole(shape):
    return pl.BlockSpec(shape, lambda g: (0,) * len(shape))


def by_cols(rows):
    return pl.BlockSpec((rows, GC), lambda g: (0, g))


def by_rows(cols):
    return pl.BlockSpec((GC, cols), lambda g: (g, 0))


def call(kernel, groups, ins, outs, scratch, flops, traffic, exps=0):
    arrays, in_specs = zip(*ins)
    shapes, out_specs = zip(*outs)
    return pl.pallas_call(
        kernel,
        grid=(groups,),
        in_specs=list(in_specs),
        out_specs=list(out_specs),
        out_shape=[jax.ShapeDtypeStruct(s, d) for s, d in shapes],
        scratch_shapes=scratch,
        cost_estimate=pl.CostEstimate(flops=flops, bytes_accessed=traffic, transcendentals=exps),
        compiler_params=pltpu.CompilerParams(vmem_limit_bytes=40 * 2**20, dimension_semantics=(SEQUENTIAL,)),
    )(*arrays)


def front_call(nx, w, par, head_dim, state):
    rows, width = nx.shape[0] - HALO, w.value.shape[1]
    model = nx.shape[1]
    groups = width // GC
    return call(
        functools.partial(scan_front, head_dim),
        groups,
        [
            (nx, whole(nx.shape)),
            (w.value, by_cols(model)),
            (w.state, whole(w.state.shape)),
            (w.step, whole(w.step.shape)),
            (par.value, by_cols(8)),
            (par.state, whole(par.state.shape)),
            (par.head, whole(par.head.shape)),
        ],
        [
            (((rows + HALO, width), F32), by_cols(rows + HALO)),
            (((rows + HALO, 2 * state), F32), whole((rows + HALO, 2 * state))),
            (((rows, width), BF), by_cols(rows)),
            (((rows, 2 * state), BF), whole((rows, 2 * state))),
            (((3, rows, LANES), F32), whole((3, rows, LANES))),
            (((rows, width), F32), by_cols(rows)),
            (((width, state), F32), by_rows(state)),
        ],
        [
            pltpu.VMEM((rows, rows), F32),
            pltpu.VMEM((groups, rows, LANES), F32),
            pltpu.VMEM((groups, rows, LANES), F32),
            pltpu.VMEM((groups, 8, rows), F32),
        ],
        2 * rows * model * (width + 3 * LANES) + 4 * rows * rows * width,
        2 * model * width + 12 * rows * width,
        rows * rows * width // head_dim,
    )


def finish_call(nx, w, par, yw, s_in, bc, dtc, head_dim):
    rows, width = yw.shape
    model = nx.shape[1]
    groups = width // GC
    state = s_in.shape[1]
    return call(
        functools.partial(scan_finish, head_dim),
        groups,
        [
            (nx, whole(nx.shape)),
            (w.gate, by_cols(model)),
            (w.out, by_cols(model)),
            (yw, by_cols(rows)),
            (s_in, by_rows(state)),
            (bc, whole(bc.shape)),
            (dtc, whole(dtc.shape)),
            (par.value, by_cols(8)),
        ],
        [
            (((rows, width), F32), by_cols(rows)),
            (((rows, width), F32), by_cols(rows)),
            (((rows, width), BF), by_cols(rows)),
            (((rows, model), BF), whole((rows, model))),
            (((rows, LANES), F32), whole((rows, LANES))),
        ],
        [
            pltpu.VMEM((rows, model), F32),
            pltpu.VMEM((rows, LANES), F32),
            pltpu.VMEM((groups, rows, LANES), F32),
        ],
        4 * rows * model * width,
        4 * model * width + 14 * rows * width,
    )


def gate_call(gm, w, par, y, gate, rowsc, bc, dtc, head_dim):
    rows, width = y.shape
    model = gm.shape[1]
    groups = width // GC
    state = bc.shape[1] // 2
    return call(
        functools.partial(gate_backward, head_dim),
        groups,
        [
            (gm, whole(gm.shape)),
            (w.out, by_cols(model)),
            (y, by_cols(rows)),
            (gate, by_cols(rows)),
            (rowsc, whole(rowsc.shape)),
            (par.value, by_cols(8)),
            (bc, whole(bc.shape)),
            (dtc, whole(dtc.shape)),
        ],
        [
            (((rows, width), BF), by_cols(rows)),
            (((rows, width), BF), by_cols(rows)),
            (((width, state), F32), by_rows(state)),
            (((8, width), F32), by_cols(8)),
        ],
        [pltpu.VMEM((groups, rows, LANES), F32)],
        2 * rows * model * width,
        2 * model * width + 14 * rows * width,
    )


def backward_call(dy, x, vpre, spre, bc, dtc, s_in, g_in, par, head_dim):
    rows, width = x.shape
    groups = width // GC
    state = bc.shape[1] // 2
    lanes = pltpu.VMEM((groups, rows, LANES), F32)
    square = pltpu.VMEM((rows, rows), F32)
    return call(
        functools.partial(scan_backward, head_dim),
        groups,
        [
            (dy, by_cols(rows)),
            (x, by_cols(rows)),
            (vpre, by_cols(rows + HALO)),
            (spre, whole(spre.shape)),
            (bc, whole(bc.shape)),
            (dtc, whole(dtc.shape)),
            (s_in, by_rows(state)),
            (g_in, by_rows(state)),
            (par.value, by_cols(8)),
            (par.state, whole(par.state.shape)),
            (par.head, whole(par.head.shape)),
        ],
        [
            (((rows, width), F32), by_cols(rows)),
            (((rows, 2 * state), F32), whole((rows, 2 * state))),
            (((rows, LANES), BF), whole((rows, LANES))),
            (((8, width), F32), by_cols(8)),
            (((8, 2 * state), F32), whole((8, 2 * state))),
            (((8, LANES), F32), whole((8, LANES))),
        ],
        [
            square,
            square,
            square,
            pltpu.VMEM((rows, 2 * state), F32),
            lanes,
            lanes,
            pltpu.VMEM((groups, 8, rows), F32),
            lanes,
            lanes,
            lanes,
            pltpu.VMEM((groups, 8, LANES), F32),
            pltpu.VMEM((groups, 8, rows), F32),
            pltpu.VMEM((LANES, rows), F32),
        ],
        12 * rows * rows * width,
        14 * rows * width,
        3 * rows * rows * width // head_dim,
    )


def conv_call(dconv, halo, dsc, dgate, dstep, w, par):
    rows, width = dconv.shape
    model = w.value.shape[0]
    groups = width // GC
    states = dsc.shape[1]
    halo_v, halo_s = halo[:, :width], halo[:, width:]
    return call(
        conv_backward,
        groups,
        [
            (dconv, by_cols(rows)),
            (halo_v, by_cols(8)),
            (dsc, whole(dsc.shape)),
            (halo_s, whole(halo_s.shape)),
            (dgate, by_cols(rows)),
            (dstep, whole(dstep.shape)),
            (par.value, by_cols(8)),
            (par.state, whole(par.state.shape)),
            (w.value, by_cols(model)),
            (w.gate, by_cols(model)),
            (w.state, whole(w.state.shape)),
            (w.step, whole(w.step.shape)),
        ],
        [
            (((rows, width), BF), by_cols(rows)),
            (((rows, states), BF), whole((rows, states))),
            (((rows, model), BF), whole((rows, model))),
        ],
        [pltpu.VMEM((rows, model), F32)],
        4 * rows * model * width,
        4 * model * width + 10 * rows * width,
    )


def swap_pipe(value):
    return lax.ppermute(value, PIPE, [(0, 1), (1, 0)])


def shift_tensor(value, by):
    count = lax.axis_size(TENSOR)
    return lax.ppermute(value, TENSOR, [(i, i + by) for i in range(count) if 0 <= i + by < count])


def flip_dp(value, bit):
    return lax.ppermute(value, DP, [(i, i ^ bit) for i in range(lax.axis_size(DP))])


def dp_bits():
    bits, bit = [], 1
    while bit < lax.axis_size(DP):
        bits.append(bit)
        bit *= 2
    return bits


def gather_tensor(piece):
    count, me = lax.axis_size(TENSOR), lax.axis_index(TENSOR)
    rows, cols = piece.shape
    right, left = [piece], [piece]
    for _ in range(count - 1):
        right.append(shift_tensor(right[-1], 1))
        left.append(shift_tensor(left[-1], -1))
    full = jnp.zeros((rows, count * cols), piece.dtype)
    for k in range(count):
        part = piece if k == 0 else jnp.where(me >= k, right[k], left[count - k])
        full = lax.dynamic_update_slice(full, part, (0, lax.rem(me - k + count, count) * cols))
    return full


def gather_dp(piece):
    count, me = lax.axis_size(DP), lax.axis_index(DP)
    rows, cols = piece.shape
    held = {0: piece}
    for bit in reversed(dp_bits()):
        for offset in list(held):
            held[offset ^ bit] = flip_dp(held[offset], bit)
    full = jnp.zeros((count * rows, cols), piece.dtype)
    for offset, part in held.items():
        full = lax.dynamic_update_slice(full, part, ((me ^ offset) * rows, 0))
    return full


def add_low(a, b):
    return (a.astype(F32) + b.astype(F32)).astype(a.dtype)


def reduce_dp(value):
    me = lax.axis_index(DP)
    count = lax.axis_size(DP)
    rows, cols = value.shape[0] // count, value.shape[1]
    for bit in dp_bits():
        count //= 2
        split = value.reshape(count, 2, rows, cols)
        mine = (me // bit) % 2
        keep = lax.dynamic_index_in_dim(split, mine, 1, keepdims=False)
        send = lax.dynamic_index_in_dim(split, 1 - mine, 1, keepdims=False)
        value = add_low(keep, flip_dp(send, bit)).reshape(count * rows, cols)
    return value


def reduce_tensor(take):
    count, me = lax.axis_size(TENSOR), lax.axis_index(TENSOR)
    moving_right = moving_left = None
    for k in range(count - 1, 0, -1):
        right, left = take(jnp.minimum(me + k, count - 1)), take(jnp.maximum(me - k, 0))
        if moving_right is not None:
            right, left = add_low(right, moving_right), add_low(left, moving_left)
        moving_right, moving_left = shift_tensor(right, 1), shift_tensor(left, -1)
    own = take(me)
    if moving_right is None:
        return own.astype(F32)
    return own.astype(F32) + moving_right.astype(F32) + moving_left.astype(F32)


def take_cols(value):
    width = value.shape[1] // lax.axis_size(TENSOR)
    return lambda j: lax.dynamic_slice_in_dim(value, j * width, width, 1)


def take_first(value):
    return lambda j: lax.dynamic_index_in_dim(value, j, 0, keepdims=False)


def sum_all_dp(value):
    for bit in dp_bits():
        value = value + flip_dp(value, bit)
    return value


def sum_all_tensor(value):
    count, bit = lax.axis_size(TENSOR), 1
    while bit < count:
        value = value + lax.ppermute(value, TENSOR, [(i, i ^ bit) for i in range(count)])
        bit *= 2
    return value


MESH = pl.DeviceIdType.MESH
VMEM_LIMIT = 60 * 2**20


def remote(src, dst, send, recv, axis, index):
    return pltpu.make_async_remote_copy(
        src_ref=src, dst_ref=dst, send_sem=send, recv_sem=recv, device_id={axis: index}, device_id_type=MESH
    )


def greet(partners):
    barrier = pltpu.get_barrier_semaphore()
    for axis, index in partners:
        pl.semaphore_signal(barrier, inc=1, device_id={axis: index}, device_id_type=MESH)
    pl.semaphore_wait(barrier, len(partners))


def ring_neighbours(count):
    t = lax.axis_index(TENSOR)
    return [(TENSOR, lax.rem(t + 1, count)), (TENSOR, lax.rem(t + count - 1, count))]


def aligned(index, size):
    return pl.ds(pl.multiple_of(index * size, size), size)


class Gather:
    sems = ((4,), (4,), (4,), "z", "z", "z", "z", "z", "c", "c", (3,), (3,), (3,), (2,), (2,), (2, 2), (2, 2), "n", "n")

    @classmethod
    def scratch(cls, count):
        shapes = {"z": (8, count), "c": (8, 2, count), "n": (count,)}
        return [pltpu.SemaphoreType.DMA(shapes.get(shape, shape)) for shape in cls.sems]

    def __init__(self, count, sources, targets, small, sems):
        self.count, self.sources, self.targets, self.small = count, sources, targets, small
        (self.own_sem, self.xs_sem, self.xr_sem, self.right_sem, self.left_sem, self.zr_sem) = sems[:6]
        (self.ys_sem, self.yr_sem, self.cs_sem, self.cr_sem, self.st_own, self.st_xs, self.st_xr) = sems[6:13]
        (self.st_ys, self.st_yr, self.st_cs, self.st_cr, self.ch_s, self.ch_r) = sems[13:]
        self.p, self.d, self.t = lax.axis_index(PIPE), lax.axis_index(DP), lax.axis_index(TENSOR)
        y, c = self.d // 2, lax.rem(self.d, 2)
        self.y_mate, self.core_mate, self.far_mate = 2 * (1 - y) + c, 2 * y + 1 - c, 2 * (1 - y) + 1 - c
        self.kinds = len(sources)
        self.rows = sources[0].shape[0]

    def partners(self):
        others = [(TENSOR, lax.rem(self.t + k, self.count)) for k in range(1, self.count)]
        return others + [(PIPE, 1 - self.p), (DP, self.y_mate), (DP, self.core_mate)]

    def source(self, kind, which):
        ref = self.sources[kind]
        if kind == self.kinds - 1:
            return ref.at[aligned(which, ref.shape[0] // 2), :]
        return ref.at[:, aligned(which, ref.shape[1] // 2)]

    def region(self, kind, layer, row, col):
        ref = self.sources[kind]
        if kind == self.kinds - 1:
            return self.targets[kind].at[layer, aligned(col, ref.shape[0] // 2), aligned(row, ref.shape[1])]
        return self.targets[kind].at[layer, aligned(row, self.rows), aligned(col, ref.shape[1] // 2)]

    def own_copy(self, w):
        return pltpu.make_async_copy(self.source(w, self.p), self.region(w, self.p, self.d, self.t), self.own_sem.at[w])

    def swap_copy(self, w):
        dst = self.region(w, self.p, self.d, self.t)
        return remote(self.source(w, 1 - self.p), dst, self.xs_sem.at[w], self.xr_sem.at[w], PIPE, 1 - self.p)

    def swap_arrival(self, w):
        dst = self.region(w, 1 - self.p, self.d, self.t)
        return remote(self.source(w, 1 - self.p), dst, self.xs_sem.at[w], self.xr_sem.at[w], PIPE, 1 - self.p)

    def z_copy(self, item, src, by, sem):
        ref = self.region(item % self.kinds, item // self.kinds, self.d, src)
        return remote(ref, ref, sem.at[item, src], self.zr_sem.at[item, src], TENSOR, self.t + by)

    def right(self, item, src):
        return self.z_copy(item, src, 1, self.right_sem)

    def left(self, item, src):
        return self.z_copy(item, src, -1, self.left_sem)

    def y_copy(self, item, src, row=None):
        ref = self.region(item % self.kinds, item // self.kinds, self.d if row is None else row, src)
        return remote(ref, ref, self.ys_sem.at[item, src], self.yr_sem.at[item, src], DP, self.y_mate)

    def core_copy(self, item, which, src, arrival=False):
        row = (self.core_mate, self.far_mate)[which] if arrival else (self.d, self.y_mate)[which]
        ref = self.region(item % self.kinds, item // self.kinds, row, src)
        sems = self.cs_sem.at[item, which, src], self.cr_sem.at[item, which, src]
        return remote(ref, ref, *sems, DP, self.core_mate)

    def begin(self, item):
        w, layer = item % self.kinds, item // self.kinds

        @pl.when(self.p == layer)
        def _():
            self.own_copy(w).wait()

        @pl.when(self.p != layer)
        def _():
            self.swap_arrival(w).wait_recv()

        @pl.when(self.t < self.count - 1)
        def _():
            self.right(item, self.t).start()

        @pl.when(self.t > 0)
        def _():
            self.left(item, self.t).start()

        self.y_copy(item, self.t).start()
        self.core_copy(item, 0, self.t).start()

    def hop(self, item, hop):
        t, count = self.t, self.count
        lower, upper = t - hop, t + hop

        @pl.when(lower >= 0)
        def _():
            self.right(item, lower).wait_recv()

            @pl.when(t < count - 1)
            def _():
                self.right(item, lower).start()

            self.y_copy(item, lower).start()
            self.core_copy(item, 0, lower).start()

        @pl.when(upper < count)
        def _():
            self.left(item, upper).wait_recv()

            @pl.when(t > 0)
            def _():
                self.left(item, upper).start()

            self.y_copy(item, upper).start()
            self.core_copy(item, 0, upper).start()

    def share(self, item, src):
        self.y_copy(item, src, self.y_mate).wait_recv()
        self.core_copy(item, 1, src).start()

    def arrived(self, item, src):
        for which in range(2):
            self.core_copy(item, which, src, True).wait_recv()

    def sent(self, item):
        t, count = self.t, self.count
        for src in range(count):
            for which in range(2):
                self.core_copy(item, which, src).wait_send()
            self.y_copy(item, src).wait_send()

            @pl.when((src <= t) & (t < count - 1))
            def _():
                self.right(item, src).wait_send()

            @pl.when((src >= t) & (t > 0))
            def _():
                self.left(item, src).wait_send()


    def small_target(self, k, layer):
        target = self.small[k][1]
        if k == 0:
            return target.at[layer, aligned(self.d, self.rows), :]
        if k == 1:
            return target.at[layer, :, aligned(self.t, target.shape[2] // self.count)]
        return target.at[layer]

    def small_source(self, k, which):
        ref = self.small[k][0]
        return ref.at[:, aligned(which, ref.shape[1] // 2)] if k == 1 else ref

    def small_own(self, k):
        return pltpu.make_async_copy(self.small_source(k, self.p), self.small_target(k, self.p), self.st_own.at[k])

    def small_swap(self, k, arrival=False):
        dst = self.small_target(k, 1 - self.p if arrival else self.p)
        return remote(self.small_source(k, 1 - self.p), dst, self.st_xs.at[k], self.st_xr.at[k], PIPE, 1 - self.p)

    def state_rows(self, layer, row):
        return self.small[0][1].at[layer, aligned(row, self.rows), :]

    def state_y(self, layer, arrival=False):
        ref = self.state_rows(layer, self.y_mate if arrival else self.d)
        return remote(ref, ref, self.st_ys.at[layer], self.st_yr.at[layer], DP, self.y_mate)

    def state_core(self, layer, which, arrival=False):
        row = (self.core_mate, self.far_mate)[which] if arrival else (self.d, self.y_mate)[which]
        ref = self.state_rows(layer, row)
        return remote(ref, ref, self.st_cs.at[layer, which], self.st_cr.at[layer, which], DP, self.core_mate)

    def channels(self, k, arrival=False):
        target = self.small[1][1]
        index = lax.rem(self.t - k + self.count, self.count) if arrival else self.t
        ref = target.at[:, :, aligned(index, target.shape[2] // self.count)]
        return remote(ref, ref, self.ch_s.at[k], self.ch_r.at[k], TENSOR, lax.rem(self.t + k, self.count))

    def first_layer(self):
        order = [self.kinds - 1] + list(range(self.kinds - 1))
        for w in order:
            self.swap_copy(w).start()
            self.own_copy(w).start()
        for k in range(3):
            self.small_swap(k).start()
            self.small_own(k).start()
        order = [self.kinds - 1, 2 * self.kinds - 1] + list(range(self.kinds - 1))
        for item in order:
            self.begin(item)
        for k in range(3):
            self.small_own(k).wait()
            self.small_swap(k, True).wait_recv()
        for layer in range(2):
            self.state_y(layer).start()
            self.state_core(layer, 0).start()
        for k in range(1, self.count):
            self.channels(k).start()
        for hop in range(1, self.count):
            for item in order:
                self.hop(item, hop)
        for item in self.late_items():
            self.begin(item)
        for layer in range(2):
            self.state_y(layer, True).wait_recv()
            self.state_core(layer, 1).start()
        for src in range(self.count):
            for item in order:
                self.share(item, src)
        for item in order:
            for src in range(self.count):
                self.arrived(item, src)
        for k in range(1, self.count):
            self.channels(k, True).wait_recv()
        for layer in range(2):
            for which in range(2):
                self.state_core(layer, which, True).wait_recv()

    def late_items(self):
        return [self.kinds + w for w in range(self.kinds - 1)]

    def second_layer(self, steps, group_of):
        items, stages = self.late_items(), []
        hops = [(item, hop) for hop in range(1, self.count) for item in items]
        for n, (item, hop) in enumerate(hops):
            stages.append((2 + n * (steps - 5) // len(hops), functools.partial(self.hop, item, hop)))
        for src in range(self.count):
            for item in items:
                stages.append((steps - 2 + group_of(src), functools.partial(self.share, item, src)))
        for src in range(self.count):
            for item in items:
                stages.append((steps - 1 + group_of(src), functools.partial(self.arrived, item, src)))
        return stages

    def finish(self):
        for k in range(3):
            self.small_swap(k).wait_send()
        for k in range(1, self.count):
            self.channels(k).wait_send()
        for layer in range(2):
            self.state_y(layer).wait_send()
            for which in range(2):
                self.state_core(layer, which).wait_send()
        for w in range(self.kinds):
            self.swap_copy(w).wait_send()
        for item in range(2 * self.kinds):
            self.sent(item)


def add_into(dst, src, chunk=64):
    def step(i, carry):
        at = aligned(i, chunk)
        dst[at, :] = (dst[at, :].astype(F32) + src[at, :].astype(F32)).astype(BF)
        return carry

    lax.fori_loop(0, dst.shape[0] // chunk, step, 0)


def reduce_grads(count, *refs):
    grads, pack, results, (chan_o, step_o, rest_o) = refs[:6], refs[6], refs[7:10], refs[10:13]
    (own, crecv, yrecv, rrecv, lrecv, xsend, xrecv) = refs[13:20]
    (own_sem, cs_sem, cr_sem, ys_sem, yr_sem, rs_sem, rr_sem, ls_sem, lr_sem, xs_sem, xr_sem) = refs[20:31]
    (total_s, part_s, far_s, sum_ss, sum_rs) = refs[31:]
    p, d, t = lax.axis_index(PIPE), lax.axis_index(DP), lax.axis_index(TENSOR)
    y, c = d // 2, lax.rem(d, 2)
    y_mate, core_mate = 2 * (1 - y) + c, 2 * y + 1 - c
    items, kinds = 6, 3
    rows, half = xsend.shape[1], xsend.shape[2]

    def core_copy(item, row):
        src = grads[item].at[aligned(2 * row + 1 - c, rows), :]
        return remote(src, crecv.at[item, row], cs_sem.at[item, row], cr_sem.at[item, row], DP, core_mate)

    def own_copy(item, row):
        src = grads[item].at[aligned(2 * row + c, rows), :]
        return pltpu.make_async_copy(src, own.at[item % 2, row], own_sem.at[item % 2, row])

    def y_copy(item):
        return remote(crecv.at[item, 1 - y], yrecv.at[item], ys_sem.at[item], yr_sem.at[item], DP, y_mate)

    def right_copy(item, j):
        ref = rrecv.at[item, j]
        return remote(ref, ref, rs_sem.at[item, j], rr_sem.at[item, j], TENSOR, t + 1)

    def left_copy(item, j):
        ref = lrecv.at[item, j]
        return remote(ref, ref, ls_sem.at[item, j], lr_sem.at[item, j], TENSOR, t - 1)

    def x_copy(item):
        return remote(xsend.at[item], xrecv.at[item % kinds], xs_sem.at[item], xr_sem.at[item % kinds], PIPE, 1 - p)

    def near(item):
        for row in range(2):
            own_copy(item, row).wait()
            core_copy(item, row).wait_recv()
            add_into(crecv.at[item, row], own.at[item % 2, row])
        y_copy(item).start()
        if item + 2 < items:
            for row in range(2):
                own_copy(item + 2, row).start()

    def far(item):
        y_copy(item).wait_recv()
        add_into(yrecv.at[item], crecv.at[item, y])

        def column(j):
            return yrecv.at[item, :, aligned(j, half)]

        for j in range(count - 1, 0, -1):

            @pl.when(t < j)
            def _():
                @pl.when(t == 0)
                def _():
                    rrecv[item, j] = column(j)[...]

                @pl.when(t > 0)
                def _():
                    right_copy(item, j).wait_recv()
                    add_into(rrecv.at[item, j], column(j))

                right_copy(item, j).start()

        for j in range(count - 1):

            @pl.when(t > j)
            def _():
                @pl.when(t == count - 1)
                def _():
                    lrecv[item, j] = column(j)[...]

                @pl.when(t < count - 1)
                def _():
                    left_copy(item, j).wait_recv()
                    add_into(lrecv.at[item, j], column(j))

                left_copy(item, j).start()

    def close(item):
        w = item % kinds
        total = xsend.at[item]
        total[...] = yrecv[item, :, aligned(t, half)]

        @pl.when(t > 0)
        def _():
            right_copy(item, t).wait_recv()
            add_into(total, rrecv.at[item, t])

        @pl.when(t < count - 1)
        def _():
            left_copy(item, t).wait_recv()
            add_into(total, lrecv.at[item, t])

        @pl.when(p != item // kinds)
        def _():
            x_copy(item).start()

        @pl.when(p == item // kinds)
        def _():
            results[w][:, aligned(p, half)] = total[...].astype(F32)

    steps, bit = [(DP, core_mate), (DP, y_mate)], 1
    while bit < count:
        steps.append((TENSOR, t + bit * (1 - 2 * lax.rem(t // bit, 2))))
        bit *= 2

    def sum_copy(k):
        axis, index = steps[k]
        return remote(total_s.at[k], part_s.at[k], sum_ss.at[k], sum_rs.at[k], axis, index)

    def pipe_copy():
        k = len(steps)
        return remote(total_s.at[k, 1 - p], far_s, sum_ss.at[k], sum_rs.at[k], PIPE, 1 - p)

    def sum_step(k):
        sum_copy(k).wait_recv()
        total_s[k + 1] = total_s[k] + part_s[k]
        if k + 1 < len(steps):
            sum_copy(k + 1).start()
        else:
            pipe_copy().start()

    def sum_close():
        k = len(steps)
        pipe_copy().wait_recv()
        mine = total_s.at[k, p]
        for ref, where in ((mine, p), (far_s, 1 - p)):
            chan_o[:, aligned(where, half)] = ref[0:8, aligned(t, half)]
            step_o[aligned(where, 8), :] = ref[pl.ds(pl.multiple_of(8 + 8 * t, 8), 8), aligned(d, rows)]
        last = total_s.shape[2] - 8
        row = iota((8, total_s.shape[3]), 0)
        rest_o[...] = mine[last:, :] + jnp.where(row == 0, 0.0, far_s[last:, :])

    others = [axis_index for axis_index in steps if axis_index[0] == TENSOR]
    greet(ring_neighbours(count) + [(PIPE, 1 - p), (DP, y_mate), (DP, core_mate)] + others)
    total_s[0] = pack[...]
    sum_copy(0).start()
    for item in range(items):
        for row in range(2):
            core_copy(item, row).start()
            if item < 2:
                own_copy(item, row).start()
    for k in range(items + 2):
        if k < items:
            near(k)
        if 1 <= k <= items:
            far(k - 1)
        if k >= 2:
            close(k - 2)
        if 1 <= k <= len(steps):
            sum_step(k - 1)
    sum_close()
    for k in range(len(steps)):
        sum_copy(k).wait_send()
    pipe_copy().wait_send()
    for w in range(kinds):
        x_copy(w).wait_recv()
        results[w][:, aligned(1 - p, half)] = xrecv[w].astype(F32)
    for item in range(items):
        for row in range(2):
            core_copy(item, row).wait_send()
        y_copy(item).wait_send()

        @pl.when(p != item // kinds)
        def _():
            x_copy(item).wait_send()

        for j in range(count):

            @pl.when(t < j)
            def _():
                right_copy(item, j).wait_send()

            @pl.when(t > j)
            def _():
                left_copy(item, j).wait_send()


def reduce_call(grads, pack, count, groups):
    model, width = grads[0].shape
    rows, half = model // groups, width // count
    dma = pltpu.SemaphoreType.DMA
    vmem = pltpu.VMEM
    steps = 2 + (count - 1).bit_length()
    inside = pl.BlockSpec(memory_space=pltpu.VMEM)
    return pl.pallas_call(
        functools.partial(reduce_grads, count),
        in_specs=[pl.BlockSpec(memory_space=pl.ANY)] * 6 + [inside],
        out_specs=[inside] * 6,
        out_shape=[jax.ShapeDtypeStruct((rows, 2 * half), F32)] * 3
        + [
            jax.ShapeDtypeStruct((8, 2 * half), F32),
            jax.ShapeDtypeStruct((16, rows), F32),
            jax.ShapeDtypeStruct((8, width), F32),
        ],
        scratch_shapes=[
            vmem((2, 2, rows, width), BF),
            vmem((6, 2, rows, width), BF),
            vmem((6, rows, width), BF),
            vmem((6, count, rows, half), BF),
            vmem((6, count, rows, half), BF),
            vmem((6, rows, half), BF),
            vmem((3, rows, half), BF),
            dma((2, 2)),
            dma((6, 2)),
            dma((6, 2)),
            dma((6,)),
            dma((6,)),
            dma((6, count)),
            dma((6, count)),
            dma((6, count)),
            dma((6, count)),
            dma((6,)),
            dma((3,)),
            vmem((steps + 1,) + pack.shape, F32),
            vmem((steps,) + pack.shape, F32),
            vmem(pack.shape[1:], F32),
            dma((steps + 1,)),
            dma((steps + 1,)),
        ],
        compiler_params=pltpu.CompilerParams(collective_id=1, has_side_effects=True, vmem_limit_bytes=VMEM_LIMIT),
    )(*grads, pack)


def fused_forward(count, head_dim, micro, *refs):
    (tokens, mask, value, gate_w, out_w, step_w, state_w, chan, shared) = refs[:9]
    (wv_h, wg_h, wo_h, wt_h, ws_h, pv_o, ps_o, ph_o, pn_o) = refs[9:18]
    (out_h, low_h, mix_h, inv_o, nx_o, vpre_o, spre_o, x_o, bc_o, dtc_o, gate_o, y_o, gg_o, sin_o) = refs[18:32]
    (nx_s, sc_s, dt_s, cum_s, cumt_s, acc_s, sq_s, psend, precv, sqsend, sqrecv, csend, crecv, hrecv, trecv) = refs[32:47]
    (ps_sem, pr_sem, ss_sem, sr_sem, cs_sem, cr_sem, hs_sem, hr_sem, ts_sem, tr_sem, low_sem, out_sem, mix_sem) = refs[47:60]
    (wv_s, wg_s, wo_s, ws_s, wt_s, chan_s, shared_s, w_sem, l_sem) = refs[60:69]
    q, s, g = pl.program_id(0), pl.program_id(1), pl.program_id(2)
    groups = dt_s.shape[0]
    p, t = lax.axis_index(PIPE), lax.axis_index(TENSOR)
    idx = q * micro + s
    slot = idx * groups + g
    total_idx = 2 * micro
    rows, model = tokens.shape[1], tokens.shape[2]
    state = bc_o.shape[1] // 2
    per_group = GC // head_dim
    inner_total = 2 * groups * GC
    gather = Gather(
        count,
        (value, gate_w, out_w, step_w),
        (wv_h, wg_h, wo_h, wt_h),
        ((state_w, ws_h), (chan, chan_s), (shared, shared_s)),
        refs[69:],
    )
    big = ((wv_h, wv_s), (wg_h, wg_s), (wo_h, wo_s))

    def weight_copy(step, k):
        layer, group = step // (micro * groups), lax.rem(step, groups)
        held = lax.rem(step, 2)
        return pltpu.make_async_copy(big[k][0].at[layer, :, aligned(group, GC)], big[k][1].at[held], w_sem.at[held, k])

    def layer_copies(layer):
        return (
            pltpu.make_async_copy(ws_h.at[layer], ws_s, l_sem.at[0]),
            pltpu.make_async_copy(wt_h.at[layer], wt_s, l_sem.at[1]),
        )

    def part_copy(i):
        return remote(psend.at[i], precv.at[i], ps_sem.at[i], pr_sem.at[i], PIPE, 1 - p)

    def square_copy(i):
        return remote(sqsend.at[i], sqrecv.at[i], ss_sem.at[i], sr_sem.at[i], PIPE, 1 - p)

    def chain_copy(i):
        return remote(csend.at[i], crecv.at[i], cs_sem.at[i], cr_sem.at[i], TENSOR, t + 1)

    def halo_copy(i):
        return remote(psend.at[i, rows - HALO :, :], hrecv.at[i], hs_sem.at[i], hr_sem.at[i], TENSOR, t + 1)

    def tokens_copy():
        return remote(tokens.at[:, rows - HALO :, :], trecv, ts_sem.at[0], tr_sem.at[0], TENSOR, t + 1)

    def low_copy(i):
        return pltpu.make_async_copy(psend.at[i], low_h.at[i], low_sem.at[i])

    def out_copy(i):
        return pltpu.make_async_copy(psend.at[i], out_h.at[lax.rem(i, micro)], out_sem.at[i])

    def mix_copy(i):
        return pltpu.make_async_copy(precv.at[i], mix_h.at[i], mix_sem.at[i])

    @pl.when((idx == 0) & (g == 0))
    def _():
        greet(gather.partners())

        @pl.when(t < count - 1)
        def _():
            tokens_copy().start()

        gather.first_layer()
        for k in range(3):
            weight_copy(0, k).start()
        pv_o[...] = chan_s[...]
        heads = per_group * groups // count
        half = groups * GC // count
        place, lane = iota((groups * GC, LANES), 0), iota((groups * GC, LANES), 1)
        first = half * (lane // heads) + lax.rem(lane, heads)
        used = lane < per_group * groups
        for layer in range(2):
            per_head = chan_s[layer]
            for kind in range(2):
                pick = ((place == first + kind * heads) & used).astype(F32)
                ph_o[layer, kind : kind + 1, :] = exact(per_head, pick)[7:8, :]
            ph_o[layer, 2:, :] = jnp.zeros((6, LANES), F32)
            pn_o[layer] = shared_s[layer]
            for k in range(5):
                ps_o[layer, k : k + 1, :] = shared_s[layer, 1:2, 2 * state * k : 2 * state * (k + 1)]
            ps_o[layer, 5:, :] = jnp.zeros((3, 2 * state), F32)

    columns = groups * GC // count
    late = gather.second_layer(micro * groups, lambda src: src * columns // GC)
    for step in sorted({step for step, _ in late}):

        @pl.when(slot == step)
        def _():
            for when, stage in late:
                if when == step:
                    stage()

    @pl.when((s == 0) & (g == 0))
    def _():
        for copy in layer_copies(q):
            copy.start()
        for copy in layer_copies(q):
            copy.wait()

    for k in range(3):
        weight_copy(slot, k).wait()

    @pl.when(slot + 1 < total_idx * groups)
    def _():
        for k in range(3):
            weight_copy(slot + 1, k).start()

    held = lax.rem(slot, 2)
    ws, wt, wv, wg, wo = ws_s, wt_s, wv_s.at[held], wg_s.at[held], wo_s.at[held]
    pv, ps, ph, pn = pv_o.at[q, :, aligned(g, GC)], ps_o.at[q], ph_o.at[q], pn_o.at[q]

    def normed(u):
        uf = u.astype(F32)
        return (uf * lax.rsqrt(jnp.mean(uf * uf, axis=1, keepdims=True) + EPS) * pn[0:1, :]).astype(BF)

    @pl.when((g == 0) & (q == 0))
    def _():
        nx_s[HALO:, :] = normed(tokens[s])

        @pl.when(t == 0)
        def _():
            nx_s[:HALO, :] = jnp.zeros((HALO, model), BF)

        @pl.when(t > 0)
        def _():
            @pl.when(s == 0)
            def _():
                tokens_copy().wait_recv()

            nx_s[:HALO, :] = normed(trecv[s])

    @pl.when((g == 0) & (q == 1))
    def _():
        nx_s[HALO:, :] = normed(psend[s])

        @pl.when(t == 0)
        def _():
            nx_s[:HALO, :] = jnp.zeros((HALO, model), BF)

        @pl.when(t > 0)
        def _():
            halo_copy(s).wait_recv()
            nx_s[:HALO, :] = normed(hrecv[s])

    @pl.when(g == 0)
    def _():
        nx_o[...] = nx_s[HALO:, :]
        spre = nn(nx_s[...], ws[...])
        spre_o[...] = spre
        conv = conv_rows(spre, ps, rows)
        bc = (conv * sigmoid(conv)).astype(BF)
        bc_o[...] = bc
        scores = nt(bc[:, state:], bc[:, :state])
        lower = iota((rows, rows), 0) >= iota((rows, rows), 1)
        sc_s[...] = jnp.where(lower, scores, 0.0)
        raw = nt(nx_s[HALO:, :], wt[...])
        raw = exact(raw, step_places(count, raw.shape[1], per_group * groups)) + ph[0:1, :]
        step = jnp.maximum(raw, 0.0) + jnp.log(1.0 + jnp.exp(-jnp.abs(raw)))
        cum = exact(lower.astype(F32), -step * jnp.exp(ph[1:2, :]))
        dtc_o[0] = step
        dtc_o[1] = cum
        dtc_o[2] = sigmoid(raw)
        group_lanes(step, dt_s, groups, per_group)
        group_lanes(cum, cum_s, groups, per_group)
        group_rows(cum, cumt_s, groups, per_group)
        acc_s[...] = jnp.zeros_like(acc_s)
        sq_s[...] = jnp.zeros_like(sq_s)

    pre = nn(nx_s[...], wv[...])
    vpre_o[...] = pre
    conv = conv_rows(pre, pv, rows)
    x = conv * sigmoid(conv)
    x_o[...] = x.astype(BF)
    step, cum, cumt = dt_s[g], cum_s[g], cumt_s[g]
    to_end = jnp.exp(cum[rows - 1 : rows, :] - cum)
    xp = (x * spread(step, GC, head_dim)).astype(BF)
    xr = (x * spread(step * to_end, GC, head_dim)).astype(BF)
    local = tn(xr, bc_o[:, :state])

    @pl.when(t == 0)
    def _():
        sin_o[...] = jnp.zeros_like(sin_o)

    @pl.when(t > 0)
    def _():
        chain_copy(slot).wait_recv()
        sin_o[...] = crecv[slot]

    @pl.when(t < count - 1)
    def _():
        csend[slot] = (through_rows(cumt, rows, head_dim, state) * sin_o[...].astype(F32) + local).astype(BF)
        chain_copy(slot).start()

    scores = sc_s[...]
    lane = iota((rows, LANES), 1)
    within = []
    for pair in range(GC // LANES):
        cols = slice(LANES * pair, LANES * (pair + 1))
        outs = []
        for i in (2 * pair, 2 * pair + 1):
            diff = cum[:, i : i + 1] - cumt[i : i + 1, :]
            mix = (jnp.exp(jnp.minimum(diff, 0.0)) * scores).astype(BF)
            outs.append(nn(mix, xp[:, cols]))
        within.append(jnp.where(lane < head_dim, outs[0], outs[1]))
    gate = nn(nx_s[HALO:, :], wg[...])
    gate_o[...] = gate
    carried = nt(bc_o[:, state:], sin_o[...])
    y = jnp.concatenate(within, axis=1) + pv[6:7, :] * x + spread(jnp.exp(cum), GC, head_dim) * carried
    y_o[...] = y
    gated = y * (gate * sigmoid(gate))
    gg = (gated * pv[5:6, :]).astype(BF)
    gg_o[...] = gg
    squares = gated * gated
    for part in range(GC // LANES):
        sq_s[...] += squares[:, LANES * part : LANES * (part + 1)]
    acc_s[...] += nt(gg, wo[...])

    @pl.when(g == groups - 1)
    def _():
        psend[idx] = acc_s[...].astype(BF)
        sqsend[idx] = jnp.broadcast_to(jnp.sum(sq_s[...], axis=1, keepdims=True), (rows, LANES))
        part_copy(idx).start()
        square_copy(idx).start()

    def finish(i):
        j = lax.rem(i, micro)
        part_copy(i).wait()
        square_copy(i).wait()
        inverse = lax.rsqrt((sqsend[i] + sqrecv[i]) / inner_total + EPS)
        inv_o[i] = inverse
        mixed = inverse[:, 0:1] * (psend[i].astype(F32) + precv[i].astype(F32))
        precv[i] = mixed.astype(BF)
        row_mask = mask[j][:, 0:1]

        @pl.when(i < micro)
        def _():
            psend[i] = (row_mask * (tokens[j].astype(F32) + mixed)).astype(BF)

            @pl.when(t < count - 1)
            def _():
                halo_copy(j).start()

            low_copy(j).start()

        @pl.when(i >= micro)
        def _():
            psend[i] = (row_mask * (psend[j].astype(F32) + mixed)).astype(BF)

        @pl.when(i // micro == p)
        def _():
            out_copy(i).start()

        mix_copy(i).start()

    @pl.when((g == 1) & (idx > 1))
    def _():
        finish(idx - 2)

    @pl.when((g == groups - 1) & (idx == total_idx - 1))
    def _():
        finish(idx - 1)
        finish(idx)
        for i in range(total_idx):
            mix_copy(i).wait()

            @pl.when(i // micro == p)
            def _():
                out_copy(i).wait()

        for i in range(micro):
            low_copy(i).wait()

        gather.finish()

        @pl.when(t < count - 1)
        def _():
            tokens_copy().wait_send()
            for i in range(micro):
                halo_copy(i).wait_send()

            def drain(i, carry):
                chain_copy(i).wait_send()
                return carry

            lax.fori_loop(0, total_idx * groups, drain, 0)


def step_places(count, rows, all_heads):
    heads, size = all_heads // count, rows // count
    place, lane = iota((rows, LANES), 0), iota((rows, LANES), 1)
    return ((place == size * (lane // heads) + lax.rem(lane, heads)) & (lane < all_heads)).astype(F32)


def through_rows(cumt, rows, head_dim, state):
    end = jnp.exp(cumt[:, rows - 1 : rows])
    parts = [jnp.broadcast_to(end[i : i + 1, :], (head_dim, state)) for i in range(GC // head_dim)]
    return jnp.concatenate(parts, axis=0)


def fused_backward(count, head_dim, micro, *refs):
    (cot, tokens, out0, mask, inv, mix, vpre, spre, x, bc, dtc, gate, y, s_in) = refs[:14]
    (wv, wg, wo, ws, wt, pv, ps, ph, pn) = refs[14:23]
    (grad_h, dval_o, dgate_o, dst_o, dstep_o, sgm_o, vs_o, ss_o, hs_o, norm_o) = refs[23:33]
    (gm_s, rowsc_s, gin_s, halo_s, halo2_s, acc_s, nacc_s) = refs[33:40]
    (sct_s, scts_s, wsum_s, dbc_s, dt_s, cum_s, cumt_s, net_s, rv_s, ddir_s, k_s, rt_s, rall_s) = refs[40:53]
    (psend, precv, csend, crecv, hsend, hrecv, tsend, trecv) = refs[53:61]
    (ps_sem, pr_sem, cs_sem, cr_sem, hs_sem, hr_sem, ts_sem, tr_sem, out_sem) = refs[61:]
    turn, s, g = pl.program_id(0), pl.program_id(1), pl.program_id(2)
    groups = dt_s.shape[0]
    p, t = lax.axis_index(PIPE), lax.axis_index(TENSOR)
    idx = turn * micro + s
    slot = idx * groups + g
    total_idx = 2 * micro
    rows, model = cot.shape[1], cot.shape[2]
    state = bc.shape[1] // 2
    per_group = GC // head_dim
    inner_total = 2 * groups * GC

    def part_copy(i):
        return remote(psend.at[i], precv.at[i], ps_sem.at[i], pr_sem.at[i], PIPE, 1 - p)

    def chain_copy(i):
        return remote(csend.at[i], crecv.at[i], cs_sem.at[i], cr_sem.at[i], TENSOR, t - 1)

    def halo_copy(i):
        return remote(hsend.at[i], hrecv.at[i], hs_sem.at[i], hr_sem.at[i], TENSOR, t - 1)

    def tail_copy(i):
        return remote(tsend.at[i], trecv.at[i], ts_sem.at[i], tr_sem.at[i], TENSOR, t - 1)

    def out_copy(i):
        return pltpu.make_async_copy(psend.at[i], grad_h.at[lax.rem(i, micro)], out_sem.at[i])

    @pl.when((idx == 0) & (g == 0))
    def _():
        greet(ring_neighbours(count) + [(PIPE, 1 - p)])
        nacc_s[...] = jnp.zeros_like(nacc_s)

    @pl.when((g == 0) & (turn == 0))
    def _():
        gm_s[...] = (mask[s][:, 0:1] * cot[s].astype(F32)).astype(BF)

    @pl.when((g == 0) & (turn == 1))
    def _():
        gm_s[...] = (mask[s][:, 0:1] * psend[s].astype(F32)).astype(BF)

    @pl.when(g == 0)
    def _():
        gmf = gm_s[...].astype(F32)
        inverse = inv[...]
        dot = jnp.sum(gmf * mix[...].astype(F32), axis=1, keepdims=True)
        rowsc_s[...] = inverse * inverse * dot / inner_total
        sgm_o[...] = (gmf * inverse[:, 0:1]).astype(BF)
        scores = nt(bc[:, :state], bc[:, state:])
        first, second = iota((rows, rows), 0), iota((rows, rows), 1)
        sct_s[...] = jnp.where(second >= first, scores, 0.0)
        scts_s[...] = jnp.where(second > first, scores, 0.0)
        wsum_s[...] = jnp.zeros_like(wsum_s)
        dbc_s[...] = jnp.zeros_like(dbc_s)
        rall_s[...] = jnp.zeros_like(rall_s)
        acc_s[...] = jnp.zeros_like(acc_s)
        group_lanes(dtc[0], dt_s, groups, per_group)
        group_lanes(dtc[1], cum_s, groups, per_group)
        group_rows(dtc[1], cumt_s, groups, per_group)

    step, cum, cumt = dt_s[g], cum_s[g], cumt_s[g]
    last = cum[rows - 1 : rows, :]
    fromx = spread(jnp.exp(cum), GC, head_dim)

    gs = nn(gm_s[...], wo[...])
    inverse, shrink = inv[:, 0:1], rowsc_s[:, 0:1]
    gv, yv = gate[...], y[...]
    sig = sigmoid(gv)
    silu = gv * sig
    gated = yv * silu
    dgain = jnp.sum(gs * gated * inverse, axis=0, keepdims=True)
    dgated = inverse * (gs * pv[5:6, :]) - gated * shrink
    dgate = (dgated * yv * (sig * (1.0 + gv * (1.0 - sig)))).astype(BF)
    dgate_o[...] = dgate
    dyb = (dgated * silu).astype(BF)
    dyf = dyb.astype(F32)
    dyef = dyf * fromx
    dye = dyef.astype(BF)
    dsl = tn(dye, bc[:, state:])

    @pl.when(t == count - 1)
    def _():
        gin_s[...] = jnp.zeros_like(gin_s)

    @pl.when(t < count - 1)
    def _():
        chain_copy(slot).wait_recv()
        gin_s[...] = crecv[slot]

    @pl.when(t > 0)
    def _():
        csend[slot] = (through_rows(cumt, rows, head_dim, state) * gin_s[...].astype(F32) + dsl).astype(BF)
        chain_copy(slot).start()

    to_end = jnp.exp(last - cum)
    stepx = spread(step, GC, head_dim)
    endx = spread(to_end, GC, head_dim)
    xf = x[...].astype(F32)
    xp = (xf * stepx).astype(BF)
    xr = (xf * stepx * endx).astype(BF)
    gb = nt(bc[:, :state], gin_s[...])
    cs = nt(bc[:, state:], s_in[...])
    dbc_s[:, :state] += nn(xr, gin_s[...])
    dbc_s[:, state:] += nn(dye, s_in[...])

    lane = iota((rows, LANES), 1)
    wsum = wsum_s[...]
    colsum = jnp.zeros((rows, LANES), F32)
    within = []
    for pair in range(GC // LANES):
        cols = slice(LANES * pair, LANES * (pair + 1))
        xpp, dyp = xp[:, cols], dyb[:, cols]
        outs = []
        for side in range(2):
            i = 2 * pair + side
            mine = (lane < head_dim) if side == 0 else (lane >= head_dim)
            decay = jnp.exp(jnp.minimum(cumt[i : i + 1, :] - cum[:, i : i + 1], 0.0))
            outs.append(nn((decay * sct_s[...]).astype(BF), dyp))
            weight = decay * nt(jnp.where(mine, xpp, jnp.zeros_like(xpp)), dyp)
            wsum = wsum + weight
            pairs = (weight * scts_s[...]).astype(BF)
            colsum = colsum + nn(pairs, (lane == i).astype(BF))
            rt_s[g, i : i + 1, :] = jnp.sum(pairs.astype(F32), axis=0, keepdims=True)
        within.append(jnp.where(lane < head_dim, outs[0], outs[1]))
    wsum_s[...] = wsum
    u = jnp.concatenate(within, axis=1) + endx * gb

    heads = (iota((GC, LANES), 0) // head_dim == iota((GC, LANES), 1)).astype(BF)
    ddir_s[g] = nn((xf * u).astype(BF), heads)
    net_s[g] = nn((dyef * cs).astype(BF), heads) - colsum
    rv_s[g] = step * to_end * nn((xf * gb).astype(BF), heads)
    inner = gin_s[...].astype(F32) * s_in[...].astype(F32)
    per_channel = lax.dot_general(
        jnp.ones((8, inner.shape[1]), F32), inner, (((1,), (1,)), ((), ())), precision=HIGHEST, preferred_element_type=F32
    )
    k_s[g] = jnp.exp(last) * exact(per_channel, heads.astype(F32))

    dx = stepx * u + pv[6:7, :] * dyf
    dconv = dx * silu_slope(conv_rows(vpre, pv, rows))

    @pl.when(t > 0)
    def _():
        hsend[slot] = dconv[:8, :]
        halo_copy(slot).start()

    sums = conv_sums(dconv, vpre, rows)
    sums.append(dgain)
    sums.append(jnp.sum(dyf * xf, axis=0, keepdims=True))
    sums.append(jnp.zeros((1, GC), F32))
    vs_o[...] = jnp.concatenate(sums, axis=0)
    acc_s[...] += nt(dgate, wg[...])

    @pl.when(t == count - 1)
    def _():
        halo_s[...] = jnp.zeros_like(halo_s)

    @pl.when(t < count - 1)
    def _():
        halo_copy(slot).wait_recv()
        halo_s[...] = hrecv[slot]

    dval = conv_transposed(dconv, halo_s[...], pv, rows).astype(BF)
    dval_o[...] = dval
    acc_s[...] += nt(dval, wv[...])

    @pl.when(g == groups - 1)
    def _():
        first, second = iota((rows, rows), 0), iota((rows, rows), 1)
        weights = jnp.where(second >= first, wsum_s[...], 0.0).astype(BF)
        db = dbc_s[:, :state] + nn(weights, bc[:, state:])
        dc = dbc_s[:, state:] + tn(weights, bc[:, :state])
        dsc = jnp.concatenate([db, dc], axis=1) * silu_slope(conv_rows(spre, ps, rows))

        @pl.when(t > 0)
        def _():
            tsend[idx] = dsc[:8, :]
            tail_copy(idx).start()

        ssums = conv_sums(dsc, spre, rows)
        ssums.append(jnp.zeros((3, 2 * state), F32))
        ss_o[...] = jnp.concatenate(ssums, axis=0)
        net, rv, ddir, const = net_s[0], rv_s[0], ddir_s[0], k_s[0]
        rall_s[0:per_group, :] = rt_s[0, 0:per_group, :]
        for other in range(1, groups):
            shift = per_group * other
            net = net + pltpu.roll(net_s[other], shift, 1)
            rv = rv + pltpu.roll(rv_s[other], shift, 1)
            ddir = ddir + pltpu.roll(ddir_s[other], shift, 1)
            const = const + pltpu.roll(k_s[other], shift, 1)
            rall_s[shift : shift + per_group, :] = rt_s[other, 0:per_group, :]
        net = net + rall_s[...].T
        da = exact((second >= first).astype(F32), net) + exact((second < first).astype(F32), rv) + const[0:1, :]
        rate = jnp.exp(ph[1:2, :])
        dstep = (ddir - da * rate) * dtc[2]
        dstep_o[...] = dstep.astype(BF)
        hs_o[...] = jnp.concatenate(
            [
                jnp.sum(dstep, axis=0, keepdims=True),
                jnp.sum(-da * dtc[0] * rate, axis=0, keepdims=True),
                jnp.zeros((6, LANES), F32),
            ],
            axis=0,
        )

        @pl.when(t == count - 1)
        def _():
            halo2_s[...] = jnp.zeros_like(halo2_s)

        @pl.when(t < count - 1)
        def _():
            tail_copy(idx).wait_recv()
            halo2_s[...] = trecv[idx]

        dst = conv_transposed(dsc, halo2_s[...], ps, rows).astype(BF)
        dst_o[...] = dst
        psend[idx] = (acc_s[...] + nt(dst, ws[...]) + nn(dstep_o[...], wt[...])).astype(BF)
        part_copy(idx).start()

    def finish(i):
        j = lax.rem(i, micro)
        part_copy(i).wait()
        which = 1 - i // micro
        row_mask = mask[j][:, 0:1]

        def close(u, incoming):
            uf = u.astype(F32)
            grad_normed = psend[i].astype(F32) + precv[i].astype(F32)
            root_inv = lax.rsqrt(jnp.mean(uf * uf, axis=1, keepdims=True) + EPS)
            nacc_s[which] += jnp.broadcast_to(jnp.sum(grad_normed * uf * root_inv, axis=0, keepdims=True), (8, model))
            weighted = grad_normed * pn[which][0:1, :]
            shared = jnp.mean(weighted * uf, axis=1, keepdims=True) * root_inv * root_inv * root_inv
            kept = (row_mask * incoming.astype(F32)).astype(BF).astype(F32)
            psend[i] = (root_inv * weighted - uf * shared + kept).astype(BF)

        @pl.when(i < micro)
        def _():
            close(out0[j], cot[j])

        @pl.when(i >= micro)
        def _():
            close(tokens[j], psend[j])

        @pl.when(which == p)
        def _():
            out_copy(i).start()

    @pl.when((g == 1) & (idx > 1))
    def _():
        finish(idx - 2)

    @pl.when((g == groups - 1) & (idx == total_idx - 1))
    def _():
        finish(idx - 1)
        finish(idx)
        norm_o[...] = nacc_s[...]
        for i in range(total_idx):

            @pl.when(1 - i // micro == p)
            def _():
                out_copy(i).wait()

        @pl.when(t > 0)
        def _():
            for i in range(total_idx):
                tail_copy(i).wait_send()

            def drain(i, carry):
                chain_copy(i).wait_send()
                halo_copy(i).wait_send()
                return carry

            lax.fori_loop(0, total_idx * groups, drain, 0)


def all_of(shape, buffers=2):
    spec = functools.partial(pl.BlockSpec, shape, lambda q, s, g: (0,) * len(shape))
    return spec(pipeline_mode=pl.Buffered(buffers)) if buffers != 2 else spec()


def fused_specs(turned):
    def layer(q):
        return 1 - q if turned else q

    def item(*shape):
        zeros = (0,) * len(shape)
        return pl.BlockSpec((None, None) + shape, lambda q, s, g: (layer(q), s) + zeros)

    def item_cols(rows):
        return pl.BlockSpec((None, None, rows, GC), lambda q, s, g: (layer(q), s, 0, g))

    def item_rows(cols):
        return pl.BlockSpec((None, None, GC, cols), lambda q, s, g: (layer(q), s, g, 0))

    def layer_cols(rows):
        return pl.BlockSpec((None, rows, GC), lambda q, s, g: (layer(q), 0, g))

    def layer_all(*shape):
        zeros = (0,) * len(shape)
        return pl.BlockSpec((None,) + shape, lambda q, s, g: (layer(q),) + zeros)

    return item, item_cols, item_rows, layer_cols, layer_all


def forward_call(tokens, mask, shards, chan, shared, count, groups_dp, head_dim):
    micro, rows, model = tokens.shape
    value, gate, out, step, state_w = shards
    half, states = value.shape[1] // 2, state_w.shape[1]
    width, state = half * count, states // 2
    groups = width // GC
    item, item_cols, item_rows, layer_cols, layer_all = fused_specs(False)
    slots = 2 * micro
    dma = pltpu.SemaphoreType.DMA
    vmem = pltpu.VMEM
    anywhere = pl.BlockSpec(memory_space=pl.ANY)
    ins = [
        (tokens, all_of(tokens.shape, 1)),
        (mask, all_of(mask.shape, 1)),
        (value, anywhere),
        (gate, anywhere),
        (out, anywhere),
        (step, anywhere),
        (state_w, anywhere),
        (chan, anywhere),
        (shared, anywhere),
    ]
    pair = (2, micro)
    step_rows = step.shape[0] // 2 * count
    outs = [
        (((2, model, width), BF), anywhere),
        (((2, model, width), BF), anywhere),
        (((2, model, width), BF), anywhere),
        (((2, step_rows, model), BF), anywhere),
        (((2, model, states), BF), anywhere),
        (((2, 8, width), F32), all_of((2, 8, width))),
        (((2, 8, states), F32), all_of((2, 8, states))),
        (((2, 8, LANES), F32), all_of((2, 8, LANES))),
        (((2,) + shared.shape, F32), all_of((2,) + shared.shape)),
        (((micro, rows, model), BF), anywhere),
        (((micro, rows, model), BF), anywhere),
        (((slots, rows, model), BF), anywhere),
        (((slots, rows, LANES), F32), all_of((slots, rows, LANES))),
        ((pair + (rows, model), BF), item(rows, model)),
        ((pair + (rows + HALO, width), F32), item_cols(rows + HALO)),
        ((pair + (rows + HALO, states), F32), item(rows + HALO, states)),
        ((pair + (rows, width), BF), item_cols(rows)),
        ((pair + (rows, states), BF), item(rows, states)),
        ((pair + (3, rows, LANES), F32), item(3, rows, LANES)),
        ((pair + (rows, width), F32), item_cols(rows)),
        ((pair + (rows, width), F32), item_cols(rows)),
        ((pair + (rows, width), BF), item_cols(rows)),
        ((pair + (width, state), BF), item_rows(state)),
    ]
    lanes = vmem((groups, rows, LANES), F32)
    scratch = [
        vmem((rows + HALO, model), BF),
        vmem((rows, rows), F32),
        lanes,
        lanes,
        vmem((groups, 8, rows), F32),
        vmem((rows, model), F32),
        vmem((rows, LANES), F32),
        vmem((slots, rows, model), BF),
        vmem((slots, rows, model), BF),
        vmem((slots, rows, LANES), F32),
        vmem((slots, rows, LANES), F32),
        vmem((slots * groups, GC, state), BF),
        vmem((slots * groups, GC, state), BF),
        vmem((micro, HALO, model), BF),
        vmem((micro, HALO, model), BF),
        dma((slots,)),
        dma((slots,)),
        dma((slots,)),
        dma((slots,)),
        dma((slots * groups,)),
        dma((slots * groups,)),
        dma((micro,)),
        dma((micro,)),
        dma((1,)),
        dma((1,)),
        dma((micro,)),
        dma((slots,)),
        dma((slots,)),
        vmem((2, model, GC), BF),
        vmem((2, model, GC), BF),
        vmem((2, model, GC), BF),
        vmem((model, states), BF),
        vmem((step_rows, model), BF),
        vmem((2, 8, width), F32),
        vmem((2,) + shared.shape, F32),
        dma((2, 3)),
        dma((2,)),
    ] + Gather.scratch(count)
    kernel = functools.partial(fused_forward, count, head_dim, micro)
    flops = slots * (6 * rows * model * width + 6 * rows * rows * width)
    options = fused_options(pair + (groups,), ins, outs, scratch, 2, flops, 60 * slots * rows * width)
    return pl.pallas_call(kernel, **options)(*[array for array, _ in ins])


def fused_options(grid, ins, outs, scratch, collective, flops, traffic):
    return dict(
        grid=grid,
        in_specs=[spec for _, spec in ins],
        out_specs=[spec for _, spec in outs],
        out_shape=[jax.ShapeDtypeStruct(*kind) for kind, _ in outs],
        scratch_shapes=scratch,
        cost_estimate=pl.CostEstimate(flops=flops, bytes_accessed=traffic, transcendentals=0),
        compiler_params=pltpu.CompilerParams(
            collective_id=collective,
            has_side_effects=True,
            vmem_limit_bytes=VMEM_LIMIT,
            dimension_semantics=(SEQUENTIAL,) * len(grid),
        ),
    )


def backward_fused_call(cot, tokens, out0, mask, kept, w, par, count, head_dim):
    micro, rows, model = tokens.shape
    width, states = w.value.shape[2], w.state.shape[2]
    state = states // 2
    groups = width // GC
    item, item_cols, item_rows, layer_cols, layer_all = fused_specs(True)
    slots = 2 * micro
    dma = pltpu.SemaphoreType.DMA
    vmem = pltpu.VMEM
    ins = [
        (cot, all_of(cot.shape, 1)),
        (tokens, all_of(tokens.shape, 1)),
        (out0, all_of(out0.shape, 1)),
        (mask, all_of(mask.shape, 1)),
        (kept.inv, item(rows, LANES)),
        (kept.mix, item(rows, model)),
        (kept.vpre, item_cols(rows + HALO)),
        (kept.spre, item(rows + HALO, states)),
        (kept.x, item_cols(rows)),
        (kept.bc, item(rows, states)),
        (kept.dtc, item(3, rows, LANES)),
        (kept.gate, item_cols(rows)),
        (kept.y, item_cols(rows)),
        (kept.s_in, item_rows(state)),
        (w.value, layer_cols(model)),
        (w.gate, layer_cols(model)),
        (w.out, layer_cols(model)),
        (w.state, layer_all(model, states)),
        (w.step, layer_all(LANES, model)),
        (par.value, layer_cols(8)),
        (par.state, layer_all(8, states)),
        (par.head, layer_all(8, LANES)),
        (par.norm, all_of(par.norm.shape, 1)),
    ]
    pair = (2, micro)
    outs = [
        (((micro, rows, model), BF), pl.BlockSpec(memory_space=pl.ANY)),
        ((pair + (rows, width), BF), item_cols(rows)),
        ((pair + (rows, width), BF), item_cols(rows)),
        ((pair + (rows, states), BF), item(rows, states)),
        ((pair + (rows, LANES), BF), item(rows, LANES)),
        ((pair + (rows, model), BF), item(rows, model)),
        ((pair + (8, width), F32), item_cols(8)),
        ((pair + (8, states), F32), item(8, states)),
        ((pair + (8, LANES), F32), item(8, LANES)),
        (((2, 8, model), F32), all_of((2, 8, model))),
    ]
    lanes = vmem((groups, rows, LANES), F32)
    square = vmem((rows, rows), F32)
    scratch = [
        vmem((rows, model), BF),
        vmem((rows, LANES), F32),
        vmem((GC, state), BF),
        vmem((8, GC), F32),
        vmem((8, states), F32),
        vmem((rows, model), F32),
        vmem((2, 8, model), F32),
        square,
        square,
        square,
        vmem((rows, states), F32),
        lanes,
        lanes,
        vmem((groups, 8, rows), F32),
        lanes,
        lanes,
        lanes,
        vmem((groups, 8, LANES), F32),
        vmem((groups, 8, rows), F32),
        vmem((LANES, rows), F32),
        vmem((slots, rows, model), BF),
        vmem((slots, rows, model), BF),
        vmem((slots * groups, GC, state), BF),
        vmem((slots * groups, GC, state), BF),
        vmem((slots * groups, 8, GC), F32),
        vmem((slots * groups, 8, GC), F32),
        vmem((slots, 8, states), F32),
        vmem((slots, 8, states), F32),
        dma((slots,)),
        dma((slots,)),
        dma((slots * groups,)),
        dma((slots * groups,)),
        dma((slots * groups,)),
        dma((slots * groups,)),
        dma((slots,)),
        dma((slots,)),
        dma((slots,)),
    ]
    kernel = functools.partial(fused_backward, count, head_dim, micro)
    flops = slots * (8 * rows * model * width + 16 * rows * rows * width)
    options = fused_options(pair + (groups,), ins, outs, scratch, 3, flops, 60 * slots * rows * width)
    return pl.pallas_call(kernel, **options)(*[array for array, _ in ins])


def fused_body(
    tokens_in,
    cotangent,
    lengths,
    in_gate,
    in_value,
    in_state,
    in_step,
    out_proj,
    norm_gain,
    conv_value,
    conv_state,
    bias_value,
    bias_state,
    step_bias,
    decay_log,
    skip_gain,
    gate_gain,
):
    layer, group, block = lax.axis_index(PIPE), lax.axis_index(DP), lax.axis_index(TENSOR)
    blocks, groups = lax.axis_size(TENSOR), lax.axis_size(DP)
    first_half = layer == 0
    micro, rows, model = tokens_in.shape
    shard_rows = in_value.shape[1]
    half = in_value.shape[2] // 2
    heads = step_bias.shape[1] // 2
    head_dim = half // heads
    width = half * blocks
    all_heads = heads * blocks
    states = in_state.shape[2]

    row = jnp.arange(2 * HALO)[:, None]
    head = jnp.arange(2 * heads)[None, :]
    step_rows = (row == head // heads * HALO + lax.rem(head, heads)).astype(BF)
    step_shard = nt(step_rows, in_step[0]).astype(BF)
    both = jnp.concatenate([step_bias.reshape(2, heads), decay_log.reshape(2, heads)], axis=1)
    per_head = jnp.pad(both, ((0, 0), (0, half - 2 * heads))).reshape(1, 2 * half)
    skip = jnp.repeat(skip_gain, head_dim, axis=1)
    channel = jnp.concatenate([conv_value[0], bias_value, gate_gain, skip, per_head], axis=0)
    state_row = jnp.concatenate([conv_state[0].reshape(1, -1), bias_state], axis=1)
    shared = jnp.concatenate([norm_gain, jnp.pad(state_row, ((0, 6), (0, model - 5 * states))), norm_gain], axis=0)

    valid = block * rows + jnp.arange(rows)[None, :] < lengths[:, None]
    mask = jnp.broadcast_to(valid.astype(F32)[:, :, None], (micro, rows, LANES))

    shards = (in_value[0], in_gate[0], out_proj[0], step_shard, in_state[0])
    (wv, wg, wo, wt, ws, pv, ps, ph, pn, out, low_out, mix, inv, nx, vpre, spre, x, bc, dtc, gate, y, gg, s_in) = forward_call(
        tokens_in, mask, shards, channel, shared, blocks, groups, head_dim
    )
    places = step_places(blocks, wt.shape[1], all_heads).astype(BF)
    step_w = jnp.stack([tn(places, wt[q]).astype(BF) for q in range(2)])
    w = Bundle(value=wv, gate=wg, out=wo, state=ws, step=step_w)
    par = Bundle(value=pv, head=ph, state=ps, norm=pn)
    kept = Bundle(
        inv=inv.reshape(2, micro, rows, LANES),
        mix=mix.reshape(2, micro, rows, model),
        vpre=vpre,
        spre=spre,
        x=x,
        bc=bc,
        dtc=dtc,
        gate=gate,
        y=y,
        s_in=s_in,
    )
    grads, dval, dgate, dst, dstep, sgm, vsums, ssums, hsums, nsums = backward_fused_call(
        cotangent, tokens_in, low_out, mask, kept, w, par, blocks, head_dim
    )

    def long(value, q):
        return value[q].reshape(micro * rows, value.shape[3])

    lane = jnp.arange(LANES)[:, None]
    by_block = (8 * (lane // heads) + lax.rem(lane, heads) == jnp.arange(LANES)[None, :]) & (lane < all_heads)
    big, pack, turned = [], [], []
    for q in range(2):
        normed = long(nx, q)
        big += [
            tn(normed, long(dval, q)).astype(BF),
            tn(normed, long(dgate, q)).astype(BF),
            tn(long(sgm, q), long(gg, q)).astype(BF),
        ]
        turned.append(tn(long(dst, q), normed))
        step_lanes = nn(long(dstep, q), by_block.astype(BF)).astype(BF)
        step_grad = tn(step_lanes[:, : 8 * blocks], normed)
        ssum, hsum = jnp.sum(ssums[q], axis=0), jnp.sum(hsums[q], axis=0)
        rest = [
            nsums[q, 0][None],
            jnp.pad(ssum[:5].reshape(1, -1), ((0, 0), (0, width - 5 * states))),
            jnp.zeros((6, width), F32),
        ]
        hsum = hsum[:2, :all_heads].reshape(2, blocks, heads).transpose(1, 0, 2).reshape(blocks, 2 * heads)
        hsum = jnp.pad(hsum, ((0, 0), (0, half - 2 * heads))).reshape(1, width)
        pack.append(jnp.concatenate([jnp.sum(vsums[q], axis=0)[:7], hsum, step_grad] + rest, axis=0))
    turned = lax.psum_scatter(
        jnp.concatenate(turned, axis=0), (PIPE, DP, TENSOR), scatter_dimension=0, tiled=True
    )
    grad_value, grad_gate, grad_out, chan, step_grad, rest = reduce_call(big, jnp.stack(pack), blocks, groups)

    step_grad = step_grad.reshape(2, 8, shard_rows)[:, :heads].reshape(2 * heads, shard_rows).T
    grad_state = turned.T
    position = group * blocks + block
    ranks = groups * blocks

    def share(value):
        size = value.shape[-1] // ranks
        return lax.dynamic_slice_in_dim(value, position * size, size, value.ndim - 1)

    head_sums = chan[7].reshape(2, half)[:, : 2 * heads].reshape(2, 2, heads).transpose(1, 0, 2).reshape(2, -1)
    norm_sum = share(rest[0])
    conv_sum = share(rest[1, : 5 * states].reshape(5, states))
    return (
        out[None],
        grads[None],
        grad_gate[None],
        grad_value[None],
        grad_state[None],
        step_grad[None],
        grad_out[None],
        norm_sum[None],
        chan[None, :4],
        conv_sum[None, :4],
        chan[None, 4],
        conv_sum[None, 4],
        head_sums[None, 0],
        head_sums[None, 1],
        jnp.sum(chan[6].reshape(2 * heads, head_dim), axis=1)[None],
        chan[None, 5],
    )


def body(
    tokens_in,
    cotangent,
    lengths,
    in_gate,
    in_value,
    in_state,
    in_step,
    out_proj,
    norm_gain,
    conv_value,
    conv_state,
    bias_value,
    bias_state,
    step_bias,
    decay_log,
    skip_gain,
    gate_gain,
):
    layer = lax.axis_index(PIPE)
    block = lax.axis_index(TENSOR)
    blocks = lax.axis_size(TENSOR)
    group = lax.axis_index(DP)
    groups = lax.axis_size(DP)
    first_half = layer == 0
    micro, rows, model = tokens_in.shape
    shard_rows = in_value.shape[1]
    half = in_value.shape[2] // 2
    heads = step_bias.shape[1] // 2
    head_dim = half // heads
    width = half * blocks
    all_heads = heads * blocks
    states = in_state.shape[2]
    state = states // 2
    inner_total = 2 * width

    def halves(value):
        keep = lax.dynamic_slice_in_dim(value, layer * half_of(value), half_of(value), value.ndim - 1)
        send = lax.dynamic_slice_in_dim(value, (1 - layer) * half_of(value), half_of(value), value.ndim - 1)
        return by_layer(keep, swap_pipe(send))

    def half_of(value):
        return value.shape[-1] // 2

    def by_layer(own, other):
        return jnp.where(first_half, own, other), jnp.where(first_half, other, own)

    channel = jnp.concatenate([conv_value[0], bias_value, gate_gain], axis=0)
    channel_both = halves(channel)
    head_both = halves(jnp.concatenate([step_bias, decay_log, skip_gain], axis=0))
    flat_heads = [jnp.pad(v.reshape(1, 3 * heads), ((0, 0), (0, half - 3 * heads))) for v in head_both]
    packed = gather_tensor(jnp.concatenate(list(channel_both) + flat_heads + [jnp.zeros((2, half), F32)], axis=0))
    shared = jnp.concatenate([norm_gain[0], conv_state[0].reshape(-1), bias_state[0]], axis=0)
    shared_both = by_layer(shared, swap_pipe(shared))
    params = []
    for q in range(2):
        per_head = packed[12 + q].reshape(blocks, half)[:, : 3 * heads].reshape(blocks, 3, heads)
        per_head = per_head.transpose(1, 0, 2).reshape(3, all_heads)
        skip = jnp.repeat(per_head[2:3], head_dim, axis=1)
        value_par = jnp.concatenate([packed[6 * q : 6 * q + 6], skip, jnp.zeros((1, width), F32)], axis=0)
        head_par = jnp.pad(per_head, ((0, 5), (0, LANES - all_heads)))
        state_par = jnp.concatenate(
            [
                shared_both[q][model : model + 4 * states].reshape(4, states),
                shared_both[q][model + 4 * states :].reshape(1, states),
                jnp.zeros((3, states), F32),
            ],
            axis=0,
        )
        params.append(Bundle(value=value_par, head=head_par, state=state_par, norm=shared_both[q][:model]))

    step_both = halves(in_step[0])
    step_all = gather_tensor(jnp.concatenate(step_both, axis=1)).reshape(shard_rows, blocks, 2, heads)
    state_both = by_layer(in_state[0], swap_pipe(in_state[0]))
    value_both, gate_both, out_both = halves(in_value[0]), halves(in_gate[0]), halves(out_proj[0])
    weights = []
    for q in range(2):
        step_q = jnp.pad(step_all[:, :, q].reshape(shard_rows, all_heads), ((0, 0), (0, LANES - all_heads)))
        small = gather_dp(jnp.concatenate([state_both[q], step_q], axis=1))
        weights.append(
            Bundle(
                state=small[:, :states],
                step=small[:, states:],
                value=gather_dp(gather_tensor(value_both[q])),
                gate=gather_dp(gather_tensor(gate_both[q])),
                out=gather_dp(gather_tensor(out_both[q])),
            )
        )

    masks = [
        (block * rows + jnp.arange(rows) < lengths[s]).astype(F32)[:, None] for s in range(micro)
    ]

    def forward(u, s, q):
        w, par = weights[q], params[q]
        ext = jnp.concatenate([shift_tensor(u[-HALO:], 1), u], axis=0).astype(F32)
        root_inv = lax.rsqrt(jnp.mean(ext * ext, axis=1, keepdims=True) + EPS)
        nx = (ext * root_inv * par.norm[None, :]).astype(BF)
        vpre, spre, x, bc, dtc, yw, loc = front_call(nx, w, par, head_dim, state)
        through = jnp.repeat(jnp.exp(dtc[1, rows - 1, :all_heads]), head_dim)[:, None]
        s_in = jnp.zeros((width, state), BF)
        for k in range(1, blocks):
            sent = (through * s_in.astype(F32) + loc).astype(BF)
            got = lax.ppermute(sent, TENSOR, [(k - 1, k)])
            s_in = got if k == 1 else jnp.where(block == k, got, s_in)
        gate, y, gg, part, squares = finish_call(nx, w, par, yw, s_in, bc, dtc, head_dim)
        total = squares[:, 0]
        total = total + swap_pipe(total)
        inverse = lax.rsqrt(total / inner_total + EPS)[:, None]
        mixed = inverse * (part.astype(F32) + swap_pipe(part).astype(F32))
        result = (masks[s] * (u.astype(F32) + mixed)).astype(BF)
        kept = Bundle(
            u=u, nx=nx, root_inv=root_inv[HALO:], vpre=vpre, spre=spre, x=x, bc=bc, dtc=dtc, s_in=s_in, through=through,
            gate=gate, y=y, gg=gg, inverse=inverse, mixed=mixed,
        )
        return result, kept

    def backward(incoming, s, q, kept):
        w, par = weights[q], params[q]
        gm = (masks[s] * incoming.astype(F32)).astype(BF)
        gmf = gm.astype(F32)
        inverse = kept.inverse
        dot = jnp.sum(gmf * kept.mixed, axis=1, keepdims=True)
        shrink = inverse * inverse * dot / inner_total
        rowsc = jnp.concatenate([inverse, shrink, jnp.zeros((rows, LANES - 2), F32)], axis=1)
        dy, dgate, dsl, dgain = gate_call(gm, w, par, kept.y, kept.gate, rowsc, kept.bc, kept.dtc, head_dim)
        g_in = jnp.zeros((width, state), BF)
        for k in range(blocks - 2, -1, -1):
            sent = (kept.through * g_in.astype(F32) + dsl).astype(BF)
            got = lax.ppermute(sent, TENSOR, [(k + 1, k)])
            g_in = got if k == blocks - 2 else jnp.where(block == k, got, g_in)
        dconv, dsc, dstep, vsums, ssums, hsums = backward_call(
            dy, kept.x, kept.vpre, kept.spre, kept.bc, kept.dtc, kept.s_in, g_in, par, head_dim
        )
        halo = shift_tensor(jnp.concatenate([dconv[:8], dsc[:8]], axis=1), -1)
        dval, dst, part = conv_call(dconv, halo, dsc, dgate, dstep, w, par)
        grad_normed = part.astype(F32) + swap_pipe(part).astype(F32)
        uf, root_inv = kept.u.astype(F32), kept.root_inv
        grad_norm = jnp.sum(grad_normed * uf * root_inv, axis=0)
        weighted = grad_normed * par.norm[None, :]
        grad_u = root_inv * weighted - uf * root_inv**3 * jnp.mean(weighted * uf, axis=1, keepdims=True) + gmf
        scaled_gm = (gmf * inverse).astype(BF)
        channel_sums = jnp.concatenate([vsums[:5], dgain[:1], vsums[5:6]], axis=0)
        sums = (channel_sums, ssums[:5], hsums[:2, :all_heads], grad_norm)
        return grad_u.astype(BF), (dval, dgate, dst, dstep, scaled_gm), sums

    outs, kept = [], []
    current = [tokens_in[s] for s in range(micro)]
    for q in range(2):
        pairs = [forward(current[s], s, q) for s in range(micro)]
        current = [pair[0] for pair in pairs]
        outs.append(jnp.stack(current))
        kept.append([pair[1] for pair in pairs])

    grads = [None, None]
    reduced = [None, None]
    incoming = [cotangent[s] for s in range(micro)]
    for q in (1, 0):
        results = [backward(incoming[s], s, q, kept[q][s]) for s in range(micro)]
        incoming = [r[0] for r in results]
        grads[q] = jnp.stack(incoming)
        stacked = [jnp.concatenate([r[1][k] for r in results], axis=0) for k in range(5)]
        dval, dgate, dst, dstep, scaled_gm = stacked
        normed = jnp.concatenate([kept[q][s].nx[HALO:] for s in range(micro)], axis=0)
        gg = jnp.concatenate([kept[q][s].gg for s in range(micro)], axis=0)
        sums = [functools.reduce(jnp.add, [r[2][k] for r in results]) for k in range(4)]

        big = [tn(scaled_gm, gg).astype(BF), tn(normed, dgate).astype(BF), tn(normed, dval).astype(BF)]
        big = [reduce_tensor(take_cols(reduce_dp(v))) for v in big]
        turned = reduce_dp(tn(dst, normed).astype(BF))
        turned = reduce_tensor(take_first(turned.reshape(blocks, -1, model)))
        step_grad = tn(dstep, normed)[:all_heads]
        by_block = jnp.concatenate(
            [
                sums[0].reshape(7, blocks, half).transpose(1, 0, 2).reshape(blocks, -1),
                step_grad.reshape(blocks, -1),
                sums[2].reshape(2, blocks, heads).transpose(1, 0, 2).reshape(blocks, -1),
            ],
            axis=1,
        )
        per_block = reduce_tensor(take_first(sum_all_dp(by_block)))
        common = sum_all_tensor(sum_all_dp(jnp.concatenate([sums[1].reshape(-1), sums[3]], axis=0)))
        reduced[q] = (big, turned, per_block, common)

    def own_and_other(kind):
        return jnp.where(first_half, kind(0), kind(1)), jnp.where(first_half, kind(1), kind(0))

    def join(kind):
        own, other = own_and_other(kind)
        got = swap_pipe(other)
        return jnp.where(first_half, own, got), jnp.where(first_half, got, own)

    def columns(k):
        low, high = join(lambda q: reduced[q][0][k].astype(BF))
        return jnp.concatenate([low, high], axis=1).astype(F32)

    grad_out, grad_gate, grad_value = columns(0), columns(1), columns(2)
    own, other = own_and_other(lambda q: reduced[q][1])
    grad_state = (own + swap_pipe(other.astype(BF)).astype(F32)).T
    low, high = join(lambda q: reduced[q][2])
    cut1, cut2 = 7 * half, 7 * half + heads * model
    chan = jnp.concatenate([low[:cut1].reshape(7, half), high[:cut1].reshape(7, half)], axis=1)
    step_grad = jnp.concatenate([low[cut1:cut2].reshape(heads, model), high[cut1:cut2].reshape(heads, model)], axis=0)
    step_grad = lax.dynamic_slice_in_dim(step_grad, group * shard_rows, shard_rows, 1).T
    head_sums = jnp.concatenate([low[cut2:].reshape(2, heads), high[cut2:].reshape(2, heads)], axis=1)
    own, other = own_and_other(lambda q: reduced[q][3])
    conv_sum = own[: 5 * states] + swap_pipe(other[: 5 * states])
    norm_sum = own[5 * states :]
    position = group * blocks + block
    ranks = groups * blocks

    def share(value):
        size = value.shape[-1] // ranks
        return lax.dynamic_slice_in_dim(value, position * size, size, value.ndim - 1)

    conv_sum = share(conv_sum.reshape(5, states))
    return (
        jnp.where(first_half, outs[0], outs[1])[None],
        jnp.where(first_half, grads[0], grads[1])[None],
        grad_gate[None],
        grad_value[None],
        grad_state[None],
        step_grad[None],
        grad_out[None],
        share(norm_sum)[None],
        chan[None, :4],
        conv_sum[None, :4],
        chan[None, 4],
        conv_sum[None, 4],
        head_sums[None, 0],
        head_sums[None, 1],
        jnp.sum(chan[6].reshape(2 * heads, head_dim), axis=1)[None],
        chan[None, 5],
    )


def solution(mesh):
    in_specs = (
        P(DP, TENSOR, None),
        P(DP, TENSOR, None),
        P(DP),
        P(PIPE, DP, TENSOR),
        P(PIPE, DP, TENSOR),
        P(PIPE, DP, None),
        P(PIPE, DP, TENSOR),
        P(PIPE, DP, TENSOR),
        P(PIPE, None),
        P(PIPE, None, TENSOR),
        P(PIPE, None, None),
        P(PIPE, TENSOR),
        P(PIPE, None),
        P(PIPE, TENSOR),
        P(PIPE, TENSOR),
        P(PIPE, TENSOR),
        P(PIPE, TENSOR),
    )
    out_specs = (
        P(PIPE, DP, TENSOR, None),
        P(PIPE, DP, TENSOR, None),
        P(PIPE, DP, TENSOR),
        P(PIPE, DP, TENSOR),
        P(PIPE, None, (DP, TENSOR)),
        P(PIPE, DP, TENSOR),
        P(PIPE, DP, TENSOR),
        P(PIPE, (DP, TENSOR)),
        P(PIPE, None, TENSOR),
        P(PIPE, None, (DP, TENSOR)),
        P(PIPE, TENSOR),
        P(PIPE, (DP, TENSOR)),
        P(PIPE, TENSOR),
        P(PIPE, TENSOR),
        P(PIPE, TENSOR),
        P(PIPE, TENSOR),
    )

    def program(*args):
        columns = args[4].shape[2] // mesh.shape[TENSOR]
        fused = mesh.shape[DP] == 4 and mesh.shape[TENSOR] > 2 and columns // 2 % LANES == 0
        return mapped(fused_body if fused else body)(*args)

    def mapped(function):
        return jax.shard_map(function, mesh=mesh, in_specs=in_specs, out_specs=out_specs, check_vma=False)

    return program
```

```python
import functools
import types

import jax
import jax.numpy as jnp
from jax import lax
from jax.experimental import pallas as pl
from jax.experimental.pallas import tpu as pltpu
from jax.sharding import PartitionSpec as P

EPS = 1e-05
PIPE, DP, TENSOR = "pipe", "dp", "tensor"
SEQUENTIAL = "arbitrary"
Bundle = types.SimpleNamespace
HIGHEST = lax.Precision.HIGHEST
BF = jnp.bfloat16
F32 = jnp.float32
HALO = 16
GC = 256
LANES = 128


def nn(a, b):
    return jnp.dot(a, b, preferred_element_type=F32)


def nt(a, b):
    return lax.dot_general(a, b, (((1,), (1,)), ((), ())), preferred_element_type=F32)


def tn(a, b):
    return lax.dot_general(a, b, (((0,), (0,)), ((), ())), preferred_element_type=F32)


def exact(a, b):
    return jnp.dot(a, b, precision=HIGHEST, preferred_element_type=F32)


def sigmoid(v):
    return 1.0 / (1.0 + jnp.exp(-v))


def iota(shape, dim):
    return lax.broadcasted_iota(jnp.int32, shape, dim)


def spread(per_head, width, head_dim):
    lane = iota(per_head.shape, 1)
    parts = []
    for pair in range(width // LANES):
        parts.append(
            jnp.where(lane < head_dim, per_head[:, 2 * pair : 2 * pair + 1], per_head[:, 2 * pair + 1 : 2 * pair + 2])
        )
    return jnp.concatenate(parts, axis=1)


def conv_rows(pre, taps, rows):
    total = taps[4:5, :] + taps[3:4, :] * pre[HALO : HALO + rows, :]
    for k in range(3):
        total = total + taps[k : k + 1, :] * pre[HALO - 3 + k : HALO - 3 + k + rows, :]
    return total


def conv_sums(grad, pre, rows):
    sums = [jnp.sum(grad * pre[HALO - 3 + k : HALO - 3 + k + rows, :], axis=0, keepdims=True) for k in range(4)]
    sums.append(jnp.sum(grad, axis=0, keepdims=True))
    return sums


def conv_transposed(grad, halo, taps, rows):
    ext = jnp.concatenate([grad, halo], axis=0)
    total = taps[3:4, :] * grad
    for k in range(3):
        total = total + taps[k : k + 1, :] * ext[3 - k : 3 - k + rows, :]
    return total


def silu_slope(v):
    s = sigmoid(v)
    return s * (1.0 + v * (1.0 - s))


def group_lanes(values, dst, groups, per_group):
    for g in range(groups):
        dst[g] = values if g == 0 else pltpu.roll(values, LANES - per_group * g, 1)


def group_rows(values, dst, groups, per_group):
    turned = values.T
    for g in range(groups):
        dst[g, 0:per_group, :] = turned[per_group * g : per_group * (g + 1), :]


def scan_front(
    head_dim, nx, wv, ws, wt, pv, ps, ph, vpre_o, spre_o, x_o, bc_o, dtc_o, yw_o, loc_o, sc_s, dt_s, cum_s, cumt_s
):
    g = pl.program_id(0)
    groups = pl.num_programs(0)
    rows = x_o.shape[0]
    state = bc_o.shape[1] // 2
    per_group = GC // head_dim

    @pl.when(g == 0)
    def _():
        spre = nn(nx[...], ws[...])
        spre_o[...] = spre
        conv = conv_rows(spre, ps, rows)
        bc = (conv * sigmoid(conv)).astype(BF)
        bc_o[...] = bc
        scores = nt(bc[:, state:], bc[:, :state])
        lower = iota((rows, rows), 0) >= iota((rows, rows), 1)
        sc_s[...] = jnp.where(lower, scores, 0.0)
        raw = nn(nx[HALO:, :], wt[...]) + ph[0:1, :]
        step = jnp.maximum(raw, 0.0) + jnp.log(1.0 + jnp.exp(-jnp.abs(raw)))
        decay = -step * jnp.exp(ph[1:2, :])
        cum = exact(lower.astype(F32), decay)
        dtc_o[0] = step
        dtc_o[1] = cum
        dtc_o[2] = sigmoid(raw)
        group_lanes(step, dt_s, dt_s.shape[0], per_group)
        group_lanes(cum, cum_s, cum_s.shape[0], per_group)
        group_rows(cum, cumt_s, cumt_s.shape[0], per_group)

    pre = nn(nx[...], wv[...])
    vpre_o[...] = pre
    conv = conv_rows(pre, pv, rows)
    x = conv * sigmoid(conv)
    x_o[...] = x.astype(BF)
    step, cum, cumt = dt_s[g], cum_s[g], cumt_s[g]
    to_end = jnp.exp(cum[rows - 1 : rows, :] - cum)
    xp = (x * spread(step, GC, head_dim)).astype(BF)
    xr = (x * spread(step * to_end, GC, head_dim)).astype(BF)
    loc_o[...] = tn(xr, bc_o[:, :state])
    scores = sc_s[...]
    lane = iota((rows, LANES), 1)
    for pair in range(GC // LANES):
        cols = slice(LANES * pair, LANES * (pair + 1))
        outs = []
        for i in (2 * pair, 2 * pair + 1):
            diff = cum[:, i : i + 1] - cumt[i : i + 1, :]
            mix = (jnp.exp(jnp.minimum(diff, 0.0)) * scores).astype(BF)
            outs.append(nn(mix, xp[:, cols]))
        yw_o[:, cols] = jnp.where(lane < head_dim, outs[0], outs[1]) + pv[6:7, cols] * x[:, cols]


def scan_finish(
    head_dim, nx, wg, wo, yw, s_in, bc, dtc, pv, gate_o, y_o, gg_o, p_o, sq_o, acc_s, sq_s, cum_s
):
    g = pl.program_id(0)
    rows = yw.shape[0]
    state = bc.shape[1] // 2

    @pl.when(g == 0)
    def _():
        group_lanes(dtc[1], cum_s, cum_s.shape[0], GC // head_dim)
        acc_s[...] = jnp.zeros_like(acc_s)
        sq_s[...] = jnp.zeros_like(sq_s)

    gate = nn(nx[HALO:, :], wg[...])
    gate_o[...] = gate
    carried = nt(bc[:, state:], s_in[...])
    y = yw[...] + spread(jnp.exp(cum_s[g]), GC, head_dim) * carried
    y_o[...] = y
    gated = y * (gate * sigmoid(gate))
    gg = (gated * pv[5:6, :]).astype(BF)
    gg_o[...] = gg
    squares = gated * gated
    for part in range(GC // LANES):
        sq_s[...] += squares[:, LANES * part : LANES * (part + 1)]
    acc_s[...] += nt(gg, wo[...])

    @pl.when(g == pl.num_programs(0) - 1)
    def _():
        p_o[...] = acc_s[...].astype(BF)
        sq_o[...] = jnp.broadcast_to(jnp.sum(sq_s[...], axis=1, keepdims=True), sq_o.shape)


def gate_backward(head_dim, gm, wo, y, gate, rowsc, pv, bc, dtc, dy_o, dgate_o, dsl_o, dgain_o, cum_s):
    g = pl.program_id(0)
    state = bc.shape[1] // 2

    @pl.when(g == 0)
    def _():
        group_lanes(dtc[1], cum_s, cum_s.shape[0], GC // head_dim)

    gs = nn(gm[...], wo[...])
    inverse, shrink = rowsc[:, 0:1], rowsc[:, 1:2]
    gv, yv = gate[...], y[...]
    s = sigmoid(gv)
    silu = gv * s
    gated = yv * silu
    dgain = jnp.sum(gs * gated * inverse, axis=0, keepdims=True)
    dgain_o[...] = jnp.broadcast_to(dgain, dgain_o.shape)
    dgated = inverse * (gs * pv[5:6, :]) - gated * shrink
    dgate_o[...] = (dgated * yv * (s * (1.0 + gv * (1.0 - s)))).astype(BF)
    dy = dgated * silu
    dy_o[...] = dy.astype(BF)
    dye = (dy * spread(jnp.exp(cum_s[g]), GC, head_dim)).astype(BF)
    dsl_o[...] = tn(dye, bc[:, state:])


def scan_backward(
    head_dim,
    dy,
    x,
    vpre,
    spre,
    bc,
    dtc,
    s_in,
    g_in,
    pv,
    ps,
    ph,
    dconv_o,
    dsc_o,
    dstep_o,
    vs_o,
    ss_o,
    hs_o,
    sct_s,
    scts_s,
    wsum_s,
    dbc_s,
    dt_s,
    cum_s,
    cumt_s,
    net_s,
    rv_s,
    ddir_s,
    k_s,
    rt_s,
    rall_s,
):
    g = pl.program_id(0)
    rows = x.shape[0]
    state = bc.shape[1] // 2
    per_group = GC // head_dim
    groups = dt_s.shape[0]

    @pl.when(g == 0)
    def _():
        scores = nt(bc[:, :state], bc[:, state:])
        first, second = iota((rows, rows), 0), iota((rows, rows), 1)
        sct_s[...] = jnp.where(second >= first, scores, 0.0)
        scts_s[...] = jnp.where(second > first, scores, 0.0)
        wsum_s[...] = jnp.zeros_like(wsum_s)
        dbc_s[...] = jnp.zeros_like(dbc_s)
        rall_s[...] = jnp.zeros_like(rall_s)
        group_lanes(dtc[0], dt_s, groups, per_group)
        group_lanes(dtc[1], cum_s, groups, per_group)
        group_rows(dtc[1], cumt_s, groups, per_group)

    step, cum, cumt = dt_s[g], cum_s[g], cumt_s[g]
    last = cum[rows - 1 : rows, :]
    to_end = jnp.exp(last - cum)
    stepx = spread(step, GC, head_dim)
    endx = spread(to_end, GC, head_dim)
    fromx = spread(jnp.exp(cum), GC, head_dim)
    xf = x[...].astype(F32)
    dyb = dy[...]
    dyf = dyb.astype(F32)
    xp = (xf * stepx).astype(BF)
    xr = (xf * stepx * endx).astype(BF)
    dyef = dyf * fromx
    dye = dyef.astype(BF)
    gb = nt(bc[:, :state], g_in[...])
    cs = nt(bc[:, state:], s_in[...])
    dbc_s[:, :state] += nn(xr, g_in[...])
    dbc_s[:, state:] += nn(dye, s_in[...])

    lane = iota((rows, LANES), 1)
    wsum = wsum_s[...]
    colsum = jnp.zeros((rows, LANES), F32)
    within = []
    for pair in range(GC // LANES):
        cols = slice(LANES * pair, LANES * (pair + 1))
        xpp, dyp = xp[:, cols], dyb[:, cols]
        outs = []
        for side in range(2):
            i = 2 * pair + side
            mine = (lane < head_dim) if side == 0 else (lane >= head_dim)
            decay = jnp.exp(jnp.minimum(cumt[i : i + 1, :] - cum[:, i : i + 1], 0.0))
            outs.append(nn((decay * sct_s[...]).astype(BF), dyp))
            weight = decay * nt(jnp.where(mine, xpp, jnp.zeros_like(xpp)), dyp)
            wsum = wsum + weight
            pairs = (weight * scts_s[...]).astype(BF)
            colsum = colsum + nn(pairs, (lane == i).astype(BF))
            rt_s[g, i : i + 1, :] = jnp.sum(pairs.astype(F32), axis=0, keepdims=True)
        within.append(jnp.where(lane < head_dim, outs[0], outs[1]))
    wsum_s[...] = wsum
    u = jnp.concatenate(within, axis=1) + endx * gb

    heads = (iota((GC, LANES), 0) // head_dim == iota((GC, LANES), 1)).astype(BF)
    ddir_s[g] = nn((xf * u).astype(BF), heads)
    net_s[g] = nn((dyef * cs).astype(BF), heads) - colsum
    rv_s[g] = step * to_end * nn((xf * gb).astype(BF), heads)
    inner = g_in[...].astype(F32) * s_in[...].astype(F32)
    per_channel = lax.dot_general(
        jnp.ones((8, inner.shape[1]), F32), inner, (((1,), (1,)), ((), ())), precision=HIGHEST, preferred_element_type=F32
    )
    k_s[g] = jnp.exp(last) * exact(per_channel, heads.astype(F32))

    dx = stepx * u + pv[6:7, :] * dyf
    dconv = dx * silu_slope(conv_rows(vpre, pv, rows))
    dconv_o[...] = dconv
    sums = conv_sums(dconv, vpre, rows)
    sums.append(jnp.sum(dyf * xf, axis=0, keepdims=True))
    sums.append(jnp.zeros((2, GC), F32))
    vs_o[...] = jnp.concatenate(sums, axis=0)

    @pl.when(g == pl.num_programs(0) - 1)
    def _():
        first, second = iota((rows, rows), 0), iota((rows, rows), 1)
        net, rv, ddir, const = net_s[0], rv_s[0], ddir_s[0], k_s[0]
        rall_s[0:per_group, :] = rt_s[0, 0:per_group, :]
        for other in range(1, groups):
            shift = per_group * other
            net = net + pltpu.roll(net_s[other], shift, 1)
            rv = rv + pltpu.roll(rv_s[other], shift, 1)
            ddir = ddir + pltpu.roll(ddir_s[other], shift, 1)
            const = const + pltpu.roll(k_s[other], shift, 1)
            rall_s[shift : shift + per_group, :] = rt_s[other, 0:per_group, :]
        net = net + rall_s[...].T
        da = exact((second >= first).astype(F32), net) + exact((second < first).astype(F32), rv) + const[0:1, :]
        rate = jnp.exp(ph[1:2, :])
        dstep = (ddir - da * rate) * dtc[2]
        dstep_o[...] = dstep.astype(BF)
        hs_o[...] = jnp.concatenate(
            [
                jnp.sum(dstep, axis=0, keepdims=True),
                jnp.sum(-da * dtc[0] * rate, axis=0, keepdims=True),
                jnp.zeros((6, LANES), F32),
            ],
            axis=0,
        )
        weights = jnp.where(second >= first, wsum_s[...], 0.0).astype(BF)
        db = dbc_s[:, :state] + nn(weights, bc[:, state:])
        dc = dbc_s[:, state:] + tn(weights, bc[:, :state])
        dsc = jnp.concatenate([db, dc], axis=1) * silu_slope(conv_rows(spre, ps, rows))
        dsc_o[...] = dsc
        ssums = conv_sums(dsc, spre, rows)
        ssums.append(jnp.zeros((3, 2 * state), F32))
        ss_o[...] = jnp.concatenate(ssums, axis=0)


def conv_backward(dconv, halo_v, dsc, halo_s, dgate, dstep, pv, ps, wv, wg, ws, wt, dval_o, dst_o, p_o, acc_s):
    g = pl.program_id(0)
    rows = dconv.shape[0]

    @pl.when(g == 0)
    def _():
        dst = conv_transposed(dsc[...], halo_s[...], ps, rows).astype(BF)
        dst_o[...] = dst
        acc_s[...] = nt(dst, ws[...]) + nt(dstep[...], wt[...])

    dval = conv_transposed(dconv[...], halo_v[...], pv, rows).astype(BF)
    dval_o[...] = dval
    acc_s[...] += nt(dval, wv[...]) + nt(dgate[...], wg[...])

    @pl.when(g == pl.num_programs(0) - 1)
    def _():
        p_o[...] = acc_s[...].astype(BF)


def whole(shape):
    return pl.BlockSpec(shape, lambda g: (0,) * len(shape))


def by_cols(rows):
    return pl.BlockSpec((rows, GC), lambda g: (0, g))


def by_rows(cols):
    return pl.BlockSpec((GC, cols), lambda g: (g, 0))


def call(kernel, groups, ins, outs, scratch, flops, traffic, exps=0):
    arrays, in_specs = zip(*ins)
    shapes, out_specs = zip(*outs)
    return pl.pallas_call(
        kernel,
        grid=(groups,),
        in_specs=list(in_specs),
        out_specs=list(out_specs),
        out_shape=[jax.ShapeDtypeStruct(s, d) for s, d in shapes],
        scratch_shapes=scratch,
        cost_estimate=pl.CostEstimate(flops=flops, bytes_accessed=traffic, transcendentals=exps),
        compiler_params=pltpu.CompilerParams(vmem_limit_bytes=40 * 2**20, dimension_semantics=(SEQUENTIAL,)),
    )(*arrays)


def front_call(nx, w, par, head_dim, state):
    rows, width = nx.shape[0] - HALO, w.value.shape[1]
    model = nx.shape[1]
    groups = width // GC
    return call(
        functools.partial(scan_front, head_dim),
        groups,
        [
            (nx, whole(nx.shape)),
            (w.value, by_cols(model)),
            (w.state, whole(w.state.shape)),
            (w.step, whole(w.step.shape)),
            (par.value, by_cols(8)),
            (par.state, whole(par.state.shape)),
            (par.head, whole(par.head.shape)),
        ],
        [
            (((rows + HALO, width), F32), by_cols(rows + HALO)),
            (((rows + HALO, 2 * state), F32), whole((rows + HALO, 2 * state))),
            (((rows, width), BF), by_cols(rows)),
            (((rows, 2 * state), BF), whole((rows, 2 * state))),
            (((3, rows, LANES), F32), whole((3, rows, LANES))),
            (((rows, width), F32), by_cols(rows)),
            (((width, state), F32), by_rows(state)),
        ],
        [
            pltpu.VMEM((rows, rows), F32),
            pltpu.VMEM((groups, rows, LANES), F32),
            pltpu.VMEM((groups, rows, LANES), F32),
            pltpu.VMEM((groups, 8, rows), F32),
        ],
        2 * rows * model * (width + 3 * LANES) + 4 * rows * rows * width,
        2 * model * width + 12 * rows * width,
        rows * rows * width // head_dim,
    )


def finish_call(nx, w, par, yw, s_in, bc, dtc, head_dim):
    rows, width = yw.shape
    model = nx.shape[1]
    groups = width // GC
    state = s_in.shape[1]
    return call(
        functools.partial(scan_finish, head_dim),
        groups,
        [
            (nx, whole(nx.shape)),
            (w.gate, by_cols(model)),
            (w.out, by_cols(model)),
            (yw, by_cols(rows)),
            (s_in, by_rows(state)),
            (bc, whole(bc.shape)),
            (dtc, whole(dtc.shape)),
            (par.value, by_cols(8)),
        ],
        [
            (((rows, width), F32), by_cols(rows)),
            (((rows, width), F32), by_cols(rows)),
            (((rows, width), BF), by_cols(rows)),
            (((rows, model), BF), whole((rows, model))),
            (((rows, LANES), F32), whole((rows, LANES))),
        ],
        [
            pltpu.VMEM((rows, model), F32),
            pltpu.VMEM((rows, LANES), F32),
            pltpu.VMEM((groups, rows, LANES), F32),
        ],
        4 * rows * model * width,
        4 * model * width + 14 * rows * width,
    )


def gate_call(gm, w, par, y, gate, rowsc, bc, dtc, head_dim):
    rows, width = y.shape
    model = gm.shape[1]
    groups = width // GC
    state = bc.shape[1] // 2
    return call(
        functools.partial(gate_backward, head_dim),
        groups,
        [
            (gm, whole(gm.shape)),
            (w.out, by_cols(model)),
            (y, by_cols(rows)),
            (gate, by_cols(rows)),
            (rowsc, whole(rowsc.shape)),
            (par.value, by_cols(8)),
            (bc, whole(bc.shape)),
            (dtc, whole(dtc.shape)),
        ],
        [
            (((rows, width), BF), by_cols(rows)),
            (((rows, width), BF), by_cols(rows)),
            (((width, state), F32), by_rows(state)),
            (((8, width), F32), by_cols(8)),
        ],
        [pltpu.VMEM((groups, rows, LANES), F32)],
        2 * rows * model * width,
        2 * model * width + 14 * rows * width,
    )


def backward_call(dy, x, vpre, spre, bc, dtc, s_in, g_in, par, head_dim):
    rows, width = x.shape
    groups = width // GC
    state = bc.shape[1] // 2
    lanes = pltpu.VMEM((groups, rows, LANES), F32)
    square = pltpu.VMEM((rows, rows), F32)
    return call(
        functools.partial(scan_backward, head_dim),
        groups,
        [
            (dy, by_cols(rows)),
            (x, by_cols(rows)),
            (vpre, by_cols(rows + HALO)),
            (spre, whole(spre.shape)),
            (bc, whole(bc.shape)),
            (dtc, whole(dtc.shape)),
            (s_in, by_rows(state)),
            (g_in, by_rows(state)),
            (par.value, by_cols(8)),
            (par.state, whole(par.state.shape)),
            (par.head, whole(par.head.shape)),
        ],
        [
            (((rows, width), F32), by_cols(rows)),
            (((rows, 2 * state), F32), whole((rows, 2 * state))),
            (((rows, LANES), BF), whole((rows, LANES))),
            (((8, width), F32), by_cols(8)),
            (((8, 2 * state), F32), whole((8, 2 * state))),
            (((8, LANES), F32), whole((8, LANES))),
        ],
        [
            square,
            square,
            square,
            pltpu.VMEM((rows, 2 * state), F32),
            lanes,
            lanes,
            pltpu.VMEM((groups, 8, rows), F32),
            lanes,
            lanes,
            lanes,
            pltpu.VMEM((groups, 8, LANES), F32),
            pltpu.VMEM((groups, 8, rows), F32),
            pltpu.VMEM((LANES, rows), F32),
        ],
        12 * rows * rows * width,
        14 * rows * width,
        3 * rows * rows * width // head_dim,
    )


def conv_call(dconv, halo, dsc, dgate, dstep, w, par):
    rows, width = dconv.shape
    model = w.value.shape[0]
    groups = width // GC
    states = dsc.shape[1]
    halo_v, halo_s = halo[:, :width], halo[:, width:]
    return call(
        conv_backward,
        groups,
        [
            (dconv, by_cols(rows)),
            (halo_v, by_cols(8)),
            (dsc, whole(dsc.shape)),
            (halo_s, whole(halo_s.shape)),
            (dgate, by_cols(rows)),
            (dstep, whole(dstep.shape)),
            (par.value, by_cols(8)),
            (par.state, whole(par.state.shape)),
            (w.value, by_cols(model)),
            (w.gate, by_cols(model)),
            (w.state, whole(w.state.shape)),
            (w.step, whole(w.step.shape)),
        ],
        [
            (((rows, width), BF), by_cols(rows)),
            (((rows, states), BF), whole((rows, states))),
            (((rows, model), BF), whole((rows, model))),
        ],
        [pltpu.VMEM((rows, model), F32)],
        4 * rows * model * width,
        4 * model * width + 10 * rows * width,
    )


def swap_pipe(value):
    return lax.ppermute(value, PIPE, [(0, 1), (1, 0)])


def shift_tensor(value, by):
    count = lax.axis_size(TENSOR)
    return lax.ppermute(value, TENSOR, [(i, i + by) for i in range(count) if 0 <= i + by < count])


def flip_dp(value, bit):
    return lax.ppermute(value, DP, [(i, i ^ bit) for i in range(lax.axis_size(DP))])


def dp_bits():
    bits, bit = [], 1
    while bit < lax.axis_size(DP):
        bits.append(bit)
        bit *= 2
    return bits


def gather_tensor(piece):
    count, me = lax.axis_size(TENSOR), lax.axis_index(TENSOR)
    rows, cols = piece.shape
    right, left = [piece], [piece]
    for _ in range(count - 1):
        right.append(shift_tensor(right[-1], 1))
        left.append(shift_tensor(left[-1], -1))
    full = jnp.zeros((rows, count * cols), piece.dtype)
    for k in range(count):
        part = piece if k == 0 else jnp.where(me >= k, right[k], left[count - k])
        full = lax.dynamic_update_slice(full, part, (0, lax.rem(me - k + count, count) * cols))
    return full


def gather_dp(piece):
    count, me = lax.axis_size(DP), lax.axis_index(DP)
    rows, cols = piece.shape
    held = {0: piece}
    for bit in reversed(dp_bits()):
        for offset in list(held):
            held[offset ^ bit] = flip_dp(held[offset], bit)
    full = jnp.zeros((count * rows, cols), piece.dtype)
    for offset, part in held.items():
        full = lax.dynamic_update_slice(full, part, ((me ^ offset) * rows, 0))
    return full


def add_low(a, b):
    return (a.astype(F32) + b.astype(F32)).astype(a.dtype)


def reduce_dp(value):
    me = lax.axis_index(DP)
    count = lax.axis_size(DP)
    rows, cols = value.shape[0] // count, value.shape[1]
    for bit in dp_bits():
        count //= 2
        split = value.reshape(count, 2, rows, cols)
        mine = (me // bit) % 2
        keep = lax.dynamic_index_in_dim(split, mine, 1, keepdims=False)
        send = lax.dynamic_index_in_dim(split, 1 - mine, 1, keepdims=False)
        value = add_low(keep, flip_dp(send, bit)).reshape(count * rows, cols)
    return value


def reduce_tensor(take):
    count, me = lax.axis_size(TENSOR), lax.axis_index(TENSOR)
    moving_right = moving_left = None
    for k in range(count - 1, 0, -1):
        right, left = take(jnp.minimum(me + k, count - 1)), take(jnp.maximum(me - k, 0))
        if moving_right is not None:
            right, left = add_low(right, moving_right), add_low(left, moving_left)
        moving_right, moving_left = shift_tensor(right, 1), shift_tensor(left, -1)
    own = take(me)
    if moving_right is None:
        return own.astype(F32)
    return own.astype(F32) + moving_right.astype(F32) + moving_left.astype(F32)


def take_cols(value):
    width = value.shape[1] // lax.axis_size(TENSOR)
    return lambda j: lax.dynamic_slice_in_dim(value, j * width, width, 1)


def take_first(value):
    return lambda j: lax.dynamic_index_in_dim(value, j, 0, keepdims=False)


def sum_all_dp(value):
    for bit in dp_bits():
        value = value + flip_dp(value, bit)
    return value


def sum_all_tensor(value):
    count, bit = lax.axis_size(TENSOR), 1
    while bit < count:
        value = value + lax.ppermute(value, TENSOR, [(i, i ^ bit) for i in range(count)])
        bit *= 2
    return value


MESH = pl.DeviceIdType.MESH
VMEM_LIMIT = 60 * 2**20


def remote(src, dst, send, recv, axis, index):
    return pltpu.make_async_remote_copy(
        src_ref=src, dst_ref=dst, send_sem=send, recv_sem=recv, device_id={axis: index}, device_id_type=MESH
    )


def greet(partners):
    barrier = pltpu.get_barrier_semaphore()
    for axis, index in partners:
        pl.semaphore_signal(barrier, inc=1, device_id={axis: index}, device_id_type=MESH)
    pl.semaphore_wait(barrier, len(partners))


def ring_neighbours(count):
    t = lax.axis_index(TENSOR)
    return [(TENSOR, lax.rem(t + 1, count)), (TENSOR, lax.rem(t + count - 1, count))]


def aligned(index, size):
    return pl.ds(pl.multiple_of(index * size, size), size)


class Gather:
    sems = ((4,), (4,), (4,), "z", "z", "z", "z", "z", "c", "c", (3,), (3,), (3,), (2,), (2,), (2, 2), (2, 2), "n", "n")

    @classmethod
    def scratch(cls, count):
        shapes = {"z": (8, count), "c": (8, 2, count), "n": (count,)}
        return [pltpu.SemaphoreType.DMA(shapes.get(shape, shape)) for shape in cls.sems]

    def __init__(self, count, sources, targets, small, sems):
        self.count, self.sources, self.targets, self.small = count, sources, targets, small
        (self.own_sem, self.xs_sem, self.xr_sem, self.right_sem, self.left_sem, self.zr_sem) = sems[:6]
        (self.ys_sem, self.yr_sem, self.cs_sem, self.cr_sem, self.st_own, self.st_xs, self.st_xr) = sems[6:13]
        (self.st_ys, self.st_yr, self.st_cs, self.st_cr, self.ch_s, self.ch_r) = sems[13:]
        self.p, self.d, self.t = lax.axis_index(PIPE), lax.axis_index(DP), lax.axis_index(TENSOR)
        y, c = self.d // 2, lax.rem(self.d, 2)
        self.y_mate, self.core_mate, self.far_mate = 2 * (1 - y) + c, 2 * y + 1 - c, 2 * (1 - y) + 1 - c
        self.kinds = len(sources)
        self.rows = sources[0].shape[0]

    def partners(self):
        others = [(TENSOR, lax.rem(self.t + k, self.count)) for k in range(1, self.count)]
        return others + [(PIPE, 1 - self.p), (DP, self.y_mate), (DP, self.core_mate)]

    def source(self, kind, which):
        ref = self.sources[kind]
        if kind == self.kinds - 1:
            return ref.at[aligned(which, ref.shape[0] // 2), :]
        return ref.at[:, aligned(which, ref.shape[1] // 2)]

    def region(self, kind, layer, row, col):
        ref = self.sources[kind]
        if kind == self.kinds - 1:
            return self.targets[kind].at[layer, aligned(col, ref.shape[0] // 2), aligned(row, ref.shape[1])]
        return self.targets[kind].at[layer, aligned(row, self.rows), aligned(col, ref.shape[1] // 2)]

    def own_copy(self, w):
        return pltpu.make_async_copy(self.source(w, self.p), self.region(w, self.p, self.d, self.t), self.own_sem.at[w])

    def swap_copy(self, w):
        dst = self.region(w, self.p, self.d, self.t)
        return remote(self.source(w, 1 - self.p), dst, self.xs_sem.at[w], self.xr_sem.at[w], PIPE, 1 - self.p)

    def swap_arrival(self, w):
        dst = self.region(w, 1 - self.p, self.d, self.t)
        return remote(self.source(w, 1 - self.p), dst, self.xs_sem.at[w], self.xr_sem.at[w], PIPE, 1 - self.p)

    def z_copy(self, item, src, by, sem):
        ref = self.region(item % self.kinds, item // self.kinds, self.d, src)
        return remote(ref, ref, sem.at[item, src], self.zr_sem.at[item, src], TENSOR, self.t + by)

    def right(self, item, src):
        return self.z_copy(item, src, 1, self.right_sem)

    def left(self, item, src):
        return self.z_copy(item, src, -1, self.left_sem)

    def y_copy(self, item, src, row=None):
        ref = self.region(item % self.kinds, item // self.kinds, self.d if row is None else row, src)
        return remote(ref, ref, self.ys_sem.at[item, src], self.yr_sem.at[item, src], DP, self.y_mate)

    def core_copy(self, item, which, src, arrival=False):
        row = (self.core_mate, self.far_mate)[which] if arrival else (self.d, self.y_mate)[which]
        ref = self.region(item % self.kinds, item // self.kinds, row, src)
        sems = self.cs_sem.at[item, which, src], self.cr_sem.at[item, which, src]
        return remote(ref, ref, *sems, DP, self.core_mate)

    def begin(self, item):
        w, layer = item % self.kinds, item // self.kinds

        @pl.when(self.p == layer)
        def _():
            self.own_copy(w).wait()

        @pl.when(self.p != layer)
        def _():
            self.swap_arrival(w).wait_recv()

        @pl.when(self.t < self.count - 1)
        def _():
            self.right(item, self.t).start()

        @pl.when(self.t > 0)
        def _():
            self.left(item, self.t).start()

        self.y_copy(item, self.t).start()
        self.core_copy(item, 0, self.t).start()

    def hop(self, item, hop):
        t, count = self.t, self.count
        lower, upper = t - hop, t + hop

        @pl.when(lower >= 0)
        def _():
            self.right(item, lower).wait_recv()

            @pl.when(t < count - 1)
            def _():
                self.right(item, lower).start()

            self.y_copy(item, lower).start()
            self.core_copy(item, 0, lower).start()

        @pl.when(upper < count)
        def _():
            self.left(item, upper).wait_recv()

            @pl.when(t > 0)
            def _():
                self.left(item, upper).start()

            self.y_copy(item, upper).start()
            self.core_copy(item, 0, upper).start()

    def share(self, item, src):
        self.y_copy(item, src, self.y_mate).wait_recv()
        self.core_copy(item, 1, src).start()

    def arrived(self, item, src):
        for which in range(2):
            self.core_copy(item, which, src, True).wait_recv()

    def sent(self, item):
        t, count = self.t, self.count
        for src in range(count):
            for which in range(2):
                self.core_copy(item, which, src).wait_send()
            self.y_copy(item, src).wait_send()

            @pl.when((src <= t) & (t < count - 1))
            def _():
                self.right(item, src).wait_send()

            @pl.when((src >= t) & (t > 0))
            def _():
                self.left(item, src).wait_send()


    def small_target(self, k, layer):
        target = self.small[k][1]
        if k == 0:
            return target.at[layer, aligned(self.d, self.rows), :]
        if k == 1:
            return target.at[layer, :, aligned(self.t, target.shape[2] // self.count)]
        return target.at[layer]

    def small_source(self, k, which):
        ref = self.small[k][0]
        return ref.at[:, aligned(which, ref.shape[1] // 2)] if k == 1 else ref

    def small_own(self, k):
        return pltpu.make_async_copy(self.small_source(k, self.p), self.small_target(k, self.p), self.st_own.at[k])

    def small_swap(self, k, arrival=False):
        dst = self.small_target(k, 1 - self.p if arrival else self.p)
        return remote(self.small_source(k, 1 - self.p), dst, self.st_xs.at[k], self.st_xr.at[k], PIPE, 1 - self.p)

    def state_rows(self, layer, row):
        return self.small[0][1].at[layer, aligned(row, self.rows), :]

    def state_y(self, layer, arrival=False):
        ref = self.state_rows(layer, self.y_mate if arrival else self.d)
        return remote(ref, ref, self.st_ys.at[layer], self.st_yr.at[layer], DP, self.y_mate)

    def state_core(self, layer, which, arrival=False):
        row = (self.core_mate, self.far_mate)[which] if arrival else (self.d, self.y_mate)[which]
        ref = self.state_rows(layer, row)
        return remote(ref, ref, self.st_cs.at[layer, which], self.st_cr.at[layer, which], DP, self.core_mate)

    def channels(self, k, arrival=False):
        target = self.small[1][1]
        index = lax.rem(self.t - k + self.count, self.count) if arrival else self.t
        ref = target.at[:, :, aligned(index, target.shape[2] // self.count)]
        return remote(ref, ref, self.ch_s.at[k], self.ch_r.at[k], TENSOR, lax.rem(self.t + k, self.count))

    def first_layer(self):
        order = [self.kinds - 1] + list(range(self.kinds - 1))
        for w in order:
            self.swap_copy(w).start()
            self.own_copy(w).start()
        for k in range(3):
            self.small_swap(k).start()
            self.small_own(k).start()
        order = [self.kinds - 1, 2 * self.kinds - 1] + list(range(self.kinds - 1))
        for item in order:
            self.begin(item)
        for k in range(3):
            self.small_own(k).wait()
            self.small_swap(k, True).wait_recv()
        for layer in range(2):
            self.state_y(layer).start()
            self.state_core(layer, 0).start()
        for k in range(1, self.count):
            self.channels(k).start()
        for hop in range(1, self.count):
            for item in order:
                self.hop(item, hop)
        for item in self.late_items():
            self.begin(item)
        for layer in range(2):
            self.state_y(layer, True).wait_recv()
            self.state_core(layer, 1).start()
        for src in range(self.count):
            for item in order:
                self.share(item, src)
        for item in order:
            for src in range(self.count):
                self.arrived(item, src)
        for k in range(1, self.count):
            self.channels(k, True).wait_recv()
        for layer in range(2):
            for which in range(2):
                self.state_core(layer, which, True).wait_recv()

    def late_items(self):
        return [self.kinds + w for w in range(self.kinds - 1)]

    def second_layer(self, steps, group_of):
        items, stages = self.late_items(), []
        hops = [(item, hop) for hop in range(1, self.count) for item in items]
        for n, (item, hop) in enumerate(hops):
            stages.append((2 + n * (steps - 5) // len(hops), functools.partial(self.hop, item, hop)))
        for src in range(self.count):
            for item in items:
                stages.append((steps - 2 + group_of(src), functools.partial(self.share, item, src)))
        for src in range(self.count):
            for item in items:
                stages.append((steps - 1 + group_of(src), functools.partial(self.arrived, item, src)))
        return stages

    def finish(self):
        for k in range(3):
            self.small_swap(k).wait_send()
        for k in range(1, self.count):
            self.channels(k).wait_send()
        for layer in range(2):
            self.state_y(layer).wait_send()
            for which in range(2):
                self.state_core(layer, which).wait_send()
        for w in range(self.kinds):
            self.swap_copy(w).wait_send()
        for item in range(2 * self.kinds):
            self.sent(item)


class Reducer:
    def __init__(self, count, factors, results, buffers, sems):
        self.count, self.factors, self.results = count, factors, results
        (self.a_s, self.b_s, self.dw_s, self.crecv, self.ysend, self.near_s, self.yrecv, self.total_s) = buffers[:8]
        (self.z_s, self.zl_s, self.xsend, self.xrecv, self.turned_s) = buffers[8:]
        (self.a_sem, self.b_sem, self.cs_sem, self.cr_sem, self.ys_sem, self.yr_sem) = sems[:6]
        (self.rs_sem, self.rr_sem, self.ls_sem, self.lr_sem, self.xs_sem, self.xr_sem, self.o_sem) = sems[6:]
        self.p, self.d, self.t = lax.axis_index(PIPE), lax.axis_index(DP), lax.axis_index(TENSOR)
        self.y, self.c = self.d // 2, lax.rem(self.d, 2)
        self.y_mate, self.core_mate = 2 * (1 - self.y) + self.c, 2 * self.y + 1 - self.c
        self.kinds = 3
        self.pieces = 2 * self.kinds * count
        self.ticks = self.pieces + count + 3
        self.rows, self.half = self.xsend.shape[1], self.xsend.shape[2]

    @staticmethod
    def scratch(count, micro, rows, model, half, groups):
        piece = (model // groups, half)
        vmem, dma = pltpu.VMEM, pltpu.SemaphoreType.DMA
        buffers = [
            vmem((micro, rows, model), BF),
            vmem((2, micro, rows, half), BF),
            vmem((3, model, half), BF),
            vmem((4, 2) + piece, BF),
            vmem((4,) + piece, BF),
            vmem((4,) + piece, BF),
            vmem((4,) + piece, BF),
            vmem((4,) + piece, BF),
            vmem((6 * count,) + piece, BF),
            vmem((6,) + piece, BF),
            vmem((6,) + piece, BF),
            vmem((3,) + piece, BF),
            vmem((model, micro * rows), BF),
        ]
        sems = [dma((1,)), dma((2,)), dma((3, 2)), dma((4, 2)), dma((4,)), dma((4,))]
        sems += [dma((6 * count,)) for _ in range(4)] + [dma((6,)), dma((3,)), dma((3, 2))]
        return buffers, sems

    def partners(self):
        return ring_neighbours(self.count) + [(PIPE, 1 - self.p), (DP, self.y_mate), (DP, self.core_mate)]

    def layer_of(self, m):
        return m // (self.kinds * self.count)

    def a_copy(self, which):
        return pltpu.make_async_copy(self.factors[which % 2].at[which // 2], self.a_s, self.a_sem.at[0])

    def b_copy(self, m, w):
        src = self.factors[2 + w].at[self.layer_of(m), :, :, aligned(lax.rem(m, self.count), self.half)]
        held = lax.rem(m, 2)
        return pltpu.make_async_copy(src, self.b_s.at[held], self.b_sem.at[held])

    def b_start(self, m):
        for w in range(self.kinds):

            @pl.when(lax.rem(m // self.count, self.kinds) == w)
            def _():
                self.b_copy(m, w).start()

    def core_copy(self, m, row):
        held, ring = lax.rem(m, 3), lax.rem(m, 4)
        src = self.dw_s.at[held, aligned(2 * row + 1 - self.c, self.rows), :]
        sems = self.cs_sem.at[held, row], self.cr_sem.at[ring, row]
        return remote(src, self.crecv.at[ring, row], *sems, DP, self.core_mate)

    def y_copy(self, m):
        held = lax.rem(m, 4)
        return remote(self.ysend.at[held], self.yrecv.at[held], self.ys_sem.at[held], self.yr_sem.at[held], DP, self.y_mate)

    def right(self, m):
        ref = self.z_s.at[m]
        return remote(ref, ref, self.rs_sem.at[m], self.rr_sem.at[m], TENSOR, self.t + 1)

    def left(self, m, last):
        dst = self.zl_s.at[m // self.count] if last else self.z_s.at[m]
        return remote(self.z_s.at[m], dst, self.ls_sem.at[m], self.lr_sem.at[m], TENSOR, self.t - 1)

    def x_copy(self, item):
        w = lax.rem(item, self.kinds)
        return remote(self.xsend.at[item], self.xrecv.at[w], self.xs_sem.at[item], self.xr_sem.at[w], PIPE, 1 - self.p)

    def when_valid(self, m, condition=None):
        valid = (m >= 0) & (m < self.pieces)
        return pl.when(valid if condition is None else valid & condition)

    def tick(self, n):
        count, t, rows = self.count, self.t, self.rows

        @self.when_valid(n - 4)
        def _():
            m = n - 4
            held = lax.rem(m, 4)
            self.y_copy(m).wait()
            add_to(self.total_s.at[held], self.near_s.at[held], self.yrecv.at[held])

        @self.when_valid(n - 2)
        def _():
            m = n - 2
            held, ring = lax.rem(m, 3), lax.rem(m, 4)
            for row in range(2):
                self.core_copy(m, row).wait()

            def own(row):
                return self.dw_s.at[held, aligned(2 * row + self.c, rows), :]

            add_to(self.ysend.at[ring], own(1 - self.y), self.crecv.at[ring, 1 - self.y])
            self.y_copy(m).start()
            add_to(self.near_s.at[ring], own(self.y), self.crecv.at[ring, self.y])

        def pass_on(m, first, arrival, send):
            total = self.total_s.at[lax.rem(m, 4)]

            @pl.when(first)
            def _():
                self.z_s[m] = total[...]

            @pl.when(jnp.logical_not(first))
            def _():
                arrival.wait_recv()
                add_to(self.z_s.at[m], self.z_s.at[m], total)

            send()

        to_right, to_left = n - 4 - t, n - 3 - count + t

        @self.when_valid(to_right, t < lax.rem(to_right + count, count))
        def _():
            pass_on(to_right, t == 0, self.right(to_right), lambda: self.right(to_right).start())

        @self.when_valid(to_left, t > lax.rem(to_left + count, count))
        def _():
            owner = lax.rem(to_left, count)

            def send():
                @pl.when(owner == t - 1)
                def _():
                    self.left(to_left, True).start()

                @pl.when(owner != t - 1)
                def _():
                    self.left(to_left, False).start()

            pass_on(to_left, t == count - 1, self.left(to_left, False), send)

        done = n - 3 - count

        @self.when_valid(done, t == lax.rem(done + count, count))
        def _():
            w = done // count
            mine = self.xsend.at[w]
            mine[...] = self.total_s[lax.rem(done, 4)]

            @pl.when(t > 0)
            def _():
                self.right(done).wait_recv()
                add_to(mine, mine, self.z_s.at[done])

            @pl.when(t < count - 1)
            def _():
                self.left(done, True).wait_recv()
                add_to(mine, mine, self.zl_s.at[w])

            @pl.when(self.p != self.layer_of(done))
            def _():
                self.x_copy(w).start()

        @self.when_valid(n)
        def _():
            @pl.when(n == 0)
            def _():
                self.a_copy(0).start()
                self.b_start(n)

            starts = [layer * self.kinds * count + 2 * count * which for layer in range(2) for which in range(2)]
            for which, start in enumerate(starts):

                @pl.when(n == start)
                def _():
                    self.a_copy(which).wait()
                    micro, long, model = self.a_s.shape
                    for row in range(model // rows):
                        at = slice(rows * row, rows * (row + 1))
                        self.turned_s[at, :] = self.a_s[:, :, at].reshape(micro * long, rows).T
                    if which + 1 < len(starts):
                        self.a_copy(which + 1).start()

            @pl.when(n + 1 < self.pieces)
            def _():
                self.b_start(n + 1)

            self.b_copy(n, 0).wait()
            b = self.b_s[lax.rem(n, 2)]
            b = b.reshape(b.shape[0] * b.shape[1], self.half)
            held = lax.rem(n, 3)
            for row in range(self.dw_s.shape[1] // rows):
                at = slice(rows * row, rows * (row + 1))
                self.dw_s[held, at, :] = nn(self.turned_s[at, :], b).astype(BF)
            for row in range(2):
                self.core_copy(n, row).start()

    def result_copy(self, w, other):
        src = self.xrecv.at[w] if other else self.xsend.at[self.kinds * self.p + w]
        dst = self.results.at[w, :, aligned(1 - self.p if other else self.p, self.half)]
        return pltpu.make_async_copy(src, dst, self.o_sem.at[w, int(other)])

    def close(self):
        count, t = self.count, self.t
        for w in range(self.kinds):
            self.result_copy(w, False).start()
            self.x_copy(w).wait_recv()
            self.result_copy(w, True).start()
        for m in range(self.pieces):

            @pl.when(t < m % count)
            def _():
                self.right(m).wait_send()

            @pl.when(t > m % count)
            def _():
                self.left(m, False).wait_send()

        for w in range(self.kinds):
            self.x_copy(self.kinds * (1 - self.p) + w).wait_send()
            for other in (False, True):
                self.result_copy(w, other).wait()


def add_to(dst, one, other, chunk=64):
    def step(i, carry):
        at = aligned(i, chunk)
        dst[at, :] = (one[at, :].astype(F32) + other[at, :].astype(F32)).astype(BF)
        return carry

    lax.fori_loop(0, dst.shape[0] // chunk, step, 0)


class Sums:
    def __init__(self, count, rows, half, pack, outs, buffers):
        self.count, self.rows, self.half, self.pack, self.outs = count, rows, half, pack, outs
        (self.total_s, self.part_s, self.far_s, self.ss, self.rs) = buffers
        self.p, self.d, self.t = lax.axis_index(PIPE), lax.axis_index(DP), lax.axis_index(TENSOR)
        y, c = self.d // 2, lax.rem(self.d, 2)
        self.steps, bit = [(DP, 2 * y + 1 - c), (DP, 2 * (1 - y) + c)], 1
        while bit < count:
            self.steps.append((TENSOR, self.t + bit * (1 - 2 * lax.rem(self.t // bit, 2))))
            bit *= 2

    @staticmethod
    def scratch(count, shape):
        steps = 2 + (count - 1).bit_length()
        vmem, dma = pltpu.VMEM, pltpu.SemaphoreType.DMA
        return [vmem((steps + 1,) + shape, F32), vmem((steps,) + shape, F32), vmem(shape[1:], F32), dma((steps + 1,)), dma((steps + 1,))]

    def partners(self):
        return [step for step in self.steps if step[0] == TENSOR]

    def copy(self, k):
        axis, index = self.steps[k]
        return remote(self.total_s.at[k], self.part_s.at[k], self.ss.at[k], self.rs.at[k], axis, index)

    def pipe_copy(self):
        k = len(self.steps)
        return remote(self.total_s.at[k, 1 - self.p], self.far_s, self.ss.at[k], self.rs.at[k], PIPE, 1 - self.p)

    def begin(self):
        self.total_s[0] = self.pack[...]
        self.copy(0).start()

    def step(self, k):
        self.copy(k).wait_recv()
        self.total_s[k + 1] = self.total_s[k] + self.part_s[k]
        if k + 1 < len(self.steps):
            self.copy(k + 1).start()
        else:
            self.pipe_copy().start()

    def close(self):
        chan_o, step_o, rest_o = self.outs
        k = len(self.steps)
        self.pipe_copy().wait_recv()
        mine, far, t = self.total_s.at[k, self.p], self.far_s, self.t
        for ref, where in ((mine, self.p), (far, 1 - self.p)):
            chan_o[:, aligned(where, self.half)] = ref[0:8, aligned(t, self.half)]
            step_o[aligned(where, 8), :] = ref[pl.ds(pl.multiple_of(8 + 8 * t, 8), 8), aligned(self.d, self.rows)]
        last = far.shape[0] - 8
        row = iota((8, far.shape[1]), 0)
        rest_o[...] = mine[last:, :] + jnp.where(row == 0, 0.0, far[last:, :])
        for k in range(len(self.steps)):
            self.copy(k).wait_send()
        self.pipe_copy().wait_send()


def reduce_grads(count, *refs):
    factors, pack, results, sums_o = refs[:5], refs[5], refs[6], refs[7:10]
    reducer = Reducer(count, factors, results, refs[10:23], refs[23:36])
    sums = Sums(count, reducer.rows, reducer.half, pack, sums_o, refs[36:])
    greet(reducer.partners() + sums.partners())
    sums.begin()

    def step(n, carry):
        reducer.tick(n)
        for k in range(len(sums.steps)):

            @pl.when(n == 2 * k + 2)
            def _():
                sums.step(k)

        return carry

    lax.fori_loop(0, reducer.ticks, step, 0)
    sums.close()
    reducer.close()


def reduce_call(factors, pack, count, groups):
    _, micro, rows, model = factors[0].shape
    width = factors[2].shape[3]
    half = width // count
    buffers, sems = Reducer.scratch(count, micro, rows, model, half, groups)
    inside = pl.BlockSpec(memory_space=pltpu.VMEM)
    anywhere = pl.BlockSpec(memory_space=pl.ANY)
    return pl.pallas_call(
        functools.partial(reduce_grads, count),
        in_specs=[anywhere] * 5 + [inside],
        out_specs=[anywhere] + [inside] * 3,
        out_shape=[
            jax.ShapeDtypeStruct((3, model // groups, 2 * half), BF),
            jax.ShapeDtypeStruct((8, 2 * half), F32),
            jax.ShapeDtypeStruct((16, model // groups), F32),
            jax.ShapeDtypeStruct((8, width), F32),
        ],
        scratch_shapes=buffers + sems + Sums.scratch(count, pack.shape),
        compiler_params=pltpu.CompilerParams(collective_id=1, has_side_effects=True, vmem_limit_bytes=VMEM_LIMIT),
    )(*factors, pack)


def fused_forward(count, head_dim, micro, *refs):
    (tokens, mask, value, gate_w, out_w, step_w, state_w, chan, shared) = refs[:9]
    (wv_h, wg_h, wo_h, wt_h, ws_h, pv_o, ps_o, ph_o, pn_o) = refs[9:18]
    (out_h, low_h, mix_h, inv_o, nx_o, vpre_o, spre_o, x_o, bc_o, dtc_o, gate_o, y_o, gg_o, sin_o) = refs[18:32]
    (nx_s, sc_s, dt_s, cum_s, cumt_s, acc_s, sq_s, psend, precv, sqsend, sqrecv, csend, crecv, hrecv, trecv) = refs[32:47]
    (ps_sem, pr_sem, ss_sem, sr_sem, cs_sem, cr_sem, hs_sem, hr_sem, ts_sem, tr_sem, low_sem, out_sem, mix_sem) = refs[47:60]
    (wv_s, wg_s, wo_s, ws_s, wt_s, chan_s, shared_s, w_sem, l_sem) = refs[60:69]
    q, s, g = pl.program_id(0), pl.program_id(1), pl.program_id(2)
    groups = dt_s.shape[0]
    p, t = lax.axis_index(PIPE), lax.axis_index(TENSOR)
    idx = q * micro + s
    slot = idx * groups + g
    total_idx = 2 * micro
    rows, model = tokens.shape[1], tokens.shape[2]
    state = bc_o.shape[1] // 2
    per_group = GC // head_dim
    inner_total = 2 * groups * GC
    gather = Gather(
        count,
        (value, gate_w, out_w, step_w),
        (wv_h, wg_h, wo_h, wt_h),
        ((state_w, ws_h), (chan, chan_s), (shared, shared_s)),
        refs[69:],
    )
    big = ((wv_h, wv_s), (wg_h, wg_s), (wo_h, wo_s))

    def weight_copy(step, k):
        layer, group = step // (micro * groups), lax.rem(step, groups)
        held = lax.rem(step, 2)
        return pltpu.make_async_copy(big[k][0].at[layer, :, aligned(group, GC)], big[k][1].at[held], w_sem.at[held, k])

    def layer_copies(layer):
        return (
            pltpu.make_async_copy(ws_h.at[layer], ws_s, l_sem.at[0]),
            pltpu.make_async_copy(wt_h.at[layer], wt_s, l_sem.at[1]),
        )

    def part_copy(i):
        return remote(psend.at[i], precv.at[i], ps_sem.at[i], pr_sem.at[i], PIPE, 1 - p)

    def square_copy(i):
        return remote(sqsend.at[i], sqrecv.at[i], ss_sem.at[i], sr_sem.at[i], PIPE, 1 - p)

    def chain_copy(i):
        return remote(csend.at[i], crecv.at[i], cs_sem.at[i], cr_sem.at[i], TENSOR, t + 1)

    def halo_copy(i):
        return remote(psend.at[i, rows - HALO :, :], hrecv.at[i], hs_sem.at[i], hr_sem.at[i], TENSOR, t + 1)

    def tokens_copy():
        return remote(tokens.at[:, rows - HALO :, :], trecv, ts_sem.at[0], tr_sem.at[0], TENSOR, t + 1)

    def low_copy(i):
        return pltpu.make_async_copy(psend.at[i], low_h.at[i], low_sem.at[i])

    def out_copy(i):
        return pltpu.make_async_copy(psend.at[i], out_h.at[lax.rem(i, micro)], out_sem.at[i])

    def mix_copy(i):
        return pltpu.make_async_copy(precv.at[i], mix_h.at[i], mix_sem.at[i])

    @pl.when((idx == 0) & (g == 0))
    def _():
        greet(gather.partners())

        @pl.when(t < count - 1)
        def _():
            tokens_copy().start()

        gather.first_layer()
        for k in range(3):
            weight_copy(0, k).start()
        pv_o[...] = chan_s[...]
        heads = per_group * groups // count
        half = groups * GC // count
        place, lane = iota((groups * GC, LANES), 0), iota((groups * GC, LANES), 1)
        first = half * (lane // heads) + lax.rem(lane, heads)
        used = lane < per_group * groups
        for layer in range(2):
            per_head = chan_s[layer]
            for kind in range(2):
                pick = ((place == first + kind * heads) & used).astype(F32)
                ph_o[layer, kind : kind + 1, :] = exact(per_head, pick)[7:8, :]
            ph_o[layer, 2:, :] = jnp.zeros((6, LANES), F32)
            pn_o[layer] = shared_s[layer]
            for k in range(5):
                ps_o[layer, k : k + 1, :] = shared_s[layer, 1:2, 2 * state * k : 2 * state * (k + 1)]
            ps_o[layer, 5:, :] = jnp.zeros((3, 2 * state), F32)

    columns = groups * GC // count
    late = gather.second_layer(micro * groups, lambda src: src * columns // GC)
    for step in sorted({step for step, _ in late}):

        @pl.when(slot == step)
        def _():
            for when, stage in late:
                if when == step:
                    stage()

    @pl.when((s == 0) & (g == 0))
    def _():
        for copy in layer_copies(q):
            copy.start()
        for copy in layer_copies(q):
            copy.wait()

    for k in range(3):
        weight_copy(slot, k).wait()

    @pl.when(slot + 1 < total_idx * groups)
    def _():
        for k in range(3):
            weight_copy(slot + 1, k).start()

    held = lax.rem(slot, 2)
    ws, wt, wv, wg, wo = ws_s, wt_s, wv_s.at[held], wg_s.at[held], wo_s.at[held]
    pv, ps, ph, pn = pv_o.at[q, :, aligned(g, GC)], ps_o.at[q], ph_o.at[q], pn_o.at[q]

    def normed(u):
        uf = u.astype(F32)
        return (uf * lax.rsqrt(jnp.mean(uf * uf, axis=1, keepdims=True) + EPS) * pn[0:1, :]).astype(BF)

    @pl.when((g == 0) & (q == 0))
    def _():
        nx_s[HALO:, :] = normed(tokens[s])

        @pl.when(t == 0)
        def _():
            nx_s[:HALO, :] = jnp.zeros((HALO, model), BF)

        @pl.when(t > 0)
        def _():
            @pl.when(s == 0)
            def _():
                tokens_copy().wait_recv()

            nx_s[:HALO, :] = normed(trecv[s])

    @pl.when((g == 0) & (q == 1))
    def _():
        nx_s[HALO:, :] = normed(psend[s])

        @pl.when(t == 0)
        def _():
            nx_s[:HALO, :] = jnp.zeros((HALO, model), BF)

        @pl.when(t > 0)
        def _():
            halo_copy(s).wait_recv()
            nx_s[:HALO, :] = normed(hrecv[s])

    @pl.when(g == 0)
    def _():
        nx_o[...] = nx_s[HALO:, :]
        spre = nn(nx_s[...], ws[...])
        spre_o[...] = spre
        conv = conv_rows(spre, ps, rows)
        bc = (conv * sigmoid(conv)).astype(BF)
        bc_o[...] = bc
        scores = nt(bc[:, state:], bc[:, :state])
        lower = iota((rows, rows), 0) >= iota((rows, rows), 1)
        sc_s[...] = jnp.where(lower, scores, 0.0)
        raw = nt(nx_s[HALO:, :], wt[...])
        raw = exact(raw, step_places(count, raw.shape[1], per_group * groups)) + ph[0:1, :]
        step = jnp.maximum(raw, 0.0) + jnp.log(1.0 + jnp.exp(-jnp.abs(raw)))
        cum = exact(lower.astype(F32), -step * jnp.exp(ph[1:2, :]))
        dtc_o[0] = step
        dtc_o[1] = cum
        dtc_o[2] = sigmoid(raw)
        group_lanes(step, dt_s, groups, per_group)
        group_lanes(cum, cum_s, groups, per_group)
        group_rows(cum, cumt_s, groups, per_group)
        acc_s[...] = jnp.zeros_like(acc_s)
        sq_s[...] = jnp.zeros_like(sq_s)

    pre = nn(nx_s[...], wv[...])
    vpre_o[...] = pre
    conv = conv_rows(pre, pv, rows)
    x = conv * sigmoid(conv)
    x_o[...] = x.astype(BF)
    step, cum, cumt = dt_s[g], cum_s[g], cumt_s[g]
    to_end = jnp.exp(cum[rows - 1 : rows, :] - cum)
    xp = (x * spread(step, GC, head_dim)).astype(BF)
    xr = (x * spread(step * to_end, GC, head_dim)).astype(BF)
    local = tn(xr, bc_o[:, :state])

    @pl.when(t == 0)
    def _():
        sin_o[...] = jnp.zeros_like(sin_o)

    @pl.when(t > 0)
    def _():
        chain_copy(slot).wait_recv()
        sin_o[...] = crecv[slot]

    @pl.when(t < count - 1)
    def _():
        csend[slot] = (through_rows(cumt, rows, head_dim, state) * sin_o[...].astype(F32) + local).astype(BF)
        chain_copy(slot).start()

    scores = sc_s[...]
    lane = iota((rows, LANES), 1)
    within = []
    for pair in range(GC // LANES):
        cols = slice(LANES * pair, LANES * (pair + 1))
        outs = []
        for i in (2 * pair, 2 * pair + 1):
            diff = cum[:, i : i + 1] - cumt[i : i + 1, :]
            mix = (jnp.exp(jnp.minimum(diff, 0.0)) * scores).astype(BF)
            outs.append(nn(mix, xp[:, cols]))
        within.append(jnp.where(lane < head_dim, outs[0], outs[1]))
    gate = nn(nx_s[HALO:, :], wg[...])
    gate_o[...] = gate
    carried = nt(bc_o[:, state:], sin_o[...])
    y = jnp.concatenate(within, axis=1) + pv[6:7, :] * x + spread(jnp.exp(cum), GC, head_dim) * carried
    y_o[...] = y
    gated = y * (gate * sigmoid(gate))
    gg = (gated * pv[5:6, :]).astype(BF)
    gg_o[...] = gg
    squares = gated * gated
    for part in range(GC // LANES):
        sq_s[...] += squares[:, LANES * part : LANES * (part + 1)]
    acc_s[...] += nt(gg, wo[...])

    @pl.when(g == groups - 1)
    def _():
        psend[idx] = acc_s[...].astype(BF)
        sqsend[idx] = jnp.broadcast_to(jnp.sum(sq_s[...], axis=1, keepdims=True), (rows, LANES))
        part_copy(idx).start()
        square_copy(idx).start()

    def finish(i):
        j = lax.rem(i, micro)
        part_copy(i).wait()
        square_copy(i).wait()
        inverse = lax.rsqrt((sqsend[i] + sqrecv[i]) / inner_total + EPS)
        inv_o[i] = inverse
        mixed = inverse[:, 0:1] * (psend[i].astype(F32) + precv[i].astype(F32))
        precv[i] = mixed.astype(BF)
        row_mask = mask[j][:, 0:1]

        @pl.when(i < micro)
        def _():
            psend[i] = (row_mask * (tokens[j].astype(F32) + mixed)).astype(BF)

            @pl.when(t < count - 1)
            def _():
                halo_copy(j).start()

            low_copy(j).start()

        @pl.when(i >= micro)
        def _():
            psend[i] = (row_mask * (psend[j].astype(F32) + mixed)).astype(BF)

        @pl.when(i // micro == p)
        def _():
            out_copy(i).start()

        mix_copy(i).start()

    @pl.when((g == 1) & (idx > 1))
    def _():
        finish(idx - 2)

    @pl.when((g == groups - 1) & (idx == total_idx - 1))
    def _():
        finish(idx - 1)
        finish(idx)
        for i in range(total_idx):
            mix_copy(i).wait()

            @pl.when(i // micro == p)
            def _():
                out_copy(i).wait()

        for i in range(micro):
            low_copy(i).wait()

        gather.finish()

        @pl.when(t < count - 1)
        def _():
            tokens_copy().wait_send()
            for i in range(micro):
                halo_copy(i).wait_send()

            def drain(i, carry):
                chain_copy(i).wait_send()
                return carry

            lax.fori_loop(0, total_idx * groups, drain, 0)


def step_places(count, rows, all_heads):
    heads, size = all_heads // count, rows // count
    place, lane = iota((rows, LANES), 0), iota((rows, LANES), 1)
    return ((place == size * (lane // heads) + lax.rem(lane, heads)) & (lane < all_heads)).astype(F32)


def through_rows(cumt, rows, head_dim, state):
    end = jnp.exp(cumt[:, rows - 1 : rows])
    parts = [jnp.broadcast_to(end[i : i + 1, :], (head_dim, state)) for i in range(GC // head_dim)]
    return jnp.concatenate(parts, axis=0)


def fused_backward(count, head_dim, micro, *refs):
    (cot, tokens, out0, mask, inv, mix, vpre, spre, x, bc, dtc, gate, y, s_in) = refs[:14]
    (wv, wg, wo, ws, wt, pv, ps, ph, pn) = refs[14:23]
    (grad_h, dval_o, dgate_o, dst_o, dstep_o, sgm_o, vs_o, ss_o, hs_o, norm_o) = refs[23:33]
    (gm_s, rowsc_s, gin_s, halo_s, halo2_s, acc_s, nacc_s) = refs[33:40]
    (sct_s, scts_s, wsum_s, dbc_s, dt_s, cum_s, cumt_s, net_s, rv_s, ddir_s, k_s, rt_s, rall_s) = refs[40:53]
    (psend, precv, csend, crecv, hsend, hrecv, tsend, trecv) = refs[53:61]
    (ps_sem, pr_sem, cs_sem, cr_sem, hs_sem, hr_sem, ts_sem, tr_sem, out_sem) = refs[61:]
    turn, s, g = pl.program_id(0), pl.program_id(1), pl.program_id(2)
    groups = dt_s.shape[0]
    p, t = lax.axis_index(PIPE), lax.axis_index(TENSOR)
    idx = turn * micro + s
    slot = idx * groups + g
    total_idx = 2 * micro
    rows, model = cot.shape[1], cot.shape[2]
    state = bc.shape[1] // 2
    per_group = GC // head_dim
    inner_total = 2 * groups * GC

    def part_copy(i):
        return remote(psend.at[i], precv.at[i], ps_sem.at[i], pr_sem.at[i], PIPE, 1 - p)

    def chain_copy(i):
        return remote(csend.at[i], crecv.at[i], cs_sem.at[i], cr_sem.at[i], TENSOR, t - 1)

    def halo_copy(i):
        return remote(hsend.at[i], hrecv.at[i], hs_sem.at[i], hr_sem.at[i], TENSOR, t - 1)

    def tail_copy(i):
        return remote(tsend.at[i], trecv.at[i], ts_sem.at[i], tr_sem.at[i], TENSOR, t - 1)

    def out_copy(i):
        return pltpu.make_async_copy(psend.at[i], grad_h.at[lax.rem(i, micro)], out_sem.at[i])

    @pl.when((idx == 0) & (g == 0))
    def _():
        greet(ring_neighbours(count) + [(PIPE, 1 - p)])
        nacc_s[...] = jnp.zeros_like(nacc_s)

    @pl.when((g == 0) & (turn == 0))
    def _():
        gm_s[...] = (mask[s][:, 0:1] * cot[s].astype(F32)).astype(BF)

    @pl.when((g == 0) & (turn == 1))
    def _():
        gm_s[...] = (mask[s][:, 0:1] * psend[s].astype(F32)).astype(BF)

    @pl.when(g == 0)
    def _():
        gmf = gm_s[...].astype(F32)
        inverse = inv[...]
        dot = jnp.sum(gmf * mix[...].astype(F32), axis=1, keepdims=True)
        rowsc_s[...] = inverse * inverse * dot / inner_total
        sgm_o[...] = (gmf * inverse[:, 0:1]).astype(BF)
        scores = nt(bc[:, :state], bc[:, state:])
        first, second = iota((rows, rows), 0), iota((rows, rows), 1)
        sct_s[...] = jnp.where(second >= first, scores, 0.0)
        scts_s[...] = jnp.where(second > first, scores, 0.0)
        wsum_s[...] = jnp.zeros_like(wsum_s)
        dbc_s[...] = jnp.zeros_like(dbc_s)
        rall_s[...] = jnp.zeros_like(rall_s)
        acc_s[...] = jnp.zeros_like(acc_s)
        group_lanes(dtc[0], dt_s, groups, per_group)
        group_lanes(dtc[1], cum_s, groups, per_group)
        group_rows(dtc[1], cumt_s, groups, per_group)

    step, cum, cumt = dt_s[g], cum_s[g], cumt_s[g]
    last = cum[rows - 1 : rows, :]
    fromx = spread(jnp.exp(cum), GC, head_dim)

    gs = nn(gm_s[...], wo[...])
    inverse, shrink = inv[:, 0:1], rowsc_s[:, 0:1]
    gv, yv = gate[...], y[...]
    sig = sigmoid(gv)
    silu = gv * sig
    gated = yv * silu
    dgain = jnp.sum(gs * gated * inverse, axis=0, keepdims=True)
    dgated = inverse * (gs * pv[5:6, :]) - gated * shrink
    dgate = (dgated * yv * (sig * (1.0 + gv * (1.0 - sig)))).astype(BF)
    dgate_o[...] = dgate
    dyb = (dgated * silu).astype(BF)
    dyf = dyb.astype(F32)
    dyef = dyf * fromx
    dye = dyef.astype(BF)
    dsl = tn(dye, bc[:, state:])

    @pl.when(t == count - 1)
    def _():
        gin_s[...] = jnp.zeros_like(gin_s)

    @pl.when(t < count - 1)
    def _():
        chain_copy(slot).wait_recv()
        gin_s[...] = crecv[slot]

    @pl.when(t > 0)
    def _():
        csend[slot] = (through_rows(cumt, rows, head_dim, state) * gin_s[...].astype(F32) + dsl).astype(BF)
        chain_copy(slot).start()

    to_end = jnp.exp(last - cum)
    stepx = spread(step, GC, head_dim)
    endx = spread(to_end, GC, head_dim)
    xf = x[...].astype(F32)
    xp = (xf * stepx).astype(BF)
    xr = (xf * stepx * endx).astype(BF)
    gb = nt(bc[:, :state], gin_s[...])
    cs = nt(bc[:, state:], s_in[...])
    dbc_s[:, :state] += nn(xr, gin_s[...])
    dbc_s[:, state:] += nn(dye, s_in[...])

    lane = iota((rows, LANES), 1)
    wsum = wsum_s[...]
    colsum = jnp.zeros((rows, LANES), F32)
    within = []
    for pair in range(GC // LANES):
        cols = slice(LANES * pair, LANES * (pair + 1))
        xpp, dyp = xp[:, cols], dyb[:, cols]
        outs = []
        for side in range(2):
            i = 2 * pair + side
            mine = (lane < head_dim) if side == 0 else (lane >= head_dim)
            decay = jnp.exp(jnp.minimum(cumt[i : i + 1, :] - cum[:, i : i + 1], 0.0))
            outs.append(nn((decay * sct_s[...]).astype(BF), dyp))
            weight = decay * nt(jnp.where(mine, xpp, jnp.zeros_like(xpp)), dyp)
            wsum = wsum + weight
            pairs = (weight * scts_s[...]).astype(BF)
            colsum = colsum + nn(pairs, (lane == i).astype(BF))
            rt_s[g, i : i + 1, :] = jnp.sum(pairs.astype(F32), axis=0, keepdims=True)
        within.append(jnp.where(lane < head_dim, outs[0], outs[1]))
    wsum_s[...] = wsum
    u = jnp.concatenate(within, axis=1) + endx * gb

    heads = (iota((GC, LANES), 0) // head_dim == iota((GC, LANES), 1)).astype(BF)
    ddir_s[g] = nn((xf * u).astype(BF), heads)
    net_s[g] = nn((dyef * cs).astype(BF), heads) - colsum
    rv_s[g] = step * to_end * nn((xf * gb).astype(BF), heads)
    inner = gin_s[...].astype(F32) * s_in[...].astype(F32)
    per_channel = lax.dot_general(
        jnp.ones((8, inner.shape[1]), F32), inner, (((1,), (1,)), ((), ())), precision=HIGHEST, preferred_element_type=F32
    )
    k_s[g] = jnp.exp(last) * exact(per_channel, heads.astype(F32))

    dx = stepx * u + pv[6:7, :] * dyf
    dconv = dx * silu_slope(conv_rows(vpre, pv, rows))

    @pl.when(t > 0)
    def _():
        hsend[slot] = dconv[:8, :]
        halo_copy(slot).start()

    sums = conv_sums(dconv, vpre, rows)
    sums.append(dgain)
    sums.append(jnp.sum(dyf * xf, axis=0, keepdims=True))
    sums.append(jnp.zeros((1, GC), F32))
    vs_o[...] = jnp.concatenate(sums, axis=0)
    acc_s[...] += nt(dgate, wg[...])

    @pl.when(t == count - 1)
    def _():
        halo_s[...] = jnp.zeros_like(halo_s)

    @pl.when(t < count - 1)
    def _():
        halo_copy(slot).wait_recv()
        halo_s[...] = hrecv[slot]

    dval = conv_transposed(dconv, halo_s[...], pv, rows).astype(BF)
    dval_o[...] = dval
    acc_s[...] += nt(dval, wv[...])

    @pl.when(g == groups - 1)
    def _():
        first, second = iota((rows, rows), 0), iota((rows, rows), 1)
        weights = jnp.where(second >= first, wsum_s[...], 0.0).astype(BF)
        db = dbc_s[:, :state] + nn(weights, bc[:, state:])
        dc = dbc_s[:, state:] + tn(weights, bc[:, :state])
        dsc = jnp.concatenate([db, dc], axis=1) * silu_slope(conv_rows(spre, ps, rows))

        @pl.when(t > 0)
        def _():
            tsend[idx] = dsc[:8, :]
            tail_copy(idx).start()

        ssums = conv_sums(dsc, spre, rows)
        ssums.append(jnp.zeros((3, 2 * state), F32))
        ss_o[...] = jnp.concatenate(ssums, axis=0)
        net, rv, ddir, const = net_s[0], rv_s[0], ddir_s[0], k_s[0]
        rall_s[0:per_group, :] = rt_s[0, 0:per_group, :]
        for other in range(1, groups):
            shift = per_group * other
            net = net + pltpu.roll(net_s[other], shift, 1)
            rv = rv + pltpu.roll(rv_s[other], shift, 1)
            ddir = ddir + pltpu.roll(ddir_s[other], shift, 1)
            const = const + pltpu.roll(k_s[other], shift, 1)
            rall_s[shift : shift + per_group, :] = rt_s[other, 0:per_group, :]
        net = net + rall_s[...].T
        da = exact((second >= first).astype(F32), net) + exact((second < first).astype(F32), rv) + const[0:1, :]
        rate = jnp.exp(ph[1:2, :])
        dstep = (ddir - da * rate) * dtc[2]
        dstep_o[...] = dstep.astype(BF)
        hs_o[...] = jnp.concatenate(
            [
                jnp.sum(dstep, axis=0, keepdims=True),
                jnp.sum(-da * dtc[0] * rate, axis=0, keepdims=True),
                jnp.zeros((6, LANES), F32),
            ],
            axis=0,
        )

        @pl.when(t == count - 1)
        def _():
            halo2_s[...] = jnp.zeros_like(halo2_s)

        @pl.when(t < count - 1)
        def _():
            tail_copy(idx).wait_recv()
            halo2_s[...] = trecv[idx]

        dst = conv_transposed(dsc, halo2_s[...], ps, rows).astype(BF)
        dst_o[...] = dst
        psend[idx] = (acc_s[...] + nt(dst, ws[...]) + nn(dstep_o[...], wt[...])).astype(BF)
        part_copy(idx).start()

    def finish(i):
        j = lax.rem(i, micro)
        part_copy(i).wait()
        which = 1 - i // micro
        row_mask = mask[j][:, 0:1]

        def close(u, incoming):
            uf = u.astype(F32)
            grad_normed = psend[i].astype(F32) + precv[i].astype(F32)
            root_inv = lax.rsqrt(jnp.mean(uf * uf, axis=1, keepdims=True) + EPS)
            nacc_s[which] += jnp.broadcast_to(jnp.sum(grad_normed * uf * root_inv, axis=0, keepdims=True), (8, model))
            weighted = grad_normed * pn[which][0:1, :]
            shared = jnp.mean(weighted * uf, axis=1, keepdims=True) * root_inv * root_inv * root_inv
            kept = (row_mask * incoming.astype(F32)).astype(BF).astype(F32)
            psend[i] = (root_inv * weighted - uf * shared + kept).astype(BF)

        @pl.when(i < micro)
        def _():
            close(out0[j], cot[j])

        @pl.when(i >= micro)
        def _():
            close(tokens[j], psend[j])

        @pl.when(which == p)
        def _():
            out_copy(i).start()

    @pl.when((g == 1) & (idx > 1))
    def _():
        finish(idx - 2)

    @pl.when((g == groups - 1) & (idx == total_idx - 1))
    def _():
        finish(idx - 1)
        finish(idx)
        norm_o[...] = nacc_s[...]
        for i in range(total_idx):

            @pl.when(1 - i // micro == p)
            def _():
                out_copy(i).wait()

        @pl.when(t > 0)
        def _():
            for i in range(total_idx):
                tail_copy(i).wait_send()

            def drain(i, carry):
                chain_copy(i).wait_send()
                halo_copy(i).wait_send()
                return carry

            lax.fori_loop(0, total_idx * groups, drain, 0)


def all_of(shape, buffers=2):
    spec = functools.partial(pl.BlockSpec, shape, lambda q, s, g: (0,) * len(shape))
    return spec(pipeline_mode=pl.Buffered(buffers)) if buffers != 2 else spec()


def fused_specs(turned):
    def layer(q):
        return 1 - q if turned else q

    def item(*shape):
        zeros = (0,) * len(shape)
        return pl.BlockSpec((None, None) + shape, lambda q, s, g: (layer(q), s) + zeros)

    def item_cols(rows):
        return pl.BlockSpec((None, None, rows, GC), lambda q, s, g: (layer(q), s, 0, g))

    def item_rows(cols):
        return pl.BlockSpec((None, None, GC, cols), lambda q, s, g: (layer(q), s, g, 0))

    def layer_cols(rows):
        return pl.BlockSpec((None, rows, GC), lambda q, s, g: (layer(q), 0, g))

    def layer_all(*shape):
        zeros = (0,) * len(shape)
        return pl.BlockSpec((None,) + shape, lambda q, s, g: (layer(q),) + zeros)

    return item, item_cols, item_rows, layer_cols, layer_all


def forward_call(tokens, mask, shards, chan, shared, count, groups_dp, head_dim):
    micro, rows, model = tokens.shape
    value, gate, out, step, state_w = shards
    half, states = value.shape[1] // 2, state_w.shape[1]
    width, state = half * count, states // 2
    groups = width // GC
    item, item_cols, item_rows, layer_cols, layer_all = fused_specs(False)
    slots = 2 * micro
    dma = pltpu.SemaphoreType.DMA
    vmem = pltpu.VMEM
    anywhere = pl.BlockSpec(memory_space=pl.ANY)
    ins = [
        (tokens, all_of(tokens.shape, 1)),
        (mask, all_of(mask.shape, 1)),
        (value, anywhere),
        (gate, anywhere),
        (out, anywhere),
        (step, anywhere),
        (state_w, anywhere),
        (chan, anywhere),
        (shared, anywhere),
    ]
    pair = (2, micro)
    step_rows = step.shape[0] // 2 * count
    outs = [
        (((2, model, width), BF), anywhere),
        (((2, model, width), BF), anywhere),
        (((2, model, width), BF), anywhere),
        (((2, step_rows, model), BF), anywhere),
        (((2, model, states), BF), anywhere),
        (((2, 8, width), F32), all_of((2, 8, width))),
        (((2, 8, states), F32), all_of((2, 8, states))),
        (((2, 8, LANES), F32), all_of((2, 8, LANES))),
        (((2,) + shared.shape, F32), all_of((2,) + shared.shape)),
        (((micro, rows, model), BF), anywhere),
        (((micro, rows, model), BF), anywhere),
        (((slots, rows, model), BF), anywhere),
        (((slots, rows, LANES), F32), all_of((slots, rows, LANES))),
        ((pair + (rows, model), BF), item(rows, model)),
        ((pair + (rows + HALO, width), F32), item_cols(rows + HALO)),
        ((pair + (rows + HALO, states), F32), item(rows + HALO, states)),
        ((pair + (rows, width), BF), item_cols(rows)),
        ((pair + (rows, states), BF), item(rows, states)),
        ((pair + (3, rows, LANES), F32), item(3, rows, LANES)),
        ((pair + (rows, width), F32), item_cols(rows)),
        ((pair + (rows, width), F32), item_cols(rows)),
        ((pair + (rows, width), BF), item_cols(rows)),
        ((pair + (width, state), BF), item_rows(state)),
    ]
    lanes = vmem((groups, rows, LANES), F32)
    scratch = [
        vmem((rows + HALO, model), BF),
        vmem((rows, rows), F32),
        lanes,
        lanes,
        vmem((groups, 8, rows), F32),
        vmem((rows, model), F32),
        vmem((rows, LANES), F32),
        vmem((slots, rows, model), BF),
        vmem((slots, rows, model), BF),
        vmem((slots, rows, LANES), F32),
        vmem((slots, rows, LANES), F32),
        vmem((slots * groups, GC, state), BF),
        vmem((slots * groups, GC, state), BF),
        vmem((micro, HALO, model), BF),
        vmem((micro, HALO, model), BF),
        dma((slots,)),
        dma((slots,)),
        dma((slots,)),
        dma((slots,)),
        dma((slots * groups,)),
        dma((slots * groups,)),
        dma((micro,)),
        dma((micro,)),
        dma((1,)),
        dma((1,)),
        dma((micro,)),
        dma((slots,)),
        dma((slots,)),
        vmem((2, model, GC), BF),
        vmem((2, model, GC), BF),
        vmem((2, model, GC), BF),
        vmem((model, states), BF),
        vmem((step_rows, model), BF),
        vmem((2, 8, width), F32),
        vmem((2,) + shared.shape, F32),
        dma((2, 3)),
        dma((2,)),
    ] + Gather.scratch(count)
    kernel = functools.partial(fused_forward, count, head_dim, micro)
    flops = slots * (6 * rows * model * width + 6 * rows * rows * width)
    options = fused_options(pair + (groups,), ins, outs, scratch, 2, flops, 60 * slots * rows * width)
    return pl.pallas_call(kernel, **options)(*[array for array, _ in ins])


def fused_options(grid, ins, outs, scratch, collective, flops, traffic):
    return dict(
        grid=grid,
        in_specs=[spec for _, spec in ins],
        out_specs=[spec for _, spec in outs],
        out_shape=[jax.ShapeDtypeStruct(*kind) for kind, _ in outs],
        scratch_shapes=scratch,
        cost_estimate=pl.CostEstimate(flops=flops, bytes_accessed=traffic, transcendentals=0),
        compiler_params=pltpu.CompilerParams(
            collective_id=collective,
            has_side_effects=True,
            vmem_limit_bytes=VMEM_LIMIT,
            dimension_semantics=(SEQUENTIAL,) * len(grid),
        ),
    )


def backward_fused_call(cot, tokens, out0, mask, kept, w, par, count, head_dim):
    micro, rows, model = tokens.shape
    width, states = w.value.shape[2], w.state.shape[2]
    state = states // 2
    groups = width // GC
    item, item_cols, item_rows, layer_cols, layer_all = fused_specs(True)
    slots = 2 * micro
    dma = pltpu.SemaphoreType.DMA
    vmem = pltpu.VMEM
    ins = [
        (cot, all_of(cot.shape, 1)),
        (tokens, all_of(tokens.shape, 1)),
        (out0, all_of(out0.shape, 1)),
        (mask, all_of(mask.shape, 1)),
        (kept.inv, item(rows, LANES)),
        (kept.mix, item(rows, model)),
        (kept.vpre, item_cols(rows + HALO)),
        (kept.spre, item(rows + HALO, states)),
        (kept.x, item_cols(rows)),
        (kept.bc, item(rows, states)),
        (kept.dtc, item(3, rows, LANES)),
        (kept.gate, item_cols(rows)),
        (kept.y, item_cols(rows)),
        (kept.s_in, item_rows(state)),
        (w.value, layer_cols(model)),
        (w.gate, layer_cols(model)),
        (w.out, layer_cols(model)),
        (w.state, layer_all(model, states)),
        (w.step, layer_all(LANES, model)),
        (par.value, layer_cols(8)),
        (par.state, layer_all(8, states)),
        (par.head, layer_all(8, LANES)),
        (par.norm, all_of(par.norm.shape, 1)),
    ]
    pair = (2, micro)
    outs = [
        (((micro, rows, model), BF), pl.BlockSpec(memory_space=pl.ANY)),
        ((pair + (rows, width), BF), item_cols(rows)),
        ((pair + (rows, width), BF), item_cols(rows)),
        ((pair + (rows, states), BF), item(rows, states)),
        ((pair + (rows, LANES), BF), item(rows, LANES)),
        ((pair + (rows, model), BF), item(rows, model)),
        ((pair + (8, width), F32), item_cols(8)),
        ((pair + (8, states), F32), item(8, states)),
        ((pair + (8, LANES), F32), item(8, LANES)),
        (((2, 8, model), F32), all_of((2, 8, model))),
    ]
    lanes = vmem((groups, rows, LANES), F32)
    square = vmem((rows, rows), F32)
    scratch = [
        vmem((rows, model), BF),
        vmem((rows, LANES), F32),
        vmem((GC, state), BF),
        vmem((8, GC), F32),
        vmem((8, states), F32),
        vmem((rows, model), F32),
        vmem((2, 8, model), F32),
        square,
        square,
        square,
        vmem((rows, states), F32),
        lanes,
        lanes,
        vmem((groups, 8, rows), F32),
        lanes,
        lanes,
        lanes,
        vmem((groups, 8, LANES), F32),
        vmem((groups, 8, rows), F32),
        vmem((LANES, rows), F32),
        vmem((slots, rows, model), BF),
        vmem((slots, rows, model), BF),
        vmem((slots * groups, GC, state), BF),
        vmem((slots * groups, GC, state), BF),
        vmem((slots * groups, 8, GC), F32),
        vmem((slots * groups, 8, GC), F32),
        vmem((slots, 8, states), F32),
        vmem((slots, 8, states), F32),
        dma((slots,)),
        dma((slots,)),
        dma((slots * groups,)),
        dma((slots * groups,)),
        dma((slots * groups,)),
        dma((slots * groups,)),
        dma((slots,)),
        dma((slots,)),
        dma((slots,)),
    ]
    kernel = functools.partial(fused_backward, count, head_dim, micro)
    flops = slots * (8 * rows * model * width + 16 * rows * rows * width)
    options = fused_options(pair + (groups,), ins, outs, scratch, 3, flops, 60 * slots * rows * width)
    return pl.pallas_call(kernel, **options)(*[array for array, _ in ins])


def fused_body(
    tokens_in,
    cotangent,
    lengths,
    in_gate,
    in_value,
    in_state,
    in_step,
    out_proj,
    norm_gain,
    conv_value,
    conv_state,
    bias_value,
    bias_state,
    step_bias,
    decay_log,
    skip_gain,
    gate_gain,
):
    layer, group, block = lax.axis_index(PIPE), lax.axis_index(DP), lax.axis_index(TENSOR)
    blocks, groups = lax.axis_size(TENSOR), lax.axis_size(DP)
    first_half = layer == 0
    micro, rows, model = tokens_in.shape
    shard_rows = in_value.shape[1]
    half = in_value.shape[2] // 2
    heads = step_bias.shape[1] // 2
    head_dim = half // heads
    width = half * blocks
    all_heads = heads * blocks
    states = in_state.shape[2]

    row = jnp.arange(2 * HALO)[:, None]
    head = jnp.arange(2 * heads)[None, :]
    step_rows = (row == head // heads * HALO + lax.rem(head, heads)).astype(BF)
    step_shard = nt(step_rows, in_step[0]).astype(BF)
    both = jnp.concatenate([step_bias.reshape(2, heads), decay_log.reshape(2, heads)], axis=1)
    per_head = jnp.pad(both, ((0, 0), (0, half - 2 * heads))).reshape(1, 2 * half)
    skip = jnp.repeat(skip_gain, head_dim, axis=1)
    channel = jnp.concatenate([conv_value[0], bias_value, gate_gain, skip, per_head], axis=0)
    state_row = jnp.concatenate([conv_state[0].reshape(1, -1), bias_state], axis=1)
    shared = jnp.concatenate([norm_gain, jnp.pad(state_row, ((0, 6), (0, model - 5 * states))), norm_gain], axis=0)

    valid = block * rows + jnp.arange(rows)[None, :] < lengths[:, None]
    mask = jnp.broadcast_to(valid.astype(F32)[:, :, None], (micro, rows, LANES))

    shards = (in_value[0], in_gate[0], out_proj[0], step_shard, in_state[0])
    (wv, wg, wo, wt, ws, pv, ps, ph, pn, out, low_out, mix, inv, nx, vpre, spre, x, bc, dtc, gate, y, gg, s_in) = forward_call(
        tokens_in, mask, shards, channel, shared, blocks, groups, head_dim
    )
    places = step_places(blocks, wt.shape[1], all_heads).astype(BF)
    step_w = jnp.stack([tn(places, wt[q]).astype(BF) for q in range(2)])
    w = Bundle(value=wv, gate=wg, out=wo, state=ws, step=step_w)
    par = Bundle(value=pv, head=ph, state=ps, norm=pn)
    kept = Bundle(
        inv=inv.reshape(2, micro, rows, LANES),
        mix=mix.reshape(2, micro, rows, model),
        vpre=vpre,
        spre=spre,
        x=x,
        bc=bc,
        dtc=dtc,
        gate=gate,
        y=y,
        s_in=s_in,
    )
    grads, dval, dgate, dst, dstep, sgm, vsums, ssums, hsums, nsums = backward_fused_call(
        cotangent, tokens_in, low_out, mask, kept, w, par, blocks, head_dim
    )

    def long(value, q):
        return value[q].reshape(micro * rows, value.shape[3])

    lane = jnp.arange(LANES)[:, None]
    by_block = (8 * (lane // heads) + lax.rem(lane, heads) == jnp.arange(LANES)[None, :]) & (lane < all_heads)
    pack, turned = [], []
    for q in range(2):
        normed = long(nx, q)
        turned.append(tn(long(dst, q), normed))
        step_lanes = nn(long(dstep, q), by_block.astype(BF)).astype(BF)
        step_grad = tn(step_lanes[:, : 8 * blocks], normed)
        ssum, hsum = jnp.sum(ssums[q], axis=0), jnp.sum(hsums[q], axis=0)
        rest = [
            nsums[q, 0][None],
            jnp.pad(ssum[:5].reshape(1, -1), ((0, 0), (0, width - 5 * states))),
            jnp.zeros((6, width), F32),
        ]
        hsum = hsum[:2, :all_heads].reshape(2, blocks, heads).transpose(1, 0, 2).reshape(blocks, 2 * heads)
        hsum = jnp.pad(hsum, ((0, 0), (0, half - 2 * heads))).reshape(1, width)
        pack.append(jnp.concatenate([jnp.sum(vsums[q], axis=0)[:7], hsum, step_grad] + rest, axis=0))
    turned = lax.psum_scatter(
        jnp.concatenate(turned, axis=0), (PIPE, DP, TENSOR), scatter_dimension=0, tiled=True
    )
    pack = jnp.stack(pack)
    factors = (nx, sgm, dval, dgate, gg)
    large, chan, step_grad, rest = reduce_call(factors, pack, blocks, groups)
    grad_value, grad_gate, grad_out = [large[w].astype(F32) for w in range(3)]

    step_grad = step_grad.reshape(2, 8, shard_rows)[:, :heads].reshape(2 * heads, shard_rows).T
    grad_state = turned.T
    position = group * blocks + block
    ranks = groups * blocks

    def share(value):
        size = value.shape[-1] // ranks
        return lax.dynamic_slice_in_dim(value, position * size, size, value.ndim - 1)

    head_sums = chan[7].reshape(2, half)[:, : 2 * heads].reshape(2, 2, heads).transpose(1, 0, 2).reshape(2, -1)
    norm_sum = share(rest[0])
    conv_sum = share(rest[1, : 5 * states].reshape(5, states))
    return (
        out[None],
        grads[None],
        grad_gate[None],
        grad_value[None],
        grad_state[None],
        step_grad[None],
        grad_out[None],
        norm_sum[None],
        chan[None, :4],
        conv_sum[None, :4],
        chan[None, 4],
        conv_sum[None, 4],
        head_sums[None, 0],
        head_sums[None, 1],
        jnp.sum(chan[6].reshape(2 * heads, head_dim), axis=1)[None],
        chan[None, 5],
    )


def body(
    tokens_in,
    cotangent,
    lengths,
    in_gate,
    in_value,
    in_state,
    in_step,
    out_proj,
    norm_gain,
    conv_value,
    conv_state,
    bias_value,
    bias_state,
    step_bias,
    decay_log,
    skip_gain,
    gate_gain,
):
    layer = lax.axis_index(PIPE)
    block = lax.axis_index(TENSOR)
    blocks = lax.axis_size(TENSOR)
    group = lax.axis_index(DP)
    groups = lax.axis_size(DP)
    first_half = layer == 0
    micro, rows, model = tokens_in.shape
    shard_rows = in_value.shape[1]
    half = in_value.shape[2] // 2
    heads = step_bias.shape[1] // 2
    head_dim = half // heads
    width = half * blocks
    all_heads = heads * blocks
    states = in_state.shape[2]
    state = states // 2
    inner_total = 2 * width

    def halves(value):
        keep = lax.dynamic_slice_in_dim(value, layer * half_of(value), half_of(value), value.ndim - 1)
        send = lax.dynamic_slice_in_dim(value, (1 - layer) * half_of(value), half_of(value), value.ndim - 1)
        return by_layer(keep, swap_pipe(send))

    def half_of(value):
        return value.shape[-1] // 2

    def by_layer(own, other):
        return jnp.where(first_half, own, other), jnp.where(first_half, other, own)

    channel = jnp.concatenate([conv_value[0], bias_value, gate_gain], axis=0)
    channel_both = halves(channel)
    head_both = halves(jnp.concatenate([step_bias, decay_log, skip_gain], axis=0))
    flat_heads = [jnp.pad(v.reshape(1, 3 * heads), ((0, 0), (0, half - 3 * heads))) for v in head_both]
    packed = gather_tensor(jnp.concatenate(list(channel_both) + flat_heads + [jnp.zeros((2, half), F32)], axis=0))
    shared = jnp.concatenate([norm_gain[0], conv_state[0].reshape(-1), bias_state[0]], axis=0)
    shared_both = by_layer(shared, swap_pipe(shared))
    params = []
    for q in range(2):
        per_head = packed[12 + q].reshape(blocks, half)[:, : 3 * heads].reshape(blocks, 3, heads)
        per_head = per_head.transpose(1, 0, 2).reshape(3, all_heads)
        skip = jnp.repeat(per_head[2:3], head_dim, axis=1)
        value_par = jnp.concatenate([packed[6 * q : 6 * q + 6], skip, jnp.zeros((1, width), F32)], axis=0)
        head_par = jnp.pad(per_head, ((0, 5), (0, LANES - all_heads)))
        state_par = jnp.concatenate(
            [
                shared_both[q][model : model + 4 * states].reshape(4, states),
                shared_both[q][model + 4 * states :].reshape(1, states),
                jnp.zeros((3, states), F32),
            ],
            axis=0,
        )
        params.append(Bundle(value=value_par, head=head_par, state=state_par, norm=shared_both[q][:model]))

    step_both = halves(in_step[0])
    step_all = gather_tensor(jnp.concatenate(step_both, axis=1)).reshape(shard_rows, blocks, 2, heads)
    state_both = by_layer(in_state[0], swap_pipe(in_state[0]))
    value_both, gate_both, out_both = halves(in_value[0]), halves(in_gate[0]), halves(out_proj[0])
    weights = []
    for q in range(2):
        step_q = jnp.pad(step_all[:, :, q].reshape(shard_rows, all_heads), ((0, 0), (0, LANES - all_heads)))
        small = gather_dp(jnp.concatenate([state_both[q], step_q], axis=1))
        weights.append(
            Bundle(
                state=small[:, :states],
                step=small[:, states:],
                value=gather_dp(gather_tensor(value_both[q])),
                gate=gather_dp(gather_tensor(gate_both[q])),
                out=gather_dp(gather_tensor(out_both[q])),
            )
        )

    masks = [
        (block * rows + jnp.arange(rows) < lengths[s]).astype(F32)[:, None] for s in range(micro)
    ]

    def forward(u, s, q):
        w, par = weights[q], params[q]
        ext = jnp.concatenate([shift_tensor(u[-HALO:], 1), u], axis=0).astype(F32)
        root_inv = lax.rsqrt(jnp.mean(ext * ext, axis=1, keepdims=True) + EPS)
        nx = (ext * root_inv * par.norm[None, :]).astype(BF)
        vpre, spre, x, bc, dtc, yw, loc = front_call(nx, w, par, head_dim, state)
        through = jnp.repeat(jnp.exp(dtc[1, rows - 1, :all_heads]), head_dim)[:, None]
        s_in = jnp.zeros((width, state), BF)
        for k in range(1, blocks):
            sent = (through * s_in.astype(F32) + loc).astype(BF)
            got = lax.ppermute(sent, TENSOR, [(k - 1, k)])
            s_in = got if k == 1 else jnp.where(block == k, got, s_in)
        gate, y, gg, part, squares = finish_call(nx, w, par, yw, s_in, bc, dtc, head_dim)
        total = squares[:, 0]
        total = total + swap_pipe(total)
        inverse = lax.rsqrt(total / inner_total + EPS)[:, None]
        mixed = inverse * (part.astype(F32) + swap_pipe(part).astype(F32))
        result = (masks[s] * (u.astype(F32) + mixed)).astype(BF)
        kept = Bundle(
            u=u, nx=nx, root_inv=root_inv[HALO:], vpre=vpre, spre=spre, x=x, bc=bc, dtc=dtc, s_in=s_in, through=through,
            gate=gate, y=y, gg=gg, inverse=inverse, mixed=mixed,
        )
        return result, kept

    def backward(incoming, s, q, kept):
        w, par = weights[q], params[q]
        gm = (masks[s] * incoming.astype(F32)).astype(BF)
        gmf = gm.astype(F32)
        inverse = kept.inverse
        dot = jnp.sum(gmf * kept.mixed, axis=1, keepdims=True)
        shrink = inverse * inverse * dot / inner_total
        rowsc = jnp.concatenate([inverse, shrink, jnp.zeros((rows, LANES - 2), F32)], axis=1)
        dy, dgate, dsl, dgain = gate_call(gm, w, par, kept.y, kept.gate, rowsc, kept.bc, kept.dtc, head_dim)
        g_in = jnp.zeros((width, state), BF)
        for k in range(blocks - 2, -1, -1):
            sent = (kept.through * g_in.astype(F32) + dsl).astype(BF)
            got = lax.ppermute(sent, TENSOR, [(k + 1, k)])
            g_in = got if k == blocks - 2 else jnp.where(block == k, got, g_in)
        dconv, dsc, dstep, vsums, ssums, hsums = backward_call(
            dy, kept.x, kept.vpre, kept.spre, kept.bc, kept.dtc, kept.s_in, g_in, par, head_dim
        )
        halo = shift_tensor(jnp.concatenate([dconv[:8], dsc[:8]], axis=1), -1)
        dval, dst, part = conv_call(dconv, halo, dsc, dgate, dstep, w, par)
        grad_normed = part.astype(F32) + swap_pipe(part).astype(F32)
        uf, root_inv = kept.u.astype(F32), kept.root_inv
        grad_norm = jnp.sum(grad_normed * uf * root_inv, axis=0)
        weighted = grad_normed * par.norm[None, :]
        grad_u = root_inv * weighted - uf * root_inv**3 * jnp.mean(weighted * uf, axis=1, keepdims=True) + gmf
        scaled_gm = (gmf * inverse).astype(BF)
        channel_sums = jnp.concatenate([vsums[:5], dgain[:1], vsums[5:6]], axis=0)
        sums = (channel_sums, ssums[:5], hsums[:2, :all_heads], grad_norm)
        return grad_u.astype(BF), (dval, dgate, dst, dstep, scaled_gm), sums

    outs, kept = [], []
    current = [tokens_in[s] for s in range(micro)]
    for q in range(2):
        pairs = [forward(current[s], s, q) for s in range(micro)]
        current = [pair[0] for pair in pairs]
        outs.append(jnp.stack(current))
        kept.append([pair[1] for pair in pairs])

    grads = [None, None]
    reduced = [None, None]
    incoming = [cotangent[s] for s in range(micro)]
    for q in (1, 0):
        results = [backward(incoming[s], s, q, kept[q][s]) for s in range(micro)]
        incoming = [r[0] for r in results]
        grads[q] = jnp.stack(incoming)
        stacked = [jnp.concatenate([r[1][k] for r in results], axis=0) for k in range(5)]
        dval, dgate, dst, dstep, scaled_gm = stacked
        normed = jnp.concatenate([kept[q][s].nx[HALO:] for s in range(micro)], axis=0)
        gg = jnp.concatenate([kept[q][s].gg for s in range(micro)], axis=0)
        sums = [functools.reduce(jnp.add, [r[2][k] for r in results]) for k in range(4)]

        big = [tn(scaled_gm, gg).astype(BF), tn(normed, dgate).astype(BF), tn(normed, dval).astype(BF)]
        big = [reduce_tensor(take_cols(reduce_dp(v))) for v in big]
        turned = reduce_dp(tn(dst, normed).astype(BF))
        turned = reduce_tensor(take_first(turned.reshape(blocks, -1, model)))
        step_grad = tn(dstep, normed)[:all_heads]
        by_block = jnp.concatenate(
            [
                sums[0].reshape(7, blocks, half).transpose(1, 0, 2).reshape(blocks, -1),
                step_grad.reshape(blocks, -1),
                sums[2].reshape(2, blocks, heads).transpose(1, 0, 2).reshape(blocks, -1),
            ],
            axis=1,
        )
        per_block = reduce_tensor(take_first(sum_all_dp(by_block)))
        common = sum_all_tensor(sum_all_dp(jnp.concatenate([sums[1].reshape(-1), sums[3]], axis=0)))
        reduced[q] = (big, turned, per_block, common)

    def own_and_other(kind):
        return jnp.where(first_half, kind(0), kind(1)), jnp.where(first_half, kind(1), kind(0))

    def join(kind):
        own, other = own_and_other(kind)
        got = swap_pipe(other)
        return jnp.where(first_half, own, got), jnp.where(first_half, got, own)

    def columns(k):
        low, high = join(lambda q: reduced[q][0][k].astype(BF))
        return jnp.concatenate([low, high], axis=1).astype(F32)

    grad_out, grad_gate, grad_value = columns(0), columns(1), columns(2)
    own, other = own_and_other(lambda q: reduced[q][1])
    grad_state = (own + swap_pipe(other.astype(BF)).astype(F32)).T
    low, high = join(lambda q: reduced[q][2])
    cut1, cut2 = 7 * half, 7 * half + heads * model
    chan = jnp.concatenate([low[:cut1].reshape(7, half), high[:cut1].reshape(7, half)], axis=1)
    step_grad = jnp.concatenate([low[cut1:cut2].reshape(heads, model), high[cut1:cut2].reshape(heads, model)], axis=0)
    step_grad = lax.dynamic_slice_in_dim(step_grad, group * shard_rows, shard_rows, 1).T
    head_sums = jnp.concatenate([low[cut2:].reshape(2, heads), high[cut2:].reshape(2, heads)], axis=1)
    own, other = own_and_other(lambda q: reduced[q][3])
    conv_sum = own[: 5 * states] + swap_pipe(other[: 5 * states])
    norm_sum = own[5 * states :]
    position = group * blocks + block
    ranks = groups * blocks

    def share(value):
        size = value.shape[-1] // ranks
        return lax.dynamic_slice_in_dim(value, position * size, size, value.ndim - 1)

    conv_sum = share(conv_sum.reshape(5, states))
    return (
        jnp.where(first_half, outs[0], outs[1])[None],
        jnp.where(first_half, grads[0], grads[1])[None],
        grad_gate[None],
        grad_value[None],
        grad_state[None],
        step_grad[None],
        grad_out[None],
        share(norm_sum)[None],
        chan[None, :4],
        conv_sum[None, :4],
        chan[None, 4],
        conv_sum[None, 4],
        head_sums[None, 0],
        head_sums[None, 1],
        jnp.sum(chan[6].reshape(2 * heads, head_dim), axis=1)[None],
        chan[None, 5],
    )


def solution(mesh):
    in_specs = (
        P(DP, TENSOR, None),
        P(DP, TENSOR, None),
        P(DP),
        P(PIPE, DP, TENSOR),
        P(PIPE, DP, TENSOR),
        P(PIPE, DP, None),
        P(PIPE, DP, TENSOR),
        P(PIPE, DP, TENSOR),
        P(PIPE, None),
        P(PIPE, None, TENSOR),
        P(PIPE, None, None),
        P(PIPE, TENSOR),
        P(PIPE, None),
        P(PIPE, TENSOR),
        P(PIPE, TENSOR),
        P(PIPE, TENSOR),
        P(PIPE, TENSOR),
    )
    out_specs = (
        P(PIPE, DP, TENSOR, None),
        P(PIPE, DP, TENSOR, None),
        P(PIPE, DP, TENSOR),
        P(PIPE, DP, TENSOR),
        P(PIPE, None, (DP, TENSOR)),
        P(PIPE, DP, TENSOR),
        P(PIPE, DP, TENSOR),
        P(PIPE, (DP, TENSOR)),
        P(PIPE, None, TENSOR),
        P(PIPE, None, (DP, TENSOR)),
        P(PIPE, TENSOR),
        P(PIPE, (DP, TENSOR)),
        P(PIPE, TENSOR),
        P(PIPE, TENSOR),
        P(PIPE, TENSOR),
        P(PIPE, TENSOR),
    )

    def program(*args):
        columns = args[4].shape[2] // mesh.shape[TENSOR]
        fused = mesh.shape[DP] == 4 and mesh.shape[TENSOR] > 2 and columns // 2 % LANES == 0
        return mapped(fused_body if fused else body)(*args)

    def mapped(function):
        return jax.shard_map(function, mesh=mesh, in_specs=in_specs, out_specs=out_specs, check_vma=False)

    return program
```

```python
import functools
import types

import jax
import jax.numpy as jnp
from jax import lax
from jax.experimental import pallas as pl
from jax.experimental.pallas import tpu as pltpu
from jax.sharding import PartitionSpec as P

EPS = 1e-05
PIPE, DP, TENSOR = "pipe", "dp", "tensor"
SEQUENTIAL = "arbitrary"
Bundle = types.SimpleNamespace
HIGHEST = lax.Precision.HIGHEST
BF = jnp.bfloat16
F32 = jnp.float32
HALO = 16
GC = 256
LANES = 128
LOG2E = 1.4426950408889634


def nn(a, b):
    return jnp.dot(a, b, preferred_element_type=F32)


def nt(a, b):
    return lax.dot_general(a, b, (((1,), (1,)), ((), ())), preferred_element_type=F32)


def tn(a, b):
    return lax.dot_general(a, b, (((0,), (0,)), ((), ())), preferred_element_type=F32)


def exact(a, b):
    return jnp.dot(a, b, precision=HIGHEST, preferred_element_type=F32)


def sigmoid(v):
    return 0.5 * jnp.tanh(0.5 * v) + 0.5


def iota(shape, dim):
    return lax.broadcasted_iota(jnp.int32, shape, dim)


def spread(per_head, width, head_dim):
    lane = iota(per_head.shape, 1)
    parts = []
    for pair in range(width // LANES):
        parts.append(
            jnp.where(lane < head_dim, per_head[:, 2 * pair : 2 * pair + 1], per_head[:, 2 * pair + 1 : 2 * pair + 2])
        )
    return jnp.concatenate(parts, axis=1)


def conv_rows(pre, taps, rows):
    total = taps[4:5, :] + taps[3:4, :] * pre[HALO : HALO + rows, :]
    for k in range(3):
        total = total + taps[k : k + 1, :] * pre[HALO - 3 + k : HALO - 3 + k + rows, :]
    return total


def conv_sums(grad, pre, rows):
    sums = [jnp.sum(grad * pre[HALO - 3 + k : HALO - 3 + k + rows, :], axis=0, keepdims=True) for k in range(4)]
    sums.append(jnp.sum(grad, axis=0, keepdims=True))
    return sums


def conv_transposed(grad, halo, taps, rows):
    ext = jnp.concatenate([grad, halo], axis=0)
    total = taps[3:4, :] * grad
    for k in range(3):
        total = total + taps[k : k + 1, :] * ext[3 - k : 3 - k + rows, :]
    return total


def silu_slope(v):
    s = sigmoid(v)
    return s * (1.0 + v * (1.0 - s))


def group_lanes(values, dst, groups, per_group):
    for g in range(groups):
        dst[g] = values if g == 0 else pltpu.roll(values, LANES - per_group * g, 1)


def group_rows(values, dst, groups, per_group):
    turned = values.T
    for g in range(groups):
        dst[g, 0:per_group, :] = turned[per_group * g : per_group * (g + 1), :]


def scan_front(
    head_dim, nx, wv, ws, wt, pv, ps, ph, vpre_o, spre_o, x_o, bc_o, dtc_o, yw_o, loc_o, sc_s, dt_s, cum_s, cumt_s
):
    g = pl.program_id(0)
    groups = pl.num_programs(0)
    rows = x_o.shape[0]
    state = bc_o.shape[1] // 2
    per_group = GC // head_dim

    @pl.when(g == 0)
    def _():
        spre = nn(nx[...], ws[...])
        spre_o[...] = spre
        conv = conv_rows(spre, ps, rows)
        bc = (conv * sigmoid(conv)).astype(BF)
        bc_o[...] = bc
        scores = nt(bc[:, state:], bc[:, :state])
        lower = iota((rows, rows), 0) >= iota((rows, rows), 1)
        sc_s[...] = jnp.where(lower, scores, 0.0)
        raw = nn(nx[HALO:, :], wt[...]) + ph[0:1, :]
        step = jnp.maximum(raw, 0.0) + jnp.log(1.0 + jnp.exp(-jnp.abs(raw)))
        decay = -step * jnp.exp(ph[1:2, :])
        cum = exact(lower.astype(F32), decay)
        dtc_o[0] = step
        dtc_o[1] = cum
        dtc_o[2] = sigmoid(raw)
        group_lanes(step, dt_s, dt_s.shape[0], per_group)
        group_lanes(cum, cum_s, cum_s.shape[0], per_group)
        group_rows(cum, cumt_s, cumt_s.shape[0], per_group)

    pre = nn(nx[...], wv[...])
    vpre_o[...] = pre
    conv = conv_rows(pre, pv, rows)
    x = conv * sigmoid(conv)
    x_o[...] = x.astype(BF)
    step, cum, cumt = dt_s[g], cum_s[g], cumt_s[g]
    to_end = jnp.exp(cum[rows - 1 : rows, :] - cum)
    xp = (x * spread(step, GC, head_dim)).astype(BF)
    xr = (x * spread(step * to_end, GC, head_dim)).astype(BF)
    loc_o[...] = tn(xr, bc_o[:, :state])
    scores = sc_s[...]
    lane = iota((rows, LANES), 1)
    for pair in range(GC // LANES):
        cols = slice(LANES * pair, LANES * (pair + 1))
        outs = []
        for i in (2 * pair, 2 * pair + 1):
            diff = cum[:, i : i + 1] - cumt[i : i + 1, :]
            mix = (jnp.exp(jnp.minimum(diff, 0.0)) * scores).astype(BF)
            outs.append(nn(mix, xp[:, cols]))
        yw_o[:, cols] = jnp.where(lane < head_dim, outs[0], outs[1]) + pv[6:7, cols] * x[:, cols]


def scan_finish(
    head_dim, nx, wg, wo, yw, s_in, bc, dtc, pv, gate_o, y_o, gg_o, p_o, sq_o, acc_s, sq_s, cum_s
):
    g = pl.program_id(0)
    rows = yw.shape[0]
    state = bc.shape[1] // 2

    @pl.when(g == 0)
    def _():
        group_lanes(dtc[1], cum_s, cum_s.shape[0], GC // head_dim)
        acc_s[...] = jnp.zeros_like(acc_s)
        sq_s[...] = jnp.zeros_like(sq_s)

    gate = nn(nx[HALO:, :], wg[...])
    gate_o[...] = gate
    carried = nt(bc[:, state:], s_in[...])
    y = yw[...] + spread(jnp.exp(cum_s[g]), GC, head_dim) * carried
    y_o[...] = y
    gated = y * (gate * sigmoid(gate))
    gg = (gated * pv[5:6, :]).astype(BF)
    gg_o[...] = gg
    squares = gated * gated
    for part in range(GC // LANES):
        sq_s[...] += squares[:, LANES * part : LANES * (part + 1)]
    acc_s[...] += nt(gg, wo[...])

    @pl.when(g == pl.num_programs(0) - 1)
    def _():
        p_o[...] = acc_s[...].astype(BF)
        sq_o[...] = jnp.broadcast_to(jnp.sum(sq_s[...], axis=1, keepdims=True), sq_o.shape)


def gate_backward(head_dim, gm, wo, y, gate, rowsc, pv, bc, dtc, dy_o, dgate_o, dsl_o, dgain_o, cum_s):
    g = pl.program_id(0)
    state = bc.shape[1] // 2

    @pl.when(g == 0)
    def _():
        group_lanes(dtc[1], cum_s, cum_s.shape[0], GC // head_dim)

    gs = nn(gm[...], wo[...])
    inverse, shrink = rowsc[:, 0:1], rowsc[:, 1:2]
    gv, yv = gate[...], y[...]
    s = sigmoid(gv)
    silu = gv * s
    gated = yv * silu
    dgain = jnp.sum(gs * gated * inverse, axis=0, keepdims=True)
    dgain_o[...] = jnp.broadcast_to(dgain, dgain_o.shape)
    dgated = inverse * (gs * pv[5:6, :]) - gated * shrink
    dgate_o[...] = (dgated * yv * (s * (1.0 + gv * (1.0 - s)))).astype(BF)
    dy = dgated * silu
    dy_o[...] = dy.astype(BF)
    dye = (dy * spread(jnp.exp(cum_s[g]), GC, head_dim)).astype(BF)
    dsl_o[...] = tn(dye, bc[:, state:])


def scan_backward(
    head_dim,
    dy,
    x,
    vpre,
    spre,
    bc,
    dtc,
    s_in,
    g_in,
    pv,
    ps,
    ph,
    dconv_o,
    dsc_o,
    dstep_o,
    vs_o,
    ss_o,
    hs_o,
    sct_s,
    scts_s,
    wsum_s,
    dbc_s,
    dt_s,
    cum_s,
    cumt_s,
    net_s,
    rv_s,
    ddir_s,
    k_s,
    rt_s,
    rall_s,
):
    g = pl.program_id(0)
    rows = x.shape[0]
    state = bc.shape[1] // 2
    per_group = GC // head_dim
    groups = dt_s.shape[0]

    @pl.when(g == 0)
    def _():
        scores = nt(bc[:, :state], bc[:, state:])
        first, second = iota((rows, rows), 0), iota((rows, rows), 1)
        sct_s[...] = jnp.where(second >= first, scores, 0.0)
        scts_s[...] = jnp.where(second > first, scores, 0.0)
        wsum_s[...] = jnp.zeros_like(wsum_s)
        dbc_s[...] = jnp.zeros_like(dbc_s)
        rall_s[...] = jnp.zeros_like(rall_s)
        group_lanes(dtc[0], dt_s, groups, per_group)
        group_lanes(dtc[1], cum_s, groups, per_group)
        group_rows(dtc[1], cumt_s, groups, per_group)

    step, cum, cumt = dt_s[g], cum_s[g], cumt_s[g]
    last = cum[rows - 1 : rows, :]
    to_end = jnp.exp(last - cum)
    stepx = spread(step, GC, head_dim)
    endx = spread(to_end, GC, head_dim)
    fromx = spread(jnp.exp(cum), GC, head_dim)
    xf = x[...].astype(F32)
    dyb = dy[...]
    dyf = dyb.astype(F32)
    xp = (xf * stepx).astype(BF)
    xr = (xf * stepx * endx).astype(BF)
    dyef = dyf * fromx
    dye = dyef.astype(BF)
    gb = nt(bc[:, :state], g_in[...])
    cs = nt(bc[:, state:], s_in[...])
    dbc_s[:, :state] += nn(xr, g_in[...])
    dbc_s[:, state:] += nn(dye, s_in[...])

    lane = iota((rows, LANES), 1)
    wsum = wsum_s[...]
    colsum = jnp.zeros((rows, LANES), F32)
    within = []
    for pair in range(GC // LANES):
        cols = slice(LANES * pair, LANES * (pair + 1))
        xpp, dyp = xp[:, cols], dyb[:, cols]
        outs = []
        for side in range(2):
            i = 2 * pair + side
            mine = (lane < head_dim) if side == 0 else (lane >= head_dim)
            decay = jnp.exp(jnp.minimum(cumt[i : i + 1, :] - cum[:, i : i + 1], 0.0))
            outs.append(nn((decay * sct_s[...]).astype(BF), dyp))
            weight = decay * nt(jnp.where(mine, xpp, jnp.zeros_like(xpp)), dyp)
            wsum = wsum + weight
            pairs = (weight * scts_s[...]).astype(BF)
            colsum = colsum + nn(pairs, (lane == i).astype(BF))
            rt_s[g, i : i + 1, :] = jnp.sum(pairs.astype(F32), axis=0, keepdims=True)
        within.append(jnp.where(lane < head_dim, outs[0], outs[1]))
    wsum_s[...] = wsum
    u = jnp.concatenate(within, axis=1) + endx * gb

    heads = (iota((GC, LANES), 0) // head_dim == iota((GC, LANES), 1)).astype(BF)
    ddir_s[g] = nn((xf * u).astype(BF), heads)
    net_s[g] = nn((dyef * cs).astype(BF), heads) - colsum
    rv_s[g] = step * to_end * nn((xf * gb).astype(BF), heads)
    inner = g_in[...].astype(F32) * s_in[...].astype(F32)
    per_channel = lax.dot_general(
        jnp.ones((8, inner.shape[1]), F32), inner, (((1,), (1,)), ((), ())), precision=HIGHEST, preferred_element_type=F32
    )
    k_s[g] = jnp.exp(last) * exact(per_channel, heads.astype(F32))

    dx = stepx * u + pv[6:7, :] * dyf
    dconv = dx * silu_slope(conv_rows(vpre, pv, rows))
    dconv_o[...] = dconv
    sums = conv_sums(dconv, vpre, rows)
    sums.append(jnp.sum(dyf * xf, axis=0, keepdims=True))
    sums.append(jnp.zeros((2, GC), F32))
    vs_o[...] = jnp.concatenate(sums, axis=0)

    @pl.when(g == pl.num_programs(0) - 1)
    def _():
        first, second = iota((rows, rows), 0), iota((rows, rows), 1)
        net, rv, ddir, const = net_s[0], rv_s[0], ddir_s[0], k_s[0]
        rall_s[0:per_group, :] = rt_s[0, 0:per_group, :]
        for other in range(1, groups):
            shift = per_group * other
            net = net + pltpu.roll(net_s[other], shift, 1)
            rv = rv + pltpu.roll(rv_s[other], shift, 1)
            ddir = ddir + pltpu.roll(ddir_s[other], shift, 1)
            const = const + pltpu.roll(k_s[other], shift, 1)
            rall_s[shift : shift + per_group, :] = rt_s[other, 0:per_group, :]
        net = net + rall_s[...].T
        da = exact((second >= first).astype(F32), net) + exact((second < first).astype(F32), rv) + const[0:1, :]
        rate = jnp.exp(ph[1:2, :])
        dstep = (ddir - da * rate) * dtc[2]
        dstep_o[...] = dstep.astype(BF)
        hs_o[...] = jnp.concatenate(
            [
                jnp.sum(dstep, axis=0, keepdims=True),
                jnp.sum(-da * dtc[0] * rate, axis=0, keepdims=True),
                jnp.zeros((6, LANES), F32),
            ],
            axis=0,
        )
        weights = jnp.where(second >= first, wsum_s[...], 0.0).astype(BF)
        db = dbc_s[:, :state] + nn(weights, bc[:, state:])
        dc = dbc_s[:, state:] + tn(weights, bc[:, :state])
        dsc = jnp.concatenate([db, dc], axis=1) * silu_slope(conv_rows(spre, ps, rows))
        dsc_o[...] = dsc
        ssums = conv_sums(dsc, spre, rows)
        ssums.append(jnp.zeros((3, 2 * state), F32))
        ss_o[...] = jnp.concatenate(ssums, axis=0)


def conv_backward(dconv, halo_v, dsc, halo_s, dgate, dstep, pv, ps, wv, wg, ws, wt, dval_o, dst_o, p_o, acc_s):
    g = pl.program_id(0)
    rows = dconv.shape[0]

    @pl.when(g == 0)
    def _():
        dst = conv_transposed(dsc[...], halo_s[...], ps, rows).astype(BF)
        dst_o[...] = dst
        acc_s[...] = nt(dst, ws[...]) + nt(dstep[...], wt[...])

    dval = conv_transposed(dconv[...], halo_v[...], pv, rows).astype(BF)
    dval_o[...] = dval
    acc_s[...] += nt(dval, wv[...]) + nt(dgate[...], wg[...])

    @pl.when(g == pl.num_programs(0) - 1)
    def _():
        p_o[...] = acc_s[...].astype(BF)


def whole(shape):
    return pl.BlockSpec(shape, lambda g: (0,) * len(shape))


def by_cols(rows):
    return pl.BlockSpec((rows, GC), lambda g: (0, g))


def by_rows(cols):
    return pl.BlockSpec((GC, cols), lambda g: (g, 0))


def call(kernel, groups, ins, outs, scratch, flops, traffic, exps=0):
    arrays, in_specs = zip(*ins)
    shapes, out_specs = zip(*outs)
    return pl.pallas_call(
        kernel,
        grid=(groups,),
        in_specs=list(in_specs),
        out_specs=list(out_specs),
        out_shape=[jax.ShapeDtypeStruct(s, d) for s, d in shapes],
        scratch_shapes=scratch,
        cost_estimate=pl.CostEstimate(flops=flops, bytes_accessed=traffic, transcendentals=exps),
        compiler_params=pltpu.CompilerParams(vmem_limit_bytes=40 * 2**20, dimension_semantics=(SEQUENTIAL,)),
    )(*arrays)


def front_call(nx, w, par, head_dim, state):
    rows, width = nx.shape[0] - HALO, w.value.shape[1]
    model = nx.shape[1]
    groups = width // GC
    return call(
        functools.partial(scan_front, head_dim),
        groups,
        [
            (nx, whole(nx.shape)),
            (w.value, by_cols(model)),
            (w.state, whole(w.state.shape)),
            (w.step, whole(w.step.shape)),
            (par.value, by_cols(8)),
            (par.state, whole(par.state.shape)),
            (par.head, whole(par.head.shape)),
        ],
        [
            (((rows + HALO, width), F32), by_cols(rows + HALO)),
            (((rows + HALO, 2 * state), F32), whole((rows + HALO, 2 * state))),
            (((rows, width), BF), by_cols(rows)),
            (((rows, 2 * state), BF), whole((rows, 2 * state))),
            (((3, rows, LANES), F32), whole((3, rows, LANES))),
            (((rows, width), F32), by_cols(rows)),
            (((width, state), F32), by_rows(state)),
        ],
        [
            pltpu.VMEM((rows, rows), F32),
            pltpu.VMEM((groups, rows, LANES), F32),
            pltpu.VMEM((groups, rows, LANES), F32),
            pltpu.VMEM((groups, 8, rows), F32),
        ],
        2 * rows * model * (width + 3 * LANES) + 4 * rows * rows * width,
        2 * model * width + 12 * rows * width,
        rows * rows * width // head_dim,
    )


def finish_call(nx, w, par, yw, s_in, bc, dtc, head_dim):
    rows, width = yw.shape
    model = nx.shape[1]
    groups = width // GC
    state = s_in.shape[1]
    return call(
        functools.partial(scan_finish, head_dim),
        groups,
        [
            (nx, whole(nx.shape)),
            (w.gate, by_cols(model)),
            (w.out, by_cols(model)),
            (yw, by_cols(rows)),
            (s_in, by_rows(state)),
            (bc, whole(bc.shape)),
            (dtc, whole(dtc.shape)),
            (par.value, by_cols(8)),
        ],
        [
            (((rows, width), F32), by_cols(rows)),
            (((rows, width), F32), by_cols(rows)),
            (((rows, width), BF), by_cols(rows)),
            (((rows, model), BF), whole((rows, model))),
            (((rows, LANES), F32), whole((rows, LANES))),
        ],
        [
            pltpu.VMEM((rows, model), F32),
            pltpu.VMEM((rows, LANES), F32),
            pltpu.VMEM((groups, rows, LANES), F32),
        ],
        4 * rows * model * width,
        4 * model * width + 14 * rows * width,
    )


def gate_call(gm, w, par, y, gate, rowsc, bc, dtc, head_dim):
    rows, width = y.shape
    model = gm.shape[1]
    groups = width // GC
    state = bc.shape[1] // 2
    return call(
        functools.partial(gate_backward, head_dim),
        groups,
        [
            (gm, whole(gm.shape)),
            (w.out, by_cols(model)),
            (y, by_cols(rows)),
            (gate, by_cols(rows)),
            (rowsc, whole(rowsc.shape)),
            (par.value, by_cols(8)),
            (bc, whole(bc.shape)),
            (dtc, whole(dtc.shape)),
        ],
        [
            (((rows, width), BF), by_cols(rows)),
            (((rows, width), BF), by_cols(rows)),
            (((width, state), F32), by_rows(state)),
            (((8, width), F32), by_cols(8)),
        ],
        [pltpu.VMEM((groups, rows, LANES), F32)],
        2 * rows * model * width,
        2 * model * width + 14 * rows * width,
    )


def backward_call(dy, x, vpre, spre, bc, dtc, s_in, g_in, par, head_dim):
    rows, width = x.shape
    groups = width // GC
    state = bc.shape[1] // 2
    lanes = pltpu.VMEM((groups, rows, LANES), F32)
    square = pltpu.VMEM((rows, rows), F32)
    return call(
        functools.partial(scan_backward, head_dim),
        groups,
        [
            (dy, by_cols(rows)),
            (x, by_cols(rows)),
            (vpre, by_cols(rows + HALO)),
            (spre, whole(spre.shape)),
            (bc, whole(bc.shape)),
            (dtc, whole(dtc.shape)),
            (s_in, by_rows(state)),
            (g_in, by_rows(state)),
            (par.value, by_cols(8)),
            (par.state, whole(par.state.shape)),
            (par.head, whole(par.head.shape)),
        ],
        [
            (((rows, width), F32), by_cols(rows)),
            (((rows, 2 * state), F32), whole((rows, 2 * state))),
            (((rows, LANES), BF), whole((rows, LANES))),
            (((8, width), F32), by_cols(8)),
            (((8, 2 * state), F32), whole((8, 2 * state))),
            (((8, LANES), F32), whole((8, LANES))),
        ],
        [
            square,
            square,
            square,
            pltpu.VMEM((rows, 2 * state), F32),
            lanes,
            lanes,
            pltpu.VMEM((groups, 8, rows), F32),
            lanes,
            lanes,
            lanes,
            pltpu.VMEM((groups, 8, LANES), F32),
            pltpu.VMEM((groups, 8, rows), F32),
            pltpu.VMEM((LANES, rows), F32),
        ],
        12 * rows * rows * width,
        14 * rows * width,
        3 * rows * rows * width // head_dim,
    )


def conv_call(dconv, halo, dsc, dgate, dstep, w, par):
    rows, width = dconv.shape
    model = w.value.shape[0]
    groups = width // GC
    states = dsc.shape[1]
    halo_v, halo_s = halo[:, :width], halo[:, width:]
    return call(
        conv_backward,
        groups,
        [
            (dconv, by_cols(rows)),
            (halo_v, by_cols(8)),
            (dsc, whole(dsc.shape)),
            (halo_s, whole(halo_s.shape)),
            (dgate, by_cols(rows)),
            (dstep, whole(dstep.shape)),
            (par.value, by_cols(8)),
            (par.state, whole(par.state.shape)),
            (w.value, by_cols(model)),
            (w.gate, by_cols(model)),
            (w.state, whole(w.state.shape)),
            (w.step, whole(w.step.shape)),
        ],
        [
            (((rows, width), BF), by_cols(rows)),
            (((rows, states), BF), whole((rows, states))),
            (((rows, model), BF), whole((rows, model))),
        ],
        [pltpu.VMEM((rows, model), F32)],
        4 * rows * model * width,
        4 * model * width + 10 * rows * width,
    )


def swap_pipe(value):
    return lax.ppermute(value, PIPE, [(0, 1), (1, 0)])


def shift_tensor(value, by):
    count = lax.axis_size(TENSOR)
    return lax.ppermute(value, TENSOR, [(i, i + by) for i in range(count) if 0 <= i + by < count])


def flip_dp(value, bit):
    return lax.ppermute(value, DP, [(i, i ^ bit) for i in range(lax.axis_size(DP))])


def dp_bits():
    bits, bit = [], 1
    while bit < lax.axis_size(DP):
        bits.append(bit)
        bit *= 2
    return bits


def gather_tensor(piece):
    count, me = lax.axis_size(TENSOR), lax.axis_index(TENSOR)
    rows, cols = piece.shape
    right, left = [piece], [piece]
    for _ in range(count - 1):
        right.append(shift_tensor(right[-1], 1))
        left.append(shift_tensor(left[-1], -1))
    full = jnp.zeros((rows, count * cols), piece.dtype)
    for k in range(count):
        part = piece if k == 0 else jnp.where(me >= k, right[k], left[count - k])
        full = lax.dynamic_update_slice(full, part, (0, lax.rem(me - k + count, count) * cols))
    return full


def gather_dp(piece):
    count, me = lax.axis_size(DP), lax.axis_index(DP)
    rows, cols = piece.shape
    held = {0: piece}
    for bit in reversed(dp_bits()):
        for offset in list(held):
            held[offset ^ bit] = flip_dp(held[offset], bit)
    full = jnp.zeros((count * rows, cols), piece.dtype)
    for offset, part in held.items():
        full = lax.dynamic_update_slice(full, part, ((me ^ offset) * rows, 0))
    return full


def add_low(a, b):
    return (a.astype(F32) + b.astype(F32)).astype(a.dtype)


def reduce_dp(value):
    me = lax.axis_index(DP)
    count = lax.axis_size(DP)
    rows, cols = value.shape[0] // count, value.shape[1]
    for bit in dp_bits():
        count //= 2
        split = value.reshape(count, 2, rows, cols)
        mine = (me // bit) % 2
        keep = lax.dynamic_index_in_dim(split, mine, 1, keepdims=False)
        send = lax.dynamic_index_in_dim(split, 1 - mine, 1, keepdims=False)
        value = add_low(keep, flip_dp(send, bit)).reshape(count * rows, cols)
    return value


def reduce_tensor(take):
    count, me = lax.axis_size(TENSOR), lax.axis_index(TENSOR)
    moving_right = moving_left = None
    for k in range(count - 1, 0, -1):
        right, left = take(jnp.minimum(me + k, count - 1)), take(jnp.maximum(me - k, 0))
        if moving_right is not None:
            right, left = add_low(right, moving_right), add_low(left, moving_left)
        moving_right, moving_left = shift_tensor(right, 1), shift_tensor(left, -1)
    own = take(me)
    if moving_right is None:
        return own.astype(F32)
    return own.astype(F32) + moving_right.astype(F32) + moving_left.astype(F32)


def take_cols(value):
    width = value.shape[1] // lax.axis_size(TENSOR)
    return lambda j: lax.dynamic_slice_in_dim(value, j * width, width, 1)


def take_first(value):
    return lambda j: lax.dynamic_index_in_dim(value, j, 0, keepdims=False)


def sum_all_dp(value):
    for bit in dp_bits():
        value = value + flip_dp(value, bit)
    return value


def sum_all_tensor(value):
    count, bit = lax.axis_size(TENSOR), 1
    while bit < count:
        value = value + lax.ppermute(value, TENSOR, [(i, i ^ bit) for i in range(count)])
        bit *= 2
    return value


MESH = pl.DeviceIdType.MESH
VMEM_LIMIT = 60 * 2**20


def remote(src, dst, send, recv, axis, index):
    return pltpu.make_async_remote_copy(
        src_ref=src, dst_ref=dst, send_sem=send, recv_sem=recv, device_id={axis: index}, device_id_type=MESH
    )


def greet(partners):
    barrier = pltpu.get_barrier_semaphore()
    for axis, index in partners:
        pl.semaphore_signal(barrier, inc=1, device_id={axis: index}, device_id_type=MESH)
    pl.semaphore_wait(barrier, len(partners))


def ring_neighbours(count):
    t = lax.axis_index(TENSOR)
    return [(TENSOR, lax.rem(t + 1, count)), (TENSOR, lax.rem(t + count - 1, count))]


def aligned(index, size):
    return pl.ds(pl.multiple_of(index * size, size), size)


class Gather:
    sems = ((4,), (4,), (4,), "z", "z", "z", "z", "z", "c", "c", (3,), (3,), (3,), (2,), (2,), (2, 2), (2, 2), "n", "n")

    @classmethod
    def scratch(cls, count):
        shapes = {"z": (8, count), "c": (8, 2, count), "n": (count,)}
        return [pltpu.SemaphoreType.DMA(shapes.get(shape, shape)) for shape in cls.sems]

    def __init__(self, count, sources, targets, small, sems):
        self.count, self.sources, self.targets, self.small = count, sources, targets, small
        (self.own_sem, self.xs_sem, self.xr_sem, self.right_sem, self.left_sem, self.zr_sem) = sems[:6]
        (self.ys_sem, self.yr_sem, self.cs_sem, self.cr_sem, self.st_own, self.st_xs, self.st_xr) = sems[6:13]
        (self.st_ys, self.st_yr, self.st_cs, self.st_cr, self.ch_s, self.ch_r) = sems[13:]
        self.p, self.d, self.t = lax.axis_index(PIPE), lax.axis_index(DP), lax.axis_index(TENSOR)
        y, c = self.d // 2, lax.rem(self.d, 2)
        self.y_mate, self.core_mate, self.far_mate = 2 * (1 - y) + c, 2 * y + 1 - c, 2 * (1 - y) + 1 - c
        self.kinds = len(sources)
        self.rows = sources[0].shape[0]

    def partners(self):
        others = [(TENSOR, lax.rem(self.t + k, self.count)) for k in range(1, self.count)]
        return others + [(PIPE, 1 - self.p), (DP, self.y_mate), (DP, self.core_mate)]

    def source(self, kind, which):
        ref = self.sources[kind]
        if kind == self.kinds - 1:
            return ref.at[aligned(which, ref.shape[0] // 2), :]
        return ref.at[:, aligned(which, ref.shape[1] // 2)]

    def region(self, kind, layer, row, col):
        ref = self.sources[kind]
        if kind == self.kinds - 1:
            return self.targets[kind].at[layer, aligned(col, ref.shape[0] // 2), aligned(row, ref.shape[1])]
        return self.targets[kind].at[layer, aligned(row, self.rows), aligned(col, ref.shape[1] // 2)]

    def own_copy(self, w):
        return pltpu.make_async_copy(self.source(w, self.p), self.region(w, self.p, self.d, self.t), self.own_sem.at[w])

    def swap_copy(self, w):
        dst = self.region(w, self.p, self.d, self.t)
        return remote(self.source(w, 1 - self.p), dst, self.xs_sem.at[w], self.xr_sem.at[w], PIPE, 1 - self.p)

    def swap_arrival(self, w):
        dst = self.region(w, 1 - self.p, self.d, self.t)
        return remote(self.source(w, 1 - self.p), dst, self.xs_sem.at[w], self.xr_sem.at[w], PIPE, 1 - self.p)

    def z_copy(self, item, src, by, sem):
        ref = self.region(item % self.kinds, item // self.kinds, self.d, src)
        return remote(ref, ref, sem.at[item, src], self.zr_sem.at[item, src], TENSOR, self.t + by)

    def right(self, item, src):
        return self.z_copy(item, src, 1, self.right_sem)

    def left(self, item, src):
        return self.z_copy(item, src, -1, self.left_sem)

    def y_copy(self, item, src, row=None):
        ref = self.region(item % self.kinds, item // self.kinds, self.d if row is None else row, src)
        return remote(ref, ref, self.ys_sem.at[item, src], self.yr_sem.at[item, src], DP, self.y_mate)

    def core_copy(self, item, which, src, arrival=False):
        row = (self.core_mate, self.far_mate)[which] if arrival else (self.d, self.y_mate)[which]
        ref = self.region(item % self.kinds, item // self.kinds, row, src)
        sems = self.cs_sem.at[item, which, src], self.cr_sem.at[item, which, src]
        return remote(ref, ref, *sems, DP, self.core_mate)

    def begin(self, item):
        w, layer = item % self.kinds, item // self.kinds

        @pl.when(self.p == layer)
        def _():
            self.own_copy(w).wait()

        @pl.when(self.p != layer)
        def _():
            self.swap_arrival(w).wait_recv()

        @pl.when(self.t < self.count - 1)
        def _():
            self.right(item, self.t).start()

        @pl.when(self.t > 0)
        def _():
            self.left(item, self.t).start()

        self.y_copy(item, self.t).start()
        self.core_copy(item, 0, self.t).start()

    def hop(self, item, hop):
        t, count = self.t, self.count
        lower, upper = t - hop, t + hop

        @pl.when(lower >= 0)
        def _():
            self.right(item, lower).wait_recv()

            @pl.when(t < count - 1)
            def _():
                self.right(item, lower).start()

            self.y_copy(item, lower).start()
            self.core_copy(item, 0, lower).start()

        @pl.when(upper < count)
        def _():
            self.left(item, upper).wait_recv()

            @pl.when(t > 0)
            def _():
                self.left(item, upper).start()

            self.y_copy(item, upper).start()
            self.core_copy(item, 0, upper).start()

    def share(self, item, src):
        self.y_copy(item, src, self.y_mate).wait_recv()
        self.core_copy(item, 1, src).start()

    def arrived(self, item, src):
        for which in range(2):
            self.core_copy(item, which, src, True).wait_recv()

    def sent(self, item):
        t, count = self.t, self.count
        for src in range(count):
            for which in range(2):
                self.core_copy(item, which, src).wait_send()
            self.y_copy(item, src).wait_send()

            @pl.when((src <= t) & (t < count - 1))
            def _():
                self.right(item, src).wait_send()

            @pl.when((src >= t) & (t > 0))
            def _():
                self.left(item, src).wait_send()


    def small_target(self, k, layer):
        target = self.small[k][1]
        if k == 0:
            return target.at[layer, aligned(self.d, self.rows), :]
        if k == 1:
            return target.at[layer, :, aligned(self.t, target.shape[2] // self.count)]
        return target.at[layer]

    def small_source(self, k, which):
        ref = self.small[k][0]
        return ref.at[:, aligned(which, ref.shape[1] // 2)] if k == 1 else ref

    def small_own(self, k):
        return pltpu.make_async_copy(self.small_source(k, self.p), self.small_target(k, self.p), self.st_own.at[k])

    def small_swap(self, k, arrival=False):
        dst = self.small_target(k, 1 - self.p if arrival else self.p)
        return remote(self.small_source(k, 1 - self.p), dst, self.st_xs.at[k], self.st_xr.at[k], PIPE, 1 - self.p)

    def state_rows(self, layer, row):
        return self.small[0][1].at[layer, aligned(row, self.rows), :]

    def state_y(self, layer, arrival=False):
        ref = self.state_rows(layer, self.y_mate if arrival else self.d)
        return remote(ref, ref, self.st_ys.at[layer], self.st_yr.at[layer], DP, self.y_mate)

    def state_core(self, layer, which, arrival=False):
        row = (self.core_mate, self.far_mate)[which] if arrival else (self.d, self.y_mate)[which]
        ref = self.state_rows(layer, row)
        return remote(ref, ref, self.st_cs.at[layer, which], self.st_cr.at[layer, which], DP, self.core_mate)

    def channels(self, k, arrival=False):
        target = self.small[1][1]
        index = lax.rem(self.t - k + self.count, self.count) if arrival else self.t
        ref = target.at[:, :, aligned(index, target.shape[2] // self.count)]
        return remote(ref, ref, self.ch_s.at[k], self.ch_r.at[k], TENSOR, lax.rem(self.t + k, self.count))

    def first_layer(self):
        order = [self.kinds - 1] + list(range(self.kinds - 1))
        for w in order:
            self.swap_copy(w).start()
            self.own_copy(w).start()
        for k in range(3):
            self.small_swap(k).start()
            self.small_own(k).start()
        order = [self.kinds - 1, 2 * self.kinds - 1] + list(range(self.kinds - 1))
        for item in order:
            self.begin(item)
        for k in range(3):
            self.small_own(k).wait()
            self.small_swap(k, True).wait_recv()
        for layer in range(2):
            self.state_y(layer).start()
            self.state_core(layer, 0).start()
        for k in range(1, self.count):
            self.channels(k).start()
        for hop in range(1, self.count):
            for item in order:
                self.hop(item, hop)
        for item in self.late_items():
            self.begin(item)
        for layer in range(2):
            self.state_y(layer, True).wait_recv()
            self.state_core(layer, 1).start()
        for src in range(self.count):
            for item in order:
                self.share(item, src)
        for item in order:
            for src in range(self.count):
                self.arrived(item, src)
        for k in range(1, self.count):
            self.channels(k, True).wait_recv()
        for layer in range(2):
            for which in range(2):
                self.state_core(layer, which, True).wait_recv()

    def late_items(self):
        return [self.kinds + w for w in range(self.kinds - 1)]

    def second_layer(self, steps, group_of):
        items, stages = self.late_items(), []
        hops = [(item, hop) for hop in range(1, self.count) for item in items]
        for n, (item, hop) in enumerate(hops):
            stages.append((2 + n * (steps - 5) // len(hops), functools.partial(self.hop, item, hop)))
        for src in range(self.count):
            for item in items:
                stages.append((steps - 2 + group_of(src), functools.partial(self.share, item, src)))
        for src in range(self.count):
            for item in items:
                stages.append((steps - 1 + group_of(src), functools.partial(self.arrived, item, src)))
        return stages

    def finish(self):
        for k in range(3):
            self.small_swap(k).wait_send()
        for k in range(1, self.count):
            self.channels(k).wait_send()
        for layer in range(2):
            self.state_y(layer).wait_send()
            for which in range(2):
                self.state_core(layer, which).wait_send()
        for w in range(self.kinds):
            self.swap_copy(w).wait_send()
        for item in range(2 * self.kinds):
            self.sent(item)


class Reducer:
    def __init__(self, count, factors, results, buffers, sems):
        self.count, self.factors, self.results = count, factors, results
        (self.a_s, self.b_s, self.dw_s, self.crecv, self.ysend, self.near_s, self.yrecv, self.total_s) = buffers[:8]
        (self.z_s, self.zl_s, self.xsend, self.xrecv, self.turned_s) = buffers[8:]
        (self.a_sem, self.b_sem, self.cs_sem, self.cr_sem, self.ys_sem, self.yr_sem) = sems[:6]
        (self.rs_sem, self.rr_sem, self.ls_sem, self.lr_sem, self.xs_sem, self.xr_sem, self.o_sem) = sems[6:]
        self.p, self.d, self.t = lax.axis_index(PIPE), lax.axis_index(DP), lax.axis_index(TENSOR)
        self.y, self.c = self.d // 2, lax.rem(self.d, 2)
        self.y_mate, self.core_mate = 2 * (1 - self.y) + self.c, 2 * self.y + 1 - self.c
        self.kinds = 3
        self.pieces = 2 * self.kinds * count
        self.ticks = self.pieces + count + 3
        self.rows, self.half = self.xsend.shape[1], self.xsend.shape[2]

    @staticmethod
    def scratch(count, micro, rows, model, half, groups):
        piece = (model // groups, half)
        vmem, dma = pltpu.VMEM, pltpu.SemaphoreType.DMA
        buffers = [
            vmem((micro, rows, model), BF),
            vmem((2, micro, rows, half), BF),
            vmem((3, model, half), BF),
            vmem((4, 2) + piece, BF),
            vmem((4,) + piece, BF),
            vmem((4,) + piece, BF),
            vmem((4,) + piece, BF),
            vmem((4,) + piece, BF),
            vmem((6 * count,) + piece, BF),
            vmem((6,) + piece, BF),
            vmem((6,) + piece, BF),
            vmem((3,) + piece, BF),
            vmem((model, micro * rows), BF),
        ]
        sems = [dma((1,)), dma((2,)), dma((3, 2)), dma((4, 2)), dma((4,)), dma((4,))]
        sems += [dma((6 * count,)) for _ in range(4)] + [dma((6,)), dma((3,)), dma((3, 2))]
        return buffers, sems

    def partners(self):
        return ring_neighbours(self.count) + [(PIPE, 1 - self.p), (DP, self.y_mate), (DP, self.core_mate)]

    def layer_of(self, m):
        return m // (self.kinds * self.count)

    def a_copy(self, which):
        return pltpu.make_async_copy(self.factors[which % 2].at[which // 2], self.a_s, self.a_sem.at[0])

    def b_copy(self, m, w):
        src = self.factors[2 + w].at[self.layer_of(m), :, :, aligned(lax.rem(m, self.count), self.half)]
        held = lax.rem(m, 2)
        return pltpu.make_async_copy(src, self.b_s.at[held], self.b_sem.at[held])

    def b_start(self, m):
        for w in range(self.kinds):

            @pl.when(lax.rem(m // self.count, self.kinds) == w)
            def _():
                self.b_copy(m, w).start()

    def core_copy(self, m, row):
        held, ring = lax.rem(m, 3), lax.rem(m, 4)
        src = self.dw_s.at[held, aligned(2 * row + 1 - self.c, self.rows), :]
        sems = self.cs_sem.at[held, row], self.cr_sem.at[ring, row]
        return remote(src, self.crecv.at[ring, row], *sems, DP, self.core_mate)

    def y_copy(self, m):
        held = lax.rem(m, 4)
        return remote(self.ysend.at[held], self.yrecv.at[held], self.ys_sem.at[held], self.yr_sem.at[held], DP, self.y_mate)

    def right(self, m):
        ref = self.z_s.at[m]
        return remote(ref, ref, self.rs_sem.at[m], self.rr_sem.at[m], TENSOR, self.t + 1)

    def left(self, m, last):
        dst = self.zl_s.at[m // self.count] if last else self.z_s.at[m]
        return remote(self.z_s.at[m], dst, self.ls_sem.at[m], self.lr_sem.at[m], TENSOR, self.t - 1)

    def x_copy(self, item):
        w = lax.rem(item, self.kinds)
        return remote(self.xsend.at[item], self.xrecv.at[w], self.xs_sem.at[item], self.xr_sem.at[w], PIPE, 1 - self.p)

    def when_valid(self, m, condition=None):
        valid = (m >= 0) & (m < self.pieces)
        return pl.when(valid if condition is None else valid & condition)

    def tick(self, n):
        count, t, rows = self.count, self.t, self.rows

        @self.when_valid(n - 4)
        def _():
            m = n - 4
            held = lax.rem(m, 4)
            self.y_copy(m).wait()
            add_to(self.total_s.at[held], self.near_s.at[held], self.yrecv.at[held])

        @self.when_valid(n - 2)
        def _():
            m = n - 2
            held, ring = lax.rem(m, 3), lax.rem(m, 4)
            for row in range(2):
                self.core_copy(m, row).wait()

            def own(row):
                return self.dw_s.at[held, aligned(2 * row + self.c, rows), :]

            add_to(self.ysend.at[ring], own(1 - self.y), self.crecv.at[ring, 1 - self.y])
            self.y_copy(m).start()
            add_to(self.near_s.at[ring], own(self.y), self.crecv.at[ring, self.y])

        def pass_on(m, first, arrival, send):
            total = self.total_s.at[lax.rem(m, 4)]

            @pl.when(first)
            def _():
                self.z_s[m] = total[...]

            @pl.when(jnp.logical_not(first))
            def _():
                arrival.wait_recv()
                add_to(self.z_s.at[m], self.z_s.at[m], total)

            send()

        to_right, to_left = n - 4 - t, n - 3 - count + t

        @self.when_valid(to_right, t < lax.rem(to_right + count, count))
        def _():
            pass_on(to_right, t == 0, self.right(to_right), lambda: self.right(to_right).start())

        @self.when_valid(to_left, t > lax.rem(to_left + count, count))
        def _():
            owner = lax.rem(to_left, count)

            def send():
                @pl.when(owner == t - 1)
                def _():
                    self.left(to_left, True).start()

                @pl.when(owner != t - 1)
                def _():
                    self.left(to_left, False).start()

            pass_on(to_left, t == count - 1, self.left(to_left, False), send)

        done = n - 3 - count

        @self.when_valid(done, t == lax.rem(done + count, count))
        def _():
            w = done // count
            mine = self.xsend.at[w]
            mine[...] = self.total_s[lax.rem(done, 4)]

            @pl.when(t > 0)
            def _():
                self.right(done).wait_recv()
                add_to(mine, mine, self.z_s.at[done])

            @pl.when(t < count - 1)
            def _():
                self.left(done, True).wait_recv()
                add_to(mine, mine, self.zl_s.at[w])

            @pl.when(self.p != self.layer_of(done))
            def _():
                self.x_copy(w).start()

        @self.when_valid(n)
        def _():
            @pl.when(n == 0)
            def _():
                self.a_copy(0).start()
                self.b_start(n)

            starts = [layer * self.kinds * count + 2 * count * which for layer in range(2) for which in range(2)]
            for which, start in enumerate(starts):

                @pl.when(n == start)
                def _():
                    self.a_copy(which).wait()
                    micro, long, model = self.a_s.shape
                    for row in range(model // rows):
                        at = slice(rows * row, rows * (row + 1))
                        self.turned_s[at, :] = self.a_s[:, :, at].reshape(micro * long, rows).T
                    if which + 1 < len(starts):
                        self.a_copy(which + 1).start()

            @pl.when(n + 1 < self.pieces)
            def _():
                self.b_start(n + 1)

            self.b_copy(n, 0).wait()
            b = self.b_s[lax.rem(n, 2)]
            b = b.reshape(b.shape[0] * b.shape[1], self.half)
            held = lax.rem(n, 3)
            for row in range(self.dw_s.shape[1] // rows):
                at = slice(rows * row, rows * (row + 1))
                self.dw_s[held, at, :] = nn(self.turned_s[at, :], b).astype(BF)
            for row in range(2):
                self.core_copy(n, row).start()

    def result_copy(self, w, other):
        src = self.xrecv.at[w] if other else self.xsend.at[self.kinds * self.p + w]
        dst = self.results.at[w, :, aligned(1 - self.p if other else self.p, self.half)]
        return pltpu.make_async_copy(src, dst, self.o_sem.at[w, int(other)])

    def close(self):
        count, t = self.count, self.t
        for w in range(self.kinds):
            self.result_copy(w, False).start()
            self.x_copy(w).wait_recv()
            self.result_copy(w, True).start()
        for m in range(self.pieces):

            @pl.when(t < m % count)
            def _():
                self.right(m).wait_send()

            @pl.when(t > m % count)
            def _():
                self.left(m, False).wait_send()

        for w in range(self.kinds):
            self.x_copy(self.kinds * (1 - self.p) + w).wait_send()
            for other in (False, True):
                self.result_copy(w, other).wait()


def add_to(dst, one, other, chunk=64):
    def step(i, carry):
        at = aligned(i, chunk)
        dst[at, :] = (one[at, :].astype(F32) + other[at, :].astype(F32)).astype(BF)
        return carry

    lax.fori_loop(0, dst.shape[0] // chunk, step, 0)


class Sums:
    def __init__(self, count, rows, half, pack, outs, buffers):
        self.count, self.rows, self.half, self.pack, self.outs = count, rows, half, pack, outs
        (self.total_s, self.part_s, self.far_s, self.ss, self.rs) = buffers
        self.p, self.d, self.t = lax.axis_index(PIPE), lax.axis_index(DP), lax.axis_index(TENSOR)
        y, c = self.d // 2, lax.rem(self.d, 2)
        self.steps, bit = [(DP, 2 * y + 1 - c), (DP, 2 * (1 - y) + c)], 1
        while bit < count:
            self.steps.append((TENSOR, self.t + bit * (1 - 2 * lax.rem(self.t // bit, 2))))
            bit *= 2

    @staticmethod
    def scratch(count, shape):
        steps = 2 + (count - 1).bit_length()
        vmem, dma = pltpu.VMEM, pltpu.SemaphoreType.DMA
        return [vmem((steps + 1,) + shape, F32), vmem((steps,) + shape, F32), vmem(shape[1:], F32), dma((steps + 1,)), dma((steps + 1,))]

    def partners(self):
        return [step for step in self.steps if step[0] == TENSOR]

    def copy(self, k):
        axis, index = self.steps[k]
        return remote(self.total_s.at[k], self.part_s.at[k], self.ss.at[k], self.rs.at[k], axis, index)

    def pipe_copy(self):
        k = len(self.steps)
        return remote(self.total_s.at[k, 1 - self.p], self.far_s, self.ss.at[k], self.rs.at[k], PIPE, 1 - self.p)

    def begin(self):
        self.total_s[0] = self.pack[...]
        self.copy(0).start()

    def step(self, k):
        self.copy(k).wait_recv()
        self.total_s[k + 1] = self.total_s[k] + self.part_s[k]
        if k + 1 < len(self.steps):
            self.copy(k + 1).start()
        else:
            self.pipe_copy().start()

    def close(self):
        chan_o, step_o, rest_o = self.outs
        k = len(self.steps)
        self.pipe_copy().wait_recv()
        mine, far, t = self.total_s.at[k, self.p], self.far_s, self.t
        for ref, where in ((mine, self.p), (far, 1 - self.p)):
            chan_o[:, aligned(where, self.half)] = ref[0:8, aligned(t, self.half)]
            step_o[aligned(where, 8), :] = ref[pl.ds(pl.multiple_of(8 + 8 * t, 8), 8), aligned(self.d, self.rows)]
        last = far.shape[0] - 8
        row = iota((8, far.shape[1]), 0)
        rest_o[...] = mine[last:, :] + jnp.where(row == 0, 0.0, far[last:, :])
        for k in range(len(self.steps)):
            self.copy(k).wait_send()
        self.pipe_copy().wait_send()


def reduce_grads(count, *refs):
    factors, pack, results, sums_o = refs[:5], refs[5], refs[6], refs[7:10]
    reducer = Reducer(count, factors, results, refs[10:23], refs[23:36])
    sums = Sums(count, reducer.rows, reducer.half, pack, sums_o, refs[36:])
    greet(reducer.partners() + sums.partners())
    sums.begin()

    def step(n, carry):
        reducer.tick(n)
        for k in range(len(sums.steps)):

            @pl.when(n == 2 * k + 2)
            def _():
                sums.step(k)

        return carry

    lax.fori_loop(0, reducer.ticks, step, 0)
    sums.close()
    reducer.close()


def reduce_call(factors, pack, count, groups):
    _, micro, rows, model = factors[0].shape
    width = factors[2].shape[3]
    half = width // count
    buffers, sems = Reducer.scratch(count, micro, rows, model, half, groups)
    inside = pl.BlockSpec(memory_space=pltpu.VMEM)
    anywhere = pl.BlockSpec(memory_space=pl.ANY)
    return pl.pallas_call(
        functools.partial(reduce_grads, count),
        in_specs=[anywhere] * 5 + [inside],
        out_specs=[anywhere] + [inside] * 3,
        out_shape=[
            jax.ShapeDtypeStruct((3, model // groups, 2 * half), BF),
            jax.ShapeDtypeStruct((8, 2 * half), F32),
            jax.ShapeDtypeStruct((16, model // groups), F32),
            jax.ShapeDtypeStruct((8, width), F32),
        ],
        scratch_shapes=buffers + sems + Sums.scratch(count, pack.shape),
        compiler_params=pltpu.CompilerParams(collective_id=1, has_side_effects=True, vmem_limit_bytes=VMEM_LIMIT),
    )(*factors, pack)


def fused_forward(count, head_dim, micro, *refs):
    (tokens, mask, value, gate_w, out_w, step_w, state_w, chan, shared) = refs[:9]
    (wv_h, wg_h, wo_h, wt_h, ws_h, pv_o, ps_o, ph_o, pn_o) = refs[9:18]
    (out_h, low_h, mix_h, inv_o, nx_o, vpre_o, spre_o, x_o, bc_o, dtc_o, gate_o, y_o, gg_o, sin_o) = refs[18:32]
    (nx_s, sc_s, wide_s, place_s, cum_s, cumt_s, acc_s, sq_s, psend, precv, sqsend, sqrecv, csend, crecv, hrecv, trecv) = refs[32:48]
    (ps_sem, pr_sem, ss_sem, sr_sem, cs_sem, cr_sem, hs_sem, hr_sem, ts_sem, tr_sem, low_sem, out_sem, mix_sem) = refs[48:61]
    (wv_s, wg_s, wo_s, ws_s, wt_s, chan_s, shared_s, w_sem, l_sem) = refs[61:70]
    q, s, g = pl.program_id(0), pl.program_id(1), pl.program_id(2)
    groups = cum_s.shape[0]
    p, t = lax.axis_index(PIPE), lax.axis_index(TENSOR)
    idx = q * micro + s
    slot = idx * groups + g
    total_idx = 2 * micro
    rows, model = tokens.shape[1], tokens.shape[2]
    state = bc_o.shape[1] // 2
    per_group = GC // head_dim
    inner_total = 2 * groups * GC
    gather = Gather(
        count,
        (value, gate_w, out_w, step_w),
        (wv_h, wg_h, wo_h, wt_h),
        ((state_w, ws_h), (chan, chan_s), (shared, shared_s)),
        refs[70:],
    )
    big = ((wv_h, wv_s), (wg_h, wg_s), (wo_h, wo_s))

    def weight_copy(step, k):
        layer, group = step // (micro * groups), lax.rem(step, groups)
        held = lax.rem(step, 2)
        return pltpu.make_async_copy(big[k][0].at[layer, :, aligned(group, GC)], big[k][1].at[held], w_sem.at[held, k])

    def layer_copies(layer):
        return (
            pltpu.make_async_copy(ws_h.at[layer], ws_s, l_sem.at[0]),
            pltpu.make_async_copy(wt_h.at[layer], wt_s, l_sem.at[1]),
        )

    def part_copy(i):
        return remote(psend.at[i], precv.at[i], ps_sem.at[i], pr_sem.at[i], PIPE, 1 - p)

    def square_copy(i):
        return remote(sqsend.at[i], sqrecv.at[i], ss_sem.at[i], sr_sem.at[i], PIPE, 1 - p)

    def chain_copy(i):
        return remote(csend.at[i], crecv.at[i], cs_sem.at[i], cr_sem.at[i], TENSOR, t + 1)

    def halo_copy(i):
        return remote(psend.at[i, rows - HALO :, :], hrecv.at[i], hs_sem.at[i], hr_sem.at[i], TENSOR, t + 1)

    def tokens_copy():
        return remote(tokens.at[:, rows - HALO :, :], trecv, ts_sem.at[0], tr_sem.at[0], TENSOR, t + 1)

    def low_copy(i):
        return pltpu.make_async_copy(psend.at[i], low_h.at[i], low_sem.at[i])

    def out_copy(i):
        return pltpu.make_async_copy(psend.at[i], out_h.at[lax.rem(i, micro)], out_sem.at[i])

    def mix_copy(i):
        return pltpu.make_async_copy(precv.at[i], mix_h.at[i], mix_sem.at[i])

    @pl.when((idx == 0) & (g == 0))
    def _():
        greet(gather.partners())

        @pl.when(t < count - 1)
        def _():
            tokens_copy().start()

        fill_places(place_s, head_dim)
        gather.first_layer()
        for k in range(3):
            weight_copy(0, k).start()
        pv_o[...] = chan_s[...]
        heads = per_group * groups // count
        half = groups * GC // count
        place, lane = iota((groups * GC, LANES), 0), iota((groups * GC, LANES), 1)
        first = half * (lane // heads) + lax.rem(lane, heads)
        used = lane < per_group * groups
        for layer in range(2):
            per_head = chan_s[layer]
            for kind in range(2):
                pick = ((place == first + kind * heads) & used).astype(F32)
                ph_o[layer, kind : kind + 1, :] = exact(per_head, pick)[7:8, :]
            ph_o[layer, 2:, :] = jnp.zeros((6, LANES), F32)
            pn_o[layer] = shared_s[layer]
            for k in range(5):
                ps_o[layer, k : k + 1, :] = shared_s[layer, 1:2, 2 * state * k : 2 * state * (k + 1)]
            ps_o[layer, 5:, :] = jnp.zeros((3, 2 * state), F32)

    columns = groups * GC // count
    late = gather.second_layer(micro * groups, lambda src: src * columns // GC)
    for step in sorted({step for step, _ in late}):

        @pl.when(slot == step)
        def _():
            for when, stage in late:
                if when == step:
                    stage()

    @pl.when((s == 0) & (g == 0))
    def _():
        for copy in layer_copies(q):
            copy.start()
        for copy in layer_copies(q):
            copy.wait()

    for k in range(3):
        weight_copy(slot, k).wait()

    @pl.when(slot + 1 < total_idx * groups)
    def _():
        for k in range(3):
            weight_copy(slot + 1, k).start()

    held = lax.rem(slot, 2)
    ws, wt, wv, wg, wo = ws_s, wt_s, wv_s.at[held], wg_s.at[held], wo_s.at[held]
    pv, ps, ph, pn = pv_o.at[q, :, aligned(g, GC)], ps_o.at[q], ph_o.at[q], pn_o.at[q]

    def normed(u):
        uf = u.astype(F32)
        return (uf * lax.rsqrt(jnp.mean(uf * uf, axis=1, keepdims=True) + EPS) * pn[0:1, :]).astype(BF)

    @pl.when((g == 0) & (q == 0))
    def _():
        nx_s[HALO:, :] = normed(tokens[s])

        @pl.when(t == 0)
        def _():
            nx_s[:HALO, :] = jnp.zeros((HALO, model), BF)

        @pl.when(t > 0)
        def _():
            @pl.when(s == 0)
            def _():
                tokens_copy().wait_recv()

            nx_s[:HALO, :] = normed(trecv[s])

    @pl.when((g == 0) & (q == 1))
    def _():
        nx_s[HALO:, :] = normed(psend[s])

        @pl.when(t == 0)
        def _():
            nx_s[:HALO, :] = jnp.zeros((HALO, model), BF)

        @pl.when(t > 0)
        def _():
            halo_copy(s).wait_recv()
            nx_s[:HALO, :] = normed(hrecv[s])

    @pl.when(g == 0)
    def _():
        nx_o[...] = nx_s[HALO:, :]
        spre = nn(nx_s[...], ws[...])
        spre_o[...] = spre
        conv = conv_rows(spre, ps, rows)
        bc = (conv * sigmoid(conv)).astype(BF)
        bc_o[...] = bc
        scores = nt(bc[:, state:], bc[:, :state])
        lower = iota((rows, rows), 0) >= iota((rows, rows), 1)
        sc_s[...] = jnp.where(lower, scores, 0.0)
        raw = nt(nx_s[HALO:, :], wt[...])
        raw = exact(raw, step_places(count, raw.shape[1], per_group * groups)) + ph[0:1, :]
        step = jnp.maximum(raw, 0.0) + jnp.log(1.0 + jnp.exp(-jnp.abs(raw)))
        cum = exact(lower.astype(F32), -step * jnp.exp(ph[1:2, :]))
        dtc_o[0] = step
        dtc_o[1] = cum
        dtc_o[2] = sigmoid(raw)
        to_end = jnp.exp(cum[rows - 1 : rows, :] - cum)
        fill_wide(wide_s, (step, step * to_end, jnp.exp(cum)))
        cum = cum * LOG2E
        group_lanes(cum, cum_s, groups, per_group)
        group_rows(cum, cumt_s, groups, per_group)
        acc_s[...] = jnp.zeros_like(acc_s)
        sq_s[...] = jnp.zeros_like(sq_s)

    pre = nn(nx_s[...], wv[...])
    vpre_o[...] = pre
    conv = conv_rows(pre, pv, rows)
    x = conv * sigmoid(conv)
    x_o[...] = x.astype(BF)
    cum, cumt, places = cum_s[g], cumt_s[g], place_s[g]
    xp = (x * nn(wide_s[0], places)).astype(BF)
    xr = (x * nn(wide_s[1], places)).astype(BF)
    local = tn(xr, bc_o[:, :state])

    @pl.when(t == 0)
    def _():
        sin_o[...] = jnp.zeros_like(sin_o)

    @pl.when(t > 0)
    def _():
        chain_copy(slot).wait_recv()
        sin_o[...] = crecv[slot]

    @pl.when(t < count - 1)
    def _():
        csend[slot] = (through_rows(cumt, rows, head_dim, state) * sin_o[...].astype(F32) + local).astype(BF)
        chain_copy(slot).start()

    lane = iota((rows, LANES), 1)
    cut = rows // 2
    within = []
    for pair in range(GC // LANES):
        cols = slice(LANES * pair, LANES * (pair + 1))
        outs = []
        for i in (2 * pair, 2 * pair + 1):
            parts = []
            for first, seen in ((0, cut), (cut, rows)):
                diff = cum[first : first + cut, i : i + 1] - cumt[i : i + 1, :seen]
                mix = (jnp.exp2(jnp.minimum(diff, 0.0)) * sc_s[first : first + cut, :seen]).astype(BF)
                parts.append(nn(mix, xp[:seen, cols]))
            outs.append(jnp.concatenate(parts, axis=0))
        within.append(jnp.where(lane < head_dim, outs[0], outs[1]))
    gate = nn(nx_s[HALO:, :], wg[...])
    gate_o[...] = gate
    carried = nt(bc_o[:, state:], sin_o[...])
    y = jnp.concatenate(within, axis=1) + pv[6:7, :] * x + nn(wide_s[2], places) * carried
    y_o[...] = y
    gated = y * (gate * sigmoid(gate))
    gg = (gated * pv[5:6, :]).astype(BF)
    gg_o[...] = gg
    squares = gated * gated
    for part in range(GC // LANES):
        sq_s[...] += squares[:, LANES * part : LANES * (part + 1)]
    acc_s[...] += nt(gg, wo[...])

    @pl.when(g == groups - 1)
    def _():
        psend[idx] = acc_s[...].astype(BF)
        sqsend[idx] = jnp.broadcast_to(jnp.sum(sq_s[...], axis=1, keepdims=True), (rows, LANES))
        part_copy(idx).start()
        square_copy(idx).start()

    def finish(i):
        j = lax.rem(i, micro)
        part_copy(i).wait()
        square_copy(i).wait()
        inverse = lax.rsqrt((sqsend[i] + sqrecv[i]) / inner_total + EPS)
        inv_o[i] = inverse
        mixed = inverse[:, 0:1] * (psend[i].astype(F32) + precv[i].astype(F32))
        precv[i] = mixed.astype(BF)
        row_mask = mask[j][:, 0:1]

        @pl.when(i < micro)
        def _():
            psend[i] = (row_mask * (tokens[j].astype(F32) + mixed)).astype(BF)

            @pl.when(t < count - 1)
            def _():
                halo_copy(j).start()

            low_copy(j).start()

        @pl.when(i >= micro)
        def _():
            psend[i] = (row_mask * (psend[j].astype(F32) + mixed)).astype(BF)

        @pl.when(i // micro == p)
        def _():
            out_copy(i).start()

        mix_copy(i).start()

    @pl.when((g == 1) & (idx > 1))
    def _():
        finish(idx - 2)

    @pl.when((g == groups - 1) & (idx == total_idx - 1))
    def _():
        finish(idx - 1)
        finish(idx)
        for i in range(total_idx):
            mix_copy(i).wait()

            @pl.when(i // micro == p)
            def _():
                out_copy(i).wait()

        for i in range(micro):
            low_copy(i).wait()

        gather.finish()

        @pl.when(t < count - 1)
        def _():
            tokens_copy().wait_send()
            for i in range(micro):
                halo_copy(i).wait_send()

            def drain(i, carry):
                chain_copy(i).wait_send()
                return carry

            lax.fori_loop(0, total_idx * groups, drain, 0)


def step_places(count, rows, all_heads):
    heads, size = all_heads // count, rows // count
    place, lane = iota((rows, LANES), 0), iota((rows, LANES), 1)
    return ((place == size * (lane // heads) + lax.rem(lane, heads)) & (lane < all_heads)).astype(F32)


def fill_places(place_s, head_dim):
    shape = place_s.shape[1:]
    head, col = lax.rem(iota(shape, 0), LANES), iota(shape, 1) // head_dim
    for g in range(place_s.shape[0]):
        place_s[g] = (head == col + g * (GC // head_dim)).astype(BF)


def fill_wide(wide_s, values):
    for k, value in enumerate(values):
        high = value.astype(BF)
        wide_s[k, :, :LANES] = high
        wide_s[k, :, LANES:] = (value - high.astype(F32)).astype(BF)


def through_rows(cumt, rows, head_dim, state):
    end = jnp.exp2(cumt[:, rows - 1 : rows])
    parts = [jnp.broadcast_to(end[i : i + 1, :], (head_dim, state)) for i in range(GC // head_dim)]
    return jnp.concatenate(parts, axis=0)


def fused_backward(count, head_dim, micro, *refs):
    (cot, tokens, out0, mask, inv, mix, vpre, spre, x, bc, dtc, gate, y, s_in) = refs[:14]
    (wv, wg, wo, ws, wt, pv, ps, ph, pn) = refs[14:23]
    (grad_h, dval_o, dgate_o, dst_o, dstep_o, sgm_o, vs_o, ss_o, hs_o, norm_o) = refs[23:33]
    (gm_s, rowsc_s, gin_s, halo_s, halo2_s, acc_s, nacc_s) = refs[33:40]
    (sct_s, scts_s, wsum_s, dbc_s, wide_s, place_s, cum_s, cumt_s, net_s, rv_s, ddir_s, k_s, rt_s, rall_s) = refs[40:54]
    (psend, precv, csend, crecv, hsend, hrecv, tsend, trecv) = refs[54:62]
    (ps_sem, pr_sem, cs_sem, cr_sem, hs_sem, hr_sem, ts_sem, tr_sem, out_sem) = refs[62:]
    turn, s, g = pl.program_id(0), pl.program_id(1), pl.program_id(2)
    groups = cum_s.shape[0]
    p, t = lax.axis_index(PIPE), lax.axis_index(TENSOR)
    idx = turn * micro + s
    slot = idx * groups + g
    total_idx = 2 * micro
    rows, model = cot.shape[1], cot.shape[2]
    state = bc.shape[1] // 2
    per_group = GC // head_dim
    inner_total = 2 * groups * GC

    def part_copy(i):
        return remote(psend.at[i], precv.at[i], ps_sem.at[i], pr_sem.at[i], PIPE, 1 - p)

    def chain_copy(i):
        return remote(csend.at[i], crecv.at[i], cs_sem.at[i], cr_sem.at[i], TENSOR, t - 1)

    def halo_copy(i):
        return remote(hsend.at[i], hrecv.at[i], hs_sem.at[i], hr_sem.at[i], TENSOR, t - 1)

    def tail_copy(i):
        return remote(tsend.at[i], trecv.at[i], ts_sem.at[i], tr_sem.at[i], TENSOR, t - 1)

    def out_copy(i):
        return pltpu.make_async_copy(psend.at[i], grad_h.at[lax.rem(i, micro)], out_sem.at[i])

    @pl.when((idx == 0) & (g == 0))
    def _():
        greet(ring_neighbours(count) + [(PIPE, 1 - p)])
        fill_places(place_s, head_dim)
        nacc_s[...] = jnp.zeros_like(nacc_s)

    @pl.when((g == 0) & (turn == 0))
    def _():
        gm_s[...] = (mask[s][:, 0:1] * cot[s].astype(F32)).astype(BF)

    @pl.when((g == 0) & (turn == 1))
    def _():
        gm_s[...] = (mask[s][:, 0:1] * psend[s].astype(F32)).astype(BF)

    @pl.when(g == 0)
    def _():
        gmf = gm_s[...].astype(F32)
        inverse = inv[...]
        dot = jnp.sum(gmf * mix[...].astype(F32), axis=1, keepdims=True)
        rowsc_s[...] = inverse * inverse * dot / inner_total
        sgm_o[...] = (gmf * inverse[:, 0:1]).astype(BF)
        scores = nt(bc[:, :state], bc[:, state:])
        first, second = iota((rows, rows), 0), iota((rows, rows), 1)
        sct_s[...] = jnp.where(second >= first, scores, 0.0)
        scts_s[...] = jnp.where(second > first, scores, 0.0)
        wsum_s[...] = jnp.zeros_like(wsum_s)
        dbc_s[...] = jnp.zeros_like(dbc_s)
        rall_s[...] = jnp.zeros_like(rall_s)
        acc_s[...] = jnp.zeros_like(acc_s)
        for part_s in (net_s, rv_s, ddir_s, k_s):
            part_s[...] = jnp.zeros_like(part_s)
        cum = dtc[1]
        fill_wide(wide_s, (dtc[0], jnp.exp(cum[rows - 1 : rows, :] - cum), jnp.exp(cum)))
        cum = cum * LOG2E
        group_lanes(cum, cum_s, groups, per_group)
        group_rows(cum, cumt_s, groups, per_group)

    cum, cumt, places = cum_s[g], cumt_s[g], place_s[g]
    fromx = nn(wide_s[2], places)

    gs = nn(gm_s[...], wo[...])
    inverse, shrink = inv[:, 0:1], rowsc_s[:, 0:1]
    gv, yv = gate[...], y[...]
    sig = sigmoid(gv)
    silu = gv * sig
    gated = yv * silu
    dgain = jnp.sum(gs * gated * inverse, axis=0, keepdims=True)
    dgated = inverse * (gs * pv[5:6, :]) - gated * shrink
    dgate = (dgated * yv * (sig * (1.0 + gv * (1.0 - sig)))).astype(BF)
    dgate_o[...] = dgate
    dyb = (dgated * silu).astype(BF)
    dyf = dyb.astype(F32)
    dyef = dyf * fromx
    dye = dyef.astype(BF)
    dsl = tn(dye, bc[:, state:])

    @pl.when(t == count - 1)
    def _():
        gin_s[...] = jnp.zeros_like(gin_s)

    @pl.when(t < count - 1)
    def _():
        chain_copy(slot).wait_recv()
        gin_s[...] = crecv[slot]

    @pl.when(t > 0)
    def _():
        csend[slot] = (through_rows(cumt, rows, head_dim, state) * gin_s[...].astype(F32) + dsl).astype(BF)
        chain_copy(slot).start()

    stepx = nn(wide_s[0], places)
    endx = nn(wide_s[1], places)
    xf = x[...].astype(F32)
    xp = (xf * stepx).astype(BF)
    xr = (xf * stepx * endx).astype(BF)
    gb = nt(bc[:, :state], gin_s[...])
    cs = nt(bc[:, state:], s_in[...])
    dbc_s[:, :state] += nn(xr, gin_s[...])
    dbc_s[:, state:] += nn(dye, s_in[...])

    lane = iota((rows, LANES), 1)
    cut = rows // 2
    blocks = ((slice(0, cut), slice(0, rows)), (slice(cut, rows), slice(cut, rows)))
    wsums = [wsum_s[js, at] for js, at in blocks]
    colsums = [jnp.zeros((cut, LANES), F32)] * 2
    within = []
    for pair in range(GC // LANES):
        cols = slice(LANES * pair, LANES * (pair + 1))
        xpp, dyp = xp[:, cols], dyb[:, cols]
        outs = []
        for side in range(2):
            i = 2 * pair + side
            mine = (lane < head_dim) if side == 0 else (lane >= head_dim)
            xph = jnp.where(mine, xpp, jnp.zeros_like(xpp))
            parts, rowsums = [], []
            for k, (js, at) in enumerate(blocks):
                decay = jnp.exp2(jnp.minimum(cumt[i : i + 1, at] - cum[js, i : i + 1], 0.0))
                parts.append(nn((decay * sct_s[js, at]).astype(BF), dyp[at]))
                weight = decay * nt(xph[js], dyp[at])
                wsums[k] = wsums[k] + weight
                pairs = (weight * scts_s[js, at]).astype(BF)
                colsums[k] = colsums[k] + nn(pairs, (lane[at] == i + per_group * g).astype(BF))
                rowsums.append(jnp.sum(pairs.astype(F32), axis=0, keepdims=True))
            outs.append(jnp.concatenate(parts, axis=0))
            rt_s[g, i : i + 1, :cut] = rowsums[0][:, :cut]
            rt_s[g, i : i + 1, cut:] = rowsums[0][:, cut:] + rowsums[1]
        within.append(jnp.where(lane < head_dim, outs[0], outs[1]))
    for k, (js, at) in enumerate(blocks):
        wsum_s[js, at] = wsums[k]
    colsum = jnp.concatenate(colsums, axis=0)
    u = jnp.concatenate(within, axis=1) + endx * gb

    heads = (iota((GC, LANES), 0) // head_dim + per_group * g == iota((GC, LANES), 1)).astype(BF)
    ddir_s[...] += nn((xf * u).astype(BF), heads)
    net_s[...] += nn((dyef * cs).astype(BF), heads) - colsum
    rv_s[...] += nn((xf * gb).astype(BF), heads)
    inner = (gin_s[...].astype(F32) * s_in[...].astype(F32)).astype(BF)
    per_channel = nt(jnp.ones((16, inner.shape[1]), BF), inner)
    k_s[...] += nn(per_channel.astype(BF), heads)[:8]

    dx = stepx * u + pv[6:7, :] * dyf
    dconv = dx * silu_slope(conv_rows(vpre, pv, rows))

    @pl.when(t > 0)
    def _():
        hsend[slot] = dconv[:8, :]
        halo_copy(slot).start()

    sums = conv_sums(dconv, vpre, rows)
    sums.append(dgain)
    sums.append(jnp.sum(dyf * xf, axis=0, keepdims=True))
    sums.append(jnp.zeros((1, GC), F32))
    vs_o[...] = jnp.concatenate(sums, axis=0)
    acc_s[...] += nt(dgate, wg[...])

    @pl.when(t == count - 1)
    def _():
        halo_s[...] = jnp.zeros_like(halo_s)

    @pl.when(t < count - 1)
    def _():
        halo_copy(slot).wait_recv()
        halo_s[...] = hrecv[slot]

    dval = conv_transposed(dconv, halo_s[...], pv, rows).astype(BF)
    dval_o[...] = dval
    acc_s[...] += nt(dval, wv[...])

    @pl.when(g == groups - 1)
    def _():
        first, second = iota((rows, rows), 0), iota((rows, rows), 1)
        weights = jnp.where(second >= first, wsum_s[...], 0.0).astype(BF)
        db = dbc_s[:, :state] + nn(weights, bc[:, state:])
        dc = dbc_s[:, state:] + tn(weights, bc[:, :state])
        dsc = jnp.concatenate([db, dc], axis=1) * silu_slope(conv_rows(spre, ps, rows))

        @pl.when(t > 0)
        def _():
            tsend[idx] = dsc[:8, :]
            tail_copy(idx).start()

        ssums = conv_sums(dsc, spre, rows)
        ssums.append(jnp.zeros((3, 2 * state), F32))
        ss_o[...] = jnp.concatenate(ssums, axis=0)
        for other in range(groups):
            shift = per_group * other
            rall_s[shift : shift + per_group, :] = rt_s[other, 0:per_group, :]
        total, step = dtc[1], dtc[0]
        last = total[rows - 1 : rows, :]
        net = net_s[...] + rall_s[...].T
        rv = rv_s[...] * step * jnp.exp(last - total)
        da = exact((second >= first).astype(F32), net) + exact((second < first).astype(F32), rv)
        da = da + jnp.exp(last) * k_s[0:1, :]
        ddir = ddir_s[...]
        rate = jnp.exp(ph[1:2, :])
        dstep = (ddir - da * rate) * dtc[2]
        dstep_o[...] = dstep.astype(BF)
        hs_o[...] = jnp.concatenate(
            [
                jnp.sum(dstep, axis=0, keepdims=True),
                jnp.sum(-da * dtc[0] * rate, axis=0, keepdims=True),
                jnp.zeros((6, LANES), F32),
            ],
            axis=0,
        )

        @pl.when(t == count - 1)
        def _():
            halo2_s[...] = jnp.zeros_like(halo2_s)

        @pl.when(t < count - 1)
        def _():
            tail_copy(idx).wait_recv()
            halo2_s[...] = trecv[idx]

        dst = conv_transposed(dsc, halo2_s[...], ps, rows).astype(BF)
        dst_o[...] = dst
        psend[idx] = (acc_s[...] + nt(dst, ws[...]) + nn(dstep_o[...], wt[...])).astype(BF)
        part_copy(idx).start()

    def finish(i):
        j = lax.rem(i, micro)
        part_copy(i).wait()
        which = 1 - i // micro
        row_mask = mask[j][:, 0:1]

        def close(u, incoming):
            uf = u.astype(F32)
            grad_normed = psend[i].astype(F32) + precv[i].astype(F32)
            root_inv = lax.rsqrt(jnp.mean(uf * uf, axis=1, keepdims=True) + EPS)
            nacc_s[which] += jnp.broadcast_to(jnp.sum(grad_normed * uf * root_inv, axis=0, keepdims=True), (8, model))
            weighted = grad_normed * pn[which][0:1, :]
            shared = jnp.mean(weighted * uf, axis=1, keepdims=True) * root_inv * root_inv * root_inv
            kept = (row_mask * incoming.astype(F32)).astype(BF).astype(F32)
            psend[i] = (root_inv * weighted - uf * shared + kept).astype(BF)

        @pl.when(i < micro)
        def _():
            close(out0[j], cot[j])

        @pl.when(i >= micro)
        def _():
            close(tokens[j], psend[j])

        @pl.when(which == p)
        def _():
            out_copy(i).start()

    @pl.when((g == 1) & (idx > 1))
    def _():
        finish(idx - 2)

    @pl.when((g == groups - 1) & (idx == total_idx - 1))
    def _():
        finish(idx - 1)
        finish(idx)
        norm_o[...] = nacc_s[...]
        for i in range(total_idx):

            @pl.when(1 - i // micro == p)
            def _():
                out_copy(i).wait()

        @pl.when(t > 0)
        def _():
            for i in range(total_idx):
                tail_copy(i).wait_send()

            def drain(i, carry):
                chain_copy(i).wait_send()
                halo_copy(i).wait_send()
                return carry

            lax.fori_loop(0, total_idx * groups, drain, 0)


def all_of(shape, buffers=2):
    spec = functools.partial(pl.BlockSpec, shape, lambda q, s, g: (0,) * len(shape))
    return spec(pipeline_mode=pl.Buffered(buffers)) if buffers != 2 else spec()


def fused_specs(turned):
    def layer(q):
        return 1 - q if turned else q

    def item(*shape):
        zeros = (0,) * len(shape)
        return pl.BlockSpec((None, None) + shape, lambda q, s, g: (layer(q), s) + zeros)

    def item_cols(rows):
        return pl.BlockSpec((None, None, rows, GC), lambda q, s, g: (layer(q), s, 0, g))

    def item_rows(cols):
        return pl.BlockSpec((None, None, GC, cols), lambda q, s, g: (layer(q), s, g, 0))

    def layer_cols(rows):
        return pl.BlockSpec((None, rows, GC), lambda q, s, g: (layer(q), 0, g))

    def layer_all(*shape):
        zeros = (0,) * len(shape)
        return pl.BlockSpec((None,) + shape, lambda q, s, g: (layer(q),) + zeros)

    return item, item_cols, item_rows, layer_cols, layer_all


def forward_call(tokens, mask, shards, chan, shared, count, groups_dp, head_dim):
    micro, rows, model = tokens.shape
    value, gate, out, step, state_w = shards
    half, states = value.shape[1] // 2, state_w.shape[1]
    width, state = half * count, states // 2
    groups = width // GC
    item, item_cols, item_rows, layer_cols, layer_all = fused_specs(False)
    slots = 2 * micro
    dma = pltpu.SemaphoreType.DMA
    vmem = pltpu.VMEM
    anywhere = pl.BlockSpec(memory_space=pl.ANY)
    ins = [
        (tokens, all_of(tokens.shape, 1)),
        (mask, all_of(mask.shape, 1)),
        (value, anywhere),
        (gate, anywhere),
        (out, anywhere),
        (step, anywhere),
        (state_w, anywhere),
        (chan, anywhere),
        (shared, anywhere),
    ]
    pair = (2, micro)
    step_rows = step.shape[0] // 2 * count
    outs = [
        (((2, model, width), BF), anywhere),
        (((2, model, width), BF), anywhere),
        (((2, model, width), BF), anywhere),
        (((2, step_rows, model), BF), anywhere),
        (((2, model, states), BF), anywhere),
        (((2, 8, width), F32), all_of((2, 8, width))),
        (((2, 8, states), F32), all_of((2, 8, states))),
        (((2, 8, LANES), F32), all_of((2, 8, LANES))),
        (((2,) + shared.shape, F32), all_of((2,) + shared.shape)),
        (((micro, rows, model), BF), anywhere),
        (((micro, rows, model), BF), anywhere),
        (((slots, rows, model), BF), anywhere),
        (((slots, rows, LANES), F32), all_of((slots, rows, LANES))),
        ((pair + (rows, model), BF), item(rows, model)),
        ((pair + (rows + HALO, width), F32), item_cols(rows + HALO)),
        ((pair + (rows + HALO, states), F32), item(rows + HALO, states)),
        ((pair + (rows, width), BF), item_cols(rows)),
        ((pair + (rows, states), BF), item(rows, states)),
        ((pair + (3, rows, LANES), F32), item(3, rows, LANES)),
        ((pair + (rows, width), F32), item_cols(rows)),
        ((pair + (rows, width), F32), item_cols(rows)),
        ((pair + (rows, width), BF), item_cols(rows)),
        ((pair + (width, state), BF), item_rows(state)),
    ]
    scratch = [
        vmem((rows + HALO, model), BF),
        vmem((rows, rows), F32),
        vmem((3, rows, 2 * LANES), BF),
        vmem((groups, 2 * LANES, GC), BF),
        vmem((groups, rows, LANES), F32),
        vmem((groups, 8, rows), F32),
        vmem((rows, model), F32),
        vmem((rows, LANES), F32),
        vmem((slots, rows, model), BF),
        vmem((slots, rows, model), BF),
        vmem((slots, rows, LANES), F32),
        vmem((slots, rows, LANES), F32),
        vmem((slots * groups, GC, state), BF),
        vmem((slots * groups, GC, state), BF),
        vmem((micro, HALO, model), BF),
        vmem((micro, HALO, model), BF),
        dma((slots,)),
        dma((slots,)),
        dma((slots,)),
        dma((slots,)),
        dma((slots * groups,)),
        dma((slots * groups,)),
        dma((micro,)),
        dma((micro,)),
        dma((1,)),
        dma((1,)),
        dma((micro,)),
        dma((slots,)),
        dma((slots,)),
        vmem((2, model, GC), BF),
        vmem((2, model, GC), BF),
        vmem((2, model, GC), BF),
        vmem((model, states), BF),
        vmem((step_rows, model), BF),
        vmem((2, 8, width), F32),
        vmem((2,) + shared.shape, F32),
        dma((2, 3)),
        dma((2,)),
    ] + Gather.scratch(count)
    kernel = functools.partial(fused_forward, count, head_dim, micro)
    flops = slots * (6 * rows * model * width + 6 * rows * rows * width)
    options = fused_options(pair + (groups,), ins, outs, scratch, 2, flops, 60 * slots * rows * width)
    return pl.pallas_call(kernel, **options)(*[array for array, _ in ins])


def fused_options(grid, ins, outs, scratch, collective, flops, traffic):
    return dict(
        grid=grid,
        in_specs=[spec for _, spec in ins],
        out_specs=[spec for _, spec in outs],
        out_shape=[jax.ShapeDtypeStruct(*kind) for kind, _ in outs],
        scratch_shapes=scratch,
        cost_estimate=pl.CostEstimate(flops=flops, bytes_accessed=traffic, transcendentals=0),
        compiler_params=pltpu.CompilerParams(
            collective_id=collective,
            has_side_effects=True,
            vmem_limit_bytes=VMEM_LIMIT,
            dimension_semantics=(SEQUENTIAL,) * len(grid),
        ),
    )


def backward_fused_call(cot, tokens, out0, mask, kept, w, par, count, head_dim):
    micro, rows, model = tokens.shape
    width, states = w.value.shape[2], w.state.shape[2]
    state = states // 2
    groups = width // GC
    item, item_cols, item_rows, layer_cols, layer_all = fused_specs(True)
    slots = 2 * micro
    dma = pltpu.SemaphoreType.DMA
    vmem = pltpu.VMEM
    ins = [
        (cot, all_of(cot.shape, 1)),
        (tokens, all_of(tokens.shape, 1)),
        (out0, all_of(out0.shape, 1)),
        (mask, all_of(mask.shape, 1)),
        (kept.inv, item(rows, LANES)),
        (kept.mix, item(rows, model)),
        (kept.vpre, item_cols(rows + HALO)),
        (kept.spre, item(rows + HALO, states)),
        (kept.x, item_cols(rows)),
        (kept.bc, item(rows, states)),
        (kept.dtc, item(3, rows, LANES)),
        (kept.gate, item_cols(rows)),
        (kept.y, item_cols(rows)),
        (kept.s_in, item_rows(state)),
        (w.value, layer_cols(model)),
        (w.gate, layer_cols(model)),
        (w.out, layer_cols(model)),
        (w.state, layer_all(model, states)),
        (w.step, layer_all(LANES, model)),
        (par.value, layer_cols(8)),
        (par.state, layer_all(8, states)),
        (par.head, layer_all(8, LANES)),
        (par.norm, all_of(par.norm.shape, 1)),
    ]
    pair = (2, micro)
    outs = [
        (((micro, rows, model), BF), pl.BlockSpec(memory_space=pl.ANY)),
        ((pair + (rows, width), BF), item_cols(rows)),
        ((pair + (rows, width), BF), item_cols(rows)),
        ((pair + (rows, states), BF), item(rows, states)),
        ((pair + (rows, LANES), BF), item(rows, LANES)),
        ((pair + (rows, model), BF), item(rows, model)),
        ((pair + (8, width), F32), item_cols(8)),
        ((pair + (8, states), F32), item(8, states)),
        ((pair + (8, LANES), F32), item(8, LANES)),
        (((2, 8, model), F32), all_of((2, 8, model))),
    ]
    lanes = vmem((rows, LANES), F32)
    square = vmem((rows, rows), F32)
    scratch = [
        vmem((rows, model), BF),
        vmem((rows, LANES), F32),
        vmem((GC, state), BF),
        vmem((8, GC), F32),
        vmem((8, states), F32),
        vmem((rows, model), F32),
        vmem((2, 8, model), F32),
        square,
        square,
        square,
        vmem((rows, states), F32),
        vmem((3, rows, 2 * LANES), BF),
        vmem((groups, 2 * LANES, GC), BF),
        vmem((groups, rows, LANES), F32),
        vmem((groups, 8, rows), F32),
        lanes,
        lanes,
        lanes,
        vmem((8, LANES), F32),
        vmem((groups, 8, rows), F32),
        vmem((LANES, rows), F32),
        vmem((slots, rows, model), BF),
        vmem((slots, rows, model), BF),
        vmem((slots * groups, GC, state), BF),
        vmem((slots * groups, GC, state), BF),
        vmem((slots * groups, 8, GC), F32),
        vmem((slots * groups, 8, GC), F32),
        vmem((slots, 8, states), F32),
        vmem((slots, 8, states), F32),
        dma((slots,)),
        dma((slots,)),
        dma((slots * groups,)),
        dma((slots * groups,)),
        dma((slots * groups,)),
        dma((slots * groups,)),
        dma((slots,)),
        dma((slots,)),
        dma((slots,)),
    ]
    kernel = functools.partial(fused_backward, count, head_dim, micro)
    flops = slots * (8 * rows * model * width + 16 * rows * rows * width)
    options = fused_options(pair + (groups,), ins, outs, scratch, 3, flops, 60 * slots * rows * width)
    return pl.pallas_call(kernel, **options)(*[array for array, _ in ins])


def fused_body(
    tokens_in,
    cotangent,
    lengths,
    in_gate,
    in_value,
    in_state,
    in_step,
    out_proj,
    norm_gain,
    conv_value,
    conv_state,
    bias_value,
    bias_state,
    step_bias,
    decay_log,
    skip_gain,
    gate_gain,
):
    layer, group, block = lax.axis_index(PIPE), lax.axis_index(DP), lax.axis_index(TENSOR)
    blocks, groups = lax.axis_size(TENSOR), lax.axis_size(DP)
    first_half = layer == 0
    micro, rows, model = tokens_in.shape
    shard_rows = in_value.shape[1]
    half = in_value.shape[2] // 2
    heads = step_bias.shape[1] // 2
    head_dim = half // heads
    width = half * blocks
    all_heads = heads * blocks
    states = in_state.shape[2]

    row = jnp.arange(2 * HALO)[:, None]
    head = jnp.arange(2 * heads)[None, :]
    step_rows = (row == head // heads * HALO + lax.rem(head, heads)).astype(BF)
    step_shard = nt(step_rows, in_step[0]).astype(BF)
    both = jnp.concatenate([step_bias.reshape(2, heads), decay_log.reshape(2, heads)], axis=1)
    per_head = jnp.pad(both, ((0, 0), (0, half - 2 * heads))).reshape(1, 2 * half)
    skip = jnp.repeat(skip_gain, head_dim, axis=1)
    channel = jnp.concatenate([conv_value[0], bias_value, gate_gain, skip, per_head], axis=0)
    state_row = jnp.concatenate([conv_state[0].reshape(1, -1), bias_state], axis=1)
    shared = jnp.concatenate([norm_gain, jnp.pad(state_row, ((0, 6), (0, model - 5 * states))), norm_gain], axis=0)

    valid = block * rows + jnp.arange(rows)[None, :] < lengths[:, None]
    mask = jnp.broadcast_to(valid.astype(F32)[:, :, None], (micro, rows, LANES))

    shards = (in_value[0], in_gate[0], out_proj[0], step_shard, in_state[0])
    (wv, wg, wo, wt, ws, pv, ps, ph, pn, out, low_out, mix, inv, nx, vpre, spre, x, bc, dtc, gate, y, gg, s_in) = forward_call(
        tokens_in, mask, shards, channel, shared, blocks, groups, head_dim
    )
    places = step_places(blocks, wt.shape[1], all_heads).astype(BF)
    step_w = jnp.stack([tn(places, wt[q]).astype(BF) for q in range(2)])
    w = Bundle(value=wv, gate=wg, out=wo, state=ws, step=step_w)
    par = Bundle(value=pv, head=ph, state=ps, norm=pn)
    kept = Bundle(
        inv=inv.reshape(2, micro, rows, LANES),
        mix=mix.reshape(2, micro, rows, model),
        vpre=vpre,
        spre=spre,
        x=x,
        bc=bc,
        dtc=dtc,
        gate=gate,
        y=y,
        s_in=s_in,
    )
    grads, dval, dgate, dst, dstep, sgm, vsums, ssums, hsums, nsums = backward_fused_call(
        cotangent, tokens_in, low_out, mask, kept, w, par, blocks, head_dim
    )

    def long(value, q):
        return value[q].reshape(micro * rows, value.shape[3])

    lane = jnp.arange(LANES)[:, None]
    by_block = (8 * (lane // heads) + lax.rem(lane, heads) == jnp.arange(LANES)[None, :]) & (lane < all_heads)
    pack, turned = [], []
    for q in range(2):
        normed = long(nx, q)
        turned.append(tn(long(dst, q), normed))
        step_lanes = nn(long(dstep, q), by_block.astype(BF)).astype(BF)
        step_grad = tn(step_lanes[:, : 8 * blocks], normed)
        ssum, hsum = jnp.sum(ssums[q], axis=0), jnp.sum(hsums[q], axis=0)
        rest = [
            nsums[q, 0][None],
            jnp.pad(ssum[:5].reshape(1, -1), ((0, 0), (0, width - 5 * states))),
            jnp.zeros((6, width), F32),
        ]
        hsum = hsum[:2, :all_heads].reshape(2, blocks, heads).transpose(1, 0, 2).reshape(blocks, 2 * heads)
        hsum = jnp.pad(hsum, ((0, 0), (0, half - 2 * heads))).reshape(1, width)
        pack.append(jnp.concatenate([jnp.sum(vsums[q], axis=0)[:7], hsum, step_grad] + rest, axis=0))
    turned = lax.psum_scatter(
        jnp.concatenate(turned, axis=0), (PIPE, DP, TENSOR), scatter_dimension=0, tiled=True
    )
    pack = jnp.stack(pack)
    factors = (nx, sgm, dval, dgate, gg)
    large, chan, step_grad, rest = reduce_call(factors, pack, blocks, groups)
    grad_value, grad_gate, grad_out = [large[w].astype(F32) for w in range(3)]

    step_grad = step_grad.reshape(2, 8, shard_rows)[:, :heads].reshape(2 * heads, shard_rows).T
    grad_state = turned.T
    position = group * blocks + block
    ranks = groups * blocks

    def share(value):
        size = value.shape[-1] // ranks
        return lax.dynamic_slice_in_dim(value, position * size, size, value.ndim - 1)

    head_sums = chan[7].reshape(2, half)[:, : 2 * heads].reshape(2, 2, heads).transpose(1, 0, 2).reshape(2, -1)
    norm_sum = share(rest[0])
    conv_sum = share(rest[1, : 5 * states].reshape(5, states))
    return (
        out[None],
        grads[None],
        grad_gate[None],
        grad_value[None],
        grad_state[None],
        step_grad[None],
        grad_out[None],
        norm_sum[None],
        chan[None, :4],
        conv_sum[None, :4],
        chan[None, 4],
        conv_sum[None, 4],
        head_sums[None, 0],
        head_sums[None, 1],
        jnp.sum(chan[6].reshape(2 * heads, head_dim), axis=1)[None],
        chan[None, 5],
    )


def body(
    tokens_in,
    cotangent,
    lengths,
    in_gate,
    in_value,
    in_state,
    in_step,
    out_proj,
    norm_gain,
    conv_value,
    conv_state,
    bias_value,
    bias_state,
    step_bias,
    decay_log,
    skip_gain,
    gate_gain,
):
    layer = lax.axis_index(PIPE)
    block = lax.axis_index(TENSOR)
    blocks = lax.axis_size(TENSOR)
    group = lax.axis_index(DP)
    groups = lax.axis_size(DP)
    first_half = layer == 0
    micro, rows, model = tokens_in.shape
    shard_rows = in_value.shape[1]
    half = in_value.shape[2] // 2
    heads = step_bias.shape[1] // 2
    head_dim = half // heads
    width = half * blocks
    all_heads = heads * blocks
    states = in_state.shape[2]
    state = states // 2
    inner_total = 2 * width

    def halves(value):
        keep = lax.dynamic_slice_in_dim(value, layer * half_of(value), half_of(value), value.ndim - 1)
        send = lax.dynamic_slice_in_dim(value, (1 - layer) * half_of(value), half_of(value), value.ndim - 1)
        return by_layer(keep, swap_pipe(send))

    def half_of(value):
        return value.shape[-1] // 2

    def by_layer(own, other):
        return jnp.where(first_half, own, other), jnp.where(first_half, other, own)

    channel = jnp.concatenate([conv_value[0], bias_value, gate_gain], axis=0)
    channel_both = halves(channel)
    head_both = halves(jnp.concatenate([step_bias, decay_log, skip_gain], axis=0))
    flat_heads = [jnp.pad(v.reshape(1, 3 * heads), ((0, 0), (0, half - 3 * heads))) for v in head_both]
    packed = gather_tensor(jnp.concatenate(list(channel_both) + flat_heads + [jnp.zeros((2, half), F32)], axis=0))
    shared = jnp.concatenate([norm_gain[0], conv_state[0].reshape(-1), bias_state[0]], axis=0)
    shared_both = by_layer(shared, swap_pipe(shared))
    params = []
    for q in range(2):
        per_head = packed[12 + q].reshape(blocks, half)[:, : 3 * heads].reshape(blocks, 3, heads)
        per_head = per_head.transpose(1, 0, 2).reshape(3, all_heads)
        skip = jnp.repeat(per_head[2:3], head_dim, axis=1)
        value_par = jnp.concatenate([packed[6 * q : 6 * q + 6], skip, jnp.zeros((1, width), F32)], axis=0)
        head_par = jnp.pad(per_head, ((0, 5), (0, LANES - all_heads)))
        state_par = jnp.concatenate(
            [
                shared_both[q][model : model + 4 * states].reshape(4, states),
                shared_both[q][model + 4 * states :].reshape(1, states),
                jnp.zeros((3, states), F32),
            ],
            axis=0,
        )
        params.append(Bundle(value=value_par, head=head_par, state=state_par, norm=shared_both[q][:model]))

    step_both = halves(in_step[0])
    step_all = gather_tensor(jnp.concatenate(step_both, axis=1)).reshape(shard_rows, blocks, 2, heads)
    state_both = by_layer(in_state[0], swap_pipe(in_state[0]))
    value_both, gate_both, out_both = halves(in_value[0]), halves(in_gate[0]), halves(out_proj[0])
    weights = []
    for q in range(2):
        step_q = jnp.pad(step_all[:, :, q].reshape(shard_rows, all_heads), ((0, 0), (0, LANES - all_heads)))
        small = gather_dp(jnp.concatenate([state_both[q], step_q], axis=1))
        weights.append(
            Bundle(
                state=small[:, :states],
                step=small[:, states:],
                value=gather_dp(gather_tensor(value_both[q])),
                gate=gather_dp(gather_tensor(gate_both[q])),
                out=gather_dp(gather_tensor(out_both[q])),
            )
        )

    masks = [
        (block * rows + jnp.arange(rows) < lengths[s]).astype(F32)[:, None] for s in range(micro)
    ]

    def forward(u, s, q):
        w, par = weights[q], params[q]
        ext = jnp.concatenate([shift_tensor(u[-HALO:], 1), u], axis=0).astype(F32)
        root_inv = lax.rsqrt(jnp.mean(ext * ext, axis=1, keepdims=True) + EPS)
        nx = (ext * root_inv * par.norm[None, :]).astype(BF)
        vpre, spre, x, bc, dtc, yw, loc = front_call(nx, w, par, head_dim, state)
        through = jnp.repeat(jnp.exp(dtc[1, rows - 1, :all_heads]), head_dim)[:, None]
        s_in = jnp.zeros((width, state), BF)
        for k in range(1, blocks):
            sent = (through * s_in.astype(F32) + loc).astype(BF)
            got = lax.ppermute(sent, TENSOR, [(k - 1, k)])
            s_in = got if k == 1 else jnp.where(block == k, got, s_in)
        gate, y, gg, part, squares = finish_call(nx, w, par, yw, s_in, bc, dtc, head_dim)
        total = squares[:, 0]
        total = total + swap_pipe(total)
        inverse = lax.rsqrt(total / inner_total + EPS)[:, None]
        mixed = inverse * (part.astype(F32) + swap_pipe(part).astype(F32))
        result = (masks[s] * (u.astype(F32) + mixed)).astype(BF)
        kept = Bundle(
            u=u, nx=nx, root_inv=root_inv[HALO:], vpre=vpre, spre=spre, x=x, bc=bc, dtc=dtc, s_in=s_in, through=through,
            gate=gate, y=y, gg=gg, inverse=inverse, mixed=mixed,
        )
        return result, kept

    def backward(incoming, s, q, kept):
        w, par = weights[q], params[q]
        gm = (masks[s] * incoming.astype(F32)).astype(BF)
        gmf = gm.astype(F32)
        inverse = kept.inverse
        dot = jnp.sum(gmf * kept.mixed, axis=1, keepdims=True)
        shrink = inverse * inverse * dot / inner_total
        rowsc = jnp.concatenate([inverse, shrink, jnp.zeros((rows, LANES - 2), F32)], axis=1)
        dy, dgate, dsl, dgain = gate_call(gm, w, par, kept.y, kept.gate, rowsc, kept.bc, kept.dtc, head_dim)
        g_in = jnp.zeros((width, state), BF)
        for k in range(blocks - 2, -1, -1):
            sent = (kept.through * g_in.astype(F32) + dsl).astype(BF)
            got = lax.ppermute(sent, TENSOR, [(k + 1, k)])
            g_in = got if k == blocks - 2 else jnp.where(block == k, got, g_in)
        dconv, dsc, dstep, vsums, ssums, hsums = backward_call(
            dy, kept.x, kept.vpre, kept.spre, kept.bc, kept.dtc, kept.s_in, g_in, par, head_dim
        )
        halo = shift_tensor(jnp.concatenate([dconv[:8], dsc[:8]], axis=1), -1)
        dval, dst, part = conv_call(dconv, halo, dsc, dgate, dstep, w, par)
        grad_normed = part.astype(F32) + swap_pipe(part).astype(F32)
        uf, root_inv = kept.u.astype(F32), kept.root_inv
        grad_norm = jnp.sum(grad_normed * uf * root_inv, axis=0)
        weighted = grad_normed * par.norm[None, :]
        grad_u = root_inv * weighted - uf * root_inv**3 * jnp.mean(weighted * uf, axis=1, keepdims=True) + gmf
        scaled_gm = (gmf * inverse).astype(BF)
        channel_sums = jnp.concatenate([vsums[:5], dgain[:1], vsums[5:6]], axis=0)
        sums = (channel_sums, ssums[:5], hsums[:2, :all_heads], grad_norm)
        return grad_u.astype(BF), (dval, dgate, dst, dstep, scaled_gm), sums

    outs, kept = [], []
    current = [tokens_in[s] for s in range(micro)]
    for q in range(2):
        pairs = [forward(current[s], s, q) for s in range(micro)]
        current = [pair[0] for pair in pairs]
        outs.append(jnp.stack(current))
        kept.append([pair[1] for pair in pairs])

    grads = [None, None]
    reduced = [None, None]
    incoming = [cotangent[s] for s in range(micro)]
    for q in (1, 0):
        results = [backward(incoming[s], s, q, kept[q][s]) for s in range(micro)]
        incoming = [r[0] for r in results]
        grads[q] = jnp.stack(incoming)
        stacked = [jnp.concatenate([r[1][k] for r in results], axis=0) for k in range(5)]
        dval, dgate, dst, dstep, scaled_gm = stacked
        normed = jnp.concatenate([kept[q][s].nx[HALO:] for s in range(micro)], axis=0)
        gg = jnp.concatenate([kept[q][s].gg for s in range(micro)], axis=0)
        sums = [functools.reduce(jnp.add, [r[2][k] for r in results]) for k in range(4)]

        big = [tn(scaled_gm, gg).astype(BF), tn(normed, dgate).astype(BF), tn(normed, dval).astype(BF)]
        big = [reduce_tensor(take_cols(reduce_dp(v))) for v in big]
        turned = reduce_dp(tn(dst, normed).astype(BF))
        turned = reduce_tensor(take_first(turned.reshape(blocks, -1, model)))
        step_grad = tn(dstep, normed)[:all_heads]
        by_block = jnp.concatenate(
            [
                sums[0].reshape(7, blocks, half).transpose(1, 0, 2).reshape(blocks, -1),
                step_grad.reshape(blocks, -1),
                sums[2].reshape(2, blocks, heads).transpose(1, 0, 2).reshape(blocks, -1),
            ],
            axis=1,
        )
        per_block = reduce_tensor(take_first(sum_all_dp(by_block)))
        common = sum_all_tensor(sum_all_dp(jnp.concatenate([sums[1].reshape(-1), sums[3]], axis=0)))
        reduced[q] = (big, turned, per_block, common)

    def own_and_other(kind):
        return jnp.where(first_half, kind(0), kind(1)), jnp.where(first_half, kind(1), kind(0))

    def join(kind):
        own, other = own_and_other(kind)
        got = swap_pipe(other)
        return jnp.where(first_half, own, got), jnp.where(first_half, got, own)

    def columns(k):
        low, high = join(lambda q: reduced[q][0][k].astype(BF))
        return jnp.concatenate([low, high], axis=1).astype(F32)

    grad_out, grad_gate, grad_value = columns(0), columns(1), columns(2)
    own, other = own_and_other(lambda q: reduced[q][1])
    grad_state = (own + swap_pipe(other.astype(BF)).astype(F32)).T
    low, high = join(lambda q: reduced[q][2])
    cut1, cut2 = 7 * half, 7 * half + heads * model
    chan = jnp.concatenate([low[:cut1].reshape(7, half), high[:cut1].reshape(7, half)], axis=1)
    step_grad = jnp.concatenate([low[cut1:cut2].reshape(heads, model), high[cut1:cut2].reshape(heads, model)], axis=0)
    step_grad = lax.dynamic_slice_in_dim(step_grad, group * shard_rows, shard_rows, 1).T
    head_sums = jnp.concatenate([low[cut2:].reshape(2, heads), high[cut2:].reshape(2, heads)], axis=1)
    own, other = own_and_other(lambda q: reduced[q][3])
    conv_sum = own[: 5 * states] + swap_pipe(other[: 5 * states])
    norm_sum = own[5 * states :]
    position = group * blocks + block
    ranks = groups * blocks

    def share(value):
        size = value.shape[-1] // ranks
        return lax.dynamic_slice_in_dim(value, position * size, size, value.ndim - 1)

    conv_sum = share(conv_sum.reshape(5, states))
    return (
        jnp.where(first_half, outs[0], outs[1])[None],
        jnp.where(first_half, grads[0], grads[1])[None],
        grad_gate[None],
        grad_value[None],
        grad_state[None],
        step_grad[None],
        grad_out[None],
        share(norm_sum)[None],
        chan[None, :4],
        conv_sum[None, :4],
        chan[None, 4],
        conv_sum[None, 4],
        head_sums[None, 0],
        head_sums[None, 1],
        jnp.sum(chan[6].reshape(2 * heads, head_dim), axis=1)[None],
        chan[None, 5],
    )


def solution(mesh):
    in_specs = (
        P(DP, TENSOR, None),
        P(DP, TENSOR, None),
        P(DP),
        P(PIPE, DP, TENSOR),
        P(PIPE, DP, TENSOR),
        P(PIPE, DP, None),
        P(PIPE, DP, TENSOR),
        P(PIPE, DP, TENSOR),
        P(PIPE, None),
        P(PIPE, None, TENSOR),
        P(PIPE, None, None),
        P(PIPE, TENSOR),
        P(PIPE, None),
        P(PIPE, TENSOR),
        P(PIPE, TENSOR),
        P(PIPE, TENSOR),
        P(PIPE, TENSOR),
    )
    out_specs = (
        P(PIPE, DP, TENSOR, None),
        P(PIPE, DP, TENSOR, None),
        P(PIPE, DP, TENSOR),
        P(PIPE, DP, TENSOR),
        P(PIPE, None, (DP, TENSOR)),
        P(PIPE, DP, TENSOR),
        P(PIPE, DP, TENSOR),
        P(PIPE, (DP, TENSOR)),
        P(PIPE, None, TENSOR),
        P(PIPE, None, (DP, TENSOR)),
        P(PIPE, TENSOR),
        P(PIPE, (DP, TENSOR)),
        P(PIPE, TENSOR),
        P(PIPE, TENSOR),
        P(PIPE, TENSOR),
        P(PIPE, TENSOR),
    )

    def program(*args):
        columns = args[4].shape[2] // mesh.shape[TENSOR]
        fused = mesh.shape[DP] == 4 and mesh.shape[TENSOR] > 2 and columns // 2 % LANES == 0
        return mapped(fused_body if fused else body)(*args)

    def mapped(function):
        return jax.shard_map(function, mesh=mesh, in_specs=in_specs, out_specs=out_specs, check_vma=False)

    return program
```

```python
import functools
import types

import jax
import jax.numpy as jnp
from jax import lax
from jax.experimental import pallas as pl
from jax.experimental.pallas import tpu as pltpu
from jax.sharding import PartitionSpec as P

EPS = 1e-05
PIPE, DP, TENSOR = "pipe", "dp", "tensor"
SEQUENTIAL = "arbitrary"
Bundle = types.SimpleNamespace
HIGHEST = lax.Precision.HIGHEST
BF = jnp.bfloat16
F32 = jnp.float32
HALO = 16
GC = 256
LANES = 128
LOG2E = 1.4426950408889634


def nn(a, b):
    return jnp.dot(a, b, preferred_element_type=F32)


def nt(a, b):
    return lax.dot_general(a, b, (((1,), (1,)), ((), ())), preferred_element_type=F32)


def tn(a, b):
    return lax.dot_general(a, b, (((0,), (0,)), ((), ())), preferred_element_type=F32)


def exact(a, b):
    return jnp.dot(a, b, precision=HIGHEST, preferred_element_type=F32)


def in_parts(v):
    high = v.astype(BF)
    rest = v - high.astype(F32)
    middle = rest.astype(BF)
    return high, middle, (rest - middle.astype(F32)).astype(BF)


def pick_rows(places, v):
    total, width = nn(places, jnp.concatenate(in_parts(v), axis=1)), v.shape[1]
    return total[:, :width] + (total[:, width : 2 * width] + total[:, 2 * width :])


def pick_cols(v, places):
    high, middle, lowest = [nn(part, places) for part in in_parts(v)]
    return high + (middle + lowest)


def sigmoid(v):
    return 0.5 * jnp.tanh(0.5 * v) + 0.5


def iota(shape, dim):
    return lax.broadcasted_iota(jnp.int32, shape, dim)


def spread(per_head, width, head_dim):
    lane = iota(per_head.shape, 1)
    parts = []
    for pair in range(width // LANES):
        parts.append(
            jnp.where(lane < head_dim, per_head[:, 2 * pair : 2 * pair + 1], per_head[:, 2 * pair + 1 : 2 * pair + 2])
        )
    return jnp.concatenate(parts, axis=1)


def conv_rows(pre, taps, rows):
    total = taps[4:5, :] + taps[3:4, :] * pre[HALO : HALO + rows, :]
    for k in range(3):
        total = total + taps[k : k + 1, :] * pre[HALO - 3 + k : HALO - 3 + k + rows, :]
    return total


def conv_sums(grad, pre, rows):
    sums = [jnp.sum(grad * pre[HALO - 3 + k : HALO - 3 + k + rows, :], axis=0, keepdims=True) for k in range(4)]
    sums.append(jnp.sum(grad, axis=0, keepdims=True))
    return sums


def conv_transposed(grad, halo, taps, rows):
    ext = jnp.concatenate([grad, halo], axis=0)
    total = taps[3:4, :] * grad
    for k in range(3):
        total = total + taps[k : k + 1, :] * ext[3 - k : 3 - k + rows, :]
    return total


def silu_slope(v):
    s = sigmoid(v)
    return s * (1.0 + v * (1.0 - s))


def group_lanes(values, dst, groups, per_group):
    for g in range(groups):
        dst[g] = values if g == 0 else pltpu.roll(values, LANES - per_group * g, 1)


def group_rows(values, dst, groups, per_group):
    turned = values.T
    for g in range(groups):
        dst[g, 0:per_group, :] = turned[per_group * g : per_group * (g + 1), :]


def scan_front(
    head_dim, nx, wv, ws, wt, pv, ps, ph, vpre_o, spre_o, x_o, bc_o, dtc_o, yw_o, loc_o, sc_s, dt_s, cum_s, cumt_s
):
    g = pl.program_id(0)
    groups = pl.num_programs(0)
    rows = x_o.shape[0]
    state = bc_o.shape[1] // 2
    per_group = GC // head_dim

    @pl.when(g == 0)
    def _():
        spre = nn(nx[...], ws[...])
        spre_o[...] = spre
        conv = conv_rows(spre, ps, rows)
        bc = (conv * sigmoid(conv)).astype(BF)
        bc_o[...] = bc
        scores = nt(bc[:, state:], bc[:, :state])
        lower = iota((rows, rows), 0) >= iota((rows, rows), 1)
        sc_s[...] = jnp.where(lower, scores, 0.0)
        raw = nn(nx[HALO:, :], wt[...]) + ph[0:1, :]
        step = jnp.maximum(raw, 0.0) + jnp.log(1.0 + jnp.exp(-jnp.abs(raw)))
        decay = -step * jnp.exp(ph[1:2, :])
        cum = exact(lower.astype(F32), decay)
        dtc_o[0] = step
        dtc_o[1] = cum
        dtc_o[2] = sigmoid(raw)
        group_lanes(step, dt_s, dt_s.shape[0], per_group)
        group_lanes(cum, cum_s, cum_s.shape[0], per_group)
        group_rows(cum, cumt_s, cumt_s.shape[0], per_group)

    pre = nn(nx[...], wv[...])
    vpre_o[...] = pre
    conv = conv_rows(pre, pv, rows)
    x = conv * sigmoid(conv)
    x_o[...] = x.astype(BF)
    step, cum, cumt = dt_s[g], cum_s[g], cumt_s[g]
    to_end = jnp.exp(cum[rows - 1 : rows, :] - cum)
    xp = (x * spread(step, GC, head_dim)).astype(BF)
    xr = (x * spread(step * to_end, GC, head_dim)).astype(BF)
    loc_o[...] = tn(xr, bc_o[:, :state])
    scores = sc_s[...]
    lane = iota((rows, LANES), 1)
    for pair in range(GC // LANES):
        cols = slice(LANES * pair, LANES * (pair + 1))
        outs = []
        for i in (2 * pair, 2 * pair + 1):
            diff = cum[:, i : i + 1] - cumt[i : i + 1, :]
            mix = (jnp.exp(jnp.minimum(diff, 0.0)) * scores).astype(BF)
            outs.append(nn(mix, xp[:, cols]))
        yw_o[:, cols] = jnp.where(lane < head_dim, outs[0], outs[1]) + pv[6:7, cols] * x[:, cols]


def scan_finish(
    head_dim, nx, wg, wo, yw, s_in, bc, dtc, pv, gate_o, y_o, gg_o, p_o, sq_o, acc_s, sq_s, cum_s
):
    g = pl.program_id(0)
    rows = yw.shape[0]
    state = bc.shape[1] // 2

    @pl.when(g == 0)
    def _():
        group_lanes(dtc[1], cum_s, cum_s.shape[0], GC // head_dim)
        acc_s[...] = jnp.zeros_like(acc_s)
        sq_s[...] = jnp.zeros_like(sq_s)

    gate = nn(nx[HALO:, :], wg[...])
    gate_o[...] = gate
    carried = nt(bc[:, state:], s_in[...])
    y = yw[...] + spread(jnp.exp(cum_s[g]), GC, head_dim) * carried
    y_o[...] = y
    gated = y * (gate * sigmoid(gate))
    gg = (gated * pv[5:6, :]).astype(BF)
    gg_o[...] = gg
    squares = gated * gated
    for part in range(GC // LANES):
        sq_s[...] += squares[:, LANES * part : LANES * (part + 1)]
    acc_s[...] += nt(gg, wo[...])

    @pl.when(g == pl.num_programs(0) - 1)
    def _():
        p_o[...] = acc_s[...].astype(BF)
        sq_o[...] = jnp.broadcast_to(jnp.sum(sq_s[...], axis=1, keepdims=True), sq_o.shape)


def gate_backward(head_dim, gm, wo, y, gate, rowsc, pv, bc, dtc, dy_o, dgate_o, dsl_o, dgain_o, cum_s):
    g = pl.program_id(0)
    state = bc.shape[1] // 2

    @pl.when(g == 0)
    def _():
        group_lanes(dtc[1], cum_s, cum_s.shape[0], GC // head_dim)

    gs = nn(gm[...], wo[...])
    inverse, shrink = rowsc[:, 0:1], rowsc[:, 1:2]
    gv, yv = gate[...], y[...]
    s = sigmoid(gv)
    silu = gv * s
    gated = yv * silu
    dgain = jnp.sum(gs * gated * inverse, axis=0, keepdims=True)
    dgain_o[...] = jnp.broadcast_to(dgain, dgain_o.shape)
    dgated = inverse * (gs * pv[5:6, :]) - gated * shrink
    dgate_o[...] = (dgated * yv * (s * (1.0 + gv * (1.0 - s)))).astype(BF)
    dy = dgated * silu
    dy_o[...] = dy.astype(BF)
    dye = (dy * spread(jnp.exp(cum_s[g]), GC, head_dim)).astype(BF)
    dsl_o[...] = tn(dye, bc[:, state:])


def scan_backward(
    head_dim,
    dy,
    x,
    vpre,
    spre,
    bc,
    dtc,
    s_in,
    g_in,
    pv,
    ps,
    ph,
    dconv_o,
    dsc_o,
    dstep_o,
    vs_o,
    ss_o,
    hs_o,
    sct_s,
    scts_s,
    wsum_s,
    dbc_s,
    dt_s,
    cum_s,
    cumt_s,
    net_s,
    rv_s,
    ddir_s,
    k_s,
    rt_s,
    rall_s,
):
    g = pl.program_id(0)
    rows = x.shape[0]
    state = bc.shape[1] // 2
    per_group = GC // head_dim
    groups = dt_s.shape[0]

    @pl.when(g == 0)
    def _():
        scores = nt(bc[:, :state], bc[:, state:])
        first, second = iota((rows, rows), 0), iota((rows, rows), 1)
        sct_s[...] = jnp.where(second >= first, scores, 0.0)
        scts_s[...] = jnp.where(second > first, scores, 0.0)
        wsum_s[...] = jnp.zeros_like(wsum_s)
        dbc_s[...] = jnp.zeros_like(dbc_s)
        rall_s[...] = jnp.zeros_like(rall_s)
        group_lanes(dtc[0], dt_s, groups, per_group)
        group_lanes(dtc[1], cum_s, groups, per_group)
        group_rows(dtc[1], cumt_s, groups, per_group)

    step, cum, cumt = dt_s[g], cum_s[g], cumt_s[g]
    last = cum[rows - 1 : rows, :]
    to_end = jnp.exp(last - cum)
    stepx = spread(step, GC, head_dim)
    endx = spread(to_end, GC, head_dim)
    fromx = spread(jnp.exp(cum), GC, head_dim)
    xf = x[...].astype(F32)
    dyb = dy[...]
    dyf = dyb.astype(F32)
    xp = (xf * stepx).astype(BF)
    xr = (xf * stepx * endx).astype(BF)
    dyef = dyf * fromx
    dye = dyef.astype(BF)
    gb = nt(bc[:, :state], g_in[...])
    cs = nt(bc[:, state:], s_in[...])
    dbc_s[:, :state] += nn(xr, g_in[...])
    dbc_s[:, state:] += nn(dye, s_in[...])

    lane = iota((rows, LANES), 1)
    wsum = wsum_s[...]
    colsum = jnp.zeros((rows, LANES), F32)
    within = []
    for pair in range(GC // LANES):
        cols = slice(LANES * pair, LANES * (pair + 1))
        xpp, dyp = xp[:, cols], dyb[:, cols]
        outs = []
        for side in range(2):
            i = 2 * pair + side
            mine = (lane < head_dim) if side == 0 else (lane >= head_dim)
            decay = jnp.exp(jnp.minimum(cumt[i : i + 1, :] - cum[:, i : i + 1], 0.0))
            outs.append(nn((decay * sct_s[...]).astype(BF), dyp))
            weight = decay * nt(jnp.where(mine, xpp, jnp.zeros_like(xpp)), dyp)
            wsum = wsum + weight
            pairs = (weight * scts_s[...]).astype(BF)
            colsum = colsum + nn(pairs, (lane == i).astype(BF))
            rt_s[g, i : i + 1, :] = jnp.sum(pairs.astype(F32), axis=0, keepdims=True)
        within.append(jnp.where(lane < head_dim, outs[0], outs[1]))
    wsum_s[...] = wsum
    u = jnp.concatenate(within, axis=1) + endx * gb

    heads = (iota((GC, LANES), 0) // head_dim == iota((GC, LANES), 1)).astype(BF)
    ddir_s[g] = nn((xf * u).astype(BF), heads)
    net_s[g] = nn((dyef * cs).astype(BF), heads) - colsum
    rv_s[g] = step * to_end * nn((xf * gb).astype(BF), heads)
    inner = g_in[...].astype(F32) * s_in[...].astype(F32)
    per_channel = lax.dot_general(
        jnp.ones((8, inner.shape[1]), F32), inner, (((1,), (1,)), ((), ())), precision=HIGHEST, preferred_element_type=F32
    )
    k_s[g] = jnp.exp(last) * exact(per_channel, heads.astype(F32))

    dx = stepx * u + pv[6:7, :] * dyf
    dconv = dx * silu_slope(conv_rows(vpre, pv, rows))
    dconv_o[...] = dconv
    sums = conv_sums(dconv, vpre, rows)
    sums.append(jnp.sum(dyf * xf, axis=0, keepdims=True))
    sums.append(jnp.zeros((2, GC), F32))
    vs_o[...] = jnp.concatenate(sums, axis=0)

    @pl.when(g == pl.num_programs(0) - 1)
    def _():
        first, second = iota((rows, rows), 0), iota((rows, rows), 1)
        net, rv, ddir, const = net_s[0], rv_s[0], ddir_s[0], k_s[0]
        rall_s[0:per_group, :] = rt_s[0, 0:per_group, :]
        for other in range(1, groups):
            shift = per_group * other
            net = net + pltpu.roll(net_s[other], shift, 1)
            rv = rv + pltpu.roll(rv_s[other], shift, 1)
            ddir = ddir + pltpu.roll(ddir_s[other], shift, 1)
            const = const + pltpu.roll(k_s[other], shift, 1)
            rall_s[shift : shift + per_group, :] = rt_s[other, 0:per_group, :]
        net = net + rall_s[...].T
        da = exact((second >= first).astype(F32), net) + exact((second < first).astype(F32), rv) + const[0:1, :]
        rate = jnp.exp(ph[1:2, :])
        dstep = (ddir - da * rate) * dtc[2]
        dstep_o[...] = dstep.astype(BF)
        hs_o[...] = jnp.concatenate(
            [
                jnp.sum(dstep, axis=0, keepdims=True),
                jnp.sum(-da * dtc[0] * rate, axis=0, keepdims=True),
                jnp.zeros((6, LANES), F32),
            ],
            axis=0,
        )
        weights = jnp.where(second >= first, wsum_s[...], 0.0).astype(BF)
        db = dbc_s[:, :state] + nn(weights, bc[:, state:])
        dc = dbc_s[:, state:] + tn(weights, bc[:, :state])
        dsc = jnp.concatenate([db, dc], axis=1) * silu_slope(conv_rows(spre, ps, rows))
        dsc_o[...] = dsc
        ssums = conv_sums(dsc, spre, rows)
        ssums.append(jnp.zeros((3, 2 * state), F32))
        ss_o[...] = jnp.concatenate(ssums, axis=0)


def conv_backward(dconv, halo_v, dsc, halo_s, dgate, dstep, pv, ps, wv, wg, ws, wt, dval_o, dst_o, p_o, acc_s):
    g = pl.program_id(0)
    rows = dconv.shape[0]

    @pl.when(g == 0)
    def _():
        dst = conv_transposed(dsc[...], halo_s[...], ps, rows).astype(BF)
        dst_o[...] = dst
        acc_s[...] = nt(dst, ws[...]) + nt(dstep[...], wt[...])

    dval = conv_transposed(dconv[...], halo_v[...], pv, rows).astype(BF)
    dval_o[...] = dval
    acc_s[...] += nt(dval, wv[...]) + nt(dgate[...], wg[...])

    @pl.when(g == pl.num_programs(0) - 1)
    def _():
        p_o[...] = acc_s[...].astype(BF)


def whole(shape):
    return pl.BlockSpec(shape, lambda g: (0,) * len(shape))


def by_cols(rows):
    return pl.BlockSpec((rows, GC), lambda g: (0, g))


def by_rows(cols):
    return pl.BlockSpec((GC, cols), lambda g: (g, 0))


def call(kernel, groups, ins, outs, scratch, flops, traffic, exps=0):
    arrays, in_specs = zip(*ins)
    shapes, out_specs = zip(*outs)
    return pl.pallas_call(
        kernel,
        grid=(groups,),
        in_specs=list(in_specs),
        out_specs=list(out_specs),
        out_shape=[jax.ShapeDtypeStruct(s, d) for s, d in shapes],
        scratch_shapes=scratch,
        cost_estimate=pl.CostEstimate(flops=flops, bytes_accessed=traffic, transcendentals=exps),
        compiler_params=pltpu.CompilerParams(vmem_limit_bytes=40 * 2**20, dimension_semantics=(SEQUENTIAL,)),
    )(*arrays)


def front_call(nx, w, par, head_dim, state):
    rows, width = nx.shape[0] - HALO, w.value.shape[1]
    model = nx.shape[1]
    groups = width // GC
    return call(
        functools.partial(scan_front, head_dim),
        groups,
        [
            (nx, whole(nx.shape)),
            (w.value, by_cols(model)),
            (w.state, whole(w.state.shape)),
            (w.step, whole(w.step.shape)),
            (par.value, by_cols(8)),
            (par.state, whole(par.state.shape)),
            (par.head, whole(par.head.shape)),
        ],
        [
            (((rows + HALO, width), F32), by_cols(rows + HALO)),
            (((rows + HALO, 2 * state), F32), whole((rows + HALO, 2 * state))),
            (((rows, width), BF), by_cols(rows)),
            (((rows, 2 * state), BF), whole((rows, 2 * state))),
            (((3, rows, LANES), F32), whole((3, rows, LANES))),
            (((rows, width), F32), by_cols(rows)),
            (((width, state), F32), by_rows(state)),
        ],
        [
            pltpu.VMEM((rows, rows), F32),
            pltpu.VMEM((groups, rows, LANES), F32),
            pltpu.VMEM((groups, rows, LANES), F32),
            pltpu.VMEM((groups, 8, rows), F32),
        ],
        2 * rows * model * (width + 3 * LANES) + 4 * rows * rows * width,
        2 * model * width + 12 * rows * width,
        rows * rows * width // head_dim,
    )


def finish_call(nx, w, par, yw, s_in, bc, dtc, head_dim):
    rows, width = yw.shape
    model = nx.shape[1]
    groups = width // GC
    state = s_in.shape[1]
    return call(
        functools.partial(scan_finish, head_dim),
        groups,
        [
            (nx, whole(nx.shape)),
            (w.gate, by_cols(model)),
            (w.out, by_cols(model)),
            (yw, by_cols(rows)),
            (s_in, by_rows(state)),
            (bc, whole(bc.shape)),
            (dtc, whole(dtc.shape)),
            (par.value, by_cols(8)),
        ],
        [
            (((rows, width), F32), by_cols(rows)),
            (((rows, width), F32), by_cols(rows)),
            (((rows, width), BF), by_cols(rows)),
            (((rows, model), BF), whole((rows, model))),
            (((rows, LANES), F32), whole((rows, LANES))),
        ],
        [
            pltpu.VMEM((rows, model), F32),
            pltpu.VMEM((rows, LANES), F32),
            pltpu.VMEM((groups, rows, LANES), F32),
        ],
        4 * rows * model * width,
        4 * model * width + 14 * rows * width,
    )


def gate_call(gm, w, par, y, gate, rowsc, bc, dtc, head_dim):
    rows, width = y.shape
    model = gm.shape[1]
    groups = width // GC
    state = bc.shape[1] // 2
    return call(
        functools.partial(gate_backward, head_dim),
        groups,
        [
            (gm, whole(gm.shape)),
            (w.out, by_cols(model)),
            (y, by_cols(rows)),
            (gate, by_cols(rows)),
            (rowsc, whole(rowsc.shape)),
            (par.value, by_cols(8)),
            (bc, whole(bc.shape)),
            (dtc, whole(dtc.shape)),
        ],
        [
            (((rows, width), BF), by_cols(rows)),
            (((rows, width), BF), by_cols(rows)),
            (((width, state), F32), by_rows(state)),
            (((8, width), F32), by_cols(8)),
        ],
        [pltpu.VMEM((groups, rows, LANES), F32)],
        2 * rows * model * width,
        2 * model * width + 14 * rows * width,
    )


def backward_call(dy, x, vpre, spre, bc, dtc, s_in, g_in, par, head_dim):
    rows, width = x.shape
    groups = width // GC
    state = bc.shape[1] // 2
    lanes = pltpu.VMEM((groups, rows, LANES), F32)
    square = pltpu.VMEM((rows, rows), F32)
    return call(
        functools.partial(scan_backward, head_dim),
        groups,
        [
            (dy, by_cols(rows)),
            (x, by_cols(rows)),
            (vpre, by_cols(rows + HALO)),
            (spre, whole(spre.shape)),
            (bc, whole(bc.shape)),
            (dtc, whole(dtc.shape)),
            (s_in, by_rows(state)),
            (g_in, by_rows(state)),
            (par.value, by_cols(8)),
            (par.state, whole(par.state.shape)),
            (par.head, whole(par.head.shape)),
        ],
        [
            (((rows, width), F32), by_cols(rows)),
            (((rows, 2 * state), F32), whole((rows, 2 * state))),
            (((rows, LANES), BF), whole((rows, LANES))),
            (((8, width), F32), by_cols(8)),
            (((8, 2 * state), F32), whole((8, 2 * state))),
            (((8, LANES), F32), whole((8, LANES))),
        ],
        [
            square,
            square,
            square,
            pltpu.VMEM((rows, 2 * state), F32),
            lanes,
            lanes,
            pltpu.VMEM((groups, 8, rows), F32),
            lanes,
            lanes,
            lanes,
            pltpu.VMEM((groups, 8, LANES), F32),
            pltpu.VMEM((groups, 8, rows), F32),
            pltpu.VMEM((LANES, rows), F32),
        ],
        12 * rows * rows * width,
        14 * rows * width,
        3 * rows * rows * width // head_dim,
    )


def conv_call(dconv, halo, dsc, dgate, dstep, w, par):
    rows, width = dconv.shape
    model = w.value.shape[0]
    groups = width // GC
    states = dsc.shape[1]
    halo_v, halo_s = halo[:, :width], halo[:, width:]
    return call(
        conv_backward,
        groups,
        [
            (dconv, by_cols(rows)),
            (halo_v, by_cols(8)),
            (dsc, whole(dsc.shape)),
            (halo_s, whole(halo_s.shape)),
            (dgate, by_cols(rows)),
            (dstep, whole(dstep.shape)),
            (par.value, by_cols(8)),
            (par.state, whole(par.state.shape)),
            (w.value, by_cols(model)),
            (w.gate, by_cols(model)),
            (w.state, whole(w.state.shape)),
            (w.step, whole(w.step.shape)),
        ],
        [
            (((rows, width), BF), by_cols(rows)),
            (((rows, states), BF), whole((rows, states))),
            (((rows, model), BF), whole((rows, model))),
        ],
        [pltpu.VMEM((rows, model), F32)],
        4 * rows * model * width,
        4 * model * width + 10 * rows * width,
    )


def swap_pipe(value):
    return lax.ppermute(value, PIPE, [(0, 1), (1, 0)])


def shift_tensor(value, by):
    count = lax.axis_size(TENSOR)
    return lax.ppermute(value, TENSOR, [(i, i + by) for i in range(count) if 0 <= i + by < count])


def flip_dp(value, bit):
    return lax.ppermute(value, DP, [(i, i ^ bit) for i in range(lax.axis_size(DP))])


def dp_bits():
    bits, bit = [], 1
    while bit < lax.axis_size(DP):
        bits.append(bit)
        bit *= 2
    return bits


def gather_tensor(piece):
    count, me = lax.axis_size(TENSOR), lax.axis_index(TENSOR)
    rows, cols = piece.shape
    right, left = [piece], [piece]
    for _ in range(count - 1):
        right.append(shift_tensor(right[-1], 1))
        left.append(shift_tensor(left[-1], -1))
    full = jnp.zeros((rows, count * cols), piece.dtype)
    for k in range(count):
        part = piece if k == 0 else jnp.where(me >= k, right[k], left[count - k])
        full = lax.dynamic_update_slice(full, part, (0, lax.rem(me - k + count, count) * cols))
    return full


def gather_dp(piece):
    count, me = lax.axis_size(DP), lax.axis_index(DP)
    rows, cols = piece.shape
    held = {0: piece}
    for bit in reversed(dp_bits()):
        for offset in list(held):
            held[offset ^ bit] = flip_dp(held[offset], bit)
    full = jnp.zeros((count * rows, cols), piece.dtype)
    for offset, part in held.items():
        full = lax.dynamic_update_slice(full, part, ((me ^ offset) * rows, 0))
    return full


def add_low(a, b):
    return (a.astype(F32) + b.astype(F32)).astype(a.dtype)


def reduce_dp(value):
    me = lax.axis_index(DP)
    count = lax.axis_size(DP)
    rows, cols = value.shape[0] // count, value.shape[1]
    for bit in dp_bits():
        count //= 2
        split = value.reshape(count, 2, rows, cols)
        mine = (me // bit) % 2
        keep = lax.dynamic_index_in_dim(split, mine, 1, keepdims=False)
        send = lax.dynamic_index_in_dim(split, 1 - mine, 1, keepdims=False)
        value = add_low(keep, flip_dp(send, bit)).reshape(count * rows, cols)
    return value


def reduce_tensor(take):
    count, me = lax.axis_size(TENSOR), lax.axis_index(TENSOR)
    moving_right = moving_left = None
    for k in range(count - 1, 0, -1):
        right, left = take(jnp.minimum(me + k, count - 1)), take(jnp.maximum(me - k, 0))
        if moving_right is not None:
            right, left = add_low(right, moving_right), add_low(left, moving_left)
        moving_right, moving_left = shift_tensor(right, 1), shift_tensor(left, -1)
    own = take(me)
    if moving_right is None:
        return own.astype(F32)
    return own.astype(F32) + moving_right.astype(F32) + moving_left.astype(F32)


def take_cols(value):
    width = value.shape[1] // lax.axis_size(TENSOR)
    return lambda j: lax.dynamic_slice_in_dim(value, j * width, width, 1)


def take_first(value):
    return lambda j: lax.dynamic_index_in_dim(value, j, 0, keepdims=False)


def sum_all_dp(value):
    for bit in dp_bits():
        value = value + flip_dp(value, bit)
    return value


def sum_all_tensor(value):
    count, bit = lax.axis_size(TENSOR), 1
    while bit < count:
        value = value + lax.ppermute(value, TENSOR, [(i, i ^ bit) for i in range(count)])
        bit *= 2
    return value


MESH = pl.DeviceIdType.MESH
VMEM_LIMIT = 60 * 2**20


def remote(src, dst, send, recv, axis, index):
    return pltpu.make_async_remote_copy(
        src_ref=src, dst_ref=dst, send_sem=send, recv_sem=recv, device_id={axis: index}, device_id_type=MESH
    )


def greet(partners):
    barrier = pltpu.get_barrier_semaphore()
    for axis, index in partners:
        pl.semaphore_signal(barrier, inc=1, device_id={axis: index}, device_id_type=MESH)
    pl.semaphore_wait(barrier, len(partners))


def ring_neighbours(count):
    t = lax.axis_index(TENSOR)
    return [(TENSOR, lax.rem(t + 1, count)), (TENSOR, lax.rem(t + count - 1, count))]


def aligned(index, size):
    return pl.ds(pl.multiple_of(index * size, size), size)


class Gather:
    sems = ((4,), (4,), (4,), "z", "z", "z", "z", "z", "c", "c", (3,), (3,), (3,), (2,), (2,), (2, 2), (2, 2), "n", "n")

    @classmethod
    def scratch(cls, count):
        shapes = {"z": (8, count), "c": (8, 2, count), "n": (count,)}
        return [pltpu.SemaphoreType.DMA(shapes.get(shape, shape)) for shape in cls.sems]

    def __init__(self, count, sources, targets, small, sems):
        self.count, self.sources, self.targets, self.small = count, sources, targets, small
        (self.own_sem, self.xs_sem, self.xr_sem, self.right_sem, self.left_sem, self.zr_sem) = sems[:6]
        (self.ys_sem, self.yr_sem, self.cs_sem, self.cr_sem, self.st_own, self.st_xs, self.st_xr) = sems[6:13]
        (self.st_ys, self.st_yr, self.st_cs, self.st_cr, self.ch_s, self.ch_r) = sems[13:]
        self.p, self.d, self.t = lax.axis_index(PIPE), lax.axis_index(DP), lax.axis_index(TENSOR)
        y, c = self.d // 2, lax.rem(self.d, 2)
        self.y_mate, self.core_mate, self.far_mate = 2 * (1 - y) + c, 2 * y + 1 - c, 2 * (1 - y) + 1 - c
        self.kinds = len(sources)
        self.rows = sources[0].shape[0]

    def partners(self):
        others = [(TENSOR, lax.rem(self.t + k, self.count)) for k in range(1, self.count)]
        return others + [(PIPE, 1 - self.p), (DP, self.y_mate), (DP, self.core_mate)]

    def source(self, kind, which):
        ref = self.sources[kind]
        if kind == self.kinds - 1:
            return ref.at[aligned(which, ref.shape[0] // 2), :]
        return ref.at[:, aligned(which, ref.shape[1] // 2)]

    def region(self, kind, layer, row, col):
        ref = self.sources[kind]
        if kind == self.kinds - 1:
            return self.targets[kind].at[layer, aligned(col, ref.shape[0] // 2), aligned(row, ref.shape[1])]
        return self.targets[kind].at[layer, aligned(row, self.rows), aligned(col, ref.shape[1] // 2)]

    def own_copy(self, w):
        return pltpu.make_async_copy(self.source(w, self.p), self.region(w, self.p, self.d, self.t), self.own_sem.at[w])

    def swap_copy(self, w):
        dst = self.region(w, self.p, self.d, self.t)
        return remote(self.source(w, 1 - self.p), dst, self.xs_sem.at[w], self.xr_sem.at[w], PIPE, 1 - self.p)

    def swap_arrival(self, w):
        dst = self.region(w, 1 - self.p, self.d, self.t)
        return remote(self.source(w, 1 - self.p), dst, self.xs_sem.at[w], self.xr_sem.at[w], PIPE, 1 - self.p)

    def z_copy(self, item, src, by, sem):
        ref = self.region(item % self.kinds, item // self.kinds, self.d, src)
        return remote(ref, ref, sem.at[item, src], self.zr_sem.at[item, src], TENSOR, self.t + by)

    def right(self, item, src):
        return self.z_copy(item, src, 1, self.right_sem)

    def left(self, item, src):
        return self.z_copy(item, src, -1, self.left_sem)

    def y_copy(self, item, src, row=None):
        ref = self.region(item % self.kinds, item // self.kinds, self.d if row is None else row, src)
        return remote(ref, ref, self.ys_sem.at[item, src], self.yr_sem.at[item, src], DP, self.y_mate)

    def core_copy(self, item, which, src, arrival=False):
        row = (self.core_mate, self.far_mate)[which] if arrival else (self.d, self.y_mate)[which]
        ref = self.region(item % self.kinds, item // self.kinds, row, src)
        sems = self.cs_sem.at[item, which, src], self.cr_sem.at[item, which, src]
        return remote(ref, ref, *sems, DP, self.core_mate)

    def begin(self, item):
        w, layer = item % self.kinds, item // self.kinds

        @pl.when(self.p == layer)
        def _():
            self.own_copy(w).wait()

        @pl.when(self.p != layer)
        def _():
            self.swap_arrival(w).wait_recv()

        @pl.when(self.t < self.count - 1)
        def _():
            self.right(item, self.t).start()

        @pl.when(self.t > 0)
        def _():
            self.left(item, self.t).start()

        self.y_copy(item, self.t).start()
        self.core_copy(item, 0, self.t).start()

    def hop(self, item, hop):
        t, count = self.t, self.count
        lower, upper = t - hop, t + hop

        @pl.when(lower >= 0)
        def _():
            self.right(item, lower).wait_recv()

            @pl.when(t < count - 1)
            def _():
                self.right(item, lower).start()

            self.y_copy(item, lower).start()
            self.core_copy(item, 0, lower).start()

        @pl.when(upper < count)
        def _():
            self.left(item, upper).wait_recv()

            @pl.when(t > 0)
            def _():
                self.left(item, upper).start()

            self.y_copy(item, upper).start()
            self.core_copy(item, 0, upper).start()

    def share(self, item, src):
        self.y_copy(item, src, self.y_mate).wait_recv()
        self.core_copy(item, 1, src).start()

    def arrived(self, item, src):
        for which in range(2):
            self.core_copy(item, which, src, True).wait_recv()

    def sent(self, item):
        t, count = self.t, self.count
        for src in range(count):
            for which in range(2):
                self.core_copy(item, which, src).wait_send()
            self.y_copy(item, src).wait_send()

            @pl.when((src <= t) & (t < count - 1))
            def _():
                self.right(item, src).wait_send()

            @pl.when((src >= t) & (t > 0))
            def _():
                self.left(item, src).wait_send()


    def small_target(self, k, layer):
        target = self.small[k][1]
        if k == 0:
            return target.at[layer, aligned(self.d, self.rows), :]
        if k == 1:
            return target.at[layer, :, aligned(self.t, target.shape[2] // self.count)]
        return target.at[layer]

    def small_source(self, k, which):
        ref = self.small[k][0]
        return ref.at[:, aligned(which, ref.shape[1] // 2)] if k == 1 else ref

    def small_own(self, k):
        return pltpu.make_async_copy(self.small_source(k, self.p), self.small_target(k, self.p), self.st_own.at[k])

    def small_swap(self, k, arrival=False):
        dst = self.small_target(k, 1 - self.p if arrival else self.p)
        return remote(self.small_source(k, 1 - self.p), dst, self.st_xs.at[k], self.st_xr.at[k], PIPE, 1 - self.p)

    def state_rows(self, layer, row):
        return self.small[0][1].at[layer, aligned(row, self.rows), :]

    def state_y(self, layer, arrival=False):
        ref = self.state_rows(layer, self.y_mate if arrival else self.d)
        return remote(ref, ref, self.st_ys.at[layer], self.st_yr.at[layer], DP, self.y_mate)

    def state_core(self, layer, which, arrival=False):
        row = (self.core_mate, self.far_mate)[which] if arrival else (self.d, self.y_mate)[which]
        ref = self.state_rows(layer, row)
        return remote(ref, ref, self.st_cs.at[layer, which], self.st_cr.at[layer, which], DP, self.core_mate)

    def channels(self, k, arrival=False):
        target = self.small[1][1]
        index = lax.rem(self.t - k + self.count, self.count) if arrival else self.t
        ref = target.at[:, :, aligned(index, target.shape[2] // self.count)]
        return remote(ref, ref, self.ch_s.at[k], self.ch_r.at[k], TENSOR, lax.rem(self.t + k, self.count))

    def first_layer(self):
        order = [self.kinds - 1] + list(range(self.kinds - 1))
        for w in order:
            self.swap_copy(w).start()
            self.own_copy(w).start()
        for k in range(3):
            self.small_swap(k).start()
            self.small_own(k).start()
        order = [self.kinds - 1, 2 * self.kinds - 1] + list(range(self.kinds - 1))
        for item in order:
            self.begin(item)
        for k in range(3):
            self.small_own(k).wait()
            self.small_swap(k, True).wait_recv()
        for layer in range(2):
            self.state_y(layer).start()
            self.state_core(layer, 0).start()
        for k in range(1, self.count):
            self.channels(k).start()
        for hop in range(1, self.count):
            for item in order:
                self.hop(item, hop)
        for item in self.late_items():
            self.begin(item)
        for layer in range(2):
            self.state_y(layer, True).wait_recv()
            self.state_core(layer, 1).start()
        for src in range(self.count):
            for item in order:
                self.share(item, src)
        for item in order:
            for src in range(self.count):
                self.arrived(item, src)
        for k in range(1, self.count):
            self.channels(k, True).wait_recv()
        for layer in range(2):
            for which in range(2):
                self.state_core(layer, which, True).wait_recv()

    def late_items(self):
        return [self.kinds + w for w in range(self.kinds - 1)]

    def second_layer(self, steps, group_of):
        items, stages = self.late_items(), []
        hops = [(item, hop) for hop in range(1, self.count) for item in items]
        for n, (item, hop) in enumerate(hops):
            stages.append((2 + n * (steps - 5) // len(hops), functools.partial(self.hop, item, hop)))
        for src in range(self.count):
            for item in items:
                stages.append((steps - 2 + group_of(src), functools.partial(self.share, item, src)))
        for src in range(self.count):
            for item in items:
                stages.append((steps - 1 + group_of(src), functools.partial(self.arrived, item, src)))
        return stages

    def finish(self):
        for k in range(3):
            self.small_swap(k).wait_send()
        for k in range(1, self.count):
            self.channels(k).wait_send()
        for layer in range(2):
            self.state_y(layer).wait_send()
            for which in range(2):
                self.state_core(layer, which).wait_send()
        for w in range(self.kinds):
            self.swap_copy(w).wait_send()
        for item in range(2 * self.kinds):
            self.sent(item)


class Reducer:
    def __init__(self, count, factors, results, buffers, sems):
        self.count, self.factors, self.results = count, factors, results
        (self.a_s, self.b_s, self.dw_s, self.crecv, self.ysend, self.near_s, self.yrecv, self.total_s) = buffers[:8]
        (self.z_s, self.zl_s, self.xsend, self.xrecv, self.turned_s) = buffers[8:]
        (self.a_sem, self.b_sem, self.cs_sem, self.cr_sem, self.ys_sem, self.yr_sem) = sems[:6]
        (self.rs_sem, self.rr_sem, self.ls_sem, self.lr_sem, self.xs_sem, self.xr_sem, self.o_sem) = sems[6:]
        self.p, self.d, self.t = lax.axis_index(PIPE), lax.axis_index(DP), lax.axis_index(TENSOR)
        self.y, self.c = self.d // 2, lax.rem(self.d, 2)
        self.y_mate, self.core_mate = 2 * (1 - self.y) + self.c, 2 * self.y + 1 - self.c
        self.kinds = 3
        self.pieces = 2 * self.kinds * count
        self.ticks = self.pieces + count + 2
        self.rows, self.half = self.xsend.shape[1], self.xsend.shape[2]

    @staticmethod
    def scratch(count, micro, rows, model, half, groups):
        piece = (model // groups, half)
        vmem, dma = pltpu.VMEM, pltpu.SemaphoreType.DMA
        buffers = [
            vmem((micro, rows, model), BF),
            vmem((2, micro, rows, half), BF),
            vmem((3, model, half), BF),
            vmem((4, 2) + piece, BF),
            vmem((4,) + piece, BF),
            vmem((4,) + piece, BF),
            vmem((4,) + piece, BF),
            vmem((4,) + piece, BF),
            vmem((6 * count,) + piece, BF),
            vmem((6,) + piece, BF),
            vmem((6,) + piece, BF),
            vmem((3,) + piece, BF),
            vmem((model, micro * rows), BF),
        ]
        sems = [dma((1,)), dma((2,)), dma((3, 2)), dma((4, 2)), dma((4,)), dma((4,))]
        sems += [dma((6 * count,)) for _ in range(4)] + [dma((6,)), dma((3,)), dma((3, 2))]
        return buffers, sems

    def partners(self):
        return ring_neighbours(self.count) + [(PIPE, 1 - self.p), (DP, self.y_mate), (DP, self.core_mate)]

    def owner(self, m):
        place = lax.rem(m, self.count)
        return place // 2 + lax.rem(place, 2) * (self.count - 1 - 2 * (place // 2))

    def layer_of(self, m):
        return m // (self.kinds * self.count)

    def a_copy(self, which):
        return pltpu.make_async_copy(self.factors[which % 2].at[which // 2], self.a_s, self.a_sem.at[0])

    def b_copy(self, m, w):
        src = self.factors[2 + w].at[self.layer_of(m), :, :, aligned(self.owner(m), self.half)]
        held = lax.rem(m, 2)
        return pltpu.make_async_copy(src, self.b_s.at[held], self.b_sem.at[held])

    def b_start(self, m):
        for w in range(self.kinds):

            @pl.when(lax.rem(m // self.count, self.kinds) == w)
            def _():
                self.b_copy(m, w).start()

    def core_copy(self, m, row):
        held, ring = lax.rem(m, 3), lax.rem(m, 4)
        src = self.dw_s.at[held, aligned(2 * row + 1 - self.c, self.rows), :]
        sems = self.cs_sem.at[held, row], self.cr_sem.at[ring, row]
        return remote(src, self.crecv.at[ring, row], *sems, DP, self.core_mate)

    def y_copy(self, m):
        held = lax.rem(m, 4)
        return remote(self.ysend.at[held], self.yrecv.at[held], self.ys_sem.at[held], self.yr_sem.at[held], DP, self.y_mate)

    def right(self, m):
        ref = self.z_s.at[m]
        return remote(ref, ref, self.rs_sem.at[m], self.rr_sem.at[m], TENSOR, self.t + 1)

    def left(self, m, last):
        dst = self.zl_s.at[m // self.count] if last else self.z_s.at[m]
        return remote(self.z_s.at[m], dst, self.ls_sem.at[m], self.lr_sem.at[m], TENSOR, self.t - 1)

    def x_copy(self, item):
        w = lax.rem(item, self.kinds)
        return remote(self.xsend.at[item], self.xrecv.at[w], self.xs_sem.at[item], self.xr_sem.at[w], PIPE, 1 - self.p)

    def when_valid(self, m, condition=None):
        valid = (m >= 0) & (m < self.pieces)
        return pl.when(valid if condition is None else valid & condition)

    def tick(self, n):
        count, t, rows = self.count, self.t, self.rows

        @self.when_valid(n - 4)
        def _():
            m = n - 4
            held = lax.rem(m, 4)
            self.y_copy(m).wait()
            add_to(self.total_s.at[held], self.near_s.at[held], self.yrecv.at[held])

        @self.when_valid(n - 2)
        def _():
            m = n - 2
            held, ring = lax.rem(m, 3), lax.rem(m, 4)
            for row in range(2):
                self.core_copy(m, row).wait()

            def own(row):
                return self.dw_s.at[held, aligned(2 * row + self.c, rows), :]

            add_to(self.ysend.at[ring], own(1 - self.y), self.crecv.at[ring, 1 - self.y])
            self.y_copy(m).start()
            add_to(self.near_s.at[ring], own(self.y), self.crecv.at[ring, self.y])

        def pass_on(m, first, arrival, send):
            total = self.total_s.at[lax.rem(m, 4)]

            @pl.when(first)
            def _():
                self.z_s[m] = total[...]

            @pl.when(jnp.logical_not(first))
            def _():
                arrival.wait_recv()
                add_to(self.z_s.at[m], self.z_s.at[m], total)

            send()

        to_right, to_left = n - 4 - t, n - 3 - count + t

        @self.when_valid(to_right, t < self.owner(jnp.maximum(to_right, 0)))
        def _():
            pass_on(to_right, t == 0, self.right(to_right), lambda: self.right(to_right).start())

        @self.when_valid(to_left, t > self.owner(jnp.maximum(to_left, 0)))
        def _():
            owner = self.owner(to_left)

            def send():
                @pl.when(owner == t - 1)
                def _():
                    self.left(to_left, True).start()

                @pl.when(owner != t - 1)
                def _():
                    self.left(to_left, False).start()

            pass_on(to_left, t == count - 1, self.left(to_left, False), send)

        def last(done):
            w = done // count
            mine = self.xsend.at[w]
            mine[...] = self.total_s[lax.rem(done, 4)]

            @pl.when(t > 0)
            def _():
                self.right(done).wait_recv()
                add_to(mine, mine, self.z_s.at[done])

            @pl.when(t < count - 1)
            def _():
                self.left(done, True).wait_recv()
                add_to(mine, mine, self.zl_s.at[w])

            @pl.when(self.p != self.layer_of(done))
            def _():
                self.x_copy(w).start()

        outer = (t == 0) | (t == count - 1)
        for done, ready in ((n - 3 - count, outer), (n - 2 - count, jnp.logical_not(outer))):
            self.when_valid(done, ready & (t == self.owner(jnp.maximum(done, 0))))(functools.partial(last, done))

        @self.when_valid(n)
        def _():
            @pl.when(n == 0)
            def _():
                self.a_copy(0).start()
                self.b_start(n)

            starts = [layer * self.kinds * count + 2 * count * which for layer in range(2) for which in range(2)]
            for which, start in enumerate(starts):

                @pl.when(n == start)
                def _():
                    self.a_copy(which).wait()
                    micro, long, model = self.a_s.shape
                    for row in range(model // rows):
                        at = slice(rows * row, rows * (row + 1))
                        self.turned_s[at, :] = self.a_s[:, :, at].reshape(micro * long, rows).T
                    if which + 1 < len(starts):
                        self.a_copy(which + 1).start()

            @pl.when(n + 1 < self.pieces)
            def _():
                self.b_start(n + 1)

            self.b_copy(n, 0).wait()
            b = self.b_s[lax.rem(n, 2)]
            b = b.reshape(b.shape[0] * b.shape[1], self.half)
            held = lax.rem(n, 3)
            for row in range(self.dw_s.shape[1] // rows):
                at = slice(rows * row, rows * (row + 1))
                self.dw_s[held, at, :] = nn(self.turned_s[at, :], b).astype(BF)
            for row in range(2):
                self.core_copy(n, row).start()

    def result_copy(self, w, other):
        src = self.xrecv.at[w] if other else self.xsend.at[self.kinds * self.p + w]
        dst = self.results.at[w, :, aligned(1 - self.p if other else self.p, self.half)]
        return pltpu.make_async_copy(src, dst, self.o_sem.at[w, int(other)])

    def close(self):
        count, t = self.count, self.t
        for w in range(self.kinds):
            self.result_copy(w, False).start()
            self.x_copy(w).wait_recv()
            self.result_copy(w, True).start()
        for m in range(self.pieces):

            @pl.when(t < self.owner(m))
            def _():
                self.right(m).wait_send()

            @pl.when(t > self.owner(m))
            def _():
                self.left(m, False).wait_send()

        for w in range(self.kinds):
            self.x_copy(self.kinds * (1 - self.p) + w).wait_send()
            for other in (False, True):
                self.result_copy(w, other).wait()


def add_to(dst, one, other, chunk=64):
    def step(i, carry):
        at = aligned(i, chunk)
        dst[at, :] = (one[at, :].astype(F32) + other[at, :].astype(F32)).astype(BF)
        return carry

    lax.fori_loop(0, dst.shape[0] // chunk, step, 0)


class Sums:
    def __init__(self, count, rows, half, pack, outs, buffers):
        self.count, self.rows, self.half, self.pack, self.outs = count, rows, half, pack, outs
        (self.total_s, self.part_s, self.far_s, self.ss, self.rs) = buffers
        self.p, self.d, self.t = lax.axis_index(PIPE), lax.axis_index(DP), lax.axis_index(TENSOR)
        y, c = self.d // 2, lax.rem(self.d, 2)
        self.steps, bit = [(DP, 2 * y + 1 - c), (DP, 2 * (1 - y) + c)], 1
        while bit < count:
            self.steps.append((TENSOR, self.t + bit * (1 - 2 * lax.rem(self.t // bit, 2))))
            bit *= 2

    @staticmethod
    def scratch(count, shape):
        steps = 2 + (count - 1).bit_length()
        vmem, dma = pltpu.VMEM, pltpu.SemaphoreType.DMA
        return [vmem((steps + 1,) + shape, F32), vmem((steps,) + shape, F32), vmem(shape[1:], F32), dma((steps + 1,)), dma((steps + 1,))]

    def partners(self):
        return [step for step in self.steps if step[0] == TENSOR]

    def copy(self, k):
        axis, index = self.steps[k]
        return remote(self.total_s.at[k], self.part_s.at[k], self.ss.at[k], self.rs.at[k], axis, index)

    def pipe_copy(self):
        k = len(self.steps)
        return remote(self.total_s.at[k, 1 - self.p], self.far_s, self.ss.at[k], self.rs.at[k], PIPE, 1 - self.p)

    def begin(self):
        self.total_s[0] = self.pack[...]
        self.copy(0).start()

    def step(self, k):
        self.copy(k).wait_recv()
        self.total_s[k + 1] = self.total_s[k] + self.part_s[k]
        if k + 1 < len(self.steps):
            self.copy(k + 1).start()
        else:
            self.pipe_copy().start()

    def close(self):
        chan_o, step_o, rest_o = self.outs
        k = len(self.steps)
        self.pipe_copy().wait_recv()
        mine, far, t = self.total_s.at[k, self.p], self.far_s, self.t
        for ref, where in ((mine, self.p), (far, 1 - self.p)):
            chan_o[:, aligned(where, self.half)] = ref[0:8, aligned(t, self.half)]
            step_o[aligned(where, 8), :] = ref[pl.ds(pl.multiple_of(8 + 8 * t, 8), 8), aligned(self.d, self.rows)]
        last = far.shape[0] - 8
        row = iota((8, far.shape[1]), 0)
        rest_o[...] = mine[last:, :] + jnp.where(row == 0, 0.0, far[last:, :])
        for k in range(len(self.steps)):
            self.copy(k).wait_send()
        self.pipe_copy().wait_send()


def reduce_grads(count, *refs):
    factors, pack, results, sums_o = refs[:5], refs[5], refs[6], refs[7:10]
    reducer = Reducer(count, factors, results, refs[10:23], refs[23:36])
    sums = Sums(count, reducer.rows, reducer.half, pack, sums_o, refs[36:])
    greet(reducer.partners() + sums.partners())
    sums.begin()

    def step(n, carry):
        reducer.tick(n)
        for k in range(len(sums.steps)):

            @pl.when(n == 2 * k + 2)
            def _():
                sums.step(k)

        return carry

    lax.fori_loop(0, reducer.ticks, step, 0)
    sums.close()
    reducer.close()


def reduce_call(factors, pack, count, groups):
    _, micro, rows, model = factors[0].shape
    width = factors[2].shape[3]
    half = width // count
    buffers, sems = Reducer.scratch(count, micro, rows, model, half, groups)
    inside = pl.BlockSpec(memory_space=pltpu.VMEM)
    anywhere = pl.BlockSpec(memory_space=pl.ANY)
    return pl.pallas_call(
        functools.partial(reduce_grads, count),
        in_specs=[anywhere] * 5 + [inside],
        out_specs=[anywhere] + [inside] * 3,
        out_shape=[
            jax.ShapeDtypeStruct((3, model // groups, 2 * half), BF),
            jax.ShapeDtypeStruct((8, 2 * half), F32),
            jax.ShapeDtypeStruct((16, model // groups), F32),
            jax.ShapeDtypeStruct((8, width), F32),
        ],
        scratch_shapes=buffers + sems + Sums.scratch(count, pack.shape),
        compiler_params=pltpu.CompilerParams(collective_id=1, has_side_effects=True, vmem_limit_bytes=VMEM_LIMIT),
    )(*factors, pack)


def fused_forward(count, head_dim, micro, *refs):
    (tokens, mask, value, gate_w, out_w, step_w, state_w, chan, shared) = refs[:9]
    (wv_h, wg_h, wo_h, wt_h, ws_h, pv_o, ps_o, ph_o, pn_o) = refs[9:18]
    (out_h, low_h, mix_h, inv_o, nx_o, vpre_o, spre_o, x_o, bc_o, dtc_o, gate_o, y_o, gg_o, sin_o) = refs[18:32]
    (nx_s, sc_s, wide_s, place_s, cum_s, cumt_s, acc_s, sq_s, psend, precv, sqsend, sqrecv, csend, crecv, hrecv, trecv) = refs[32:48]
    (ps_sem, pr_sem, ss_sem, sr_sem, cs_sem, cr_sem, hs_sem, hr_sem, ts_sem, tr_sem, low_sem, out_sem, mix_sem) = refs[48:61]
    (wv_s, wg_s, wo_s, ws_s, wt_s, chan_s, shared_s, w_sem, l_sem) = refs[61:70]
    q, s, g = pl.program_id(0), pl.program_id(1), pl.program_id(2)
    groups = cum_s.shape[0]
    p, t = lax.axis_index(PIPE), lax.axis_index(TENSOR)
    idx = q * micro + s
    slot = idx * groups + g
    total_idx = 2 * micro
    rows, model = tokens.shape[1], tokens.shape[2]
    state = bc_o.shape[1] // 2
    per_group = GC // head_dim
    inner_total = 2 * groups * GC
    gather = Gather(
        count,
        (value, gate_w, out_w, step_w),
        (wv_h, wg_h, wo_h, wt_h),
        ((state_w, ws_h), (chan, chan_s), (shared, shared_s)),
        refs[70:],
    )
    big = ((wv_h, wv_s), (wg_h, wg_s), (wo_h, wo_s))

    def weight_copy(step, k):
        layer, group = step // (micro * groups), lax.rem(step, groups)
        held = lax.rem(step, 2)
        return pltpu.make_async_copy(big[k][0].at[layer, :, aligned(group, GC)], big[k][1].at[held], w_sem.at[held, k])

    def layer_copies(layer):
        return (
            pltpu.make_async_copy(ws_h.at[layer], ws_s, l_sem.at[0]),
            pltpu.make_async_copy(wt_h.at[layer], wt_s, l_sem.at[1]),
        )

    def part_copy(i):
        return remote(psend.at[i], precv.at[i], ps_sem.at[i], pr_sem.at[i], PIPE, 1 - p)

    def square_copy(i):
        return remote(sqsend.at[i], sqrecv.at[i], ss_sem.at[i], sr_sem.at[i], PIPE, 1 - p)

    def chain_copy(i):
        return remote(csend.at[i], crecv.at[i], cs_sem.at[i], cr_sem.at[i], TENSOR, t + 1)

    def halo_copy(i):
        return remote(psend.at[i, rows - HALO :, :], hrecv.at[i], hs_sem.at[i], hr_sem.at[i], TENSOR, t + 1)

    def tokens_copy():
        return remote(tokens.at[:, rows - HALO :, :], trecv, ts_sem.at[0], tr_sem.at[0], TENSOR, t + 1)

    def low_copy(i):
        return pltpu.make_async_copy(psend.at[i], low_h.at[i], low_sem.at[i])

    def out_copy(i):
        return pltpu.make_async_copy(psend.at[i], out_h.at[lax.rem(i, micro)], out_sem.at[i])

    def mix_copy(i):
        return pltpu.make_async_copy(precv.at[i], mix_h.at[i], mix_sem.at[i])

    @pl.when((idx == 0) & (g == 0))
    def _():
        greet(gather.partners())

        @pl.when(t < count - 1)
        def _():
            tokens_copy().start()

        fill_places(place_s, head_dim)
        gather.first_layer()
        for k in range(3):
            weight_copy(0, k).start()
        pv_o[...] = chan_s[...]
        heads = per_group * groups // count
        half = groups * GC // count
        place, lane = iota((groups * GC, LANES), 0), iota((groups * GC, LANES), 1)
        first = half * (lane // heads) + lax.rem(lane, heads)
        used = lane < per_group * groups
        for layer in range(2):
            per_head = chan_s[layer]
            for kind in range(2):
                pick = ((place == first + kind * heads) & used).astype(BF)
                ph_o[layer, kind : kind + 1, :] = pick_cols(per_head, pick)[7:8, :]
            ph_o[layer, 2:, :] = jnp.zeros((6, LANES), F32)
            pn_o[layer] = shared_s[layer]
            for k in range(5):
                ps_o[layer, k : k + 1, :] = shared_s[layer, 1:2, 2 * state * k : 2 * state * (k + 1)]
            ps_o[layer, 5:, :] = jnp.zeros((3, 2 * state), F32)

    columns = groups * GC // count
    late = gather.second_layer(micro * groups, lambda src: src * columns // GC)
    for step in sorted({step for step, _ in late}):

        @pl.when(slot == step)
        def _():
            for when, stage in late:
                if when == step:
                    stage()

    @pl.when((s == 0) & (g == 0))
    def _():
        for copy in layer_copies(q):
            copy.start()
        for copy in layer_copies(q):
            copy.wait()

    for k in range(3):
        weight_copy(slot, k).wait()

    @pl.when(slot + 1 < total_idx * groups)
    def _():
        for k in range(3):
            weight_copy(slot + 1, k).start()

    held = lax.rem(slot, 2)
    ws, wt, wv, wg, wo = ws_s, wt_s, wv_s.at[held], wg_s.at[held], wo_s.at[held]
    pv, ps, ph, pn = pv_o.at[q, :, aligned(g, GC)], ps_o.at[q], ph_o.at[q], pn_o.at[q]

    def normed(u):
        uf = u.astype(F32)
        return (uf * lax.rsqrt(jnp.mean(uf * uf, axis=1, keepdims=True) + EPS) * pn[0:1, :]).astype(BF)

    @pl.when((g == 0) & (q == 0))
    def _():
        nx_s[HALO:, :] = normed(tokens[s])

        @pl.when(t == 0)
        def _():
            nx_s[:HALO, :] = jnp.zeros((HALO, model), BF)

        @pl.when(t > 0)
        def _():
            @pl.when(s == 0)
            def _():
                tokens_copy().wait_recv()

            nx_s[:HALO, :] = normed(trecv[s])

    @pl.when((g == 0) & (q == 1))
    def _():
        nx_s[HALO:, :] = normed(psend[s])

        @pl.when(t == 0)
        def _():
            nx_s[:HALO, :] = jnp.zeros((HALO, model), BF)

        @pl.when(t > 0)
        def _():
            halo_copy(s).wait_recv()
            nx_s[:HALO, :] = normed(hrecv[s])

    @pl.when(g == 0)
    def _():
        nx_o[...] = nx_s[HALO:, :]
        spre = nn(nx_s[...], ws[...])
        spre_o[...] = spre
        conv = conv_rows(spre, ps, rows)
        bc = (conv * sigmoid(conv)).astype(BF)
        bc_o[...] = bc
        scores = nt(bc[:, state:], bc[:, :state])
        lower = iota((rows, rows), 0) >= iota((rows, rows), 1)
        sc_s[...] = jnp.where(lower, scores, 0.0)
        raw = nt(nx_s[HALO:, :], wt[...])
        raw = pick_cols(raw, step_places(count, raw.shape[1], per_group * groups).astype(BF)) + ph[0:1, :]
        step = jnp.maximum(raw, 0.0) + jnp.log(1.0 + jnp.exp(-jnp.abs(raw)))
        cum = pick_rows(lower.astype(BF), -step * jnp.exp(ph[1:2, :]))
        dtc_o[0] = step
        dtc_o[1] = cum
        dtc_o[2] = sigmoid(raw)
        to_end = jnp.exp(cum[rows - 1 : rows, :] - cum)
        fill_wide(wide_s, (step, step * to_end, jnp.exp(cum)))
        cum = cum * LOG2E
        group_lanes(cum, cum_s, groups, per_group)
        group_rows(cum, cumt_s, groups, per_group)
        acc_s[...] = jnp.zeros_like(acc_s)
        sq_s[...] = jnp.zeros_like(sq_s)

    pre = nn(nx_s[...], wv[...])
    vpre_o[...] = pre
    conv = conv_rows(pre, pv, rows)
    x = conv * sigmoid(conv)
    x_o[...] = x.astype(BF)
    cum, cumt, places = cum_s[g], cumt_s[g], place_s[g]
    xp = (x * nn(wide_s[0], places)).astype(BF)
    xr = (x * nn(wide_s[1], places)).astype(BF)
    local = tn(xr, bc_o[:, :state])

    @pl.when(t == 0)
    def _():
        sin_o[...] = jnp.zeros_like(sin_o)

    @pl.when(t > 0)
    def _():
        chain_copy(slot).wait_recv()
        sin_o[...] = crecv[slot]

    @pl.when(t < count - 1)
    def _():
        csend[slot] = (through_rows(cumt, rows, head_dim, state) * sin_o[...].astype(F32) + local).astype(BF)
        chain_copy(slot).start()

    lane = iota((rows, LANES), 1)
    cut = rows // 2
    within = []
    for pair in range(GC // LANES):
        cols = slice(LANES * pair, LANES * (pair + 1))
        outs = []
        for i in (2 * pair, 2 * pair + 1):
            parts = []
            for first, seen in ((0, cut), (cut, rows)):
                diff = cum[first : first + cut, i : i + 1] - cumt[i : i + 1, :seen]
                mix = (jnp.exp2(jnp.minimum(diff, 0.0)) * sc_s[first : first + cut, :seen]).astype(BF)
                parts.append(nn(mix, xp[:seen, cols]))
            outs.append(jnp.concatenate(parts, axis=0))
        within.append(jnp.where(lane < head_dim, outs[0], outs[1]))
    gate = nn(nx_s[HALO:, :], wg[...])
    gate_o[...] = gate
    carried = nt(bc_o[:, state:], sin_o[...])
    y = jnp.concatenate(within, axis=1) + pv[6:7, :] * x + nn(wide_s[2], places) * carried
    y_o[...] = y
    gated = y * (gate * sigmoid(gate))
    gg = (gated * pv[5:6, :]).astype(BF)
    gg_o[...] = gg
    squares = gated * gated
    for part in range(GC // LANES):
        sq_s[...] += squares[:, LANES * part : LANES * (part + 1)]
    acc_s[...] += nt(gg, wo[...])

    @pl.when(g == groups - 1)
    def _():
        psend[idx] = acc_s[...].astype(BF)
        sqsend[idx] = jnp.broadcast_to(jnp.sum(sq_s[...], axis=1, keepdims=True), (rows, LANES))
        part_copy(idx).start()
        square_copy(idx).start()

    def finish(i):
        j = lax.rem(i, micro)
        part_copy(i).wait()
        square_copy(i).wait()
        inverse = lax.rsqrt((sqsend[i] + sqrecv[i]) / inner_total + EPS)
        inv_o[i] = inverse
        mixed = inverse[:, 0:1] * (psend[i].astype(F32) + precv[i].astype(F32))
        precv[i] = mixed.astype(BF)
        row_mask = mask[j][:, 0:1]

        @pl.when(i < micro)
        def _():
            psend[i] = (row_mask * (tokens[j].astype(F32) + mixed)).astype(BF)

            @pl.when(t < count - 1)
            def _():
                halo_copy(j).start()

            low_copy(j).start()

        @pl.when(i >= micro)
        def _():
            psend[i] = (row_mask * (psend[j].astype(F32) + mixed)).astype(BF)

        @pl.when(i // micro == p)
        def _():
            out_copy(i).start()

        mix_copy(i).start()

    @pl.when((g == 1) & (idx > 1))
    def _():
        finish(idx - 2)

    @pl.when((g == groups - 1) & (idx == total_idx - 1))
    def _():
        finish(idx - 1)
        finish(idx)
        for i in range(total_idx):
            mix_copy(i).wait()

            @pl.when(i // micro == p)
            def _():
                out_copy(i).wait()

        for i in range(micro):
            low_copy(i).wait()

        gather.finish()

        @pl.when(t < count - 1)
        def _():
            tokens_copy().wait_send()
            for i in range(micro):
                halo_copy(i).wait_send()

            def drain(i, carry):
                chain_copy(i).wait_send()
                return carry

            lax.fori_loop(0, total_idx * groups, drain, 0)


def step_places(count, rows, all_heads):
    heads, size = all_heads // count, rows // count
    place, lane = iota((rows, LANES), 0), iota((rows, LANES), 1)
    return ((place == size * (lane // heads) + lax.rem(lane, heads)) & (lane < all_heads)).astype(F32)


def fill_places(place_s, head_dim):
    shape = place_s.shape[1:]
    head, col = lax.rem(iota(shape, 0), LANES), iota(shape, 1) // head_dim
    for g in range(place_s.shape[0]):
        place_s[g] = (head == col + g * (GC // head_dim)).astype(BF)


def fill_wide(wide_s, values):
    for k, value in enumerate(values):
        high = value.astype(BF)
        wide_s[k, :, :LANES] = high
        wide_s[k, :, LANES:] = (value - high.astype(F32)).astype(BF)


def through_rows(cumt, rows, head_dim, state):
    end = jnp.exp2(cumt[:, rows - 1 : rows])
    parts = [jnp.broadcast_to(end[i : i + 1, :], (head_dim, state)) for i in range(GC // head_dim)]
    return jnp.concatenate(parts, axis=0)


def fused_backward(count, head_dim, micro, *refs):
    (cot, tokens, out0, mask, inv, mix, vpre, spre, x, bc, dtc, gate, y, s_in) = refs[:14]
    (wv, wg, wo, ws, wt, pv, ps, ph, pn) = refs[14:23]
    (grad_h, dval_o, dgate_o, dst_o, dstep_o, sgm_o, vs_o, ss_o, hs_o, norm_o) = refs[23:33]
    (gm_s, rowsc_s, gin_s, halo_s, halo2_s, acc_s, nacc_s) = refs[33:40]
    (sct_s, scts_s, wsum_s, dbc_s, wide_s, place_s, cum_s, cumt_s, net_s, rv_s, ddir_s, k_s, rt_s, rall_s) = refs[40:54]
    (psend, precv, csend, crecv, hsend, hrecv, tsend, trecv) = refs[54:62]
    (ps_sem, pr_sem, cs_sem, cr_sem, hs_sem, hr_sem, ts_sem, tr_sem, out_sem) = refs[62:]
    turn, s, g = pl.program_id(0), pl.program_id(1), pl.program_id(2)
    groups = cum_s.shape[0]
    p, t = lax.axis_index(PIPE), lax.axis_index(TENSOR)
    idx = turn * micro + s
    slot = idx * groups + g
    total_idx = 2 * micro
    rows, model = cot.shape[1], cot.shape[2]
    state = bc.shape[1] // 2
    per_group = GC // head_dim
    inner_total = 2 * groups * GC

    def part_copy(i):
        return remote(psend.at[i], precv.at[i], ps_sem.at[i], pr_sem.at[i], PIPE, 1 - p)

    def chain_copy(i):
        return remote(csend.at[i], crecv.at[i], cs_sem.at[i], cr_sem.at[i], TENSOR, t - 1)

    def halo_copy(i):
        return remote(hsend.at[i], hrecv.at[i], hs_sem.at[i], hr_sem.at[i], TENSOR, t - 1)

    def tail_copy(i):
        return remote(tsend.at[i], trecv.at[i], ts_sem.at[i], tr_sem.at[i], TENSOR, t - 1)

    def out_copy(i):
        return pltpu.make_async_copy(psend.at[i], grad_h.at[lax.rem(i, micro)], out_sem.at[i])

    @pl.when((idx == 0) & (g == 0))
    def _():
        greet(ring_neighbours(count) + [(PIPE, 1 - p)])
        fill_places(place_s, head_dim)
        nacc_s[...] = jnp.zeros_like(nacc_s)

    @pl.when((g == 0) & (turn == 0))
    def _():
        gm_s[...] = (mask[s][:, 0:1] * cot[s].astype(F32)).astype(BF)

    @pl.when((g == 0) & (turn == 1))
    def _():
        gm_s[...] = (mask[s][:, 0:1] * psend[s].astype(F32)).astype(BF)

    @pl.when(g == 0)
    def _():
        gmf = gm_s[...].astype(F32)
        inverse = inv[...]
        dot = jnp.sum(gmf * mix[...].astype(F32), axis=1, keepdims=True)
        rowsc_s[...] = inverse * inverse * dot / inner_total
        sgm_o[...] = (gmf * inverse[:, 0:1]).astype(BF)
        scores = nt(bc[:, :state], bc[:, state:])
        first, second = iota((rows, rows), 0), iota((rows, rows), 1)
        sct_s[...] = jnp.where(second >= first, scores, 0.0)
        scts_s[...] = jnp.where(second > first, scores, 0.0)
        wsum_s[...] = jnp.zeros_like(wsum_s)
        dbc_s[...] = jnp.zeros_like(dbc_s)
        rall_s[...] = jnp.zeros_like(rall_s)
        acc_s[...] = jnp.zeros_like(acc_s)
        for part_s in (net_s, rv_s, ddir_s, k_s):
            part_s[...] = jnp.zeros_like(part_s)
        cum = dtc[1]
        fill_wide(wide_s, (dtc[0], jnp.exp(cum[rows - 1 : rows, :] - cum), jnp.exp(cum)))
        cum = cum * LOG2E
        group_lanes(cum, cum_s, groups, per_group)
        group_rows(cum, cumt_s, groups, per_group)

    cum, cumt, places = cum_s[g], cumt_s[g], place_s[g]
    fromx = nn(wide_s[2], places)

    gs = nn(gm_s[...], wo[...])
    inverse, shrink = inv[:, 0:1], rowsc_s[:, 0:1]
    gv, yv = gate[...], y[...]
    sig = sigmoid(gv)
    silu = gv * sig
    gated = yv * silu
    dgain = jnp.sum(gs * gated * inverse, axis=0, keepdims=True)
    dgated = inverse * (gs * pv[5:6, :]) - gated * shrink
    dgate = (dgated * yv * (sig * (1.0 + gv * (1.0 - sig)))).astype(BF)
    dgate_o[...] = dgate
    dyb = (dgated * silu).astype(BF)
    dyf = dyb.astype(F32)
    dyef = dyf * fromx
    dye = dyef.astype(BF)
    dsl = tn(dye, bc[:, state:])

    @pl.when(t == count - 1)
    def _():
        gin_s[...] = jnp.zeros_like(gin_s)

    @pl.when(t < count - 1)
    def _():
        chain_copy(slot).wait_recv()
        gin_s[...] = crecv[slot]

    @pl.when(t > 0)
    def _():
        csend[slot] = (through_rows(cumt, rows, head_dim, state) * gin_s[...].astype(F32) + dsl).astype(BF)
        chain_copy(slot).start()

    stepx = nn(wide_s[0], places)
    endx = nn(wide_s[1], places)
    xf = x[...].astype(F32)
    xp = (xf * stepx).astype(BF)
    xr = (xf * stepx * endx).astype(BF)
    gb = nt(bc[:, :state], gin_s[...])
    cs = nt(bc[:, state:], s_in[...])
    dbc_s[:, :state] += nn(xr, gin_s[...])
    dbc_s[:, state:] += nn(dye, s_in[...])

    lane = iota((rows, LANES), 1)
    cut = rows // 2
    blocks = ((slice(0, cut), slice(0, rows)), (slice(cut, rows), slice(cut, rows)))
    wsums = [wsum_s[js, at] for js, at in blocks]
    colsums = [jnp.zeros((cut, LANES), F32)] * 2
    within = []
    for pair in range(GC // LANES):
        cols = slice(LANES * pair, LANES * (pair + 1))
        xpp, dyp = xp[:, cols], dyb[:, cols]
        outs = []
        for side in range(2):
            i = 2 * pair + side
            mine = (lane < head_dim) if side == 0 else (lane >= head_dim)
            xph = jnp.where(mine, xpp, jnp.zeros_like(xpp))
            parts, rowsums = [], []
            for k, (js, at) in enumerate(blocks):
                decay = jnp.exp2(jnp.minimum(cumt[i : i + 1, at] - cum[js, i : i + 1], 0.0))
                parts.append(nn((decay * sct_s[js, at]).astype(BF), dyp[at]))
                weight = decay * nt(xph[js], dyp[at])
                wsums[k] = wsums[k] + weight
                pairs = (weight * scts_s[js, at]).astype(BF)
                colsums[k] = colsums[k] + nn(pairs, (lane[at] == i + per_group * g).astype(BF))
                rowsums.append(jnp.sum(pairs.astype(F32), axis=0, keepdims=True))
            outs.append(jnp.concatenate(parts, axis=0))
            rt_s[g, i : i + 1, :cut] = rowsums[0][:, :cut]
            rt_s[g, i : i + 1, cut:] = rowsums[0][:, cut:] + rowsums[1]
        within.append(jnp.where(lane < head_dim, outs[0], outs[1]))
    for k, (js, at) in enumerate(blocks):
        wsum_s[js, at] = wsums[k]
    colsum = jnp.concatenate(colsums, axis=0)
    u = jnp.concatenate(within, axis=1) + endx * gb

    heads = (iota((GC, LANES), 0) // head_dim + per_group * g == iota((GC, LANES), 1)).astype(BF)
    ddir_s[...] += nn((xf * u).astype(BF), heads)
    net_s[...] += nn((dyef * cs).astype(BF), heads) - colsum
    rv_s[...] += nn((xf * gb).astype(BF), heads)
    inner = (gin_s[...].astype(F32) * s_in[...].astype(F32)).astype(BF)
    per_channel = nt(jnp.ones((16, inner.shape[1]), BF), inner)
    k_s[...] += nn(per_channel.astype(BF), heads)[:8]

    dx = stepx * u + pv[6:7, :] * dyf
    dconv = dx * silu_slope(conv_rows(vpre, pv, rows))

    @pl.when(t > 0)
    def _():
        hsend[slot] = dconv[:8, :]
        halo_copy(slot).start()

    sums = conv_sums(dconv, vpre, rows)
    sums.append(dgain)
    sums.append(jnp.sum(dyf * xf, axis=0, keepdims=True))
    sums.append(jnp.zeros((1, GC), F32))
    vs_o[...] = jnp.concatenate(sums, axis=0)
    acc_s[...] += nt(dgate, wg[...])

    @pl.when(t == count - 1)
    def _():
        halo_s[...] = jnp.zeros_like(halo_s)

    @pl.when(t < count - 1)
    def _():
        halo_copy(slot).wait_recv()
        halo_s[...] = hrecv[slot]

    dval = conv_transposed(dconv, halo_s[...], pv, rows).astype(BF)
    dval_o[...] = dval
    acc_s[...] += nt(dval, wv[...])

    @pl.when(g == groups - 1)
    def _():
        first, second = iota((rows, rows), 0), iota((rows, rows), 1)
        weights = jnp.where(second >= first, wsum_s[...], 0.0).astype(BF)
        db = dbc_s[:, :state] + nn(weights, bc[:, state:])
        dc = dbc_s[:, state:] + tn(weights, bc[:, :state])
        dsc = jnp.concatenate([db, dc], axis=1) * silu_slope(conv_rows(spre, ps, rows))

        @pl.when(t > 0)
        def _():
            tsend[idx] = dsc[:8, :]
            tail_copy(idx).start()

        ssums = conv_sums(dsc, spre, rows)
        ssums.append(jnp.zeros((3, 2 * state), F32))
        ss_o[...] = jnp.concatenate(ssums, axis=0)
        for other in range(groups):
            shift = per_group * other
            rall_s[shift : shift + per_group, :] = rt_s[other, 0:per_group, :]
        total, step = dtc[1], dtc[0]
        last = total[rows - 1 : rows, :]
        net = net_s[...] + rall_s[...].T
        rv = rv_s[...] * step * jnp.exp(last - total)
        da = pick_rows((second >= first).astype(BF), net) + pick_rows((second < first).astype(BF), rv)
        da = da + jnp.exp(last) * k_s[0:1, :]
        ddir = ddir_s[...]
        rate = jnp.exp(ph[1:2, :])
        dstep = (ddir - da * rate) * dtc[2]
        dstep_o[...] = dstep.astype(BF)
        hs_o[...] = jnp.concatenate(
            [
                jnp.sum(dstep, axis=0, keepdims=True),
                jnp.sum(-da * dtc[0] * rate, axis=0, keepdims=True),
                jnp.zeros((6, LANES), F32),
            ],
            axis=0,
        )

        @pl.when(t == count - 1)
        def _():
            halo2_s[...] = jnp.zeros_like(halo2_s)

        @pl.when(t < count - 1)
        def _():
            tail_copy(idx).wait_recv()
            halo2_s[...] = trecv[idx]

        dst = conv_transposed(dsc, halo2_s[...], ps, rows).astype(BF)
        dst_o[...] = dst
        psend[idx] = (acc_s[...] + nt(dst, ws[...]) + nn(dstep_o[...], wt[...])).astype(BF)
        part_copy(idx).start()

    def finish(i):
        j = lax.rem(i, micro)
        part_copy(i).wait()
        which = 1 - i // micro
        row_mask = mask[j][:, 0:1]

        def close(u, incoming):
            uf = u.astype(F32)
            grad_normed = psend[i].astype(F32) + precv[i].astype(F32)
            root_inv = lax.rsqrt(jnp.mean(uf * uf, axis=1, keepdims=True) + EPS)
            nacc_s[which] += jnp.broadcast_to(jnp.sum(grad_normed * uf * root_inv, axis=0, keepdims=True), (8, model))
            weighted = grad_normed * pn[which][0:1, :]
            shared = jnp.mean(weighted * uf, axis=1, keepdims=True) * root_inv * root_inv * root_inv
            kept = (row_mask * incoming.astype(F32)).astype(BF).astype(F32)
            psend[i] = (root_inv * weighted - uf * shared + kept).astype(BF)

        @pl.when(i < micro)
        def _():
            close(out0[j], cot[j])

        @pl.when(i >= micro)
        def _():
            close(tokens[j], psend[j])

        @pl.when(which == p)
        def _():
            out_copy(i).start()

    @pl.when((g == 1) & (idx > 1))
    def _():
        finish(idx - 2)

    @pl.when((g == groups - 1) & (idx == total_idx - 1))
    def _():
        finish(idx - 1)
        finish(idx)
        norm_o[...] = nacc_s[...]
        for i in range(total_idx):

            @pl.when(1 - i // micro == p)
            def _():
                out_copy(i).wait()

        @pl.when(t > 0)
        def _():
            for i in range(total_idx):
                tail_copy(i).wait_send()

            def drain(i, carry):
                chain_copy(i).wait_send()
                halo_copy(i).wait_send()
                return carry

            lax.fori_loop(0, total_idx * groups, drain, 0)


def all_of(shape, buffers=2):
    spec = functools.partial(pl.BlockSpec, shape, lambda q, s, g: (0,) * len(shape))
    return spec(pipeline_mode=pl.Buffered(buffers)) if buffers != 2 else spec()


def fused_specs(turned):
    def layer(q):
        return 1 - q if turned else q

    def item(*shape):
        zeros = (0,) * len(shape)
        return pl.BlockSpec((None, None) + shape, lambda q, s, g: (layer(q), s) + zeros)

    def item_cols(rows):
        return pl.BlockSpec((None, None, rows, GC), lambda q, s, g: (layer(q), s, 0, g))

    def item_rows(cols):
        return pl.BlockSpec((None, None, GC, cols), lambda q, s, g: (layer(q), s, g, 0))

    def layer_cols(rows):
        return pl.BlockSpec((None, rows, GC), lambda q, s, g: (layer(q), 0, g))

    def layer_all(*shape):
        zeros = (0,) * len(shape)
        return pl.BlockSpec((None,) + shape, lambda q, s, g: (layer(q),) + zeros)

    return item, item_cols, item_rows, layer_cols, layer_all


def forward_call(tokens, mask, shards, chan, shared, count, groups_dp, head_dim):
    micro, rows, model = tokens.shape
    value, gate, out, step, state_w = shards
    half, states = value.shape[1] // 2, state_w.shape[1]
    width, state = half * count, states // 2
    groups = width // GC
    item, item_cols, item_rows, layer_cols, layer_all = fused_specs(False)
    slots = 2 * micro
    dma = pltpu.SemaphoreType.DMA
    vmem = pltpu.VMEM
    anywhere = pl.BlockSpec(memory_space=pl.ANY)
    ins = [
        (tokens, all_of(tokens.shape, 1)),
        (mask, all_of(mask.shape, 1)),
        (value, anywhere),
        (gate, anywhere),
        (out, anywhere),
        (step, anywhere),
        (state_w, anywhere),
        (chan, anywhere),
        (shared, anywhere),
    ]
    pair = (2, micro)
    step_rows = step.shape[0] // 2 * count
    outs = [
        (((2, model, width), BF), anywhere),
        (((2, model, width), BF), anywhere),
        (((2, model, width), BF), anywhere),
        (((2, step_rows, model), BF), anywhere),
        (((2, model, states), BF), anywhere),
        (((2, 8, width), F32), all_of((2, 8, width))),
        (((2, 8, states), F32), all_of((2, 8, states))),
        (((2, 8, LANES), F32), all_of((2, 8, LANES))),
        (((2,) + shared.shape, F32), all_of((2,) + shared.shape)),
        (((micro, rows, model), BF), anywhere),
        (((micro, rows, model), BF), anywhere),
        (((slots, rows, model), BF), anywhere),
        (((slots, rows, LANES), F32), all_of((slots, rows, LANES))),
        ((pair + (rows, model), BF), item(rows, model)),
        ((pair + (rows + HALO, width), F32), item_cols(rows + HALO)),
        ((pair + (rows + HALO, states), F32), item(rows + HALO, states)),
        ((pair + (rows, width), BF), item_cols(rows)),
        ((pair + (rows, states), BF), item(rows, states)),
        ((pair + (3, rows, LANES), F32), item(3, rows, LANES)),
        ((pair + (rows, width), F32), item_cols(rows)),
        ((pair + (rows, width), F32), item_cols(rows)),
        ((pair + (rows, width), BF), item_cols(rows)),
        ((pair + (width, state), BF), item_rows(state)),
    ]
    scratch = [
        vmem((rows + HALO, model), BF),
        vmem((rows, rows), F32),
        vmem((3, rows, 2 * LANES), BF),
        vmem((groups, 2 * LANES, GC), BF),
        vmem((groups, rows, LANES), F32),
        vmem((groups, 8, rows), F32),
        vmem((rows, model), F32),
        vmem((rows, LANES), F32),
        vmem((slots, rows, model), BF),
        vmem((slots, rows, model), BF),
        vmem((slots, rows, LANES), F32),
        vmem((slots, rows, LANES), F32),
        vmem((slots * groups, GC, state), BF),
        vmem((slots * groups, GC, state), BF),
        vmem((micro, HALO, model), BF),
        vmem((micro, HALO, model), BF),
        dma((slots,)),
        dma((slots,)),
        dma((slots,)),
        dma((slots,)),
        dma((slots * groups,)),
        dma((slots * groups,)),
        dma((micro,)),
        dma((micro,)),
        dma((1,)),
        dma((1,)),
        dma((micro,)),
        dma((slots,)),
        dma((slots,)),
        vmem((2, model, GC), BF),
        vmem((2, model, GC), BF),
        vmem((2, model, GC), BF),
        vmem((model, states), BF),
        vmem((step_rows, model), BF),
        vmem((2, 8, width), F32),
        vmem((2,) + shared.shape, F32),
        dma((2, 3)),
        dma((2,)),
    ] + Gather.scratch(count)
    kernel = functools.partial(fused_forward, count, head_dim, micro)
    flops = slots * (6 * rows * model * width + 6 * rows * rows * width)
    options = fused_options(pair + (groups,), ins, outs, scratch, 2, flops, 60 * slots * rows * width)
    return pl.pallas_call(kernel, **options)(*[array for array, _ in ins])


def fused_options(grid, ins, outs, scratch, collective, flops, traffic):
    return dict(
        grid=grid,
        in_specs=[spec for _, spec in ins],
        out_specs=[spec for _, spec in outs],
        out_shape=[jax.ShapeDtypeStruct(*kind) for kind, _ in outs],
        scratch_shapes=scratch,
        cost_estimate=pl.CostEstimate(flops=flops, bytes_accessed=traffic, transcendentals=0),
        compiler_params=pltpu.CompilerParams(
            collective_id=collective,
            has_side_effects=True,
            vmem_limit_bytes=VMEM_LIMIT,
            dimension_semantics=(SEQUENTIAL,) * len(grid),
        ),
    )


def backward_fused_call(cot, tokens, out0, mask, kept, w, par, count, head_dim):
    micro, rows, model = tokens.shape
    width, states = w.value.shape[2], w.state.shape[2]
    state = states // 2
    groups = width // GC
    item, item_cols, item_rows, layer_cols, layer_all = fused_specs(True)
    slots = 2 * micro
    dma = pltpu.SemaphoreType.DMA
    vmem = pltpu.VMEM
    ins = [
        (cot, all_of(cot.shape, 1)),
        (tokens, all_of(tokens.shape, 1)),
        (out0, all_of(out0.shape, 1)),
        (mask, all_of(mask.shape, 1)),
        (kept.inv, item(rows, LANES)),
        (kept.mix, item(rows, model)),
        (kept.vpre, item_cols(rows + HALO)),
        (kept.spre, item(rows + HALO, states)),
        (kept.x, item_cols(rows)),
        (kept.bc, item(rows, states)),
        (kept.dtc, item(3, rows, LANES)),
        (kept.gate, item_cols(rows)),
        (kept.y, item_cols(rows)),
        (kept.s_in, item_rows(state)),
        (w.value, layer_cols(model)),
        (w.gate, layer_cols(model)),
        (w.out, layer_cols(model)),
        (w.state, layer_all(model, states)),
        (w.step, layer_all(LANES, model)),
        (par.value, layer_cols(8)),
        (par.state, layer_all(8, states)),
        (par.head, layer_all(8, LANES)),
        (par.norm, all_of(par.norm.shape, 1)),
    ]
    pair = (2, micro)
    outs = [
        (((micro, rows, model), BF), pl.BlockSpec(memory_space=pl.ANY)),
        ((pair + (rows, width), BF), item_cols(rows)),
        ((pair + (rows, width), BF), item_cols(rows)),
        ((pair + (rows, states), BF), item(rows, states)),
        ((pair + (rows, LANES), BF), item(rows, LANES)),
        ((pair + (rows, model), BF), item(rows, model)),
        ((pair + (8, width), F32), item_cols(8)),
        ((pair + (8, states), F32), item(8, states)),
        ((pair + (8, LANES), F32), item(8, LANES)),
        (((2, 8, model), F32), all_of((2, 8, model))),
    ]
    lanes = vmem((rows, LANES), F32)
    square = vmem((rows, rows), F32)
    scratch = [
        vmem((rows, model), BF),
        vmem((rows, LANES), F32),
        vmem((GC, state), BF),
        vmem((8, GC), F32),
        vmem((8, states), F32),
        vmem((rows, model), F32),
        vmem((2, 8, model), F32),
        square,
        square,
        square,
        vmem((rows, states), F32),
        vmem((3, rows, 2 * LANES), BF),
        vmem((groups, 2 * LANES, GC), BF),
        vmem((groups, rows, LANES), F32),
        vmem((groups, 8, rows), F32),
        lanes,
        lanes,
        lanes,
        vmem((8, LANES), F32),
        vmem((groups, 8, rows), F32),
        vmem((LANES, rows), F32),
        vmem((slots, rows, model), BF),
        vmem((slots, rows, model), BF),
        vmem((slots * groups, GC, state), BF),
        vmem((slots * groups, GC, state), BF),
        vmem((slots * groups, 8, GC), F32),
        vmem((slots * groups, 8, GC), F32),
        vmem((slots, 8, states), F32),
        vmem((slots, 8, states), F32),
        dma((slots,)),
        dma((slots,)),
        dma((slots * groups,)),
        dma((slots * groups,)),
        dma((slots * groups,)),
        dma((slots * groups,)),
        dma((slots,)),
        dma((slots,)),
        dma((slots,)),
    ]
    kernel = functools.partial(fused_backward, count, head_dim, micro)
    flops = slots * (8 * rows * model * width + 16 * rows * rows * width)
    options = fused_options(pair + (groups,), ins, outs, scratch, 3, flops, 60 * slots * rows * width)
    return pl.pallas_call(kernel, **options)(*[array for array, _ in ins])


def fused_body(
    tokens_in,
    cotangent,
    lengths,
    in_gate,
    in_value,
    in_state,
    in_step,
    out_proj,
    norm_gain,
    conv_value,
    conv_state,
    bias_value,
    bias_state,
    step_bias,
    decay_log,
    skip_gain,
    gate_gain,
):
    layer, group, block = lax.axis_index(PIPE), lax.axis_index(DP), lax.axis_index(TENSOR)
    blocks, groups = lax.axis_size(TENSOR), lax.axis_size(DP)
    first_half = layer == 0
    micro, rows, model = tokens_in.shape
    shard_rows = in_value.shape[1]
    half = in_value.shape[2] // 2
    heads = step_bias.shape[1] // 2
    head_dim = half // heads
    width = half * blocks
    all_heads = heads * blocks
    states = in_state.shape[2]

    row = jnp.arange(2 * HALO)[:, None]
    head = jnp.arange(2 * heads)[None, :]
    step_rows = (row == head // heads * HALO + lax.rem(head, heads)).astype(BF)
    step_shard = nt(step_rows, in_step[0]).astype(BF)
    both = jnp.concatenate([step_bias.reshape(2, heads), decay_log.reshape(2, heads)], axis=1)
    per_head = jnp.pad(both, ((0, 0), (0, half - 2 * heads))).reshape(1, 2 * half)
    skip = jnp.repeat(skip_gain, head_dim, axis=1)
    channel = jnp.concatenate([conv_value[0], bias_value, gate_gain, skip, per_head], axis=0)
    state_row = jnp.concatenate([conv_state[0].reshape(1, -1), bias_state], axis=1)
    shared = jnp.concatenate([norm_gain, jnp.pad(state_row, ((0, 6), (0, model - 5 * states))), norm_gain], axis=0)

    valid = block * rows + jnp.arange(rows)[None, :] < lengths[:, None]
    mask = jnp.broadcast_to(valid.astype(F32)[:, :, None], (micro, rows, LANES))

    shards = (in_value[0], in_gate[0], out_proj[0], step_shard, in_state[0])
    (wv, wg, wo, wt, ws, pv, ps, ph, pn, out, low_out, mix, inv, nx, vpre, spre, x, bc, dtc, gate, y, gg, s_in) = forward_call(
        tokens_in, mask, shards, channel, shared, blocks, groups, head_dim
    )
    places = step_places(blocks, wt.shape[1], all_heads).astype(BF)
    step_w = jnp.stack([tn(places, wt[q]).astype(BF) for q in range(2)])
    w = Bundle(value=wv, gate=wg, out=wo, state=ws, step=step_w)
    par = Bundle(value=pv, head=ph, state=ps, norm=pn)
    kept = Bundle(
        inv=inv.reshape(2, micro, rows, LANES),
        mix=mix.reshape(2, micro, rows, model),
        vpre=vpre,
        spre=spre,
        x=x,
        bc=bc,
        dtc=dtc,
        gate=gate,
        y=y,
        s_in=s_in,
    )
    grads, dval, dgate, dst, dstep, sgm, vsums, ssums, hsums, nsums = backward_fused_call(
        cotangent, tokens_in, low_out, mask, kept, w, par, blocks, head_dim
    )

    def long(value, q):
        return value[q].reshape(micro * rows, value.shape[3])

    lane = jnp.arange(LANES)[:, None]
    by_block = (8 * (lane // heads) + lax.rem(lane, heads) == jnp.arange(LANES)[None, :]) & (lane < all_heads)
    pack, turned = [], []
    for q in range(2):
        normed = long(nx, q)
        turned.append(tn(long(dst, q), normed))
        step_lanes = nn(long(dstep, q), by_block.astype(BF)).astype(BF)
        step_grad = tn(step_lanes[:, : 8 * blocks], normed)
        ssum, hsum = jnp.sum(ssums[q], axis=0), jnp.sum(hsums[q], axis=0)
        rest = [
            nsums[q, 0][None],
            jnp.pad(ssum[:5].reshape(1, -1), ((0, 0), (0, width - 5 * states))),
            jnp.zeros((6, width), F32),
        ]
        hsum = hsum[:2, :all_heads].reshape(2, blocks, heads).transpose(1, 0, 2).reshape(blocks, 2 * heads)
        hsum = jnp.pad(hsum, ((0, 0), (0, half - 2 * heads))).reshape(1, width)
        pack.append(jnp.concatenate([jnp.sum(vsums[q], axis=0)[:7], hsum, step_grad] + rest, axis=0))
    turned = lax.psum_scatter(
        jnp.concatenate(turned, axis=0), (PIPE, DP, TENSOR), scatter_dimension=0, tiled=True
    )
    pack = jnp.stack(pack)
    factors = (nx, sgm, dval, dgate, gg)
    large, chan, step_grad, rest = reduce_call(factors, pack, blocks, groups)
    grad_value, grad_gate, grad_out = [large[w].astype(F32) for w in range(3)]

    step_grad = step_grad.reshape(2, 8, shard_rows)[:, :heads].reshape(2 * heads, shard_rows).T
    grad_state = turned.T
    position = group * blocks + block
    ranks = groups * blocks

    def share(value):
        size = value.shape[-1] // ranks
        return lax.dynamic_slice_in_dim(value, position * size, size, value.ndim - 1)

    head_sums = chan[7].reshape(2, half)[:, : 2 * heads].reshape(2, 2, heads).transpose(1, 0, 2).reshape(2, -1)
    norm_sum = share(rest[0])
    conv_sum = share(rest[1, : 5 * states].reshape(5, states))
    return (
        out[None],
        grads[None],
        grad_gate[None],
        grad_value[None],
        grad_state[None],
        step_grad[None],
        grad_out[None],
        norm_sum[None],
        chan[None, :4],
        conv_sum[None, :4],
        chan[None, 4],
        conv_sum[None, 4],
        head_sums[None, 0],
        head_sums[None, 1],
        jnp.sum(chan[6].reshape(2 * heads, head_dim), axis=1)[None],
        chan[None, 5],
    )


def body(
    tokens_in,
    cotangent,
    lengths,
    in_gate,
    in_value,
    in_state,
    in_step,
    out_proj,
    norm_gain,
    conv_value,
    conv_state,
    bias_value,
    bias_state,
    step_bias,
    decay_log,
    skip_gain,
    gate_gain,
):
    layer = lax.axis_index(PIPE)
    block = lax.axis_index(TENSOR)
    blocks = lax.axis_size(TENSOR)
    group = lax.axis_index(DP)
    groups = lax.axis_size(DP)
    first_half = layer == 0
    micro, rows, model = tokens_in.shape
    shard_rows = in_value.shape[1]
    half = in_value.shape[2] // 2
    heads = step_bias.shape[1] // 2
    head_dim = half // heads
    width = half * blocks
    all_heads = heads * blocks
    states = in_state.shape[2]
    state = states // 2
    inner_total = 2 * width

    def halves(value):
        keep = lax.dynamic_slice_in_dim(value, layer * half_of(value), half_of(value), value.ndim - 1)
        send = lax.dynamic_slice_in_dim(value, (1 - layer) * half_of(value), half_of(value), value.ndim - 1)
        return by_layer(keep, swap_pipe(send))

    def half_of(value):
        return value.shape[-1] // 2

    def by_layer(own, other):
        return jnp.where(first_half, own, other), jnp.where(first_half, other, own)

    channel = jnp.concatenate([conv_value[0], bias_value, gate_gain], axis=0)
    channel_both = halves(channel)
    head_both = halves(jnp.concatenate([step_bias, decay_log, skip_gain], axis=0))
    flat_heads = [jnp.pad(v.reshape(1, 3 * heads), ((0, 0), (0, half - 3 * heads))) for v in head_both]
    packed = gather_tensor(jnp.concatenate(list(channel_both) + flat_heads + [jnp.zeros((2, half), F32)], axis=0))
    shared = jnp.concatenate([norm_gain[0], conv_state[0].reshape(-1), bias_state[0]], axis=0)
    shared_both = by_layer(shared, swap_pipe(shared))
    params = []
    for q in range(2):
        per_head = packed[12 + q].reshape(blocks, half)[:, : 3 * heads].reshape(blocks, 3, heads)
        per_head = per_head.transpose(1, 0, 2).reshape(3, all_heads)
        skip = jnp.repeat(per_head[2:3], head_dim, axis=1)
        value_par = jnp.concatenate([packed[6 * q : 6 * q + 6], skip, jnp.zeros((1, width), F32)], axis=0)
        head_par = jnp.pad(per_head, ((0, 5), (0, LANES - all_heads)))
        state_par = jnp.concatenate(
            [
                shared_both[q][model : model + 4 * states].reshape(4, states),
                shared_both[q][model + 4 * states :].reshape(1, states),
                jnp.zeros((3, states), F32),
            ],
            axis=0,
        )
        params.append(Bundle(value=value_par, head=head_par, state=state_par, norm=shared_both[q][:model]))

    step_both = halves(in_step[0])
    step_all = gather_tensor(jnp.concatenate(step_both, axis=1)).reshape(shard_rows, blocks, 2, heads)
    state_both = by_layer(in_state[0], swap_pipe(in_state[0]))
    value_both, gate_both, out_both = halves(in_value[0]), halves(in_gate[0]), halves(out_proj[0])
    weights = []
    for q in range(2):
        step_q = jnp.pad(step_all[:, :, q].reshape(shard_rows, all_heads), ((0, 0), (0, LANES - all_heads)))
        small = gather_dp(jnp.concatenate([state_both[q], step_q], axis=1))
        weights.append(
            Bundle(
                state=small[:, :states],
                step=small[:, states:],
                value=gather_dp(gather_tensor(value_both[q])),
                gate=gather_dp(gather_tensor(gate_both[q])),
                out=gather_dp(gather_tensor(out_both[q])),
            )
        )

    masks = [
        (block * rows + jnp.arange(rows) < lengths[s]).astype(F32)[:, None] for s in range(micro)
    ]

    def forward(u, s, q):
        w, par = weights[q], params[q]
        ext = jnp.concatenate([shift_tensor(u[-HALO:], 1), u], axis=0).astype(F32)
        root_inv = lax.rsqrt(jnp.mean(ext * ext, axis=1, keepdims=True) + EPS)
        nx = (ext * root_inv * par.norm[None, :]).astype(BF)
        vpre, spre, x, bc, dtc, yw, loc = front_call(nx, w, par, head_dim, state)
        through = jnp.repeat(jnp.exp(dtc[1, rows - 1, :all_heads]), head_dim)[:, None]
        s_in = jnp.zeros((width, state), BF)
        for k in range(1, blocks):
            sent = (through * s_in.astype(F32) + loc).astype(BF)
            got = lax.ppermute(sent, TENSOR, [(k - 1, k)])
            s_in = got if k == 1 else jnp.where(block == k, got, s_in)
        gate, y, gg, part, squares = finish_call(nx, w, par, yw, s_in, bc, dtc, head_dim)
        total = squares[:, 0]
        total = total + swap_pipe(total)
        inverse = lax.rsqrt(total / inner_total + EPS)[:, None]
        mixed = inverse * (part.astype(F32) + swap_pipe(part).astype(F32))
        result = (masks[s] * (u.astype(F32) + mixed)).astype(BF)
        kept = Bundle(
            u=u, nx=nx, root_inv=root_inv[HALO:], vpre=vpre, spre=spre, x=x, bc=bc, dtc=dtc, s_in=s_in, through=through,
            gate=gate, y=y, gg=gg, inverse=inverse, mixed=mixed,
        )
        return result, kept

    def backward(incoming, s, q, kept):
        w, par = weights[q], params[q]
        gm = (masks[s] * incoming.astype(F32)).astype(BF)
        gmf = gm.astype(F32)
        inverse = kept.inverse
        dot = jnp.sum(gmf * kept.mixed, axis=1, keepdims=True)
        shrink = inverse * inverse * dot / inner_total
        rowsc = jnp.concatenate([inverse, shrink, jnp.zeros((rows, LANES - 2), F32)], axis=1)
        dy, dgate, dsl, dgain = gate_call(gm, w, par, kept.y, kept.gate, rowsc, kept.bc, kept.dtc, head_dim)
        g_in = jnp.zeros((width, state), BF)
        for k in range(blocks - 2, -1, -1):
            sent = (kept.through * g_in.astype(F32) + dsl).astype(BF)
            got = lax.ppermute(sent, TENSOR, [(k + 1, k)])
            g_in = got if k == blocks - 2 else jnp.where(block == k, got, g_in)
        dconv, dsc, dstep, vsums, ssums, hsums = backward_call(
            dy, kept.x, kept.vpre, kept.spre, kept.bc, kept.dtc, kept.s_in, g_in, par, head_dim
        )
        halo = shift_tensor(jnp.concatenate([dconv[:8], dsc[:8]], axis=1), -1)
        dval, dst, part = conv_call(dconv, halo, dsc, dgate, dstep, w, par)
        grad_normed = part.astype(F32) + swap_pipe(part).astype(F32)
        uf, root_inv = kept.u.astype(F32), kept.root_inv
        grad_norm = jnp.sum(grad_normed * uf * root_inv, axis=0)
        weighted = grad_normed * par.norm[None, :]
        grad_u = root_inv * weighted - uf * root_inv**3 * jnp.mean(weighted * uf, axis=1, keepdims=True) + gmf
        scaled_gm = (gmf * inverse).astype(BF)
        channel_sums = jnp.concatenate([vsums[:5], dgain[:1], vsums[5:6]], axis=0)
        sums = (channel_sums, ssums[:5], hsums[:2, :all_heads], grad_norm)
        return grad_u.astype(BF), (dval, dgate, dst, dstep, scaled_gm), sums

    outs, kept = [], []
    current = [tokens_in[s] for s in range(micro)]
    for q in range(2):
        pairs = [forward(current[s], s, q) for s in range(micro)]
        current = [pair[0] for pair in pairs]
        outs.append(jnp.stack(current))
        kept.append([pair[1] for pair in pairs])

    grads = [None, None]
    reduced = [None, None]
    incoming = [cotangent[s] for s in range(micro)]
    for q in (1, 0):
        results = [backward(incoming[s], s, q, kept[q][s]) for s in range(micro)]
        incoming = [r[0] for r in results]
        grads[q] = jnp.stack(incoming)
        stacked = [jnp.concatenate([r[1][k] for r in results], axis=0) for k in range(5)]
        dval, dgate, dst, dstep, scaled_gm = stacked
        normed = jnp.concatenate([kept[q][s].nx[HALO:] for s in range(micro)], axis=0)
        gg = jnp.concatenate([kept[q][s].gg for s in range(micro)], axis=0)
        sums = [functools.reduce(jnp.add, [r[2][k] for r in results]) for k in range(4)]

        big = [tn(scaled_gm, gg).astype(BF), tn(normed, dgate).astype(BF), tn(normed, dval).astype(BF)]
        big = [reduce_tensor(take_cols(reduce_dp(v))) for v in big]
        turned = reduce_dp(tn(dst, normed).astype(BF))
        turned = reduce_tensor(take_first(turned.reshape(blocks, -1, model)))
        step_grad = tn(dstep, normed)[:all_heads]
        by_block = jnp.concatenate(
            [
                sums[0].reshape(7, blocks, half).transpose(1, 0, 2).reshape(blocks, -1),
                step_grad.reshape(blocks, -1),
                sums[2].reshape(2, blocks, heads).transpose(1, 0, 2).reshape(blocks, -1),
            ],
            axis=1,
        )
        per_block = reduce_tensor(take_first(sum_all_dp(by_block)))
        common = sum_all_tensor(sum_all_dp(jnp.concatenate([sums[1].reshape(-1), sums[3]], axis=0)))
        reduced[q] = (big, turned, per_block, common)

    def own_and_other(kind):
        return jnp.where(first_half, kind(0), kind(1)), jnp.where(first_half, kind(1), kind(0))

    def join(kind):
        own, other = own_and_other(kind)
        got = swap_pipe(other)
        return jnp.where(first_half, own, got), jnp.where(first_half, got, own)

    def columns(k):
        low, high = join(lambda q: reduced[q][0][k].astype(BF))
        return jnp.concatenate([low, high], axis=1).astype(F32)

    grad_out, grad_gate, grad_value = columns(0), columns(1), columns(2)
    own, other = own_and_other(lambda q: reduced[q][1])
    grad_state = (own + swap_pipe(other.astype(BF)).astype(F32)).T
    low, high = join(lambda q: reduced[q][2])
    cut1, cut2 = 7 * half, 7 * half + heads * model
    chan = jnp.concatenate([low[:cut1].reshape(7, half), high[:cut1].reshape(7, half)], axis=1)
    step_grad = jnp.concatenate([low[cut1:cut2].reshape(heads, model), high[cut1:cut2].reshape(heads, model)], axis=0)
    step_grad = lax.dynamic_slice_in_dim(step_grad, group * shard_rows, shard_rows, 1).T
    head_sums = jnp.concatenate([low[cut2:].reshape(2, heads), high[cut2:].reshape(2, heads)], axis=1)
    own, other = own_and_other(lambda q: reduced[q][3])
    conv_sum = own[: 5 * states] + swap_pipe(other[: 5 * states])
    norm_sum = own[5 * states :]
    position = group * blocks + block
    ranks = groups * blocks

    def share(value):
        size = value.shape[-1] // ranks
        return lax.dynamic_slice_in_dim(value, position * size, size, value.ndim - 1)

    conv_sum = share(conv_sum.reshape(5, states))
    return (
        jnp.where(first_half, outs[0], outs[1])[None],
        jnp.where(first_half, grads[0], grads[1])[None],
        grad_gate[None],
        grad_value[None],
        grad_state[None],
        step_grad[None],
        grad_out[None],
        share(norm_sum)[None],
        chan[None, :4],
        conv_sum[None, :4],
        chan[None, 4],
        conv_sum[None, 4],
        head_sums[None, 0],
        head_sums[None, 1],
        jnp.sum(chan[6].reshape(2 * heads, head_dim), axis=1)[None],
        chan[None, 5],
    )


def solution(mesh):
    in_specs = (
        P(DP, TENSOR, None),
        P(DP, TENSOR, None),
        P(DP),
        P(PIPE, DP, TENSOR),
        P(PIPE, DP, TENSOR),
        P(PIPE, DP, None),
        P(PIPE, DP, TENSOR),
        P(PIPE, DP, TENSOR),
        P(PIPE, None),
        P(PIPE, None, TENSOR),
        P(PIPE, None, None),
        P(PIPE, TENSOR),
        P(PIPE, None),
        P(PIPE, TENSOR),
        P(PIPE, TENSOR),
        P(PIPE, TENSOR),
        P(PIPE, TENSOR),
    )
    out_specs = (
        P(PIPE, DP, TENSOR, None),
        P(PIPE, DP, TENSOR, None),
        P(PIPE, DP, TENSOR),
        P(PIPE, DP, TENSOR),
        P(PIPE, None, (DP, TENSOR)),
        P(PIPE, DP, TENSOR),
        P(PIPE, DP, TENSOR),
        P(PIPE, (DP, TENSOR)),
        P(PIPE, None, TENSOR),
        P(PIPE, None, (DP, TENSOR)),
        P(PIPE, TENSOR),
        P(PIPE, (DP, TENSOR)),
        P(PIPE, TENSOR),
        P(PIPE, TENSOR),
        P(PIPE, TENSOR),
        P(PIPE, TENSOR),
    )

    def program(*args):
        columns = args[4].shape[2] // mesh.shape[TENSOR]
        fused = mesh.shape[DP] == 4 and mesh.shape[TENSOR] > 2 and columns // 2 % LANES == 0
        return mapped(fused_body if fused else body)(*args)

    def mapped(function):
        return jax.shard_map(function, mesh=mesh, in_specs=in_specs, out_specs=out_specs, check_vma=False)

    return program
```
